32 devices in a mesh: dp: 4 (over z), ctx: 2 (over core), tensor: 4 (over y, x).
Axes of the slice: x: 2, y: 2, z: 4, core: 2. Of those that a mesh axis runs over, the one named last changes fastest.
Arguments:
- tokens: bfloat16 [4, 4096, 1024], P('dp', 'ctx'), may hold values from -6 to 6
- doc_ids: int32 [4, 4096], P('dp'), may hold values from 0 to 2, never falling along the last dimension, each value on 1 to 3072 neighbouring positions
- norm_gain: float32 [1024], replicated, may hold values from 0.5 to 1.5
- q_proj: bfloat16 [1024, 512], P(None, 'tensor'), may hold values from -0.1875 to 0.1875
- key_value_weight: bfloat16 [1024, 256], replicated, may hold values from -0.1875 to 0.1875
- o_proj: bfloat16 [512, 1024], P('tensor'), may hold values from -2 to 2
- z_proj: bfloat16 [1024, 1536], P(None, 'tensor'), may hold values from -0.1875 to 0.1875
- x_proj: bfloat16 [1024, 1536], P(None, 'tensor'), may hold values from -0.1875 to 0.1875
- dt_proj: bfloat16 [1024, 24], P(None, 'tensor'), may hold values from -0.1875 to 0.1875
- bc_proj: bfloat16 [1024, 256], replicated, may hold values from -0.1875 to 0.1875
- conv_x: float32 [4, 1536], P(None, 'tensor'), may hold values from -3 to 3
- xconv_bias: float32 [1536], P('tensor'), may hold values from -0.5 to 0.5
- conv_bc: float32 [4, 256], replicated, may hold values from -3 to 3
- bcconv_bias: float32 [256], replicated, may hold values from -0.5 to 0.5
- dt_bias: float32 [24], P('tensor'), may hold values from -1 to 1
- a_log: float32 [24], P('tensor'), may hold values from -13 to -2.99
- skip_gain: float32 [24], P('tensor'), may hold values from 0.5 to 1.5
- gated_gain: float32 [1536], P('tensor'), may hold values from 0.5 to 1.5
- out_proj: bfloat16 [1536, 1024], P('tensor'), may hold values from -0.15625 to 0.15625
- mlp_gain: float32 [1024], replicated, may hold values from 0.5 to 1.5
- gate_proj: bfloat16 [1024, 2048], P(None, 'tensor'), may hold values from -0.1875 to 0.1875
- up_proj: bfloat16 [1024, 2048], P(None, 'tensor'), may hold values from -0.1875 to 0.1875
- down_proj: bfloat16 [2048, 1024], P('tensor'), may hold values from -0.125 to 0.125
- out_grad: bfloat16 [4, 4096, 1024], P('dp', 'ctx'), may hold values from -6 to 6
Outputs:
- layer_out: bfloat16 [4, 4096, 1024], P('dp', 'ctx')
- tokens_grad: bfloat16 [4, 4096, 1024], P('dp', 'ctx')
- norm_gain_grad: float32 [1024], replicated
- q_proj_grad: float32 [1024, 512], P(None, 'tensor')
- kv_proj_grad: float32 [1024, 256], replicated
- o_proj_grad: float32 [512, 1024], P('tensor')
- z_proj_grad: float32 [1024, 1536], P(None, 'tensor')
- x_proj_grad: float32 [1024, 1536], P(None, 'tensor')
- dt_proj_grad: float32 [1024, 24], P(None, 'tensor')
- bc_proj_grad: float32 [1024, 256], replicated
- conv_x_grad: float32 [4, 1536], P(None, 'tensor')
- xconv_bias_grad: float32 [1536], P('tensor')
- conv_bc_grad: float32 [4, 256], replicated
- bcconv_bias_grad: float32 [256], replicated
- dt_bias_grad: float32 [24], P('tensor')
- a_log_grad: float32 [24], P('tensor')
- skip_gain_grad: float32 [24], P('tensor')
- gated_gain_grad: float32 [1536], P('tensor')
- out_proj_grad: float32 [1536, 1024], P('tensor')
- mlp_gain_grad: float32 [1024], replicated
- gate_proj_grad: float32 [1024, 2048], P(None, 'tensor')
- up_proj_grad: float32 [1024, 2048], P(None, 'tensor')
- down_proj_grad: float32 [2048, 1024], P('tensor')
The draws below stay inside these ranges and needn't reach their ends.
Inputs may be any that keep to these rules, and one draw needn't show every extreme that they name: Along each sequence doc_ids never fall; every document covers 1 to 3072 positions and one covers exactly 3072.
All inputs are finite; a program needn't handle non-finite values.
Results may differ from the reference program's by a relative error of at most 0.034.
Values may be sent and summed in bfloat16 or wider, within the bound.
No kernel may reach another device: no remote copies, remote signals or barrier semaphores. Data moves between devices by JAX's collectives and lax.ppermute only.
A program may use at most 320 MiB of HBM per device.

```python
import math
import jax
import jax.numpy as jnp
import numpy as np
from jax import lax

D = 1024
QUERY_HEADS = 8
KEY_VALUE_HEADS = 2
HEAD_SIZE = 64
MH = 24
MP = 64
NS = 128
KC = 4
FF = 2048
QCH = 128
ABLK = 512
DOCS = 3
SEQ = 4096
BATCH = 4
DOC_MOST = 3072


def draw_a_log(key, part):
    level = jax.random.uniform(key, (MH,), jnp.float32)
    lowest = jnp.log(0.02 / SEQ)
    highest = jnp.log(0.05)
    return lowest + (highest - lowest) * level


def levels(stream_key, dims, shards, least, top_value):
    loudness, own = 1.0, jax.random.fold_in(stream_key, 6)
    for dim, blocks in shards:
        heights = jnp.exp(jax.random.uniform(jax.random.fold_in(own, dim), (blocks,), jnp.float32, least / len(shards), top_value / len(shards)))
        loudness = loudness * jnp.repeat(heights, dims[dim] // blocks).reshape([-1 if axis == dim else 1 for axis in range(len(dims))])
    return loudness


def split_up(count, total, most, slope):
    weights = [(1 << 20) // math.isqrt(rank ** slope) + 1 for rank in range(2, count + 1)]
    spare, holding = total - most - (count - 1), [1] * (count - 1)
    while spare > 0:
        movable = [i for i in range(count - 1) if holding[i] < most]
        pool, remaining = sum([weights[i] for i in movable]), spare
        for i in movable:
            extra = min(most - holding[i], max(1, remaining * weights[i] // pool), spare)
            holding[i] = holding[i] + extra
            spare = spare - extra
    return np.array([most] + holding)


def uneven_parts(key, count, total, limit, slope):
    if count == 2:
        one = jax.random.randint(key, (), max(1, total - limit), min(limit, total - 1) + 1)
        return jnp.stack([one, total - one])
    lengths = jnp.asarray(split_up(count, total, limit, slope), jnp.int32)
    pairs = (count - 1) // 2
    source_of, sink = lengths[1:1 + 2 * pairs:2], lengths[2:2 + 2 * pairs:2]
    room = jnp.minimum(source_of - 1, limit - sink)
    moved = jax.random.randint(jax.random.fold_in(key, 1), (pairs,), 0, 1 << 20) % (room + 1)
    lengths = lengths.at[1:1 + 2 * pairs:2].set(source_of - moved).at[2:2 + 2 * pairs:2].set(sink + moved)
    return lengths[jax.random.permutation(jax.random.fold_in(key, 2), count)]


def noise(stream_key, shape, width, limit, cuts=(), held_as=jnp.bfloat16):
    drawn = jax.random.normal(stream_key, shape, jnp.float32) * width
    if len(cuts) > 0:
        drawn = levels(stream_key, shape, cuts, -0.22, 0.18) * drawn
    return jnp.clip(drawn, min=-limit, max=limit).astype(held_as)


def setup_inputs(seed: int = 0) -> dict:
    seeds = jax.random.split(jax.random.key(seed), 25)
    return {
        "tokens": noise(seeds[0], (BATCH, SEQ, D), 1.0, 6.0, ((0, 4), (1, 2))),
        "doc_ids": jax.vmap(lambda own: jnp.searchsorted(jnp.cumsum(uneven_parts(own, DOCS, SEQ, DOC_MOST, 0)), jnp.arange(SEQ), side="right"))(jax.random.split(seeds[1], BATCH)).reshape((BATCH, SEQ)).astype(jnp.int32),
        "norm_gain": jnp.clip(1.0 + 0.1 * jax.random.normal(seeds[2], (D,), jnp.float32), 0.5, 1.5),
        "q_proj": noise(seeds[3], (D, QUERY_HEADS * HEAD_SIZE), D ** -0.5, 0.1875, ((1, 4),)),
        "key_value_weight": noise(seeds[4], (D, 2 * KEY_VALUE_HEADS * HEAD_SIZE), D ** -0.5, 0.1875),
        "o_proj": noise(seeds[5], (QUERY_HEADS * HEAD_SIZE, D), 8 ** -0.5, 2.0, ((0, 4),)),
        "z_proj": noise(seeds[6], (D, MH * MP), D ** -0.5, 0.1875, ((1, 4),)),
        "x_proj": noise(seeds[7], (D, MH * MP), D ** -0.5, 0.1875, ((1, 4),)),
        "dt_proj": noise(seeds[8], (D, MH), D ** -0.5, 0.1875, ((1, 4),)),
        "bc_proj": noise(seeds[9], (D, 2 * NS), D ** -0.5, 0.1875),
        "conv_x": noise(seeds[10], (KC, MH * MP), 0.5, 3.0, ((1, 4),), jnp.float32),
        "xconv_bias": jnp.clip(jax.random.uniform(seeds[11], (MH * MP,), jnp.float32, -0.5, 0.5) * levels(seeds[11], (MH * MP,), ((0, 4),), -0.4, 0.0), -0.5, 0.5),
        "conv_bc": noise(seeds[12], (KC, 2 * NS), 0.5, 3.0, (), jnp.float32),
        "bcconv_bias": jnp.clip(jax.random.uniform(seeds[13], (2 * NS,), jnp.float32, -0.5, 0.5), -0.5, 0.5),
        "dt_bias": jnp.clip(jax.random.uniform(seeds[14], (MH,), jnp.float32, -1.0, 1.0) * levels(seeds[14], (MH,), ((0, 4),), -0.4, 0.0), -1.0, 1.0),
        "a_log": draw_a_log(jax.random.fold_in(seeds[24], 71), 0),
        "skip_gain": jnp.clip(0.5 + 1.0 * jax.random.uniform(seeds[16], (MH,), jnp.float32) ** levels(seeds[16], (MH,), ((0, 4),), -0.2, 0.2), 0.5, 1.5),
        "gated_gain": jnp.clip(1.0 + 0.1 * jax.random.normal(seeds[17], (MH * MP,), jnp.float32), 0.5, 1.5),
        "out_proj": noise(seeds[18], (MH * MP, D), (MH * MP) ** -0.5, 0.15625, ((0, 4),)),
        "mlp_gain": jnp.clip(1.0 + 0.1 * jax.random.normal(seeds[19], (D,), jnp.float32), 0.5, 1.5),
        "gate_proj": noise(seeds[20], (D, FF), D ** -0.5, 0.1875, ((1, 4),)),
        "up_proj": noise(seeds[21], (D, FF), D ** -0.5, 0.1875, ((1, 4),)),
        "down_proj": noise(seeds[22], (FF, D), FF ** -0.5, 0.125, ((0, 4),)),
        "out_grad": noise(seeds[23], (BATCH, SEQ, D), 1.0, 6.0, ((0, 4), (1, 2))),
    }


HIGHEST = lax.Precision.HIGHEST
EPSILON = 1e-05
ROPE_BASE = 100000000000.0
WEIGHT_NAMES = ('norm_gain', 'q_proj', 'kv_proj', 'o_proj', 'z_proj', 'x_proj', 'dt_proj', 'bc_proj', 'conv_x', 'xconv_bias', 'conv_bc', 'bcconv_bias', 'dt_bias', 'a_log', 'skip_gain', 'gated_gain', 'out_proj', 'mlp_gain', 'gate_proj', 'up_proj', 'down_proj')

@jax.custom_vjp
def low(v):
    return lax.optimization_barrier(v.astype(jnp.bfloat16)).astype(jnp.float32)

@jax.custom_vjp
def low_back(v):
    return v

def low_keep(v):
    return (low(v), None)

def low_pass(kept, grad):
    return (grad,)

def back_keep(v):
    return (v, None)

def back_low(kept, grad):
    return (low(grad),)
low.defvjp(low_keep, low_pass)
low_back.defvjp(back_keep, back_low)

def matrix_multiply(left_side, right_side):
    return jnp.dot(left_side, right_side, precision=HIGHEST)

def rms_scale(values):
    return lax.rsqrt(lax.optimization_barrier(jnp.mean(values * values, axis=-1, keepdims=True)) + EPSILON)

def rope_tables(positions, head_width):
    exponent = jnp.arange(0, head_width, 2).astype(jnp.int32).astype(jnp.float32) / head_width
    frequency = ROPE_BASE ** (-exponent)
    angles = positions.astype(jnp.float32)[:, None] * frequency[None, :]
    angles = jnp.concatenate([angles, angles], axis=-1)
    return (jnp.cos(angles), jnp.sin(angles))

def rotate(values, cos_table, sine_table):
    half_dim = values.shape[-1] // 2
    turned = jnp.concatenate([-values[..., half_dim:], values[..., :half_dim]], axis=-1)
    return values * cos_table + turned * sine_table

def conv_silu(extended, doc_ext, weight, conv_bias):
    tap_count = weight.shape[0]
    count_of_rows = extended.shape[0] - tap_count + 1
    current = doc_ext[tap_count - 1:]
    summed = jnp.zeros((count_of_rows, extended.shape[1]), extended.dtype) + conv_bias[None, :]
    for tap_idx in range(tap_count):
        same_doc = (doc_ext[tap_idx:tap_idx + count_of_rows] == current).astype(extended.dtype)
        summed = summed + weight[tap_idx][None, :] * extended[tap_idx:tap_idx + count_of_rows] * same_doc[:, None]
    return jax.nn.silu(summed)

def ssd_local(x_conv, b_mat, c_mat, log_decay, dt_vals, doc_vals, doc_prev, block_len):
    count_of_rows, head_count, head_dim = x_conv.shape
    block_count = count_of_rows // block_len
    x_blocks = x_conv.reshape(block_count, block_len, head_count, head_dim)
    b_blocks = b_mat.reshape(block_count, block_len, -1)
    c_blocks = c_mat.reshape(block_count, block_len, -1)
    decay_blk = log_decay.reshape(block_count, block_len, head_count)
    dt_blk = dt_vals.reshape(block_count, block_len, head_count)
    doc_blk = doc_vals.reshape(block_count, block_len)
    cumul = jnp.cumsum(decay_blk, axis=1)
    order_idx = jnp.arange(block_len).astype(jnp.int32)
    causal = order_idx[:, None] >= order_idx[None, :]
    allowed = causal[None] & (doc_blk[:, :, None] == doc_blk[:, None, :])
    gap_vals = cumul[:, :, None, :] - cumul[:, None, :, :]
    mask_float = allowed[..., None].astype(x_conv.dtype)
    decay = jnp.exp(jnp.where(allowed[..., None], gap_vals, 0.0)) * mask_float
    inner_prod = jnp.einsum('kin,kjn->kij', c_blocks, b_blocks, precision=HIGHEST)
    x_scaled = x_blocks * dt_blk[..., None]
    weights = inner_prod[..., None] * decay
    y_intra = jnp.einsum('kijh,kjhp->kihp', weights, x_scaled, precision=HIGHEST)
    last_doc = doc_blk[:, -1]
    same_end = (doc_blk == last_doc[:, None]).astype(x_conv.dtype)
    end_weight = jnp.exp(cumul[:, -1:, :] - cumul) * same_end[..., None]
    states = jnp.einsum('kjhp,kjn->khpn', end_weight[..., None] * x_scaled, b_blocks, precision=HIGHEST)
    prev_doc = jnp.concatenate([jnp.reshape(doc_prev, (1,)).astype(jnp.int32), last_doc[:-1].astype(jnp.int32)])
    carry_keep = jnp.exp(cumul[:, -1, :]) * (last_doc == prev_doc).astype(x_conv.dtype)[:, None]

    def advance(state_now, scan_item):
        factor, fresh_state = scan_item
        return (factor[:, None, None] * state_now + fresh_state, state_now)
    zero_state = jnp.zeros(states.shape[1:], x_conv.dtype)
    final, entering = lax.scan(advance, zero_state, (carry_keep, states))
    enter_w = jnp.exp(cumul) * (doc_blk == prev_doc[:, None]).astype(x_conv.dtype)[..., None]
    y_inter = jnp.einsum('kihn,khpn->kihp', enter_w[..., None] * c_blocks[:, :, None, :], entering, precision=HIGHEST)
    outputs = (y_intra + y_inter).reshape(count_of_rows, head_count, head_dim)
    block_sums = cumul[:, -1, :]
    offsets = jnp.cumsum(block_sums, axis=0) - block_sums
    total_cum = (cumul + offsets[:, None, :]).reshape(count_of_rows, head_count)
    reach = jnp.exp(total_cum) * (doc_vals == doc_prev).astype(x_conv.dtype)[:, None]
    return (outputs, final, reach[-1], reach)

def attention_branch(normalized_input, doc_row, parameters):
    count_of_rows = normalized_input.shape[0]
    positions = jnp.arange(count_of_rows).astype(jnp.int32)
    cos_table, sine_table = rope_tables(positions, HEAD_SIZE)
    queries = low_back(matrix_multiply(normalized_input, parameters['q_proj'])).reshape(count_of_rows, QUERY_HEADS, HEAD_SIZE)
    queries = low(rotate(queries, cos_table[:, None, :], sine_table[:, None, :]))
    key_value_before_rotary = matrix_multiply(normalized_input, parameters['kv_proj']).reshape(count_of_rows, 2, KEY_VALUE_HEADS, HEAD_SIZE)
    keys_rot = low(rotate(key_value_before_rotary[:, 0], cos_table[:, None, :], sine_table[:, None, :]))
    values = low(key_value_before_rotary[:, 1])
    query_group_size = QUERY_HEADS // KEY_VALUE_HEADS
    keys_all = jnp.repeat(keys_rot, query_group_size, axis=1)
    values_all = jnp.repeat(values, query_group_size, axis=1)
    score_scale = HEAD_SIZE ** (-0.5)

    def attend(block_args):
        query_blk, pos_blk, doc_blk = block_args
        scores = low_back(jnp.einsum('qhd,khd->hqk', query_blk, keys_all, precision=HIGHEST) * score_scale)
        allowed = (pos_blk[:, None] >= positions[None, :]) & (doc_blk[:, None] == doc_row[None, :])
        scores = jnp.where(allowed[None], scores, -1e+30)
        probs = low(jax.nn.softmax(scores, axis=-1))
        return low_back(low(jnp.einsum('hqk,khd->qhd', probs, values_all, precision=HIGHEST)))
    block_count = count_of_rows // ABLK
    attended = lax.map(jax.checkpoint(attend), (queries.reshape(block_count, ABLK, QUERY_HEADS, HEAD_SIZE), positions.reshape(block_count, ABLK), doc_row.reshape(block_count, ABLK)))
    return matrix_multiply(attended.reshape(count_of_rows, QUERY_HEADS * HEAD_SIZE), parameters['o_proj'])

def mamba_branch(normalized_input, doc_row, parameters):
    count_of_rows = normalized_input.shape[0]
    gate_pre = low_back(matrix_multiply(normalized_input, parameters['z_proj']))
    x_part = low_back(low(matrix_multiply(normalized_input, parameters['x_proj'])))
    dt_raw = low_back(matrix_multiply(normalized_input, parameters['dt_proj']))
    bc_part = low(matrix_multiply(normalized_input, parameters['bc_proj']))
    conv_in = jnp.concatenate([x_part, bc_part], axis=1)
    extended = jnp.concatenate([jnp.zeros((KC - 1, conv_in.shape[1]), conv_in.dtype), conv_in], axis=0)
    doc_ext = jnp.concatenate([jnp.full((KC - 1,), -1, jnp.int32), doc_row.astype(jnp.int32)])
    conv_weight = jnp.concatenate([parameters['conv_x'], parameters['conv_bc']], axis=1)
    conv_bias = jnp.concatenate([parameters['xconv_bias'], parameters['bcconv_bias']])
    conv_out = conv_silu(extended, doc_ext, conv_weight, conv_bias)
    width_ssm = MH * MP
    x_conv = conv_out[:, :width_ssm].reshape(count_of_rows, MH, MP)
    b_mat = conv_out[:, width_ssm:width_ssm + NS]
    c_mat = conv_out[:, width_ssm + NS:]
    dt_vals = jax.nn.softplus(dt_raw + parameters['dt_bias'])
    log_decay = dt_vals * -jnp.exp(parameters['a_log'])
    outputs, _, _, _ = ssd_local(x_conv, b_mat, c_mat, log_decay, dt_vals, doc_row.astype(jnp.int32), jnp.array(-1, jnp.int32), QCH)
    ssm_out = (outputs + parameters['skip_gain'][None, :, None] * x_conv).reshape(count_of_rows, width_ssm)
    gated = ssm_out * jax.nn.silu(gate_pre)
    gated_out = low(gated * rms_scale(gated) * parameters['gated_gain'])
    return matrix_multiply(gated_out, parameters['out_proj'])

def layer_rows(inputs, doc_ids, parameters):

    def one_row(row_args):
        tokens_row, doc_row = row_args
        normalized_input = low(tokens_row * rms_scale(tokens_row) * parameters['norm_gain'])
        mixed = low_back(attention_branch(normalized_input, doc_row, parameters) + mamba_branch(normalized_input, doc_row, parameters))
        hidden = tokens_row + mixed
        normed_two = low(hidden * rms_scale(hidden) * parameters['mlp_gain'])
        gate_val = low_back(matrix_multiply(normed_two, parameters['gate_proj']))
        up_val = low_back(matrix_multiply(normed_two, parameters['up_proj']))
        act_vals = low(jax.nn.silu(gate_val) * up_val)
        return hidden + matrix_multiply(act_vals, parameters['down_proj'])
    return lax.map(jax.checkpoint(one_row), (inputs, doc_ids.astype(jnp.int32)))

def reference(tokens, doc_ids, norm_gain, q_proj, key_value_weight, o_proj, z_proj, x_proj, dt_proj, bc_proj, conv_x, xconv_bias, conv_bc, bcconv_bias, dt_bias, a_log, skip_gain, gated_gain, out_proj, mlp_gain, gate_proj, up_proj, down_proj, out_grad):
    weight_list = (norm_gain, q_proj, key_value_weight, o_proj, z_proj, x_proj, dt_proj, bc_proj, conv_x, xconv_bias, conv_bc, bcconv_bias, dt_bias, a_log, skip_gain, gated_gain, out_proj, mlp_gain, gate_proj, up_proj, down_proj)
    floats = tuple((weight_arr.astype(jnp.float32) for weight_arr in weight_list))

    def forward(inputs, weight_vals):
        parameters = dict(zip(WEIGHT_NAMES, weight_vals))
        return layer_rows(inputs, doc_ids, parameters)
    layer_out, pullback = jax.vjp(forward, tokens.astype(jnp.float32), floats)
    tokens_grad, weight_grads = pullback(out_grad.astype(jnp.float32))
    return (layer_out.astype(jnp.bfloat16), tokens_grad.astype(jnp.bfloat16), weight_grads[0], weight_grads[1], weight_grads[2], weight_grads[3], weight_grads[4], weight_grads[5], weight_grads[6], weight_grads[7], weight_grads[8], weight_grads[9], weight_grads[10], weight_grads[11], weight_grads[12], weight_grads[13], weight_grads[14], weight_grads[15], weight_grads[16], weight_grads[17], weight_grads[18], weight_grads[19], weight_grads[20])
```

```python
import jax
import numpy as np
import jax.numpy as jnp
from jax import lax
from jax.experimental import pallas as pl
from jax.experimental.pallas import tpu as pltpu
from jax.sharding import PartitionSpec as P

BF, F32 = jnp.bfloat16, jnp.float32
EPSILON = 1e-05
ROPE_BASE = 100000000000.0
HEAD_SIZE = 64
MP = 64
PROJ_ROWS = 256
BQ = 512
CHUNK = 128
VMEM_LIMIT = 48 * 1024 * 1024


def dot(left, right, dims=((1,), (0,)), precision=None):
    return lax.dot_general(
        left, right, (dims, ((), ())), precision=precision, preferred_element_type=F32
    )


def dot_bt(left, right):
    return dot(left, right, ((1,), (1,)))


def dot_at(left, right):
    return dot(left, right, ((0,), (0,)))


def lanes(shape):
    return lax.broadcasted_iota(jnp.int32, shape, len(shape) - 1)


def rows_of(shape):
    return lax.broadcasted_iota(jnp.int32, shape, 0)


def doc_start(pos, first, second):
    return jnp.where(pos >= second, second, jnp.where(pos >= first, first, 0))


def halves(low, high):
    return jnp.where(lanes((1, 128)) < 64, low, high)


def params(**kw):
    return pltpu.CompilerParams(vmem_limit_bytes=VMEM_LIMIT, **kw)


def whole(shape):
    return pl.BlockSpec(shape, lambda *_: (0,) * len(shape))


def proj_body(off, tok, gain, weight, cos, sin, *refs):
    normed_ref, qp_ref, kv_ref, xbc_ref, z_ref, dt_ref = refs[-6:]
    values = tok[...].astype(F32)
    scale = lax.rsqrt(jnp.mean(values * values, axis=-1, keepdims=True) + EPSILON)
    normed = (values * scale * gain[...]).astype(BF)
    normed_ref[...] = normed
    c, s = cos[...], sin[...]
    left = lanes((1, 128)) < 64
    att = dot(normed, weight[:, :384])
    kv, turned, qd = att[:, :128], att[:, 128:256], att[:, 256:]
    kv_ref[...] = jnp.where(left, kv * c + turned * s, kv).astype(BF)
    q_rot = qd * c + pltpu.roll(turned, 64, 1) * s
    qp_ref[...] = jnp.where(left, q_rot.astype(BF) * 0.125, 0.0).astype(BF)
    dt_ref[...] = qd.T[64:72, :]
    ssm = dot(normed, weight[:, 384:])
    x2z2 = ssm[:, 128:256]
    xbc_ref[:, :128] = ssm[:, :128].astype(BF)
    xbc_ref[:, 128:256] = jnp.where(left, x2z2, 0.0).astype(BF)
    xbc_ref[:, 256:] = ssm[:, 384:].astype(BF)
    z_ref[:, :128] = ssm[:, 256:384]
    z_ref[:, 128:] = jnp.where(left, pltpu.roll(x2z2, 64, 1), 0.0)


def project(off, tokens, gain, weight, cos, sin, before=None):
    own = tokens.shape[0]
    full = cos.shape[0]
    n = PROJ_ROWS
    outs = [
        jax.ShapeDtypeStruct((full, 1024), BF),
        jax.ShapeDtypeStruct((full, 128), BF),
        jax.ShapeDtypeStruct((full, 128), BF),
        jax.ShapeDtypeStruct((full, 512), BF),
        jax.ShapeDtypeStruct((full, 256), F32),
        jax.ShapeDtypeStruct((8, full), F32),
    ]
    at = lambda i, off: (off[0] + i, 0)
    out_specs = [pl.BlockSpec((n, o.shape[1]), at) for o in outs[:5]]
    out_specs.append(pl.BlockSpec((8, n), lambda i, off: (0, off[0] + i)))
    in_specs = [
        pl.BlockSpec((n, 1024), lambda i, off: (i, 0)),
        whole((1, 1024)),
        whole((1024, 1024)),
        pl.BlockSpec((n, 128), at),
        pl.BlockSpec((n, 128), at),
    ]
    args = [off, tokens, gain, weight, cos, sin]
    alias = {}
    if before is not None:
        in_specs += [pl.BlockSpec(memory_space=pl.ANY)] * 6
        args += list(before)
        alias = {6 + i: i for i in range(6)}
    return pl.pallas_call(
        proj_body,
        grid_spec=pltpu.PrefetchScalarGridSpec(
            num_scalar_prefetch=1, grid=(own // n,), in_specs=in_specs, out_specs=out_specs
        ),
        out_shape=outs,
        input_output_aliases=alias,
        compiler_params=params(),
        cost_estimate=pl.CostEstimate(
            flops=2 * own * 1024 * 1024, bytes_accessed=own * 6000, transcendentals=0
        ),
        name="norm_project",
    )(*args)


def block_range(qi, bounds):
    first, second = bounds[0], bounds[1]
    q0 = qi * BQ
    low = doc_start(q0, first, second) // BQ
    inner = (doc_start(q0 + BQ - 1, first, second) + BQ - 1) // BQ
    return low, jnp.minimum(jnp.maximum(inner, low), qi)


def allowed_keys(qi, kb, bounds):
    q = qi * BQ + rows_of((BQ, 1))
    k = kb * BQ + lanes((1, BQ))
    start = doc_start(q, bounds[0], bounds[1])
    return (k <= q) & (k >= start)


def attend_body(bounds, qp, kv, g2, out_ref, keep_ref):
    qi = pl.program_id(0)
    low, inner = block_range(qi, bounds)
    q = qp[...]

    def step(kb, carry, masked):
        top, total, acc = carry
        k = kv[pl.ds(pl.multiple_of(kb * BQ, BQ), BQ), :]
        s = dot_bt(q, k)
        if masked:
            s = jnp.where(allowed_keys(qi, kb, bounds), s, -1e30)
        new_top = jnp.maximum(top, jnp.max(s, axis=1, keepdims=True))
        p = jnp.exp(s - new_top)
        fade = jnp.exp(top - new_top)
        total = total * fade + jnp.sum(p, axis=1, keepdims=True)
        acc = acc * fade + dot(p.astype(BF), k)
        return new_top, total, acc

    carry = (jnp.full((BQ, 1), -1e30, F32), jnp.zeros((BQ, 1), F32), jnp.zeros((BQ, 128), F32))
    carry = lax.fori_loop(low, inner, lambda kb, c: step(kb, c, True), carry)
    carry = lax.fori_loop(inner, qi, lambda kb, c: step(kb, c, False), carry)
    top, total, acc = step(qi, carry, True)
    out = acc / total
    left = lanes((1, 128)) < 64
    out_ref[...] = jnp.where(left, g2[...], out.astype(BF))
    keep_ref[...] = jnp.where(left, top + jnp.log(total), out)


def attend(bounds, qp, kv, g2):
    full = qp.shape[0]
    block = pl.BlockSpec((BQ, 128), lambda i, *_: (i, 0))
    return pl.pallas_call(
        attend_body,
        grid_spec=pltpu.PrefetchScalarGridSpec(
            num_scalar_prefetch=1,
            grid=(full // BQ,),
            in_specs=[block, whole((full, 128)), block],
            out_specs=[block, block],
        ),
        out_shape=[
            jax.ShapeDtypeStruct((full, 128), BF),
            jax.ShapeDtypeStruct((full, 128), F32),
        ],
        compiler_params=params(),
        cost_estimate=pl.CostEstimate(
            flops=2 * full * full * 128, bytes_accessed=full * 1600, transcendentals=full * full // 2
        ),
        name="attend",
    )(bounds, qp, kv, g2)


def attend_back_body(bounds, qp, kv, keep, grad, cos, sin, dt_grad, out_ref, acc_ref):
    blocks = pl.num_programs(0)
    qi = blocks - 1 - pl.program_id(0)
    left = lanes((1, 128)) < 64

    @pl.when(pl.program_id(0) == 0)
    def _():
        acc_ref[...] = jnp.zeros_like(acc_ref)

    low, inner = block_range(qi, bounds)
    q = qp[...]
    do = jnp.where(left, 0.0, grad[...].astype(F32))
    delta = jnp.sum(do * keep[...], axis=1, keepdims=True)
    do = do.astype(BF)
    lse = keep[:, :1]

    def step(kb, dq, masked):
        at = pl.ds(pl.multiple_of(kb * BQ, BQ), BQ)
        k = kv[at, :]
        p = jnp.exp(dot_bt(q, k) - lse)
        if masked:
            p = jnp.where(allowed_keys(qi, kb, bounds), p, 0.0)
        ds = (p * (dot_bt(do, k) - delta)).astype(BF)
        acc_ref[at, :] += dot_at(ds, q) + dot_at(p.astype(BF), do)
        return dq + dot(ds, k)

    dq = jnp.zeros((BQ, 128), F32)
    dq = lax.fori_loop(low, inner, lambda kb, c: step(kb, c, True), dq)
    dq = lax.fori_loop(inner, qi, lambda kb, c: step(kb, c, False), dq)
    dq = step(qi, dq, True) * 0.125
    dkv = acc_ref[pl.ds(pl.multiple_of(qi * BQ, BQ), BQ), :]
    c, s = cos[...], sin[...]
    out_ref[:, :128] = jnp.where(left, dkv * c, dkv).astype(BF)
    out_ref[:, 128:256] = (jnp.where(left, dkv, pltpu.roll(dq, 64, 1)) * s).astype(BF)
    dt8 = jnp.concatenate([dt_grad[...], jnp.zeros((120, BQ), F32)], axis=0).T
    out_ref[:, 256:] = jnp.where(left, dq * c, pltpu.roll(dt8, 64, 1)).astype(BF)


def sent_block(i, bounds, blocks):
    half, rest = i // (blocks // 2), i % (blocks // 2)
    per = blocks // 8
    return ((half ^ bounds[3]) * 4 + ((rest // per) ^ bounds[2])) * per + rest % per


def attend_back(bounds, qp, kv, keep, grad, cos, sin, dt_grad):
    full = qp.shape[0]
    n = full // BQ
    block = pl.BlockSpec((BQ, 128), lambda i, *_: (n - 1 - i, 0))
    return pl.pallas_call(
        attend_back_body,
        grid_spec=pltpu.PrefetchScalarGridSpec(
            num_scalar_prefetch=1,
            grid=(n,),
            in_specs=[
                block,
                whole((full, 128)),
                block,
                pl.BlockSpec((BQ, 128), lambda i, b: (sent_block(n - 1 - i, b, n), 0)),
                block,
                block,
                pl.BlockSpec((8, BQ), lambda i, *_: (0, n - 1 - i)),
            ],
            out_specs=pl.BlockSpec((BQ, 384), lambda i, *_: (n - 1 - i, 0)),
            scratch_shapes=[pltpu.VMEM((full, 128), F32)],
        ),
        out_shape=jax.ShapeDtypeStruct((full, 384), BF),
        compiler_params=params(),
        cost_estimate=pl.CostEstimate(
            flops=5 * full * full * 128, bytes_accessed=full * 3000, transcendentals=full * full // 2
        ),
        name="attend_back",
    )(bounds, qp, kv, keep, grad, cos, sin, dt_grad)


def tap_mask(first_row, count, shift, bounds):
    pos = first_row + rows_of((count, 1))
    return (pos - doc_start(pos, bounds[0], bounds[1]) >= shift).astype(F32)


def conv_taps(ext_ref, r0, bounds, taps, bias):
    pre = bias + taps[3:4, :] * ext_ref[pl.ds(8, CHUNK), :]
    for shift in (1, 2, 3):
        mask = tap_mask(r0, CHUNK, shift, bounds)
        pre = pre + taps[3 - shift : 4 - shift, :] * (ext_ref[pl.ds(8 - shift, CHUNK), :] * mask)
    return pre


def chunk_decay(r0, bounds, dt_raw, head):
    lane = lanes((1, CHUNK))
    dt = jax.nn.softplus(dt_raw + head[:, 0:1])
    la = dt * head[:, 1:2]
    upper = (rows_of((CHUNK, CHUNK)) <= lanes((CHUNK, CHUNK))).astype(F32)
    cum = dot(la, upper, precision=lax.Precision.HIGHEST)
    stacked = jnp.concatenate([cum, dt, jnp.zeros((CHUNK - 16, CHUNK), F32)], axis=0).T
    cum_col, dt_col = stacked[:, 0:8], stacked[:, 8:16]
    pos = r0 + rows_of((CHUNK, 1))
    start = doc_start(pos, bounds[0], bounds[1])
    start_last = doc_start(r0 + CHUNK - 1, bounds[0], bounds[1])
    key = r0 + lane
    mask = (key <= pos) & (key >= start)
    enter = jnp.where(start < r0, jnp.exp(cum_col), 0.0)
    fade = jnp.where(pos >= start_last, jnp.exp(cum_last_row(cum_col) - cum_col), 0.0)
    keep = jnp.where(start_last < r0, jnp.exp(cum_last_row(cum_col)), 0.0)
    return dt, la, cum, dt_col, cum_col, mask, enter, fade, keep


def cum_last_row(cum_col):
    return cum_col[CHUNK - 1 : CHUNK, :]


def per_head(col):
    return halves(col[:, 0:1], col[:, 1:2]), col[:, 2:3]


def state_rows(keep):
    row = rows_of((256, 1))
    return jnp.where(row < 64, keep[:, 0:1], jnp.where(row < 128, keep[:, 1:2], keep[:, 2:3]))


def scan_body(bounds, xbc, z, dt_raw, taps, bias, head, skip, g01, g2, y_ref, s_ref, ext, state):
    i = pl.program_id(0)
    r0 = i * CHUNK

    @pl.when(i == 0)
    def _():
        ext[pl.ds(0, 8), :] = jnp.zeros((8, 512), F32)
        state[...] = jnp.zeros_like(state)

    @pl.when(i > 0)
    def _():
        ext[pl.ds(0, 8), :] = ext[pl.ds(CHUNK, 8), :]

    ext[pl.ds(8, CHUNK), :] = xbc[...].astype(F32)
    pre = conv_taps(ext, r0, bounds, taps[...], bias[...])
    conv = pre * jax.nn.sigmoid(pre)
    x01, x2 = conv[:, :128], conv[:, 128:256]
    b, c = conv[:, 256:384].astype(BF), conv[:, 384:].astype(BF)
    dt, la, cum, dt_col, cum_col, mask, enter, fade, keep = chunk_decay(
        r0, bounds, dt_raw[...], head[...]
    )
    inner = dot_bt(c, b)
    x01b, x2b = x01.astype(BF), x2.astype(BF)
    ys = []
    for h in range(3):
        gap = cum_col[:, h : h + 1] - cum[h : h + 1, :]
        decay = jnp.exp(jnp.where(mask, gap, -1e30))
        m = (inner * decay * dt[h : h + 1, :]).astype(BF)
        ys.append(dot(m, x01b if h < 2 else x2b))
    s0 = state[...]
    s_ref[0] = s0
    carried = dot_bt(c, s0.astype(BF))
    e01, e2 = per_head(enter)
    y01 = halves(ys[0], ys[1]) + e01 * carried[:, :128] + skip[:, :128] * x01
    y2 = ys[2] + e2 * carried[:, 128:] + skip[:, 128:] * x2
    w01, w2 = per_head(fade * dt_col)
    xw = jnp.concatenate([(x01 * w01).astype(BF), (x2 * w2).astype(BF)], axis=1)
    state[...] = s0 * state_rows(keep) + dot_at(xw, b)
    y_ref[:, :128] = y01
    y_ref[:, 128:] = y2
    z01, z2 = z[:, :128], z[:, 128:]
    g01[...] = (y01 * (z01 * jax.nn.sigmoid(z01))).astype(BF)
    g2[...] = (y2 * (z2 * jax.nn.sigmoid(z2))).astype(BF)


def scan_forward(bounds, xbc, z, dt_raw, taps, bias, head, skip):
    full = xbc.shape[0]
    n = full // CHUNK
    row = lambda width: pl.BlockSpec((CHUNK, width), lambda i, *_: (i, 0))
    return pl.pallas_call(
        scan_body,
        grid_spec=pltpu.PrefetchScalarGridSpec(
            num_scalar_prefetch=1,
            grid=(n,),
            in_specs=[
                row(512),
                row(256),
                pl.BlockSpec((8, CHUNK), lambda i, *_: (0, i)),
                whole((8, 512)),
                whole((1, 512)),
                whole((8, 128)),
                whole((1, 256)),
            ],
            out_specs=[
                row(128),
                row(128),
                row(256),
                pl.BlockSpec((1, 256, 128), lambda i, *_: (i, 0, 0)),
            ],
            scratch_shapes=[pltpu.VMEM((CHUNK + 8, 512), F32), pltpu.VMEM((256, 128), F32)],
        ),
        out_shape=[
            jax.ShapeDtypeStruct((full, 128), BF),
            jax.ShapeDtypeStruct((full, 128), BF),
            jax.ShapeDtypeStruct((full, 256), F32),
            jax.ShapeDtypeStruct((n, 256, 128), F32),
        ],
        compiler_params=params(),
        cost_estimate=pl.CostEstimate(
            flops=full * 600000, bytes_accessed=full * 4000, transcendentals=full * 2000
        ),
        name="scan_forward",
    )(bounds, xbc, z, dt_raw, taps, bias, head, skip)


def scan_back_body(
    bounds, xbc, before, z, y, dt_raw, s0_ref, dg01, dg2, taps, bias, head, skip,
    out_ref, dt_grad, acc, head_acc, ext, dext, dstate,
):
    step = pl.program_id(0)
    i = pl.num_programs(0) - 1 - step
    r0 = i * CHUNK
    left = lanes((1, 128)) < 64

    @pl.when(step == 0)
    def _():
        dext[pl.ds(CHUNK, 8), :] = jnp.zeros((8, 512), F32)
        dstate[...] = jnp.zeros_like(dstate)
        acc[...] = jnp.zeros_like(acc)
        head_acc[...] = jnp.zeros_like(head_acc)

    @pl.when(step > 0)
    def _():
        dext[pl.ds(CHUNK, 8), :] = dext[pl.ds(0, 8), :]

    ext[pl.ds(0, 8), :] = before[...].astype(F32)[8:, :]
    ext[pl.ds(8, CHUNK), :] = xbc[...].astype(F32)
    weights = taps[...]
    pre = conv_taps(ext, r0, bounds, weights, bias[...])
    sig = jax.nn.sigmoid(pre)
    conv = pre * sig
    x01, x2 = conv[:, :128], conv[:, 128:256]
    b, c = conv[:, 256:384].astype(BF), conv[:, 384:].astype(BF)
    dt, la, cum, dt_col, cum_col, mask, enter, fade, keep = chunk_decay(
        r0, bounds, dt_raw[...], head[...]
    )

    def gate_back(dg, zz, yy):
        s = jax.nn.sigmoid(zz)
        act = zz * s
        return dg * act, dg * yy * (s + act * (1.0 - s))

    dy01, dz01 = gate_back(dg01[...].astype(F32), z[:, :128], y[:, :128])
    dg2_only = jnp.where(left, dg2[...].astype(F32), 0.0)
    dy2, dz2 = gate_back(dg2_only, z[:, 128:], y[:, 128:])
    inner = dot_bt(c, b)
    x01b, x2b = x01.astype(BF), x2.astype(BF)
    dy01b, dy2b = dy01.astype(BF), dy2.astype(BF)
    zero = jnp.zeros_like(dy01b)
    parts = [(jnp.where(left, dy01b, zero), x01b), (jnp.where(left, zero, dy01b), x01b), (dy2b, x2b)]
    d_inner = jnp.zeros((CHUNK, CHUNK), F32)
    dxs, col_sums, direct, row_sums = [], [], [], []
    for h in range(3):
        gap = cum_col[:, h : h + 1] - cum[h : h + 1, :]
        decay = jnp.exp(jnp.where(mask, gap, -1e30))
        dt_h = dt[h : h + 1, :]
        dyh, xh = parts[h]
        dm = dot_bt(dyh, xh)
        kept = inner * decay
        m = (kept * dt_h).astype(BF)
        dxs.append(dot_at(m, dyh if h == 2 else dy01b))
        pulled = dm * kept
        d_inner = d_inner + dm * (decay * dt_h)
        weighted = pulled * dt_h
        direct.append(jnp.sum(pulled, axis=0, keepdims=True))
        col_sums.append(jnp.sum(weighted, axis=0, keepdims=True))
        row_sums.append(jnp.sum(weighted, axis=1, keepdims=True))
    s0 = s0_ref[0]
    s0b = s0.astype(BF)
    ds1 = dstate[...]
    ds1b = ds1.astype(BF)
    e01, e2 = per_head(enter)
    ey01, ey2 = dy01 * e01, dy2 * e2
    ey = jnp.concatenate([ey01.astype(BF), ey2.astype(BF)], axis=1)
    carried = dot_bt(c, s0b)
    f01, f2 = per_head(fade)
    d01, d2 = per_head(dt_col)
    back = dot_bt(b, ds1b)
    fb01, fb2 = f01 * back[:, :128], f2 * back[:, 128:]
    xw = jnp.concatenate([(x01 * (f01 * d01)).astype(BF), (x2 * (f2 * d2)).astype(BF)], axis=1)
    d_innerb = d_inner.astype(BF)
    dc = dot(d_innerb, b) + dot(ey, s0b)
    db = dot_at(d_innerb, c) + dot(xw, ds1b)
    dx01 = halves(dxs[0], dxs[1]) + d01 * fb01 + skip[:, :128] * dy01
    dx2 = dxs[2] + d2 * fb2 + skip[:, 128:] * dy2
    kept_rows = state_rows(keep)
    crossing = jnp.sum(ds1 * s0 * kept_rows, axis=1, keepdims=True)
    dstate[...] = ds1 * kept_rows + dot_at(ey, c)
    inter01, inter2 = ey01 * carried[:, :128], ey2 * carried[:, 128:]
    u01, u2 = x01 * fb01, x2 * fb2
    pick = lambda v, h: jnp.where(left if h == 0 else ~left, v, 0.0)
    side = lambda v01, v2, h: jnp.sum(pick(v01, h) if h < 2 else v2, axis=1, keepdims=True)
    lane = lanes((1, CHUNK))
    tile = jnp.zeros((CHUNK, CHUNK), F32)
    crossed = jnp.zeros((8, 1), F32)
    head_row = rows_of((8, 1))
    for h in range(3):
        u = side(u01, u2, h)
        moved = row_sums[h] + side(inter01, inter2, h) - u * dt_col[:, h : h + 1]
        tile = jnp.where(lane == h, moved, jnp.where(lane == 8 + h, u, tile))
        total = jnp.sum(crossing[64 * h : 64 * h + 64, :], axis=0, keepdims=True)
        total = total + jnp.sum(u * dt_col[:, h : h + 1], axis=0, keepdims=True)
        crossed = jnp.where(head_row == h, total, crossed)
    tile = tile.T
    stack = lambda items: jnp.concatenate(items + [jnp.zeros((5, CHUNK), F32)], axis=0)
    dcum = tile[0:8, :] - stack(col_sums) + jnp.where(lane == CHUNK - 1, crossed, 0.0)
    lower = (rows_of((CHUNK, CHUNK)) >= lanes((CHUNK, CHUNK))).astype(F32)
    dla = dot(dcum, lower, precision=lax.Precision.HIGHEST)
    ddt = stack(direct) + tile[8:16, :] + dla * head[:, 1:2]
    graw = ddt * jax.nn.sigmoid(dt_raw[...] + head[:, 0:1])
    dt_grad[...] = graw
    head_acc[0:8, :] += dla * la
    head_acc[8:16, :] += graw
    dpre = jnp.concatenate([dx01, dx2, db, dc], axis=1) * (sig + conv * (1.0 - sig))
    dext[pl.ds(0, CHUNK), :] = dpre
    din = weights[3:4, :] * dpre
    acc[3:4, :] += jnp.sum(dpre * ext[pl.ds(8, CHUNK), :], axis=0, keepdims=True)
    acc[4:5, :] += jnp.sum(dpre, axis=0, keepdims=True)
    acc[5:6, :128] += jnp.sum(dy01 * x01, axis=0, keepdims=True)
    acc[5:6, 128:256] += jnp.sum(dy2 * x2, axis=0, keepdims=True)
    for shift in (1, 2, 3):
        tap = 3 - shift
        now = tap_mask(r0, CHUNK, shift, bounds)
        acc[tap : tap + 1, :] += jnp.sum(
            dpre * (ext[pl.ds(8 - shift, CHUNK), :] * now), axis=0, keepdims=True
        )
        later = tap_mask(r0 + shift, CHUNK, shift, bounds)
        din = din + weights[tap : tap + 1, :] * (dext[pl.ds(shift, CHUNK), :] * later)
    out_ref[:, :128] = din[:, :128].astype(BF)
    out_ref[:, 128:256] = jnp.where(left, din[:, 128:256], pltpu.roll(dz2, 64, 1)).astype(BF)
    out_ref[:, 256:384] = dz01.astype(BF)
    out_ref[:, 384:] = din[:, 256:].astype(BF)


def scan_back(bounds, xbc, z, y, dt_raw, states, dg01, dg2, taps, bias, head, skip):
    full = xbc.shape[0]
    n = full // CHUNK
    row = lambda width: pl.BlockSpec((CHUNK, width), lambda i, *_: (n - 1 - i, 0))
    tall = CHUNK // 16
    sent = pl.BlockSpec((CHUNK, 128), lambda i, b: (sent_block(n - 1 - i, b, n), 0))
    dts = pl.BlockSpec((8, CHUNK), lambda i, *_: (0, n - 1 - i))
    return pl.pallas_call(
        scan_back_body,
        grid_spec=pltpu.PrefetchScalarGridSpec(
            num_scalar_prefetch=1,
            grid=(n,),
            in_specs=[
                row(512),
                pl.BlockSpec((16, 512), lambda i, *_: (jnp.maximum((n - 1 - i) * tall - 1, 0), 0)),
                row(256),
                row(256),
                dts,
                pl.BlockSpec((1, 256, 128), lambda i, *_: (n - 1 - i, 0, 0)),
                sent,
                sent,
                whole((8, 512)),
                whole((1, 512)),
                whole((8, 128)),
                whole((1, 256)),
            ],
            out_specs=[row(640), dts, whole((8, 512)), whole((16, CHUNK))],
            scratch_shapes=[
                pltpu.VMEM((CHUNK + 8, 512), F32),
                pltpu.VMEM((CHUNK + 8, 512), F32),
                pltpu.VMEM((256, 128), F32),
            ],
        ),
        out_shape=[
            jax.ShapeDtypeStruct((full, 640), BF),
            jax.ShapeDtypeStruct((8, full), F32),
            jax.ShapeDtypeStruct((8, 512), F32),
            jax.ShapeDtypeStruct((16, CHUNK), F32),
        ],
        compiler_params=params(),
        cost_estimate=pl.CostEstimate(
            flops=full * 1500000, bytes_accessed=full * 6000, transcendentals=full * 2000
        ),
        name="scan_back",
    )(bounds, xbc, xbc, z, y, dt_raw, states, dg01, dg2, taps, bias, head, skip)


ROW_BLOCK = 256


def row_body(*refs):
    g, h = refs[0:4], refs[4:8]
    tok, gout, gains, mlp_gain = refs[8:12]
    pa, pb = refs[12:20], refs[20:28]
    out_ref, two_ref, dmix_ref, dhid_ref = refs[28:32]
    act_refs, dgu_refs, gn_refs = refs[32:34], refs[34:36], refs[36:38]
    d01, d2 = refs[38:42], refs[42:46]
    mlp_acc, gain_acc = refs[46:48]
    left = lanes((1, 128)) < 64
    width = 1536.0

    @pl.when(pl.program_id(0) == 0)
    def _():
        mlp_acc[...] = jnp.zeros_like(mlp_acc)
        gain_acc[...] = jnp.zeros_like(gain_acc)

    pieces = [(r, k) for k in range(2) for r in range(4)]

    def part(ref, k):
        return ref[:, k * 128 : k * 128 + 128].astype(F32)

    squares = 0.0
    for r, k in pieces:
        first, second = part(g[r], k), part(h[r], k)
        squares = squares + first * first + jnp.where(left, second * second, 0.0)
    rg = lax.rsqrt(jnp.sum(squares, axis=1, keepdims=True) / width + EPSILON)
    mixed = 0.0
    for s, (r, k) in enumerate(pieces):
        gain = gains[s : s + 1, :]
        first = part(g[r], k) * rg * gain[:, :128]
        second = part(h[r], k)
        second = jnp.where(left, second * rg * gain[:, 128:], second)
        gn = jnp.concatenate([first.astype(BF), second.astype(BF)], axis=1)
        gn_refs[k][:, r * 256 : r * 256 + 256] = gn
        mixed = mixed + dot_bt(gn, pb[s][:, 256:])
    hidden = tok[...].astype(F32) + mixed
    scale = lax.rsqrt(jnp.mean(hidden * hidden, axis=-1, keepdims=True) + EPSILON)
    two = (hidden * scale * mlp_gain[...]).astype(BF)
    two_ref[...] = two
    grad = gout[...]
    ffn = 0.0
    dtwo = 0.0
    for s, (r, k) in enumerate(pieces):
        weight, down = pa[s][...], pb[s][:, :256]
        gu = dot(two, weight)
        gate, up = gu[:, :256], gu[:, 256:]
        sig = jax.nn.sigmoid(gate)
        silu = gate * sig
        act = (silu * up).astype(BF)
        act_refs[k][:, r * 256 : r * 256 + 256] = act
        ffn = ffn + dot_bt(act, down)
        dact = dot(grad, down)
        dgate = (dact * up * (sig + silu * (1.0 - sig))).astype(BF)
        dgu = jnp.concatenate([dgate, (dact * silu).astype(BF)], axis=1)
        dgu_refs[k][:, r * 512 : r * 512 + 512] = dgu
        dtwo = dtwo + dot_bt(dgu, weight)
    out_ref[...] = (hidden + ffn).astype(BF)
    weighted = dtwo * mlp_gain[...]
    mlp_acc[...] += jnp.sum(dtwo * (hidden * scale), axis=0, keepdims=True)
    mean = jnp.mean(weighted * hidden, axis=-1, keepdims=True)
    dhid = grad.astype(F32) + scale * weighted - hidden * (scale * scale * scale * mean)
    dhid_ref[...] = dhid
    dmix = dhid.astype(BF)
    dmix_ref[...] = dmix
    cross = 0.0
    grads = []
    for s, (r, k) in enumerate(pieces):
        dgn = dot(dmix, pb[s][:, 256:])
        first, second = dgn[:, :128], dgn[:, 128:]
        gain = gains[s : s + 1, :]
        own1, own2 = part(g[r], k), jnp.where(left, part(h[r], k), 0.0)
        t1, t2 = first * own1, second * own2
        gain_acc[s : s + 1, :128] += jnp.sum(t1 * rg, axis=0, keepdims=True)
        gain_acc[s : s + 1, 128:] += jnp.sum(t2 * rg, axis=0, keepdims=True)
        cross = cross + t1 * gain[:, :128] + t2 * gain[:, 128:]
        grads.append((first, second))
    cross = jnp.sum(cross, axis=1, keepdims=True) * (rg * rg * rg / width)
    for s, (r, k) in enumerate(pieces):
        first, second = grads[s]
        gain = gains[s : s + 1, :]
        own1, own2 = part(g[r], k), part(h[r], k)
        d01[r][:, k * 128 : k * 128 + 128] = (first * gain[:, :128] * rg - own1 * cross).astype(BF)
        ssm = second * gain[:, 128:] * rg - own2 * cross
        d2[r][:, k * 128 : k * 128 + 128] = jnp.where(left, ssm, second).astype(BF)


def row_stage(g, h, tok, gout, gains, mlp_gain, pa, pb):
    count = tok.shape[0]
    n = ROW_BLOCK
    row = lambda w: pl.BlockSpec((n, w), lambda i: (i, 0))
    once = lambda shape: pl.BlockSpec(
        shape, lambda i: (0,) * len(shape), pipeline_mode=pl.Buffered(1)
    )
    sds = jax.ShapeDtypeStruct
    return pl.pallas_call(
        row_body,
        grid=(count // n,),
        in_specs=[row(256)] * 8
        + [row(1024), row(1024), whole((8, 256)), whole((1, 1024))]
        + [once((1024, 512))] * 16,
        out_specs=[row(1024)] * 4
        + [row(1024)] * 2
        + [row(2048)] * 2
        + [row(1024)] * 2
        + [row(256)] * 8
        + [whole((1, 1024)), whole((8, 256))],
        out_shape=[sds((count, 1024), BF)] * 3
        + [sds((count, 1024), F32)]
        + [sds((count, 1024), BF)] * 2
        + [sds((count, 2048), BF)] * 2
        + [sds((count, 1024), BF)] * 2
        + [sds((count, 256), BF)] * 8
        + [sds((1, 1024), F32), sds((8, 256), F32)],
        compiler_params=pltpu.CompilerParams(vmem_limit_bytes=58 * 1024 * 1024),
        cost_estimate=pl.CostEstimate(
            flops=count * 2 * 1024 * 1024 * 16, bytes_accessed=30 * 2**20, transcendentals=0
        ),
        name="row_stage",
    )(*g, *h, tok, gout, gains, mlp_gain, *pa, *pb)


def weight_body(two, gout, dmix, dgu, act, gn, a_ref, b_ref):
    a_ref[0] = dot_at(two[...], dgu[...]).astype(BF)
    b_ref[0, :, :256] = dot_at(gout[...], act[...]).astype(BF)
    b_ref[0, :, 256:] = dot_at(dmix[...], gn[...]).astype(BF)


def weight_stage(two, gout, dmix, dgu, act, gn):
    count = two.shape[0]
    col = lambda w: pl.BlockSpec((count, w), lambda i: (0, i))
    out = pl.BlockSpec((1, 1024, 512), lambda i: (i, 0, 0))
    return pl.pallas_call(
        weight_body,
        grid=(4,),
        in_specs=[whole((count, 1024))] * 3 + [col(512), col(256), col(256)],
        out_specs=[out, out],
        out_shape=[jax.ShapeDtypeStruct((4, 1024, 512), BF)] * 2,
        compiler_params=params(),
        cost_estimate=pl.CostEstimate(
            flops=count * 2 * 1024 * 1024 * 4, bytes_accessed=16 * 2**20, transcendentals=0
        ),
        name="weight_stage",
    )(two, gout, dmix, dgu, act, gn)


def input_grad_body(off, da, ds, weight, out_ref):
    out_ref[...] = (
        dot_bt(da[...], weight[:, :384]) + dot_bt(ds[...], weight[:, 384:])
    ).astype(BF)


def input_grad(off, da, ds, weight):
    n = PROJ_ROWS
    own = da.shape[0] // 2
    at = lambda i, off: (off[0] + i, 0)
    return pl.pallas_call(
        input_grad_body,
        grid_spec=pltpu.PrefetchScalarGridSpec(
            num_scalar_prefetch=1,
            grid=(own // n,),
            in_specs=[pl.BlockSpec((n, 384), at), pl.BlockSpec((n, 640), at), whole((1024, 1024))],
            out_specs=pl.BlockSpec((n, 1024), lambda i, off: (i, 0)),
        ),
        out_shape=jax.ShapeDtypeStruct((own, 1024), BF),
        compiler_params=params(),
        cost_estimate=pl.CostEstimate(
            flops=2 * own * 1024 * 1024, bytes_accessed=own * 4096, transcendentals=0
        ),
        name="input_grad",
    )(off, da, ds, weight)


def swap(value, step):
    return lax.ppermute(value, "tensor", [(i, i ^ step) for i in range(4)])


def twin(value):
    return lax.ppermute(value, "ctx", [(0, 1), (1, 0)])


def dp_sum(value):
    if lax.axis_size("dp") != 4:
        return lax.psum(value, "dp")
    place = lax.axis_index("dp")
    inner = (place == 1) | (place == 2)
    half = value.shape[0] // 2
    first, second = value[:half], value[half:]
    near = [(0, 1), (1, 0), (2, 3), (3, 2)]
    got = lax.ppermute(jnp.where(inner, second, first), "dp", near)
    kept = (jnp.where(inner, first, second).astype(F32) + got.astype(F32)).astype(BF)
    got = lax.ppermute(kept, "dp", [(1, 2), (2, 1), (0, 3), (3, 0)])
    kept = (kept.astype(F32) + got.astype(F32)).astype(BF)
    got = lax.ppermute(kept, "dp", near)
    return jnp.concatenate([jnp.where(inner, kept, got), jnp.where(inner, got, kept)], axis=0)


def plus(a, b):
    return (a.astype(F32) + b.astype(F32)).astype(BF)


def block_at(value, index, count):
    return lax.dynamic_slice_in_dim(value, index * count, count, 0)


def gather_rows(part, t):
    count, width = part.shape
    left, right = part[:, : width // 2], part[:, width // 2 :]
    l1, r2 = swap(left, 1), swap(right, 2)
    lefts = [left, l1, swap(left, 2), swap(l1, 2)]
    rights = [right, swap(right, 1), r2, swap(r2, 1)]
    out = jnp.zeros((4 * count, width), part.dtype)
    for r in range(4):
        piece = jnp.concatenate([lefts[r], rights[r]], axis=1)
        out = lax.dynamic_update_slice_in_dim(out, piece, (t ^ r) * count, 0)
    return out


def scatter_rows(value, t):
    count = value.shape[0] // 4
    half = value.shape[1] // 2
    at = lambda r, lo: lax.dynamic_slice(
        value, ((t ^ r) * count, lo), (count, half)
    )
    sent_l = swap(jnp.concatenate([at(1, 0), at(3, 0)], axis=0), 1)
    sent_r = swap(jnp.concatenate([at(2, half), at(3, half)], axis=0), 2)
    next_l = swap(plus(at(2, 0), sent_l[count:]), 2)
    next_r = swap(plus(at(1, half), sent_r[count:]), 1)
    add = lambda a, b, c: a.astype(F32) + b.astype(F32) + c.astype(F32)
    return jnp.concatenate(
        [add(at(0, 0), sent_l[:count], next_l), add(at(0, half), sent_r[:count], next_r)], axis=1
    )


def to_rows(value, t, c):
    half = value.shape[0] // 2
    both = jnp.concatenate([block_at(value, c, half), twin(block_at(value, 1 - c, half))], axis=1)
    parts = [block_at(both, t ^ r, half // 4) for r in range(4)]
    return [parts[0]] + [swap(parts[r], r) for r in (1, 2, 3)]


def from_rows(parts):
    parts = [parts[0]] + [swap(parts[r], r) for r in (1, 2, 3)]
    width = parts[0].shape[1] // 2
    other = twin(jnp.concatenate([p[:, width:] for p in parts], axis=0))
    return jnp.concatenate([p[:, :width] for p in parts] + [other], axis=0)


def turn(weight):
    half = weight.shape[1] // 2
    return jnp.concatenate([-weight[:, half:], weight[:, :half]], axis=1)


def turn_back(grad):
    half = grad.shape[1] // 2
    return jnp.concatenate([grad[:, half:], -grad[:, :half]], axis=1)


def rope_tables(count):
    exponent = np.arange(0, HEAD_SIZE, 2).astype(np.float32) / np.float32(HEAD_SIZE)
    frequency = (np.float32(ROPE_BASE) ** (-exponent)).astype(np.float32)
    angles = np.arange(count).astype(np.float32)[:, None] * frequency[None, :]
    angles = np.concatenate([angles] * 4, axis=1)
    return (np.cos(angles).astype(np.float32), np.sin(angles).astype(np.float32))


def ordered(own, other, c, axis):
    return jnp.concatenate(
        [jnp.where(c == 0, own, other), jnp.where(c == 0, other, own)], axis=axis
    )


def local(
    tokens, doc_ids, norm_gain, q_proj, key_value_weight, o_proj, z_proj, x_proj, dt_proj,
    bc_proj, conv_x, xconv_bias, conv_bc, bcconv_bias, dt_bias, a_log, skip_gain, gated_gain,
    out_proj, mlp_gain, gate_proj, up_proj, down_proj, out_grad,
):
    t, c = lax.axis_index("tensor"), lax.axis_index("ctx")
    own_tokens, grad_out = tokens[0], out_grad[0]
    own = own_tokens.shape[0]
    full = 2 * own
    mine = own // 4
    other_tokens = twin(own_tokens)

    def cols(w):
        n = w.shape[-1] // 2
        return lax.dynamic_slice_in_dim(w, c * n, n, w.ndim - 1)

    def rows(w):
        return block_at(w, c, w.shape[0] // 2)

    pa0 = jnp.concatenate([cols(gate_proj), cols(up_proj)], axis=1)
    pb0 = jnp.concatenate([rows(down_proj).T, rows(out_proj).T, rows(o_proj).T], axis=1)
    b2 = swap(pb0, 2)
    pbs = [pb0, swap(pb0, 1), b2, swap(b2, 1)]
    a1 = swap(pa0, 1)
    pas = [pa0, a1, swap(pa0, 2), swap(a1, 2)]
    pbs = pbs + [twin(p) for p in pbs]
    pas = pas + [twin(p) for p in pas]
    gain0 = jnp.concatenate([rows(gated_gain), jnp.ones((64,), F32)])
    gain_all = lax.all_gather(gain0, ("tensor", "ctx"), axis=0, tiled=False)
    slots = [(t ^ r) * 2 + (c ^ k) for k in range(2) for r in range(4)]
    gains = jnp.stack([lax.dynamic_index_in_dim(gain_all, s, 0, False) for s in slots])

    kv_head = t // 2
    kv_cols = lambda lo: lax.dynamic_slice_in_dim(key_value_weight, lo + kv_head * 64, 64, 1)
    wk, wv, wq = kv_cols(0), kv_cols(128), cols(q_proj)
    wx, wz, wdt = cols(x_proj), cols(z_proj), cols(dt_proj)
    weight = jnp.concatenate(
        [wk, wv, turn(wk), turn(wq), wq, wdt, jnp.zeros((1024, 61), BF)]
        + [wx, wz[:, 128:], wz[:, :128], bc_proj],
        axis=1,
    )
    docs = doc_ids[0]
    bounds = jnp.stack([jnp.sum(docs < 1), jnp.sum(docs < 2), t, c]).astype(jnp.int32)
    cos, sin = rope_tables(full)
    cos, sin = jnp.asarray(cos), jnp.asarray(sin)
    steps = own // PROJ_ROWS
    own_off = jnp.reshape(c * steps, (1,)).astype(jnp.int32)
    other_off = jnp.reshape((1 - c) * steps, (1,)).astype(jnp.int32)
    gain_row = norm_gain[None]
    first = project(own_off, own_tokens, gain_row, weight, cos, sin)
    normed, qp, kv, xbc, z, dt_raw = project(
        other_off, other_tokens, gain_row, weight, cos, sin, before=first
    )

    pad = lambda v: jnp.zeros(v.shape[:-1] + (64,), F32)
    cx, cb = cols(conv_x), cols(xconv_bias)
    taps = jnp.concatenate([cx, pad(cx), conv_bc], axis=1)
    taps = jnp.concatenate([taps, jnp.zeros_like(taps)], axis=0)
    bias = jnp.concatenate([cb, pad(cb), bcconv_bias])[None]
    head = jnp.stack([cols(dt_bias), -jnp.exp(cols(a_log))], axis=1)
    head = jnp.pad(head, ((0, 5), (0, 126)))
    skip = jnp.pad(jnp.repeat(cols(skip_gain), MP), (0, 64))[None]
    g01, g2, y, states = scan_forward(bounds, xbc, z, dt_raw, taps, bias, head, skip)
    g_rows = to_rows(g01, t, c)
    tile, keep = attend(bounds, qp, kv, g2)
    h_rows = to_rows(tile, t, c)

    tok_rows = block_at(own_tokens, t, mine)
    grad_rows = block_at(grad_out, t, mine)
    res = row_stage(g_rows, h_rows, tok_rows, grad_rows, gains, mlp_gain[None], pas, pbs)
    layer_rows, two, dmix, dhid = res[0:4]
    act, dgu, gn = res[4:6], res[6:8], res[8:10]
    d01, d2 = res[10:14], res[14:18]
    mlp_part, gain_part = res[18:20]
    dg01, dg2 = from_rows(d01), from_rows(d2)
    layer_out = gather_rows(layer_rows, t)
    far_a, far_b = weight_stage(two, grad_rows, dmix, dgu[1], act[1], gn[1])
    near_a, near_b = weight_stage(two, grad_rows, dmix, dgu[0], act[0], gn[0])
    far_a, far_b = twin(far_a), twin(far_b)
    sum_a = [plus(near_a[r], far_a[r]) for r in range(4)]
    sum_b = [plus(near_b[r], far_b[r]) for r in range(4)]
    a_send = swap(jnp.stack([sum_a[1], sum_a[3]]), 1)
    b_send = swap(jnp.stack([sum_b[2], sum_b[3]]), 2)
    a_next = swap(plus(sum_a[2], a_send[1]), 2)
    b_next = swap(plus(sum_b[1], b_send[1]), 1)
    add3 = lambda a, b, d: (a.astype(F32) + b.astype(F32) + d.astype(F32)).astype(BF)
    piece_a = dp_sum(add3(sum_a[0], a_send[0], a_next))
    piece_b = dp_sum(add3(sum_b[0], b_send[0], b_next))
    twin_a, twin_b = twin(piece_a), twin(piece_b)

    ds, dt_grad, conv_acc, head_acc = scan_back(
        bounds, xbc, z, y, dt_raw, states, dg01, dg2, taps, bias, head, skip
    )
    da = attend_back(bounds, qp, kv, keep, dg2, cos, sin, dt_grad)
    sent = twin(input_grad(other_off, da, ds, weight))
    partial = input_grad(own_off, da, ds, weight)
    grad_normed = scatter_rows(plus(partial, sent), t)
    inputs = tok_rows.astype(F32)
    scale = lax.rsqrt(jnp.mean(inputs * inputs, axis=-1, keepdims=True) + EPSILON)
    weighted = grad_normed * norm_gain
    norm_part = jnp.sum(grad_normed * inputs * scale, axis=0)
    inner_mean = jnp.mean(weighted * inputs, axis=-1, keepdims=True)
    token_rows = (dhid + scale * weighted - inputs * scale**3 * inner_mean).astype(BF)
    tokens_grad = gather_rows(token_rows, t)

    dwa = dot_at(normed, da)
    dws = dot_at(normed, ds)
    dq = dwa[:, 256:320] + turn_back(dwa[:, 192:256])
    dk = dwa[:, :64] + turn_back(dwa[:, 128:192])
    alone = jnp.concatenate(
        [dq, dwa[:, 320:384], dws[:, :192], dws[:, 256:384], dws[:, 192:256]], axis=1
    ).astype(BF)
    alone = dp_sum(alone)
    alone_twin = twin(alone)
    here = (jnp.arange(2) == kv_head).astype(F32)[None, :, None]
    spread = lambda v: (v[:, None, :] * here).reshape(1024, 128)
    shared = jnp.concatenate([spread(dk), spread(dwa[:, 64:128]), dws[:, 384:]], axis=1)
    shared = lax.psum(shared.astype(BF), ("dp", "ctx", "tensor")).astype(F32)

    at_piece = jnp.zeros((8, 256), F32)
    for s, slot in enumerate(slots):
        at_piece = lax.dynamic_update_slice_in_dim(at_piece, gain_part[s : s + 1], slot, 0)
    heads = jnp.concatenate(
        [
            jnp.sum(conv_acc[5, :192].reshape(3, 64), axis=1),
            jnp.sum(head_acc[0:3], axis=1),
            jnp.sum(head_acc[8:11], axis=1),
        ]
    )
    own_small = jnp.concatenate([conv_acc[:5, :192].reshape(-1), heads])
    at_own = lax.dynamic_update_slice_in_dim(
        jnp.zeros((8, own_small.shape[0]), F32), own_small[None], t * 2 + c, 0
    )
    small, gain_sum, bc_sum, mlp_sum = lax.psum(
        (at_own, at_piece, conv_acc[:5, 256:], mlp_part[0]), ("dp", "ctx", "tensor")
    )
    norm_sum = lax.psum(norm_part, ("dp", "ctx", "tensor"))
    small = block_at(small, t, 2)
    gain_sum = block_at(gain_sum, t, 2)[:, :192].reshape(-1)
    conv_small = small[:, :960].reshape(2, 5, 192)
    conv_small = jnp.concatenate([conv_small[0], conv_small[1]], axis=1)
    head_small = small[:, 960:].reshape(2, 3, 3)
    per_head_sum = lambda i: head_small[:, i].reshape(-1)

    f = lambda lo, hi, own_part, other_part, axis: ordered(
        own_part[:, lo:hi], other_part[:, lo:hi], c, axis
    ).astype(F32)
    flip = lambda lo, hi: ordered(
        piece_b[:, lo:hi].T, twin_b[:, lo:hi].T, c, 0
    ).astype(F32)
    zcols = lambda v: jnp.concatenate([v[:, 320:448], v[:, 448:512]], axis=1)
    return (
        layer_out[None],
        tokens_grad[None],
        norm_sum,
        f(0, 64, alone, alone_twin, 1),
        shared[:, :256],
        flip(448, 512),
        ordered(zcols(alone), zcols(alone_twin), c, 1).astype(F32),
        f(128, 320, alone, alone_twin, 1),
        f(64, 67, alone, alone_twin, 1),
        shared[:, 256:],
        conv_small[:4],
        conv_small[4],
        bc_sum[:4],
        bc_sum[4],
        per_head_sum(2),
        per_head_sum(1),
        per_head_sum(0),
        gain_sum,
        flip(256, 448),
        mlp_sum,
        f(0, 256, piece_a, twin_a, 1),
        f(256, 512, piece_a, twin_a, 1),
        flip(0, 256),
    )


def solution(mesh):
    placed = (
        P("dp", "ctx", None),
        P("dp", None),
        P(),
        P(None, "tensor"),
        P(),
        P("tensor", None),
        P(None, "tensor"),
        P(None, "tensor"),
        P(None, "tensor"),
        P(),
        P(None, "tensor"),
        P("tensor"),
        P(),
        P(),
        P("tensor"),
        P("tensor"),
        P("tensor"),
        P("tensor"),
        P("tensor", None),
        P(),
        P(None, "tensor"),
        P(None, "tensor"),
        P("tensor", None),
        P("dp", "ctx", None),
    )
    return jax.shard_map(
        local,
        mesh=mesh,
        in_specs=placed,
        out_specs=(
            P("dp", "ctx", None),
            P("dp", "ctx", None),
            P(),
            P(None, "tensor"),
            P(),
            P("tensor", None),
            P(None, "tensor"),
            P(None, "tensor"),
            P(None, "tensor"),
            P(),
            P(None, "tensor"),
            P("tensor"),
            P(),
            P(),
            P("tensor"),
            P("tensor"),
            P("tensor"),
            P("tensor"),
            P("tensor", None),
            P(),
            P(None, "tensor"),
            P(None, "tensor"),
            P("tensor", None),
        ),
        check_vma=False,
    )
```

```python
import functools

import jax
import numpy as np
import jax.numpy as jnp
from jax import lax
from jax.experimental import pallas as pl
from jax.experimental.pallas import tpu as pltpu
from jax.sharding import PartitionSpec as P

BF, F32 = jnp.bfloat16, jnp.float32
EPSILON = 1e-05
ROPE_BASE = 100000000000.0
HEAD_SIZE = 64
MP = 64
PROJ_ROWS = 256
BQ = 512
CHUNK = 128
VMEM_LIMIT = 48 * 1024 * 1024
SMALL_COST = pl.CostEstimate(flops=1000000, bytes_accessed=100000, transcendentals=0)


def dot(left, right, dims=((1,), (0,)), precision=None):
    return lax.dot_general(
        left, right, (dims, ((), ())), precision=precision, preferred_element_type=F32
    )


def dot_bt(left, right):
    return dot(left, right, ((1,), (1,)))


def dot_at(left, right):
    return dot(left, right, ((0,), (0,)))


def lanes(shape):
    return lax.broadcasted_iota(jnp.int32, shape, len(shape) - 1)


def rows_of(shape):
    return lax.broadcasted_iota(jnp.int32, shape, 0)


def doc_start(pos, first, second):
    return jnp.where(pos >= second, second, jnp.where(pos >= first, first, 0))


def halves(low, high):
    return jnp.where(lanes((1, 128)) < 64, low, high)


def params(**kw):
    return pltpu.CompilerParams(vmem_limit_bytes=VMEM_LIMIT, **kw)


def whole(shape):
    return pl.BlockSpec(shape, lambda *_: (0,) * len(shape))


def proj_body(off, tok, gain, weight, cos, sin, *refs):
    normed_ref, qp_ref, kv_ref, xbc_ref, z_ref, dt_ref = refs[-6:]
    values = tok[...].astype(F32)
    scale = lax.rsqrt(jnp.mean(values * values, axis=-1, keepdims=True) + EPSILON)
    normed = (values * scale * gain[...]).astype(BF)
    normed_ref[...] = normed
    c, s = cos[...], sin[...]
    left = lanes((1, 128)) < 64
    att = dot(normed, weight[:, :384])
    kv, turned, qd = att[:, :128], att[:, 128:256], att[:, 256:]
    kv_ref[...] = jnp.where(left, kv * c + turned * s, kv).astype(BF)
    q_rot = qd * c + pltpu.roll(turned, 64, 1) * s
    qp_ref[...] = jnp.where(left, q_rot.astype(BF) * 0.125, 0.0).astype(BF)
    dt_ref[...] = qd.T[64:72, :]
    ssm = dot(normed, weight[:, 384:])
    x2z2 = ssm[:, 128:256]
    xbc_ref[:, :128] = ssm[:, :128].astype(BF)
    xbc_ref[:, 128:256] = jnp.where(left, x2z2, 0.0).astype(BF)
    xbc_ref[:, 256:] = ssm[:, 384:].astype(BF)
    z_ref[:, :128] = ssm[:, 256:384]
    z_ref[:, 128:] = jnp.where(left, pltpu.roll(x2z2, 64, 1), 0.0)


def project(off, tokens, gain, weight, cos, sin, before=None):
    own = tokens.shape[0]
    full = cos.shape[0]
    n = PROJ_ROWS
    outs = [
        jax.ShapeDtypeStruct((full, 1024), BF),
        jax.ShapeDtypeStruct((full, 128), BF),
        jax.ShapeDtypeStruct((full, 128), BF),
        jax.ShapeDtypeStruct((full, 512), BF),
        jax.ShapeDtypeStruct((full, 256), F32),
        jax.ShapeDtypeStruct((8, full), F32),
    ]
    at = lambda i, off: (off[0] + i, 0)
    out_specs = [pl.BlockSpec((n, o.shape[1]), at) for o in outs[:5]]
    out_specs.append(pl.BlockSpec((8, n), lambda i, off: (0, off[0] + i)))
    in_specs = [
        pl.BlockSpec((n, 1024), lambda i, off: (i, 0)),
        whole((1, 1024)),
        whole((1024, 1024)),
        pl.BlockSpec((n, 128), at),
        pl.BlockSpec((n, 128), at),
    ]
    args = [off, tokens, gain, weight, cos, sin]
    alias = {}
    if before is not None:
        in_specs += [pl.BlockSpec(memory_space=pl.ANY)] * 6
        args += list(before)
        alias = {6 + i: i for i in range(6)}
    return pl.pallas_call(
        proj_body,
        grid_spec=pltpu.PrefetchScalarGridSpec(
            num_scalar_prefetch=1, grid=(own // n,), in_specs=in_specs, out_specs=out_specs
        ),
        out_shape=outs,
        input_output_aliases=alias,
        compiler_params=params(),
        cost_estimate=SMALL_COST,
        name="norm_project",
    )(*args)


def turned_lanes(value):
    low = lanes((1, 128)) % 64 < 32
    return jnp.where(low, -pltpu.roll(value, 96, 1), pltpu.roll(value, 32, 1))


def prep_body(bounds, gate, up, down, mix, att, kv, q, x, z, dt, bc, weight, pack):
    n = gate.shape[0]
    pack[:, :256] = gate[...]
    pack[:, 256:512] = up[...]
    pack[:, 512:768] = down[...].T
    pack[:, 768:] = jnp.concatenate([mix[...], att[...]], axis=0).T
    first, low_kv = bounds[3] == 0, bounds[2] // 2 == 0
    lane = lanes((1, 128))
    left = lane < 64
    tile = lambda ref, i: ref[:, 128 * i : 128 * i + 128].astype(F32)
    swapped = lambda v: pltpu.roll(v, 64, 1)
    keys, values = tile(kv, 0), tile(kv, 1)
    keys = jnp.where(low_kv, keys, swapped(keys))
    values = jnp.where(low_kv, swapped(values), values)
    query = tile(q, 0)
    query = jnp.where(first, query, swapped(query))
    steps = jnp.concatenate([dt[...].astype(F32), jnp.zeros((n, 122), F32)], axis=1)
    steps = jnp.where(lane < 3, jnp.where(first, steps, pltpu.roll(steps, 125, 1)), 0.0)

    def heads(ref):
        a, b, d = tile(ref, 0), tile(ref, 1), swapped(tile(ref, 2))
        return jnp.where(first, a, jnp.where(left, swapped(b), d)), jnp.where(first, b, d)

    x01, x2 = heads(x)
    z01, z2 = heads(z)
    tiles = [
        jnp.where(left, keys, values),
        jnp.where(left, turned_lanes(keys), swapped(turned_lanes(query))),
        jnp.where(left, query, swapped(steps)),
        x01,
        jnp.where(left, x2, swapped(z2)),
        z01,
    ]
    for i, value in enumerate(tiles):
        weight[:, 128 * i : 128 * i + 128] = value.astype(BF)
    weight[:, 768:] = bc[...]


def prepare(bounds, gate, up, down, mix, att, kv, q, x, z, dt, bc):
    n = 256
    row = lambda w: pl.BlockSpec((n, w), lambda i, b: (i, 0))
    col = lambda h: pl.BlockSpec((h, n), lambda i, b: (b[3], i))
    mine = pl.BlockSpec((n, 256), lambda i, b: (i, b[3]))
    return pl.pallas_call(
        prep_body,
        grid_spec=pltpu.PrefetchScalarGridSpec(
            num_scalar_prefetch=1,
            grid=(4,),
            in_specs=[mine, mine, col(256), col(192), col(64)]
            + [row(256), row(128), row(384), row(384), row(6), row(256)],
            out_specs=[row(1024), row(1024)],
        ),
        out_shape=[jax.ShapeDtypeStruct((1024, 1024), BF)] * 2,
        compiler_params=params(),
        cost_estimate=SMALL_COST,
        name="prepare",
    )(bounds, gate, up, down, mix, att, kv, q, x, z, dt, bc)


def block_range(qi, bounds):
    first, second = bounds[0], bounds[1]
    q0 = qi * BQ
    low = doc_start(q0, first, second) // BQ
    inner = (doc_start(q0 + BQ - 1, first, second) + BQ - 1) // BQ
    return low, jnp.minimum(jnp.maximum(inner, low), qi)


def allowed_keys(qi, kb, bounds):
    q = qi * BQ + rows_of((BQ, 1))
    k = kb * BQ + lanes((1, BQ))
    start = doc_start(q, bounds[0], bounds[1])
    return (k <= q) & (k >= start)


def attend_body(bounds, qp, kv, g2, out_ref, keep_ref):
    qi = pl.program_id(0)
    low, inner = block_range(qi, bounds)
    q = qp[...]

    def step(kb, carry, masked):
        top, total, acc = carry
        k = kv[pl.ds(pl.multiple_of(kb * BQ, BQ), BQ), :]
        s = dot_bt(q, k)
        if masked:
            s = jnp.where(allowed_keys(qi, kb, bounds), s, -1e30)
        new_top = jnp.maximum(top, jnp.max(s, axis=1, keepdims=True))
        p = jnp.exp(s - new_top)
        fade = jnp.exp(top - new_top)
        total = total * fade + jnp.sum(p, axis=1, keepdims=True)
        acc = acc * fade + dot(p.astype(BF), k)
        return new_top, total, acc

    carry = (jnp.full((BQ, 1), -1e30, F32), jnp.zeros((BQ, 1), F32), jnp.zeros((BQ, 128), F32))
    carry = lax.fori_loop(low, inner, lambda kb, c: step(kb, c, True), carry)
    carry = lax.fori_loop(inner, qi, lambda kb, c: step(kb, c, False), carry)
    top, total, acc = step(qi, carry, True)
    out = acc / total
    left = lanes((1, 128)) < 64
    out_ref[...] = jnp.where(left, g2[...], out.astype(BF))
    keep_ref[...] = jnp.where(left, top + jnp.log(total), out)


def attend(bounds, qp, kv, g2):
    full = qp.shape[0]
    block = pl.BlockSpec((BQ, 128), lambda i, *_: (i, 0))
    return pl.pallas_call(
        attend_body,
        grid_spec=pltpu.PrefetchScalarGridSpec(
            num_scalar_prefetch=1,
            grid=(full // BQ,),
            in_specs=[block, whole((full, 128)), block],
            out_specs=[block, block],
        ),
        out_shape=[
            jax.ShapeDtypeStruct((full, 128), BF),
            jax.ShapeDtypeStruct((full, 128), F32),
        ],
        compiler_params=params(),
        cost_estimate=SMALL_COST,
        name="attend",
    )(bounds, qp, kv, g2)


def attend_back_body(bounds, qp, kv, keep, grad, cos, sin, out_ref, acc_ref):
    blocks = pl.num_programs(0)
    qi = blocks - 1 - pl.program_id(0)
    left = lanes((1, 128)) < 64

    @pl.when(pl.program_id(0) == 0)
    def _():
        acc_ref[...] = jnp.zeros_like(acc_ref)

    low, inner = block_range(qi, bounds)
    q = qp[...]
    do = jnp.where(left, 0.0, grad[0].astype(F32))
    delta = jnp.sum(do * keep[...], axis=1, keepdims=True)
    do = do.astype(BF)
    lse = keep[:, :1]

    def step(kb, dq, masked):
        at = pl.ds(pl.multiple_of(kb * BQ, BQ), BQ)
        k = kv[at, :]
        p = jnp.exp(dot_bt(q, k) - lse)
        if masked:
            p = jnp.where(allowed_keys(qi, kb, bounds), p, 0.0)
        ds = (p * (dot_bt(do, k) - delta)).astype(BF)
        acc_ref[at, :] += dot_at(ds, q) + dot_at(p.astype(BF), do)
        return dq + dot(ds, k)

    dq = jnp.zeros((BQ, 128), F32)
    dq = lax.fori_loop(low, inner, lambda kb, c: step(kb, c, True), dq)
    dq = lax.fori_loop(inner, qi, lambda kb, c: step(kb, c, False), dq)
    dq = step(qi, dq, True) * 0.125
    dkv = acc_ref[pl.ds(pl.multiple_of(qi * BQ, BQ), BQ), :]
    c, s = cos[...], sin[...]
    out_ref[:, :128] = jnp.where(left, dkv * c, dkv).astype(BF)
    out_ref[:, 128:256] = (jnp.where(left, dkv, pltpu.roll(dq, 64, 1)) * s).astype(BF)
    out_ref[:, 256:] = jnp.where(left, dq * c, 0.0).astype(BF)


def attend_back(bounds, qp, kv, keep, grad, cos, sin):
    full = qp.shape[0]
    n = full // BQ
    block = pl.BlockSpec((BQ, 128), lambda i, *_: (n - 1 - i, 0))
    return pl.pallas_call(
        attend_back_body,
        grid_spec=pltpu.PrefetchScalarGridSpec(
            num_scalar_prefetch=1,
            grid=(n,),
            in_specs=[
                block,
                whole((full, 128)),
                block,
                pl.BlockSpec((1, BQ, 128), lambda i, *_: (n - 1 - i, 0, 1)),
                block,
                block,
            ],
            out_specs=pl.BlockSpec((BQ, 384), lambda i, *_: (n - 1 - i, 0)),
            scratch_shapes=[pltpu.VMEM((full, 128), F32)],
        ),
        out_shape=jax.ShapeDtypeStruct((full, 384), BF),
        compiler_params=params(),
        cost_estimate=SMALL_COST,
        name="attend_back",
    )(bounds, qp, kv, keep, grad, cos, sin)


def tap_mask(first_row, count, shift, bounds):
    pos = first_row + rows_of((count, 1))
    return (pos - doc_start(pos, bounds[0], bounds[1]) >= shift).astype(F32)


def conv_taps(ext_ref, r0, bounds, taps, bias):
    pre = bias + taps[3:4, :] * ext_ref[pl.ds(8, CHUNK), :]
    for shift in (1, 2, 3):
        mask = tap_mask(r0, CHUNK, shift, bounds)
        pre = pre + taps[3 - shift : 4 - shift, :] * (ext_ref[pl.ds(8 - shift, CHUNK), :] * mask)
    return pre


def chunk_decay(r0, bounds, dt_raw, head, extra=None):
    lane = lanes((1, CHUNK))
    dt = jax.nn.softplus(dt_raw + head[:, 0:1])
    la = dt * head[:, 1:2]
    upper = (rows_of((CHUNK, CHUNK)) <= lanes((CHUNK, CHUNK))).astype(F32)
    cum = dot(la, upper, precision=lax.Precision.HIGHEST)
    rows = [cum, dt] if extra is None else [cum, dt, extra]
    used = 8 * len(rows)
    stacked = jnp.concatenate(rows + [jnp.zeros((CHUNK - used, CHUNK), F32)], axis=0).T
    cum_col, dt_col = stacked[:, 0:8], stacked[:, 8:16]
    pos = r0 + rows_of((CHUNK, 1))
    start = doc_start(pos, bounds[0], bounds[1])
    start_last = doc_start(r0 + CHUNK - 1, bounds[0], bounds[1])
    key = r0 + lane
    mask = (key <= pos) & (key >= start)
    enter = jnp.where(start < r0, jnp.exp(cum_col), 0.0)
    fade = jnp.where(pos >= start_last, jnp.exp(cum_last_row(cum_col) - cum_col), 0.0)
    keep = jnp.where(start_last < r0, jnp.exp(cum_last_row(cum_col)), 0.0)
    return dt, la, cum, dt_col, cum_col, mask, enter, fade, keep, stacked[:, 16:24]


def two_terms(value):
    high = value.astype(BF)
    return high, (value - high.astype(F32)).astype(BF)


def cum_last_row(cum_col):
    return cum_col[CHUNK - 1 : CHUNK, :]


def per_head(col):
    return halves(col[:, 0:1], col[:, 1:2]), col[:, 2:3]


def state_rows(keep):
    row = rows_of((256, 1))
    return jnp.where(row < 64, keep[:, 0:1], jnp.where(row < 128, keep[:, 1:2], keep[:, 2:3]))


def scan_body(bounds, xbc, z, dt_raw, taps, bias, head, skip, g01, g2, y_ref, s_ref, ext, state):
    i = pl.program_id(0)
    r0 = i * CHUNK

    @pl.when(i == 0)
    def _():
        ext[pl.ds(0, 8), :] = jnp.zeros((8, 512), F32)
        state[...] = jnp.zeros_like(state)

    @pl.when(i > 0)
    def _():
        ext[pl.ds(0, 8), :] = ext[pl.ds(CHUNK, 8), :]

    ext[pl.ds(8, CHUNK), :] = xbc[...].astype(F32)
    pre = conv_taps(ext, r0, bounds, taps[...], bias[...])
    conv = pre * jax.nn.sigmoid(pre)
    x01, x2 = conv[:, :128], conv[:, 128:256]
    b, c = conv[:, 256:384].astype(BF), conv[:, 384:].astype(BF)
    dt, la, cum, dt_col, cum_col, mask, enter, fade, keep, _ = chunk_decay(
        r0, bounds, dt_raw[...], head[...]
    )
    inner = dot_bt(c, b)
    x01b, x2b = x01.astype(BF), x2.astype(BF)
    ys = []
    for h in range(3):
        gap = cum_col[:, h : h + 1] - cum[h : h + 1, :]
        decay = jnp.exp(jnp.where(mask, gap, -1e30))
        m = (inner * decay * dt[h : h + 1, :]).astype(BF)
        ys.append(dot(m, x01b if h < 2 else x2b))
    s0 = state[...]
    s_ref[0] = s0
    s0b, s0c = two_terms(s0)
    carried = dot_bt(c, s0b) + dot_bt(c, s0c)
    e01, e2 = per_head(enter)
    y01 = halves(ys[0], ys[1]) + e01 * carried[:, :128] + skip[:, :128] * x01
    y2 = ys[2] + e2 * carried[:, 128:] + skip[:, 128:] * x2
    w01, w2 = per_head(fade * dt_col)
    xw = jnp.concatenate([(x01 * w01).astype(BF), (x2 * w2).astype(BF)], axis=1)
    state[...] = s0 * state_rows(keep) + dot_at(xw, b)
    y_ref[:, :128] = y01
    y_ref[:, 128:] = y2
    z01, z2 = z[:, :128], z[:, 128:]
    g01[...] = (y01 * (z01 * jax.nn.sigmoid(z01))).astype(BF)
    g2[...] = (y2 * (z2 * jax.nn.sigmoid(z2))).astype(BF)


def scan_forward(bounds, xbc, z, dt_raw, taps, bias, head, skip):
    full = xbc.shape[0]
    n = full // CHUNK
    row = lambda width: pl.BlockSpec((CHUNK, width), lambda i, *_: (i, 0))
    return pl.pallas_call(
        scan_body,
        grid_spec=pltpu.PrefetchScalarGridSpec(
            num_scalar_prefetch=1,
            grid=(n,),
            in_specs=[
                row(512),
                row(256),
                pl.BlockSpec((8, CHUNK), lambda i, *_: (0, i)),
                whole((8, 512)),
                whole((1, 512)),
                whole((8, 128)),
                whole((1, 256)),
            ],
            out_specs=[
                row(128),
                row(128),
                row(256),
                pl.BlockSpec((1, 256, 128), lambda i, *_: (i, 0, 0)),
            ],
            scratch_shapes=[pltpu.VMEM((CHUNK + 8, 512), F32), pltpu.VMEM((256, 128), F32)],
        ),
        out_shape=[
            jax.ShapeDtypeStruct((full, 128), BF),
            jax.ShapeDtypeStruct((full, 128), BF),
            jax.ShapeDtypeStruct((full, 256), F32),
            jax.ShapeDtypeStruct((n, 256, 128), F32),
        ],
        compiler_params=params(),
        cost_estimate=SMALL_COST,
        name="scan_forward",
    )(bounds, xbc, z, dt_raw, taps, bias, head, skip)


def scalar_rows(terms):
    total = terms[0:2, :] + terms[2:4, :] + terms[4:6, :]
    return jnp.concatenate([total, jnp.zeros((6, CHUNK), F32)], axis=0)


def scan_back_body(
    last, bounds, xbc, before, z, y, dt_raw, s0_ref, dn01, dn2, scal, taps, bias, head, skip, gain,
    dstate_in, dext_in, acc_in, head_in,
    out_ref, dt_grad, acc, head_acc, dstate_out, dext_out, ext, dext, dstate,
):
    step = pl.program_id(0)
    i = last - step
    r0 = i * CHUNK
    left = lanes((1, 128)) < 64

    @pl.when(step == 0)
    def _():
        dext[pl.ds(CHUNK, 8), :] = dext_in[...]
        dstate[...] = dstate_in[...]
        acc[...] = acc_in[...]
        head_acc[...] = head_in[...]

    @pl.when(step > 0)
    def _():
        dext[pl.ds(CHUNK, 8), :] = dext[pl.ds(0, 8), :]

    ext[pl.ds(0, 8), :] = before[...].astype(F32)[8:, :]
    ext[pl.ds(8, CHUNK), :] = xbc[...].astype(F32)
    weights = taps[...]
    pre = conv_taps(ext, r0, bounds, weights, bias[...])
    sig = jax.nn.sigmoid(pre)
    conv = pre * sig
    x01, x2 = conv[:, :128], conv[:, 128:256]
    b, c = conv[:, 256:384].astype(BF), conv[:, 384:].astype(BF)
    dt, la, cum, dt_col, cum_col, mask, enter, fade, keep, scalars = chunk_decay(
        r0, bounds, dt_raw[...], head[...], scalar_rows(scal[0].astype(F32))
    )
    row_scale, row_cross = scalars[:, 0:1], scalars[:, 1:2]

    def gate_back(dn, gain, zz, yy):
        s = jax.nn.sigmoid(zz)
        act = zz * s
        g = yy * act
        sent = g.astype(BF).astype(F32)
        ratio = jnp.where(g == 0.0, 1.0, sent / g)
        dg = (dn * gain * row_scale - sent * row_cross) * ratio
        return dg * act, dg * yy * (s + act * (1.0 - s))

    dy01, dz01 = gate_back(dn01[0].astype(F32), gain[:, :128], z[:, :128], y[:, :128])
    dy2, dz2 = gate_back(dn2[0].astype(F32), gain[:, 128:], z[:, 128:], y[:, 128:])
    dy2, dz2 = jnp.where(left, dy2, 0.0), jnp.where(left, dz2, 0.0)
    inner = dot_bt(c, b)
    x01b, x2b = x01.astype(BF), x2.astype(BF)
    dy01b, dy2b = dy01.astype(BF), dy2.astype(BF)
    zero = jnp.zeros_like(dy01b)
    parts = [(jnp.where(left, dy01b, zero), x01b), (jnp.where(left, zero, dy01b), x01b), (dy2b, x2b)]
    d_inner = jnp.zeros((CHUNK, CHUNK), F32)
    dxs, col_sums, direct, row_sums = [], [], [], []
    for h in range(3):
        gap = cum_col[:, h : h + 1] - cum[h : h + 1, :]
        decay = jnp.exp(jnp.where(mask, gap, -1e30))
        dt_h = dt[h : h + 1, :]
        dyh, xh = parts[h]
        dm = dot_bt(dyh, xh)
        kept = inner * decay
        m = (kept * dt_h).astype(BF)
        dxs.append(dot_at(m, dyh if h == 2 else dy01b))
        pulled = dm * kept
        d_inner = d_inner + dm * (decay * dt_h)
        weighted = pulled * dt_h
        direct.append(jnp.sum(pulled, axis=0, keepdims=True))
        col_sums.append(jnp.sum(weighted, axis=0, keepdims=True))
        row_sums.append(jnp.sum(weighted, axis=1, keepdims=True))
    s0 = s0_ref[0]
    s0b, s0c = two_terms(s0)
    ds1 = dstate[...]
    ds1b, ds1c = two_terms(ds1)
    e01, e2 = per_head(enter)
    ey01, ey2 = dy01 * e01, dy2 * e2
    ey, eyc = two_terms(jnp.concatenate([ey01, ey2], axis=1))
    carried = dot_bt(c, s0b) + dot_bt(c, s0c)
    f01, f2 = per_head(fade)
    d01, d2 = per_head(dt_col)
    back = dot_bt(b, ds1b)
    fb01, fb2 = f01 * back[:, :128], f2 * back[:, 128:]
    xw = jnp.concatenate([(x01 * (f01 * d01)).astype(BF), (x2 * (f2 * d2)).astype(BF)], axis=1)
    d_innerb = d_inner.astype(BF)
    dc = dot(d_innerb, b) + dot(ey, s0b) + dot(eyc, s0b) + dot(ey, s0c)
    db = dot_at(d_innerb, c) + dot(xw, ds1b) + dot(xw, ds1c)
    dx01 = halves(dxs[0], dxs[1]) + d01 * fb01 + skip[:, :128] * dy01
    dx2 = dxs[2] + d2 * fb2 + skip[:, 128:] * dy2
    kept_rows = state_rows(keep)
    crossing = jnp.sum(ds1 * s0 * kept_rows, axis=1, keepdims=True)
    dstate[...] = ds1 * kept_rows + dot_at(ey, c) + dot_at(eyc, c)
    inter01, inter2 = ey01 * carried[:, :128], ey2 * carried[:, 128:]
    u01, u2 = x01 * fb01, x2 * fb2
    pick = lambda v, h: jnp.where(left if h == 0 else ~left, v, 0.0)
    side = lambda v01, v2, h: jnp.sum(pick(v01, h) if h < 2 else v2, axis=1, keepdims=True)
    lane = lanes((1, CHUNK))
    tile = jnp.zeros((CHUNK, CHUNK), F32)
    crossed = jnp.zeros((8, 1), F32)
    head_row = rows_of((8, 1))
    for h in range(3):
        u = side(u01, u2, h)
        moved = row_sums[h] + side(inter01, inter2, h) - u * dt_col[:, h : h + 1]
        tile = jnp.where(lane == h, moved, jnp.where(lane == 8 + h, u, tile))
        total = jnp.sum(crossing[64 * h : 64 * h + 64, :], axis=0, keepdims=True)
        total = total + jnp.sum(u * dt_col[:, h : h + 1], axis=0, keepdims=True)
        crossed = jnp.where(head_row == h, total, crossed)
    tile = tile.T
    stack = lambda items: jnp.concatenate(items + [jnp.zeros((5, CHUNK), F32)], axis=0)
    dcum = tile[0:8, :] - stack(col_sums) + jnp.where(lane == CHUNK - 1, crossed, 0.0)
    lower = (rows_of((CHUNK, CHUNK)) >= lanes((CHUNK, CHUNK))).astype(F32)
    dla = dot(dcum, lower, precision=lax.Precision.HIGHEST)
    ddt = stack(direct) + tile[8:16, :] + dla * head[:, 1:2]
    graw = ddt * jax.nn.sigmoid(dt_raw[...] + head[:, 0:1])
    dt_grad[...] = graw
    head_acc[0:8, :] += dla * la
    head_acc[8:16, :] += graw
    dpre = jnp.concatenate([dx01, dx2, db, dc], axis=1) * (sig + conv * (1.0 - sig))
    dext[pl.ds(0, CHUNK), :] = dpre
    din = weights[3:4, :] * dpre
    acc[3:4, :] += jnp.sum(dpre * ext[pl.ds(8, CHUNK), :], axis=0, keepdims=True)
    acc[4:5, :] += jnp.sum(dpre, axis=0, keepdims=True)
    acc[5:6, :128] += jnp.sum(dy01 * x01, axis=0, keepdims=True)
    acc[5:6, 128:256] += jnp.sum(dy2 * x2, axis=0, keepdims=True)
    for shift in (1, 2, 3):
        tap = 3 - shift
        now = tap_mask(r0, CHUNK, shift, bounds)
        acc[tap : tap + 1, :] += jnp.sum(
            dpre * (ext[pl.ds(8 - shift, CHUNK), :] * now), axis=0, keepdims=True
        )
        later = tap_mask(r0 + shift, CHUNK, shift, bounds)
        din = din + weights[tap : tap + 1, :] * (dext[pl.ds(shift, CHUNK), :] * later)
    out_ref[:, :128] = din[:, :128].astype(BF)
    out_ref[:, 128:256] = jnp.where(left, din[:, 128:256], pltpu.roll(dz2, 64, 1)).astype(BF)
    out_ref[:, 256:384] = dz01.astype(BF)
    out_ref[:, 384:] = din[:, 256:].astype(BF)

    @pl.when(step == pl.num_programs(0) - 1)
    def _():
        dstate_out[...] = dstate[...]
        dext_out[...] = dext[pl.ds(0, 8), :]


def scan_back(part, carry, bounds, xbc, z, y, dt_raw, states, dn, taps, bias, head, skip, gain):
    full = xbc.shape[0]
    n = full // CHUNK
    half = n // 2
    last = n - 1 if part == 0 else half - 1
    row = lambda width: pl.BlockSpec((CHUNK, width), lambda i, *_: (last - i, 0))
    tall = CHUNK // 16
    per = n // 8
    sent = lambda col: pl.BlockSpec(
        (1, CHUNK, 128), lambda i, b: ((last - i) // per, (last - i) % per, col)
    )

    def terms(i, b):
        piece, rest = (last - i) // per, (last - i) % per
        return piece, per * (CHUNK // 16) + rest // 2, rest % 2

    carried = [whole((256, 128)), whole((8, 512)), whole((8, 512)), whole((16, CHUNK))]
    sds = jax.ShapeDtypeStruct
    return pl.pallas_call(
        functools.partial(scan_back_body, last),
        grid_spec=pltpu.PrefetchScalarGridSpec(
            num_scalar_prefetch=1,
            grid=(half,),
            in_specs=[
                row(512),
                pl.BlockSpec((16, 512), lambda i, *_: (jnp.maximum((last - i) * tall - 1, 0), 0)),
                row(256),
                row(256),
                pl.BlockSpec((8, CHUNK), lambda i, *_: (0, last - i)),
                pl.BlockSpec((1, 256, 128), lambda i, *_: (last - i, 0, 0)),
                sent(0),
                sent(1),
                pl.BlockSpec((1, 16, CHUNK), terms),
                whole((8, 512)),
                whole((1, 512)),
                whole((8, 128)),
                whole((1, 256)),
                whole((1, 256)),
            ]
            + carried,
            out_specs=[
                pl.BlockSpec((CHUNK, 640), lambda i, *_: (half - 1 - i, 0)),
                pl.BlockSpec((8, CHUNK), lambda i, *_: (0, half - 1 - i)),
                whole((8, 512)),
                whole((16, CHUNK)),
                whole((256, 128)),
                whole((8, 512)),
            ],
            scratch_shapes=[
                pltpu.VMEM((CHUNK + 8, 512), F32),
                pltpu.VMEM((CHUNK + 8, 512), F32),
                pltpu.VMEM((256, 128), F32),
            ],
        ),
        out_shape=[
            sds((full // 2, 640), BF),
            sds((8, full // 2), F32),
            sds((8, 512), F32),
            sds((16, CHUNK), F32),
            sds((256, 128), F32),
            sds((8, 512), F32),
        ],
        compiler_params=params(),
        cost_estimate=SMALL_COST,
        name="scan_back",
    )(bounds, xbc, xbc, z, y, dt_raw, states, dn, dn, dn, taps, bias, head, skip, gain, *carry)


ROW_BLOCK = 256


def row_body(bounds, g, h, tok, gout, mlp_gain, gains, *refs):
    packs, refs = refs[:10], refs[10:]
    pa, pb, slots = [], [], []
    for k, base in enumerate((0, 5)):
        for r in range(4):
            first = packs[base + r]
            second = first.at[:, 512:] if r < 3 else packs[base + 4]
            pa.append(first.at[:, 0:512])
            pb.append(second)
            slots.append((bounds[3] ^ k) * 4 + (bounds[2] ^ r))
    gain_rows = [gains[slot] for slot in slots]
    out_ref, two_ref, dmix_ref, dhid_ref = refs[0:4]
    act_refs, dgu_refs, gn_refs = refs[4:6], refs[6:8], refs[8:10]
    dn, mlp_acc, gain_acc = refs[10:13]
    step = pl.program_id(0)
    left = lanes((1, 128)) < 64
    width = 1536.0

    @pl.when(pl.program_id(0) == 0)
    def _():
        mlp_acc[...] = jnp.zeros_like(mlp_acc)
        gain_acc[...] = jnp.zeros_like(gain_acc)

    pieces = [(r, k) for k in range(2) for r in range(4)]

    def part(ref, s):
        return ref[slots[s]].astype(F32)

    squares = 0.0
    for s in range(8):
        first, second = part(g, s), part(h, s)
        squares = squares + first * first + jnp.where(left, second * second, 0.0)
    rg = lax.rsqrt(jnp.sum(squares, axis=1, keepdims=True) / width + EPSILON)
    mixed = 0.0
    for s, (r, k) in enumerate(pieces):
        gain = gain_rows[s]
        first = part(g, s) * rg * gain[:, :128]
        second = part(h, s)
        second = jnp.where(left, second * rg * gain[:, 128:], second)
        gn = jnp.concatenate([first.astype(BF), second.astype(BF)], axis=1)
        gn_refs[k][:, r * 256 : r * 256 + 256] = gn
        mixed = mixed + dot_bt(gn, pb[s][:, 256:])
    hidden = tok[...].astype(F32) + mixed
    scale = lax.rsqrt(jnp.mean(hidden * hidden, axis=-1, keepdims=True) + EPSILON)
    two = (hidden * scale * mlp_gain[...]).astype(BF)
    two_ref[...] = two
    grad = gout[...]
    ffn = 0.0
    dtwo = 0.0
    for s, (r, k) in enumerate(pieces):
        weight, down = pa[s][...], pb[s][:, :256]
        gu = dot(two, weight)
        gate, up = gu[:, :256], gu[:, 256:]
        sig = jax.nn.sigmoid(gate)
        silu = gate * sig
        act = (silu * up).astype(BF)
        act_refs[k][:, r * 256 : r * 256 + 256] = act
        ffn = ffn + dot_bt(act, down)
        dact = dot(grad, down)
        dgate = (dact * up * (sig + silu * (1.0 - sig))).astype(BF)
        dgu = jnp.concatenate([dgate, (dact * silu).astype(BF)], axis=1)
        dgu_refs[k][:, r * 512 : r * 512 + 512] = dgu
        dtwo = dtwo + dot_bt(dgu, weight)
    out_ref[...] = (hidden + ffn).astype(BF)
    weighted = dtwo * mlp_gain[...]
    mlp_acc[...] += jnp.sum(dtwo * (hidden * scale), axis=0, keepdims=True)
    mean = jnp.mean(weighted * hidden, axis=-1, keepdims=True)
    dhid = grad.astype(F32) + scale * weighted - hidden * (scale * scale * scale * mean)
    dhid_ref[...] = dhid
    dmix = dhid.astype(BF)
    dmix_ref[...] = dmix
    cross = 0.0
    for s, (r, k) in enumerate(pieces):
        dgn = dot(dmix, pb[s][:, 256:]).astype(BF)
        dn[slots[s], pl.ds(pl.multiple_of(step * ROW_BLOCK, ROW_BLOCK), ROW_BLOCK), :] = dgn
        first, second = dgn[:, :128].astype(F32), dgn[:, 128:].astype(F32)
        gain = gain_rows[s]
        own1, own2 = part(g, s), jnp.where(left, part(h, s), 0.0)
        t1, t2 = first * own1, second * own2
        gain_acc[slots[s], :, :128] += jnp.sum(t1 * rg, axis=0, keepdims=True)
        gain_acc[slots[s], :, 128:] += jnp.sum(t2 * rg, axis=0, keepdims=True)
        cross = cross + t1 * gain[:, :128] + t2 * gain[:, 128:]
    cross = jnp.sum(cross, axis=1, keepdims=True) * (rg * rg * rg / width)
    lane = lanes((1, 128))
    tile = jnp.where(lane == 0, rg, jnp.where(lane == 1, cross, 0.0))
    pair = tile.T[0:2, :]
    high = pair.astype(BF)
    rest = pair - high.astype(F32)
    middle = rest.astype(BF)
    low = (rest - middle.astype(F32)).astype(BF)
    block = jnp.concatenate(
        [v.astype(F32) for v in (high, middle, low)] + [jnp.zeros((10, ROW_BLOCK), F32)], axis=0
    ).astype(BF)
    for s in range(8):
        dn[s, pl.ds(pl.multiple_of(2 * ROW_BLOCK + step * 16, 16), 16), :] = block


def row_stage(bounds, g, h, tokens, gout, mlp_gain, gains, packs):
    n = ROW_BLOCK
    count = 2 * n
    row = lambda w: pl.BlockSpec((n, w), lambda i, b: (i, 0))
    part = pl.BlockSpec((n, 1024), lambda i, b: (2 * b[2] + i, 0))
    piece = pl.BlockSpec((8, n, 128), lambda i, b: (0, i, 0))
    once = lambda shape: pl.BlockSpec(
        shape, lambda i, b: (0,) * len(shape), pipeline_mode=pl.Buffered(1)
    )
    sds = jax.ShapeDtypeStruct
    widths = [1024] * 4 + [1024] * 2 + [2048] * 2 + [1024] * 2
    dtypes = [BF] * 3 + [F32] + [BF] * 6
    return pl.pallas_call(
        row_body,
        grid_spec=pltpu.PrefetchScalarGridSpec(
            num_scalar_prefetch=1,
            grid=(2,),
            in_specs=[piece, piece, part, part, whole((1, 1024)), whole((8, 1, 256))]
            + [once(p.shape) for p in packs],
            out_specs=[row(w) for w in widths]
            + [once((8, count + 32, 256)), whole((1, 1024)), whole((8, 1, 256))],
        ),
        out_shape=[sds((count, w), d) for w, d in zip(widths, dtypes)]
        + [sds((8, count + 32, 256), BF), sds((1, 1024), F32), sds((8, 1, 256), F32)],
        compiler_params=pltpu.CompilerParams(vmem_limit_bytes=58 * 1024 * 1024),
        cost_estimate=SMALL_COST,
        name="row_stage",
    )(bounds, g, h, tokens, gout, mlp_gain, gains, *packs)


def weight_body(two, gout, dmix, dgu, act, gn, a_ref, b_ref):
    a_ref[0] = dot_at(two[...], dgu[...]).astype(BF)
    b_ref[0, :, :256] = dot_at(gout[...], act[...]).astype(BF)
    b_ref[0, :, 256:] = dot_at(dmix[...], gn[...]).astype(BF)


def weight_stage(two, gout, dmix, dgu, act, gn):
    count = two.shape[0]
    col = lambda w: pl.BlockSpec((count, w), lambda i: (0, i))
    out = pl.BlockSpec((1, 1024, 512), lambda i: (i, 0, 0))
    return pl.pallas_call(
        weight_body,
        grid=(4,),
        in_specs=[whole((count, 1024))] * 3 + [col(512), col(256), col(256)],
        out_specs=[out, out],
        out_shape=[jax.ShapeDtypeStruct((4, 1024, 512), BF)] * 2,
        compiler_params=params(),
        cost_estimate=SMALL_COST,
        name="weight_stage",
    )(two, gout, dmix, dgu, act, gn)


def with_steps(da, dt_grad):
    count = da.shape[0]
    cols = jnp.concatenate([dt_grad, jnp.zeros((120, count), F32)], axis=0).T
    last = jnp.where(lanes((1, 128)) < 64, da[:, 256:].astype(F32), pltpu.roll(cols, 64, 1))
    return jnp.concatenate([da[:, :256], last.astype(BF)], axis=1)


def input_grad_body(da, ds, dt_grad, weight, out_ref):
    left = with_steps(da[...], dt_grad[...])
    out_ref[...] = (dot_bt(left, weight[:, :384]) + dot_bt(ds[...], weight[:, 384:])).astype(BF)


def input_grad(part, da, ds, dt_grad, weight):
    n = PROJ_ROWS
    own = ds.shape[0]
    start = 0 if part == 1 else own // n
    return pl.pallas_call(
        input_grad_body,
        grid=(own // n,),
        in_specs=[
            pl.BlockSpec((n, 384), lambda i: (start + i, 0)),
            pl.BlockSpec((n, 640), lambda i: (i, 0)),
            pl.BlockSpec((8, n), lambda i: (0, i)),
            whole((1024, 1024)),
        ],
        out_specs=pl.BlockSpec((n, 1024), lambda i: (i, 0)),
        out_shape=jax.ShapeDtypeStruct((own, 1024), BF),
        compiler_params=params(),
        cost_estimate=SMALL_COST,
        name="input_grad",
    )(da, ds, dt_grad, weight)


def project_grad_body(bounds, normed, da, ds_lo, ds_hi, dt_lo, dt_hi, alone, shared, acc_a, acc_s):
    @pl.when(pl.program_id(0) == 0)
    def _():
        acc_a[...] = jnp.zeros_like(acc_a)
        acc_s[...] = jnp.zeros_like(acc_s)

    def add(ds, dt_grad):
        acc_a[...] += dot_at(normed[...], with_steps(da[...], dt_grad[...]))
        acc_s[...] += dot_at(normed[...], ds[...])

    half = pl.num_programs(0) // 2
    pl.when(pl.program_id(0) < half)(lambda: add(ds_lo, dt_lo))
    pl.when(pl.program_id(0) >= half)(lambda: add(ds_hi, dt_hi))

    @pl.when(pl.program_id(0) == pl.num_programs(0) - 1)
    def _():
        lane = lanes((1, 128))
        left = lane < 64
        turned = acc_a[:, 128:256]
        turned = jnp.where(lane % 64 < 32, pltpu.roll(turned, 96, 1), -pltpu.roll(turned, 32, 1))
        kv = acc_a[:, :128] + jnp.where(left, turned, 0.0)
        q = acc_a[:, 256:] + jnp.where(left, pltpu.roll(turned, 64, 1), 0.0)
        alone[:, :128] = q.astype(BF)
        alone[:, 128:] = acc_s[:, :384].astype(BF)
        low = bounds[2] // 2 == 0
        swapped = pltpu.roll(kv, 64, 1)
        keys = jnp.where(left == low, jnp.where(low, kv, swapped), 0.0)
        values = jnp.where(left == low, jnp.where(low, swapped, kv), 0.0)
        shared[:, :128] = keys.astype(BF)
        shared[:, 128:256] = values.astype(BF)
        shared[:, 256:] = acc_s[:, 384:].astype(BF)


def project_grad(bounds, normed, da, ds_lo, ds_hi, dt_lo, dt_hi):
    full = normed.shape[0]
    n = 512
    half = full // n // 2
    low = lambda i: jnp.minimum(i, half - 1)
    high = lambda i: jnp.maximum(i - half, 0)
    row = lambda w: pl.BlockSpec((n, w), lambda i, *_: (i, 0))
    return pl.pallas_call(
        project_grad_body,
        grid_spec=pltpu.PrefetchScalarGridSpec(
            num_scalar_prefetch=1,
            grid=(full // n,),
            in_specs=[
                row(1024),
                row(384),
                pl.BlockSpec((n, 640), lambda i, *_: (low(i), 0)),
                pl.BlockSpec((n, 640), lambda i, *_: (high(i), 0)),
                pl.BlockSpec((8, n), lambda i, *_: (0, low(i))),
                pl.BlockSpec((8, n), lambda i, *_: (0, high(i))),
            ],
            out_specs=[whole((1024, 512))] * 2,
            scratch_shapes=[pltpu.VMEM((1024, 384), F32), pltpu.VMEM((1024, 640), F32)],
        ),
        out_shape=[jax.ShapeDtypeStruct((1024, 512), BF)] * 2,
        compiler_params=params(),
        cost_estimate=SMALL_COST,
        name="project_grad",
    )(bounds, normed, da, ds_lo, ds_hi, dt_lo, dt_hi)


def assemble_body(bounds, p0, p1, p2, l3, r3, out):
    step = pl.program_id(0)
    for r, ref in enumerate((p0, p1, p2)):

        @pl.when(step == r)
        def _(ref=ref):
            out[...] = ref[...]

    @pl.when(step == 3)
    def _():
        out[:, :512] = l3[...]
        out[:, 512:] = r3[...]


def assemble(bounds, parts):
    count = parts[0].shape[0]
    return pl.pallas_call(
        assemble_body,
        grid_spec=pltpu.PrefetchScalarGridSpec(
            num_scalar_prefetch=1,
            grid=(4,),
            in_specs=[whole(p.shape) for p in parts],
            out_specs=pl.BlockSpec((count, 1024), lambda i, b: (i ^ b[2], 0)),
        ),
        out_shape=jax.ShapeDtypeStruct((4 * count, 1024), parts[0].dtype),
        compiler_params=params(),
        cost_estimate=SMALL_COST,
        name="assemble",
    )(bounds, *parts)


def swap(value, step):
    return lax.ppermute(value, "tensor", [(i, i ^ step) for i in range(4)])


def twin(value):
    return lax.ppermute(value, "ctx", [(0, 1), (1, 0)])


def exchange(value):
    return lax.all_to_all(value, ("ctx", "tensor"), 0, 0, tiled=True)


def dp_swap(value, step):
    return lax.ppermute(value, "dp", [(i, i ^ step) for i in range(4)])


def dp_first(value):
    inner = (lax.axis_index("dp") == 1) | (lax.axis_index("dp") == 2)
    half = value.shape[0] // 2
    first, second = value[:half], value[half:]
    sent = jnp.where(inner, second, first)
    return jnp.where(inner, first, second), dp_swap(sent, 1)


def dp_second(pair):
    kept = plus(*pair)
    return kept, lax.ppermute(kept, "dp", [(1, 2), (2, 1), (0, 3), (3, 0)])


def dp_third(pair):
    kept = plus(*pair)
    return kept, dp_swap(kept, 1)


def dp_end(pair):
    inner = (lax.axis_index("dp") == 1) | (lax.axis_index("dp") == 2)
    kept, got = pair
    return jnp.concatenate([jnp.where(inner, kept, got), jnp.where(inner, got, kept)], axis=0)


def dp_sum(value):
    if lax.axis_size("dp") != 4:
        return lax.psum(value, "dp")
    return dp_end(dp_third(dp_second(dp_first(value))))


def all_sum(value):
    value = value + twin(value)
    value = value + swap(value, 1)
    value = value + swap(value, 2)
    if lax.axis_size("dp") != 4:
        return lax.psum(value, "dp")
    value = value + dp_swap(value, 1)
    return value + dp_swap(value, 2)


def together(*values):
    return lax.optimization_barrier(values)


def after(value, *before):
    return lax.optimization_barrier((value, before))[0]


def plus(a, b):
    return (a.astype(F32) + b.astype(F32)).astype(BF)


def block_at(value, index, count):
    return lax.dynamic_slice_in_dim(value, index * count, count, 0)


def core_swap(value, step, core):
    pairs = [(core * 4 + i, core * 4 + (i ^ step)) for i in range(4)]
    return lax.ppermute(value, ("ctx", "tensor"), pairs)


def scatter_first(value, t, send):
    count = value.shape[0] // 4
    half = value.shape[1] // 2
    at = lambda r, lo: lax.dynamic_slice(value, ((t ^ r) * count, lo), (count, half))
    left = send(jnp.concatenate([at(3, 0), at(1, 0)], axis=0), 1)
    right = send(jnp.concatenate([at(3, half), at(2, half)], axis=0), 2)
    return at(0, 0), at(0, half), at(2, 0), at(1, half), left, right


def scatter_second(state, send):
    left0, right0, left2, right1, left, right = state
    count = left0.shape[0]
    next_l = send(plus(left2, left[:count]), 2)
    next_r = send(plus(right1, right[:count]), 1)
    return left0, right0, left[count:], right[count:], next_l, next_r


def scatter_end(state):
    left0, right0, left, right, next_l, next_r = state
    add = lambda a, b, c: a.astype(F32) + b.astype(F32) + c.astype(F32)
    return jnp.concatenate([add(left0, left, next_l), add(right0, right, next_r)], axis=1)


def bit_scatter(value, t, c):
    for bit, send in ((c, twin), (t % 2, lambda v: swap(v, 1)), (t // 2, lambda v: swap(v, 2))):
        half = value.shape[0] // 2
        got = send(block_at(value, 1 - bit, half))
        value = plus(block_at(value, bit, half), got)
    return value


def bit_gather(value, t, c):
    for bit, send in ((t // 2, lambda v: swap(v, 2)), (t % 2, lambda v: swap(v, 1)), (c, twin)):
        value = ordered(value, send(value), bit, 0)
    return value


def rope_tables(count):
    exponent = np.arange(0, HEAD_SIZE, 2).astype(np.float32) / np.float32(HEAD_SIZE)
    frequency = (np.float32(ROPE_BASE) ** (-exponent)).astype(np.float32)
    angles = np.arange(count).astype(np.float32)[:, None] * frequency[None, :]
    angles = np.concatenate([angles] * 4, axis=1)
    return (np.cos(angles).astype(np.float32), np.sin(angles).astype(np.float32))


def ordered(own, other, c, axis):
    return jnp.concatenate(
        [jnp.where(c == 0, own, other), jnp.where(c == 0, other, own)], axis=axis
    )


def local(
    tokens, doc_ids, norm_gain, q_proj, key_value_weight, o_proj, z_proj, x_proj, dt_proj,
    bc_proj, conv_x, xconv_bias, conv_bc, bcconv_bias, dt_bias, a_log, skip_gain, gated_gain,
    out_proj, mlp_gain, gate_proj, up_proj, down_proj, out_grad,
):
    t, c = lax.axis_index("tensor"), lax.axis_index("ctx")
    own_tokens, grad_out = tokens[0], out_grad[0]
    own = own_tokens.shape[0]
    full = 2 * own
    mine = own // 4
    other_tokens = twin(own_tokens)

    def cols(w):
        n = w.shape[-1] // 2
        return lax.dynamic_slice_in_dim(w, c * n, n, w.ndim - 1)

    def rows(w):
        return block_at(w, c, w.shape[0] // 2)

    docs = doc_ids[0]
    bounds = jnp.stack([jnp.sum(docs < 1), jnp.sum(docs < 2), t, c]).astype(jnp.int32)
    weight, pack0 = prepare(
        bounds, gate_proj, up_proj, down_proj, out_proj, o_proj, key_value_weight, q_proj,
        x_proj, z_proj, dt_proj, bc_proj,
    )
    pack1, pack2 = swap(pack0, 1), swap(pack0, 2)
    own_gain = rows(gated_gain)
    gain0 = jnp.concatenate([own_gain, jnp.ones((64,), F32)])
    gains = exchange(jnp.broadcast_to(gain0[None, None], (8, 1, 256)))

    cos, sin = rope_tables(full)
    cos, sin = jnp.asarray(cos), jnp.asarray(sin)
    steps = own // PROJ_ROWS
    own_off = jnp.reshape(c * steps, (1,)).astype(jnp.int32)
    other_off = jnp.reshape((1 - c) * steps, (1,)).astype(jnp.int32)
    gain_row = norm_gain[None]
    first = project(own_off, own_tokens, gain_row, weight, cos, sin)
    normed, qp, kv, xbc, z, dt_raw = project(
        other_off, other_tokens, gain_row, weight, cos, sin, before=first
    )

    pad = lambda v: jnp.zeros(v.shape[:-1] + (64,), F32)
    cx, cb = cols(conv_x), cols(xconv_bias)
    taps = jnp.concatenate([cx, pad(cx), conv_bc], axis=1)
    taps = jnp.concatenate([taps, jnp.zeros_like(taps)], axis=0)
    bias = jnp.concatenate([cb, pad(cb), bcconv_bias])[None]
    head = jnp.stack([cols(dt_bias), -jnp.exp(cols(a_log))], axis=1)
    head = jnp.pad(head, ((0, 5), (0, 126)))
    skip = jnp.pad(jnp.repeat(cols(skip_gain), MP), (0, 64))[None]
    g01, g2, y, states = scan_forward(bounds, xbc, z, dt_raw, taps, bias, head, skip)
    g2, g01, pack1, pack2 = together(g2, g01, pack1, pack2)
    left3, right3 = pack1[:, :512], pack2[:, 512:]
    qp, left3, right3, g01 = together(qp, left3, right3, g01)
    left3, right3 = swap(left3, 2), swap(right3, 1)
    near = [pack0, pack1, pack2]
    far = [twin(v) for v in near]
    g_rows = exchange(g01.reshape(8, mine, 128))
    tile, keep = attend(bounds, qp, kv, g2)
    tile, g_rows, far = together(tile, g_rows, far)
    h_rows = exchange(tile.reshape(8, mine, 128))
    packs = near + [left3, right3] + far + [twin(left3), twin(right3)]

    res = row_stage(bounds, g_rows, h_rows, own_tokens, grad_out, mlp_gain[None], gains, packs)
    layer_rows, two, dmix, dhid = res[0:4]
    act, dgu, gn = list(res[4:6]), list(res[6:8]), list(res[8:10])
    mlp_part, gain_part = res[11:13]
    grad_rows = block_at(grad_out, t, mine)
    dn = exchange(res[10])
    far_a, far_b = weight_stage(two, grad_rows, dmix, dgu[1], act[1], gn[1])
    dgu, act, gn, far_a, far_b = together(dgu, act, gn, far_a, far_b)
    far_a, far_b = twin(far_a), twin(far_b)
    near_a, near_b = weight_stage(two, grad_rows, dmix, dgu[0], act[0], gn[0])
    dn, near_a, near_b, far_a, far_b = together(dn, near_a, near_b, far_a, far_b)
    sum_a = [plus(near_a[r], far_a[r]) for r in range(4)]
    sum_b = [plus(near_b[r], far_b[r]) for r in range(4)]
    dn, sum_a, sum_b = together(dn, sum_a, sum_b)

    a3, b3 = swap(sum_a[3], 1), swap(sum_b[3], 2)
    a1, b2 = swap(sum_a[1], 1), swap(sum_b[2], 2)
    da = attend_back(bounds, qp, kv, keep, dn, cos, sin)
    da, a3, b3 = together(da, a3, b3)
    a_next, b_next = plus(sum_a[2], a3), plus(sum_b[1], b3)
    xbc, a_next, b_next = together(xbc, a_next, b_next)
    a_next, b_next = swap(a_next, 2), swap(b_next, 1)
    own_gain_row = jnp.pad(own_gain, (0, 64))[None]
    zeros = [
        jnp.zeros((256, 128), F32),
        jnp.zeros((8, 512), F32),
        jnp.zeros((8, 512), F32),
        jnp.zeros((16, CHUNK), F32),
    ]
    back = lambda part, carry, data: scan_back(
        part, carry, bounds, data, z, y, dt_raw, states, dn, taps, bias, head, skip, own_gain_row
    )
    ds_hi, dt_hi, conv_acc, head_acc, dstate, dext = back(0, zeros, xbc)
    ds_hi, a1, b2, a_next, b_next, layer_rows = together(
        ds_hi, a1, b2, a_next, b_next, layer_rows
    )
    add3 = lambda a, b, d: (a.astype(F32) + b.astype(F32) + d.astype(F32)).astype(BF)
    piece = jnp.concatenate([add3(sum_a[0], a1, a_next), add3(sum_b[0], b2, b_next)], axis=1)
    four = lax.axis_size("dp") == 4
    reduced = dp_first(piece) if four else lax.psum(piece, "dp")
    layer1, layer2 = swap(layer_rows, 1), swap(layer_rows, 2)
    grad_hi = input_grad(0, da, ds_hi, dt_hi, weight)
    xbc, grad_hi = together(xbc, grad_hi)
    sent_hi = lax.ppermute(grad_hi, "ctx", [(0, 1)])
    ds_lo, dt_lo, conv_acc, head_acc, _, _ = back(1, (dstate, dext, conv_acc, head_acc), xbc)
    ds_lo, reduced, sent_hi, layer1, layer2 = together(ds_lo, reduced, sent_hi, layer1, layer2)
    hi_swap = lambda v, step: core_swap(v, step, 1)
    lo_swap = lambda v, step: core_swap(v, step, 0)
    grad_lo = input_grad(1, da, ds_lo, dt_lo, weight)
    grad_lo, sent_hi, reduced = together(grad_lo, sent_hi, reduced)
    sent_lo = lax.ppermute(grad_lo, "ctx", [(1, 0)])
    if four:
        reduced = dp_second(reduced)
    state_hi = scatter_first(plus(grad_hi, sent_hi), t, hi_swap)
    ds_lo, sent_lo = together(ds_lo, sent_lo)
    state_lo = scatter_first(plus(grad_lo, sent_lo), t, lo_swap)
    alone, shared = project_grad(bounds, normed, da, ds_lo, ds_hi, dt_lo, dt_hi)
    alone, shared, state_lo, state_hi = together(alone, shared, state_lo, state_hi)
    state_lo = scatter_second(state_lo, lo_swap)
    state_hi = scatter_second(state_hi, hi_swap)
    if four:
        reduced = dp_end(dp_third(reduced))
    layer3 = [swap(layer1[:, :512], 2), swap(layer2[:, 512:], 1)]
    layer_out = assemble(bounds, [layer_rows, layer1, layer2, *layer3])
    twin_piece = twin(reduced)
    piece_a, piece_b = reduced[:, :512], reduced[:, 512:]
    twin_a, twin_b = twin_piece[:, :512], twin_piece[:, 512:]
    inputs = block_at(own_tokens, t, mine).astype(F32)
    scale = lax.rsqrt(jnp.mean(inputs * inputs, axis=-1, keepdims=True) + EPSILON)

    def finish(state):
        grad_normed = scatter_end(state)
        weighted = grad_normed * norm_gain
        norm_part = jnp.sum(grad_normed * inputs * scale, axis=0)
        inner_mean = jnp.mean(weighted * inputs, axis=-1, keepdims=True)
        token_rows = (dhid + scale * weighted - inputs * scale**3 * inner_mean).astype(BF)
        return token_rows, norm_part

    state = [jnp.where(c == 1, a, b) for a, b in zip(state_hi, state_lo)]
    token_rows, norm_part = finish(state)
    tok1, tok2 = swap(token_rows, 1), swap(token_rows, 2)
    tok3 = [swap(tok1[:, :512], 2), swap(tok2[:, 512:], 1)]
    tokens_grad = assemble(bounds, [token_rows, tok1, tok2, *tok3])

    piece = bit_scatter(shared, t, c)
    both = dp_sum(jnp.concatenate([alone, piece], axis=0))
    alone, piece = both[:1024], both[1024:]
    alone_twin = twin(alone)
    shared = bit_gather(piece, t, c).astype(F32)
    place = c * 4 + t

    heads = jnp.concatenate(
        [
            jnp.sum(conv_acc[5, :192].reshape(3, 64), axis=1),
            jnp.sum(head_acc[0:3], axis=1),
            jnp.sum(head_acc[8:11], axis=1),
        ]
    )
    own_small = jnp.pad(jnp.concatenate([conv_acc[:5, :192].reshape(-1), heads]), (0, 55))
    at_own = lax.dynamic_update_slice_in_dim(
        jnp.zeros((8, 1024), F32), own_small[None], place, 0
    )
    flat = jnp.concatenate(
        [at_own.reshape(-1), gain_part.reshape(-1), conv_acc[:5, 256:].reshape(-1), mlp_part[0], norm_part]
    )
    flat = all_sum(jnp.pad(flat, (0, (-flat.shape[0]) % 1024)).reshape(-1, 128)).reshape(-1)
    norm_sum = flat[12544:13568]
    small = flat[:8192].reshape(8, 1024)
    gain_sum = flat[8192:10240].reshape(8, 256)
    bc_sum = flat[10240:11520].reshape(5, 256)
    mlp_sum = flat[11520:12544]
    both_cores = lambda v: jnp.stack([lax.dynamic_index_in_dim(v, k * 4 + t, 0, False) for k in range(2)])
    small = both_cores(small)
    gain_sum = both_cores(gain_sum)[:, :192].reshape(-1)
    conv_small = small[:, :960].reshape(2, 5, 192)
    conv_small = jnp.concatenate([conv_small[0], conv_small[1]], axis=1)
    head_small = small[:, 960:969].reshape(2, 3, 3)
    per_head_sum = lambda i: head_small[:, i].reshape(-1)

    f = lambda lo, hi, own_part, other_part, axis: ordered(
        own_part[:, lo:hi], other_part[:, lo:hi], c, axis
    ).astype(F32)
    flip = lambda lo, hi: ordered(
        piece_b[:, lo:hi].T, twin_b[:, lo:hi].T, c, 0
    ).astype(F32)
    zcols = lambda v: jnp.concatenate([v[:, 384:512], v[:, 320:384]], axis=1)
    return (
        layer_out[None],
        tokens_grad[None],
        norm_sum,
        f(0, 64, alone, alone_twin, 1),
        shared[:, :256],
        flip(448, 512),
        ordered(zcols(alone), zcols(alone_twin), c, 1).astype(F32),
        f(128, 320, alone, alone_twin, 1),
        f(64, 67, alone, alone_twin, 1),
        shared[:, 256:],
        conv_small[:4],
        conv_small[4],
        bc_sum[:4],
        bc_sum[4],
        per_head_sum(2),
        per_head_sum(1),
        per_head_sum(0),
        gain_sum,
        flip(256, 448),
        mlp_sum,
        f(0, 256, piece_a, twin_a, 1),
        f(256, 512, piece_a, twin_a, 1),
        flip(0, 256),
    )


def solution(mesh):
    placed = (
        P("dp", "ctx", None),
        P("dp", None),
        P(),
        P(None, "tensor"),
        P(),
        P("tensor", None),
        P(None, "tensor"),
        P(None, "tensor"),
        P(None, "tensor"),
        P(),
        P(None, "tensor"),
        P("tensor"),
        P(),
        P(),
        P("tensor"),
        P("tensor"),
        P("tensor"),
        P("tensor"),
        P("tensor", None),
        P(),
        P(None, "tensor"),
        P(None, "tensor"),
        P("tensor", None),
        P("dp", "ctx", None),
    )
    return jax.shard_map(
        local,
        mesh=mesh,
        in_specs=placed,
        out_specs=(
            P("dp", "ctx", None),
            P("dp", "ctx", None),
            P(),
            P(None, "tensor"),
            P(),
            P("tensor", None),
            P(None, "tensor"),
            P(None, "tensor"),
            P(None, "tensor"),
            P(),
            P(None, "tensor"),
            P("tensor"),
            P(),
            P(),
            P("tensor"),
            P("tensor"),
            P("tensor"),
            P("tensor"),
            P("tensor", None),
            P(),
            P(None, "tensor"),
            P(None, "tensor"),
            P("tensor", None),
        ),
        check_vma=False,
    )
```

```python
import functools

import jax
import numpy as np
import jax.numpy as jnp
from jax import lax
from jax.experimental import pallas as pl
from jax.experimental.pallas import tpu as pltpu
from jax.sharding import PartitionSpec as P

BF, F32 = jnp.bfloat16, jnp.float32
EPSILON = 1e-05
ROPE_BASE = 100000000000.0
HEAD_SIZE = 64
MP = 64
PROJ_ROWS = 256
BQ = 512
CHUNK = 128
VMEM_LIMIT = 48 * 1024 * 1024
FULL_VMEM = 60 * 1024 * 1024
SMALL_COST = pl.CostEstimate(flops=1000000, bytes_accessed=100000, transcendentals=0)


def dot(left, right, dims=((1,), (0,)), precision=None):
    return lax.dot_general(
        left, right, (dims, ((), ())), precision=precision, preferred_element_type=F32
    )


def dot_bt(left, right):
    return dot(left, right, ((1,), (1,)))


def dot_at(left, right):
    return dot(left, right, ((0,), (0,)))


def lanes(shape):
    return lax.broadcasted_iota(jnp.int32, shape, len(shape) - 1)


def rows_of(shape):
    return lax.broadcasted_iota(jnp.int32, shape, 0)


def doc_start(pos, first, second):
    return jnp.where(pos >= second, second, jnp.where(pos >= first, first, 0))


def halves(low, high):
    return jnp.where(lanes((1, 128)) < 64, low, high)


def params(**kw):
    return pltpu.CompilerParams(vmem_limit_bytes=VMEM_LIMIT, **kw)


def whole(shape):
    return pl.BlockSpec(shape, lambda *_: (0,) * len(shape))


def proj_body(off, tok, gain, weight, cos, sin, *refs):
    normed_ref, qp_ref, kv_ref, xbc_ref, z_ref, dt_ref = refs[-6:]
    values = tok[...].astype(F32)
    scale = lax.rsqrt(jnp.mean(values * values, axis=-1, keepdims=True) + EPSILON)
    normed = (values * scale * gain[...]).astype(BF)
    normed_ref[...] = normed
    c, s = cos[...], sin[...]
    left = lanes((1, 128)) < 64
    att = dot(normed, weight[:, :384])
    kv, turned, qd = att[:, :128], att[:, 128:256], att[:, 256:]
    kv_ref[...] = jnp.where(left, kv * c + turned * s, kv).astype(BF)
    q_rot = qd * c + pltpu.roll(turned, 64, 1) * s
    qp_ref[...] = jnp.where(left, q_rot.astype(BF) * 0.125, 0.0).astype(BF)
    dt_ref[...] = qd.T[64:72, :]
    ssm = dot(normed, weight[:, 384:])
    x2z2 = ssm[:, 128:256]
    xbc_ref[:, :128] = ssm[:, :128].astype(BF)
    xbc_ref[:, 128:256] = jnp.where(left, x2z2, 0.0).astype(BF)
    xbc_ref[:, 256:] = ssm[:, 384:].astype(BF)
    z_ref[:, :128] = ssm[:, 256:384]
    z_ref[:, 128:] = jnp.where(left, pltpu.roll(x2z2, 64, 1), 0.0)


def project(off, tokens, gain, weight, cos, sin, before=None):
    own = tokens.shape[0]
    full = cos.shape[0]
    n = PROJ_ROWS
    outs = [
        jax.ShapeDtypeStruct((full, 1024), BF),
        jax.ShapeDtypeStruct((full, 128), BF),
        jax.ShapeDtypeStruct((full, 128), BF),
        jax.ShapeDtypeStruct((full, 512), BF),
        jax.ShapeDtypeStruct((full, 256), F32),
        jax.ShapeDtypeStruct((8, full), F32),
    ]
    at = lambda i, off: (off[0] + i, 0)
    out_specs = [pl.BlockSpec((n, o.shape[1]), at) for o in outs[:5]]
    out_specs.append(pl.BlockSpec((8, n), lambda i, off: (0, off[0] + i)))
    in_specs = [
        pl.BlockSpec((n, 1024), lambda i, off: (i, 0)),
        whole((1, 1024)),
        whole((1024, 1024)),
        pl.BlockSpec((n, 128), at),
        pl.BlockSpec((n, 128), at),
    ]
    args = [off, tokens, gain, weight, cos, sin]
    alias = {}
    if before is not None:
        in_specs += [pl.BlockSpec(memory_space=pl.ANY)] * 6
        args += list(before)
        alias = {6 + i: i for i in range(6)}
    return pl.pallas_call(
        proj_body,
        grid_spec=pltpu.PrefetchScalarGridSpec(
            num_scalar_prefetch=1, grid=(own // n,), in_specs=in_specs, out_specs=out_specs
        ),
        out_shape=outs,
        input_output_aliases=alias,
        compiler_params=params(),
        cost_estimate=SMALL_COST,
        name="norm_project",
    )(*args)


def turned_lanes(value):
    low = lanes((1, 128)) % 64 < 32
    return jnp.where(low, -pltpu.roll(value, 96, 1), pltpu.roll(value, 32, 1))


def prep_body(bounds, gate, up, down, mix, att, kv, q, x, z, dt, bc, weight, pack):
    n = gate.shape[0]
    pack[:, :256] = gate[...]
    pack[:, 256:512] = up[...]
    pack[:, 512:768] = down[...].T
    pack[:, 768:] = jnp.concatenate([mix[...], att[...]], axis=0).T
    first, low_kv = bounds[3] == 0, bounds[2] // 2 == 0
    lane = lanes((1, 128))
    left = lane < 64
    tile = lambda ref, i: ref[:, 128 * i : 128 * i + 128].astype(F32)
    swapped = lambda v: pltpu.roll(v, 64, 1)
    keys, values = tile(kv, 0), tile(kv, 1)
    keys = jnp.where(low_kv, keys, swapped(keys))
    values = jnp.where(low_kv, swapped(values), values)
    query = tile(q, 0)
    query = jnp.where(first, query, swapped(query))
    steps = jnp.concatenate([dt[...].astype(F32), jnp.zeros((n, 122), F32)], axis=1)
    steps = jnp.where(lane < 3, jnp.where(first, steps, pltpu.roll(steps, 125, 1)), 0.0)

    def heads(ref):
        a, b, d = tile(ref, 0), tile(ref, 1), swapped(tile(ref, 2))
        return jnp.where(first, a, jnp.where(left, swapped(b), d)), jnp.where(first, b, d)

    x01, x2 = heads(x)
    z01, z2 = heads(z)
    tiles = [
        jnp.where(left, keys, values),
        jnp.where(left, turned_lanes(keys), swapped(turned_lanes(query))),
        jnp.where(left, query, swapped(steps)),
        x01,
        jnp.where(left, x2, swapped(z2)),
        z01,
    ]
    for i, value in enumerate(tiles):
        weight[:, 128 * i : 128 * i + 128] = value.astype(BF)
    weight[:, 768:] = bc[...]


def prepare(bounds, gate, up, down, mix, att, kv, q, x, z, dt, bc):
    n = 256
    row = lambda w: pl.BlockSpec((n, w), lambda i, b: (i, 0))
    col = lambda h: pl.BlockSpec((h, n), lambda i, b: (b[3], i))
    mine = pl.BlockSpec((n, 256), lambda i, b: (i, b[3]))
    return pl.pallas_call(
        prep_body,
        grid_spec=pltpu.PrefetchScalarGridSpec(
            num_scalar_prefetch=1,
            grid=(4,),
            in_specs=[mine, mine, col(256), col(192), col(64)]
            + [row(256), row(128), row(384), row(384), row(6), row(256)],
            out_specs=[row(1024), row(1024)],
        ),
        out_shape=[jax.ShapeDtypeStruct((1024, 1024), BF)] * 2,
        compiler_params=pltpu.CompilerParams(vmem_limit_bytes=FULL_VMEM),
        cost_estimate=SMALL_COST,
        name="prepare",
    )(bounds, gate, up, down, mix, att, kv, q, x, z, dt, bc)


def block_range(qi, bounds):
    first, second = bounds[0], bounds[1]
    q0 = qi * BQ
    low = doc_start(q0, first, second) // BQ
    inner = (doc_start(q0 + BQ - 1, first, second) + BQ - 1) // BQ
    return low, jnp.minimum(jnp.maximum(inner, low), qi)


def allowed_keys(qi, kb, bounds):
    q = qi * BQ + rows_of((BQ, 1))
    k = kb * BQ + lanes((1, BQ))
    start = doc_start(q, bounds[0], bounds[1])
    return (k <= q) & (k >= start)


def attend_body(bounds, qp, kv, g2, out_ref, keep_ref):
    qi = pl.program_id(0)
    low, inner = block_range(qi, bounds)
    q = qp[...]

    def step(kb, carry, masked):
        top, total, acc = carry
        k = kv[pl.ds(pl.multiple_of(kb * BQ, BQ), BQ), :]
        s = dot_bt(q, k)
        if masked:
            s = jnp.where(allowed_keys(qi, kb, bounds), s, -1e30)
        new_top = jnp.maximum(top, jnp.max(s, axis=1, keepdims=True))
        p = jnp.exp(s - new_top)
        fade = jnp.exp(top - new_top)
        total = total * fade + jnp.sum(p, axis=1, keepdims=True)
        acc = acc * fade + dot(p.astype(BF), k)
        return new_top, total, acc

    carry = (jnp.full((BQ, 1), -1e30, F32), jnp.zeros((BQ, 1), F32), jnp.zeros((BQ, 128), F32))
    carry = lax.fori_loop(low, inner, lambda kb, c: step(kb, c, True), carry)
    carry = lax.fori_loop(inner, qi, lambda kb, c: step(kb, c, False), carry)
    top, total, acc = step(qi, carry, True)
    out = acc / total
    left = lanes((1, 128)) < 64
    out_ref[...] = jnp.where(left, g2[...], out.astype(BF))
    keep_ref[...] = jnp.where(left, top + jnp.log(total), out)


def attend(bounds, qp, kv, g2):
    full = qp.shape[0]
    block = pl.BlockSpec((BQ, 128), lambda i, *_: (i, 0))
    return pl.pallas_call(
        attend_body,
        grid_spec=pltpu.PrefetchScalarGridSpec(
            num_scalar_prefetch=1,
            grid=(full // BQ,),
            in_specs=[block, whole((full, 128)), block],
            out_specs=[block, block],
        ),
        out_shape=[
            jax.ShapeDtypeStruct((full, 128), BF),
            jax.ShapeDtypeStruct((full, 128), F32),
        ],
        compiler_params=params(),
        cost_estimate=SMALL_COST,
        name="attend",
    )(bounds, qp, kv, g2)


def attend_back_body(bounds, qp, kv, keep, grad, cos, sin, out_ref, acc_ref):
    blocks = pl.num_programs(0)
    qi = blocks - 1 - pl.program_id(0)
    left = lanes((1, 128)) < 64

    @pl.when(pl.program_id(0) == 0)
    def _():
        acc_ref[...] = jnp.zeros_like(acc_ref)

    low, inner = block_range(qi, bounds)
    q = qp[...]
    do = jnp.where(left, 0.0, grad[0].astype(F32))
    delta = jnp.sum(do * keep[...], axis=1, keepdims=True)
    do = do.astype(BF)
    lse = keep[:, :1]

    def step(kb, dq, masked):
        at = pl.ds(pl.multiple_of(kb * BQ, BQ), BQ)
        k = kv[at, :]
        p = jnp.exp(dot_bt(q, k) - lse)
        if masked:
            p = jnp.where(allowed_keys(qi, kb, bounds), p, 0.0)
        ds = (p * (dot_bt(do, k) - delta)).astype(BF)
        acc_ref[at, :] += dot_at(ds, q) + dot_at(p.astype(BF), do)
        return dq + dot(ds, k)

    dq = jnp.zeros((BQ, 128), F32)
    dq = lax.fori_loop(low, inner, lambda kb, c: step(kb, c, True), dq)
    dq = lax.fori_loop(inner, qi, lambda kb, c: step(kb, c, False), dq)
    dq = step(qi, dq, True) * 0.125
    dkv = acc_ref[pl.ds(pl.multiple_of(qi * BQ, BQ), BQ), :]
    c, s = cos[...], sin[...]
    out_ref[:, :128] = jnp.where(left, dkv * c, dkv).astype(BF)
    out_ref[:, 128:256] = (jnp.where(left, dkv, pltpu.roll(dq, 64, 1)) * s).astype(BF)
    out_ref[:, 256:] = jnp.where(left, dq * c, 0.0).astype(BF)


def attend_back(bounds, qp, kv, keep, grad, cos, sin):
    full = qp.shape[0]
    n = full // BQ
    block = pl.BlockSpec((BQ, 128), lambda i, *_: (n - 1 - i, 0))
    return pl.pallas_call(
        attend_back_body,
        grid_spec=pltpu.PrefetchScalarGridSpec(
            num_scalar_prefetch=1,
            grid=(n,),
            in_specs=[
                block,
                whole((full, 128)),
                block,
                pl.BlockSpec((1, BQ, 128), lambda i, *_: (n - 1 - i, 0, 1)),
                block,
                block,
            ],
            out_specs=pl.BlockSpec((BQ, 384), lambda i, *_: (n - 1 - i, 0)),
            scratch_shapes=[pltpu.VMEM((full, 128), F32)],
        ),
        out_shape=jax.ShapeDtypeStruct((full, 384), BF),
        compiler_params=params(),
        cost_estimate=SMALL_COST,
        name="attend_back",
    )(bounds, qp, kv, keep, grad, cos, sin)


def tap_mask(first_row, count, shift, bounds):
    pos = first_row + rows_of((count, 1))
    return (pos - doc_start(pos, bounds[0], bounds[1]) >= shift).astype(F32)


def conv_taps(ext_ref, r0, bounds, taps, bias):
    pre = bias + taps[3:4, :] * ext_ref[pl.ds(8, CHUNK), :]
    for shift in (1, 2, 3):
        mask = tap_mask(r0, CHUNK, shift, bounds)
        pre = pre + taps[3 - shift : 4 - shift, :] * (ext_ref[pl.ds(8 - shift, CHUNK), :] * mask)
    return pre


def chunk_decay(r0, bounds, dt_raw, head, extra=None):
    lane = lanes((1, CHUNK))
    dt = jax.nn.softplus(dt_raw + head[:, 0:1])
    la = dt * head[:, 1:2]
    upper = (rows_of((CHUNK, CHUNK)) <= lanes((CHUNK, CHUNK))).astype(F32)
    cum = dot(la, upper, precision=lax.Precision.HIGHEST)
    rows = [cum, dt] if extra is None else [cum, dt, extra]
    used = 8 * len(rows)
    stacked = jnp.concatenate(rows + [jnp.zeros((CHUNK - used, CHUNK), F32)], axis=0).T
    cum_col, dt_col = stacked[:, 0:8], stacked[:, 8:16]
    pos = r0 + rows_of((CHUNK, 1))
    start = doc_start(pos, bounds[0], bounds[1])
    start_last = doc_start(r0 + CHUNK - 1, bounds[0], bounds[1])
    key = r0 + lane
    mask = (key <= pos) & (key >= start)
    enter = jnp.where(start < r0, jnp.exp(cum_col), 0.0)
    fade = jnp.where(pos >= start_last, jnp.exp(cum_last_row(cum_col) - cum_col), 0.0)
    keep = jnp.where(start_last < r0, jnp.exp(cum_last_row(cum_col)), 0.0)
    return dt, la, cum, dt_col, cum_col, mask, enter, fade, keep, stacked[:, 16:24]


def two_terms(value):
    high = value.astype(BF)
    return high, (value - high.astype(F32)).astype(BF)


def cum_last_row(cum_col):
    return cum_col[CHUNK - 1 : CHUNK, :]


def per_head(col):
    return halves(col[:, 0:1], col[:, 1:2]), col[:, 2:3]


def state_rows(keep):
    row = rows_of((256, 1))
    return jnp.where(row < 64, keep[:, 0:1], jnp.where(row < 128, keep[:, 1:2], keep[:, 2:3]))


def scan_body(bounds, xbc, z, dt_raw, taps, bias, head, skip, g01, g2, y_ref, s_ref, ext, state):
    i = pl.program_id(0)
    r0 = i * CHUNK

    @pl.when(i == 0)
    def _():
        ext[pl.ds(0, 8), :] = jnp.zeros((8, 512), F32)
        state[...] = jnp.zeros_like(state)

    @pl.when(i > 0)
    def _():
        ext[pl.ds(0, 8), :] = ext[pl.ds(CHUNK, 8), :]

    ext[pl.ds(8, CHUNK), :] = xbc[...].astype(F32)
    pre = conv_taps(ext, r0, bounds, taps[...], bias[...])
    conv = pre * jax.nn.sigmoid(pre)
    x01, x2 = conv[:, :128], conv[:, 128:256]
    b, c = conv[:, 256:384].astype(BF), conv[:, 384:].astype(BF)
    dt, la, cum, dt_col, cum_col, mask, enter, fade, keep, _ = chunk_decay(
        r0, bounds, dt_raw[...], head[...]
    )
    inner = dot_bt(c, b)
    x01b, x2b = x01.astype(BF), x2.astype(BF)
    ys = []
    for h in range(3):
        gap = cum_col[:, h : h + 1] - cum[h : h + 1, :]
        decay = jnp.exp(jnp.where(mask, gap, -1e30))
        m = (inner * decay * dt[h : h + 1, :]).astype(BF)
        ys.append(dot(m, x01b if h < 2 else x2b))
    s0 = state[...]
    s_ref[0] = s0
    s0b, s0c = two_terms(s0)
    carried = dot_bt(c, s0b) + dot_bt(c, s0c)
    e01, e2 = per_head(enter)
    y01 = halves(ys[0], ys[1]) + e01 * carried[:, :128] + skip[:, :128] * x01
    y2 = ys[2] + e2 * carried[:, 128:] + skip[:, 128:] * x2
    w01, w2 = per_head(fade * dt_col)
    xw = jnp.concatenate([(x01 * w01).astype(BF), (x2 * w2).astype(BF)], axis=1)
    state[...] = s0 * state_rows(keep) + dot_at(xw, b)
    y_ref[:, :128] = y01
    y_ref[:, 128:] = y2
    z01, z2 = z[:, :128], z[:, 128:]
    g01[...] = (y01 * (z01 * jax.nn.sigmoid(z01))).astype(BF)
    g2[...] = (y2 * (z2 * jax.nn.sigmoid(z2))).astype(BF)


def scan_forward(bounds, xbc, z, dt_raw, taps, bias, head, skip):
    full = xbc.shape[0]
    n = full // CHUNK
    row = lambda width: pl.BlockSpec((CHUNK, width), lambda i, *_: (i, 0))
    return pl.pallas_call(
        scan_body,
        grid_spec=pltpu.PrefetchScalarGridSpec(
            num_scalar_prefetch=1,
            grid=(n,),
            in_specs=[
                row(512),
                row(256),
                pl.BlockSpec((8, CHUNK), lambda i, *_: (0, i)),
                whole((8, 512)),
                whole((1, 512)),
                whole((8, 128)),
                whole((1, 256)),
            ],
            out_specs=[
                row(128),
                row(128),
                row(256),
                pl.BlockSpec((1, 256, 128), lambda i, *_: (i, 0, 0)),
            ],
            scratch_shapes=[pltpu.VMEM((CHUNK + 8, 512), F32), pltpu.VMEM((256, 128), F32)],
        ),
        out_shape=[
            jax.ShapeDtypeStruct((full, 128), BF),
            jax.ShapeDtypeStruct((full, 128), BF),
            jax.ShapeDtypeStruct((full, 256), F32),
            jax.ShapeDtypeStruct((n, 256, 128), F32),
        ],
        compiler_params=params(),
        cost_estimate=SMALL_COST,
        name="scan_forward",
    )(bounds, xbc, z, dt_raw, taps, bias, head, skip)


def scalar_rows(terms):
    total = terms[0:2, :] + terms[2:4, :] + terms[4:6, :]
    return jnp.concatenate([total, jnp.zeros((6, CHUNK), F32)], axis=0)


def scan_back_body(
    last, bounds, xbc, before, z, y, dt_raw, s0_ref, dn01, dn2, scal, taps, bias, head, skip, gain,
    dstate_in, dext_in, acc_in, head_in, *refs,
):
    out_ref, dt_grad, acc, head_acc, dstate_out, dext_out, ext, dext, dstate = refs[-9:]
    step = pl.program_id(0)
    i = last - step
    r0 = i * CHUNK
    left = lanes((1, 128)) < 64

    @pl.when(step == 0)
    def _():
        dext[pl.ds(CHUNK, 8), :] = dext_in[...]
        dstate[...] = dstate_in[...]
        acc[...] = acc_in[...]
        head_acc[...] = head_in[...]

    @pl.when(step > 0)
    def _():
        dext[pl.ds(CHUNK, 8), :] = dext[pl.ds(0, 8), :]

    ext[pl.ds(0, 8), :] = before[...].astype(F32)[8:, :]
    ext[pl.ds(8, CHUNK), :] = xbc[...].astype(F32)
    weights = taps[...]
    pre = conv_taps(ext, r0, bounds, weights, bias[...])
    sig = jax.nn.sigmoid(pre)
    conv = pre * sig
    x01, x2 = conv[:, :128], conv[:, 128:256]
    b, c = conv[:, 256:384].astype(BF), conv[:, 384:].astype(BF)
    dt, la, cum, dt_col, cum_col, mask, enter, fade, keep, scalars = chunk_decay(
        r0, bounds, dt_raw[...], head[...], scalar_rows(scal[0].astype(F32))
    )
    row_scale, row_cross = scalars[:, 0:1], scalars[:, 1:2]

    def gate_back(dn, gain, zz, yy):
        s = jax.nn.sigmoid(zz)
        act = zz * s
        g = yy * act
        sent = g.astype(BF).astype(F32)
        ratio = jnp.where(g == 0.0, 1.0, sent / g)
        dg = (dn * gain * row_scale - sent * row_cross) * ratio
        return dg * act, dg * yy * (s + act * (1.0 - s))

    dy01, dz01 = gate_back(dn01[0].astype(F32), gain[:, :128], z[:, :128], y[:, :128])
    dy2, dz2 = gate_back(dn2[0].astype(F32), gain[:, 128:], z[:, 128:], y[:, 128:])
    dy2, dz2 = jnp.where(left, dy2, 0.0), jnp.where(left, dz2, 0.0)
    inner = dot_bt(c, b)
    x01b, x2b = x01.astype(BF), x2.astype(BF)
    dy01b, dy2b = dy01.astype(BF), dy2.astype(BF)
    zero = jnp.zeros_like(dy01b)
    parts = [(jnp.where(left, dy01b, zero), x01b), (jnp.where(left, zero, dy01b), x01b), (dy2b, x2b)]
    d_inner = jnp.zeros((CHUNK, CHUNK), F32)
    dxs, col_sums, direct, row_sums = [], [], [], []
    for h in range(3):
        gap = cum_col[:, h : h + 1] - cum[h : h + 1, :]
        decay = jnp.exp(jnp.where(mask, gap, -1e30))
        dt_h = dt[h : h + 1, :]
        dyh, xh = parts[h]
        dm = dot_bt(dyh, xh)
        kept = inner * decay
        m = (kept * dt_h).astype(BF)
        dxs.append(dot_at(m, dyh if h == 2 else dy01b))
        pulled = dm * kept
        d_inner = d_inner + dm * (decay * dt_h)
        weighted = pulled * dt_h
        direct.append(jnp.sum(pulled, axis=0, keepdims=True))
        col_sums.append(jnp.sum(weighted, axis=0, keepdims=True))
        row_sums.append(jnp.sum(weighted, axis=1, keepdims=True))
    s0 = s0_ref[0]
    s0b, s0c = two_terms(s0)
    ds1 = dstate[...]
    ds1b, ds1c = two_terms(ds1)
    e01, e2 = per_head(enter)
    ey01, ey2 = dy01 * e01, dy2 * e2
    ey, eyc = two_terms(jnp.concatenate([ey01, ey2], axis=1))
    carried = dot_bt(c, s0b) + dot_bt(c, s0c)
    f01, f2 = per_head(fade)
    d01, d2 = per_head(dt_col)
    back = dot_bt(b, ds1b)
    fb01, fb2 = f01 * back[:, :128], f2 * back[:, 128:]
    xw = jnp.concatenate([(x01 * (f01 * d01)).astype(BF), (x2 * (f2 * d2)).astype(BF)], axis=1)
    d_innerb = d_inner.astype(BF)
    dc = dot(d_innerb, b) + dot(ey, s0b) + dot(eyc, s0b) + dot(ey, s0c)
    db = dot_at(d_innerb, c) + dot(xw, ds1b) + dot(xw, ds1c)
    dx01 = halves(dxs[0], dxs[1]) + d01 * fb01 + skip[:, :128] * dy01
    dx2 = dxs[2] + d2 * fb2 + skip[:, 128:] * dy2
    kept_rows = state_rows(keep)
    crossing = jnp.sum(ds1 * s0 * kept_rows, axis=1, keepdims=True)
    dstate[...] = ds1 * kept_rows + dot_at(ey, c) + dot_at(eyc, c)
    inter01, inter2 = ey01 * carried[:, :128], ey2 * carried[:, 128:]
    u01, u2 = x01 * fb01, x2 * fb2
    pick = lambda v, h: jnp.where(left if h == 0 else ~left, v, 0.0)
    side = lambda v01, v2, h: jnp.sum(pick(v01, h) if h < 2 else v2, axis=1, keepdims=True)
    lane = lanes((1, CHUNK))
    tile = jnp.zeros((CHUNK, CHUNK), F32)
    crossed = jnp.zeros((8, 1), F32)
    head_row = rows_of((8, 1))
    for h in range(3):
        u = side(u01, u2, h)
        moved = row_sums[h] + side(inter01, inter2, h) - u * dt_col[:, h : h + 1]
        tile = jnp.where(lane == h, moved, jnp.where(lane == 8 + h, u, tile))
        total = jnp.sum(crossing[64 * h : 64 * h + 64, :], axis=0, keepdims=True)
        total = total + jnp.sum(u * dt_col[:, h : h + 1], axis=0, keepdims=True)
        crossed = jnp.where(head_row == h, total, crossed)
    tile = tile.T
    stack = lambda items: jnp.concatenate(items + [jnp.zeros((5, CHUNK), F32)], axis=0)
    dcum = tile[0:8, :] - stack(col_sums) + jnp.where(lane == CHUNK - 1, crossed, 0.0)
    lower = (rows_of((CHUNK, CHUNK)) >= lanes((CHUNK, CHUNK))).astype(F32)
    dla = dot(dcum, lower, precision=lax.Precision.HIGHEST)
    ddt = stack(direct) + tile[8:16, :] + dla * head[:, 1:2]
    graw = ddt * jax.nn.sigmoid(dt_raw[...] + head[:, 0:1])
    dt_grad[...] = graw
    head_acc[0:8, :] += dla * la
    head_acc[8:16, :] += graw
    dpre = jnp.concatenate([dx01, dx2, db, dc], axis=1) * (sig + conv * (1.0 - sig))
    dext[pl.ds(0, CHUNK), :] = dpre
    din = weights[3:4, :] * dpre
    acc[3:4, :] += jnp.sum(dpre * ext[pl.ds(8, CHUNK), :], axis=0, keepdims=True)
    acc[4:5, :] += jnp.sum(dpre, axis=0, keepdims=True)
    acc[5:6, :128] += jnp.sum(dy01 * x01, axis=0, keepdims=True)
    acc[5:6, 128:256] += jnp.sum(dy2 * x2, axis=0, keepdims=True)
    for shift in (1, 2, 3):
        tap = 3 - shift
        now = tap_mask(r0, CHUNK, shift, bounds)
        acc[tap : tap + 1, :] += jnp.sum(
            dpre * (ext[pl.ds(8 - shift, CHUNK), :] * now), axis=0, keepdims=True
        )
        later = tap_mask(r0 + shift, CHUNK, shift, bounds)
        din = din + weights[tap : tap + 1, :] * (dext[pl.ds(shift, CHUNK), :] * later)
    out_ref[:, :128] = din[:, :128].astype(BF)
    out_ref[:, 128:256] = jnp.where(left, din[:, 128:256], pltpu.roll(dz2, 64, 1)).astype(BF)
    out_ref[:, 256:384] = dz01.astype(BF)
    out_ref[:, 384:] = din[:, 256:].astype(BF)

    @pl.when(step == pl.num_programs(0) - 1)
    def _():
        dstate_out[...] = dstate[...]
        dext_out[...] = dext[pl.ds(0, 8), :]


def scan_back(part, carry, before, bounds, xbc, z, y, dt_raw, states, dn, taps, bias, head, skip, gain):
    full = xbc.shape[0]
    n = full // CHUNK
    half = n // 2
    last = n - 1 if part == 0 else half - 1
    row = lambda width: pl.BlockSpec((CHUNK, width), lambda i, *_: (last - i, 0))
    tall = CHUNK // 16
    per = n // 8
    sent = lambda col: pl.BlockSpec(
        (1, CHUNK, 128), lambda i, b: ((last - i) // per, (last - i) % per, col)
    )

    def terms(i, b):
        piece, rest = (last - i) // per, (last - i) % per
        return piece, per * (CHUNK // 16) + rest // 2, rest % 2

    carried = [whole((256, 128)), whole((8, 512)), whole((8, 512)), whole((16, CHUNK))]
    sds = jax.ShapeDtypeStruct
    args = [bounds, xbc, xbc, z, y, dt_raw, states, dn, dn, dn, taps, bias, head, skip, gain]
    args += list(carry) + list(before)
    alias = {len(args) - 2: 0, len(args) - 1: 1} if before else {}
    return pl.pallas_call(
        functools.partial(scan_back_body, last),
        grid_spec=pltpu.PrefetchScalarGridSpec(
            num_scalar_prefetch=1,
            grid=(half,),
            in_specs=[
                row(512),
                pl.BlockSpec((16, 512), lambda i, *_: (jnp.maximum((last - i) * tall - 1, 0), 0)),
                row(256),
                row(256),
                pl.BlockSpec((8, CHUNK), lambda i, *_: (0, last - i)),
                pl.BlockSpec((1, 256, 128), lambda i, *_: (last - i, 0, 0)),
                sent(0),
                sent(1),
                pl.BlockSpec((1, 16, CHUNK), terms),
                whole((8, 512)),
                whole((1, 512)),
                whole((8, 128)),
                whole((1, 256)),
                whole((1, 256)),
            ]
            + carried
            + [pl.BlockSpec(memory_space=pl.ANY)] * len(before),
            out_specs=[
                row(640),
                pl.BlockSpec((8, CHUNK), lambda i, *_: (0, last - i)),
                whole((8, 512)),
                whole((16, CHUNK)),
                whole((256, 128)),
                whole((8, 512)),
            ],
            scratch_shapes=[
                pltpu.VMEM((CHUNK + 8, 512), F32),
                pltpu.VMEM((CHUNK + 8, 512), F32),
                pltpu.VMEM((256, 128), F32),
            ],
        ),
        out_shape=[
            sds((full, 640), BF),
            sds((8, full), F32),
            sds((8, 512), F32),
            sds((16, CHUNK), F32),
            sds((256, 128), F32),
            sds((8, 512), F32),
        ],
        input_output_aliases=alias,
        compiler_params=params(),
        cost_estimate=SMALL_COST,
        name="scan_back",
    )(*args)


ROW_BLOCK = 256


def row_body(bounds, g, h, tok, gout, mlp_gain, gains, *refs):
    packs, refs = refs[:10], refs[10:]
    pa, pb, slots = [], [], []
    for k, base in enumerate((0, 5)):
        for r in range(4):
            first = packs[base + r]
            second = first.at[:, 512:] if r < 3 else packs[base + 4]
            pa.append(first.at[:, 0:512])
            pb.append(second)
            slots.append((bounds[3] ^ k) * 4 + (bounds[2] ^ r))
    gain_rows = [gains[slot] for slot in slots]
    out_ref, two_ref, dmix_ref, dhid_ref = refs[0:4]
    act_refs, dgu_refs, gn_refs = refs[4:6], refs[6:8], refs[8:10]
    dn, mlp_acc, gain_acc = refs[10:13]
    step = pl.program_id(0)
    left = lanes((1, 128)) < 64
    width = 1536.0

    @pl.when(pl.program_id(0) == 0)
    def _():
        mlp_acc[...] = jnp.zeros_like(mlp_acc)
        gain_acc[...] = jnp.zeros_like(gain_acc)

    pieces = [(r, k) for k in range(2) for r in range(4)]

    def part(ref, s):
        return ref[slots[s]].astype(F32)

    squares = 0.0
    for s in range(8):
        first, second = part(g, s), part(h, s)
        squares = squares + first * first + jnp.where(left, second * second, 0.0)
    rg = lax.rsqrt(jnp.sum(squares, axis=1, keepdims=True) / width + EPSILON)
    mixed = 0.0
    for s, (r, k) in enumerate(pieces):
        gain = gain_rows[s]
        first = part(g, s) * rg * gain[:, :128]
        second = part(h, s)
        second = jnp.where(left, second * rg * gain[:, 128:], second)
        gn = jnp.concatenate([first.astype(BF), second.astype(BF)], axis=1)
        gn_refs[k][:, r * 256 : r * 256 + 256] = gn
        mixed = mixed + dot_bt(gn, pb[s][:, 256:])
    hidden = tok[...].astype(F32) + mixed
    scale = lax.rsqrt(jnp.mean(hidden * hidden, axis=-1, keepdims=True) + EPSILON)
    two = (hidden * scale * mlp_gain[...]).astype(BF)
    two_ref[...] = two
    grad = gout[...]
    ffn = 0.0
    dtwo = 0.0
    for s, (r, k) in enumerate(pieces):
        weight, down = pa[s][...], pb[s][:, :256]
        gu = dot(two, weight)
        gate, up = gu[:, :256], gu[:, 256:]
        sig = jax.nn.sigmoid(gate)
        silu = gate * sig
        act = (silu * up).astype(BF)
        act_refs[k][:, r * 256 : r * 256 + 256] = act
        ffn = ffn + dot_bt(act, down)
        dact = dot(grad, down)
        dgate = (dact * up * (sig + silu * (1.0 - sig))).astype(BF)
        dgu = jnp.concatenate([dgate, (dact * silu).astype(BF)], axis=1)
        dgu_refs[k][:, r * 512 : r * 512 + 512] = dgu
        dtwo = dtwo + dot_bt(dgu, weight)
    out_ref[...] = (hidden + ffn).astype(BF)
    weighted = dtwo * mlp_gain[...]
    mlp_acc[...] += jnp.sum(dtwo * (hidden * scale), axis=0, keepdims=True)
    mean = jnp.mean(weighted * hidden, axis=-1, keepdims=True)
    dhid = grad.astype(F32) + scale * weighted - hidden * (scale * scale * scale * mean)
    dhid_ref[...] = dhid
    dmix = dhid.astype(BF)
    dmix_ref[...] = dmix
    cross = 0.0
    for s, (r, k) in enumerate(pieces):
        dgn = dot(dmix, pb[s][:, 256:]).astype(BF)
        dn[slots[s], pl.ds(pl.multiple_of(step * ROW_BLOCK, ROW_BLOCK), ROW_BLOCK), :] = dgn
        first, second = dgn[:, :128].astype(F32), dgn[:, 128:].astype(F32)
        gain = gain_rows[s]
        own1, own2 = part(g, s), jnp.where(left, part(h, s), 0.0)
        t1, t2 = first * own1, second * own2
        gain_acc[slots[s], :, :128] += jnp.sum(t1 * rg, axis=0, keepdims=True)
        gain_acc[slots[s], :, 128:] += jnp.sum(t2 * rg, axis=0, keepdims=True)
        cross = cross + t1 * gain[:, :128] + t2 * gain[:, 128:]
    cross = jnp.sum(cross, axis=1, keepdims=True) * (rg * rg * rg / width)
    lane = lanes((1, 128))
    tile = jnp.where(lane == 0, rg, jnp.where(lane == 1, cross, 0.0))
    pair = tile.T[0:2, :]
    high = pair.astype(BF)
    rest = pair - high.astype(F32)
    middle = rest.astype(BF)
    low = (rest - middle.astype(F32)).astype(BF)
    block = jnp.concatenate(
        [v.astype(F32) for v in (high, middle, low)] + [jnp.zeros((10, ROW_BLOCK), F32)], axis=0
    ).astype(BF)
    for s in range(8):
        dn[s, pl.ds(pl.multiple_of(2 * ROW_BLOCK + step * 16, 16), 16), :] = block


def row_stage(bounds, g, h, tokens, gout, mlp_gain, gains, packs):
    n = ROW_BLOCK
    count = 2 * n
    row = lambda w: pl.BlockSpec((n, w), lambda i, b: (i, 0))
    part = pl.BlockSpec((n, 1024), lambda i, b: (2 * b[2] + i, 0))
    piece = pl.BlockSpec((8, n, 128), lambda i, b: (0, i, 0))
    once = lambda shape: pl.BlockSpec(
        shape, lambda i, b: (0,) * len(shape), pipeline_mode=pl.Buffered(1)
    )
    sds = jax.ShapeDtypeStruct
    widths = [1024] * 4 + [1024] * 2 + [2048] * 2 + [1024] * 2
    dtypes = [BF] * 3 + [F32] + [BF] * 6
    return pl.pallas_call(
        row_body,
        grid_spec=pltpu.PrefetchScalarGridSpec(
            num_scalar_prefetch=1,
            grid=(2,),
            in_specs=[piece, piece, part, part, whole((1, 1024)), whole((8, 1, 256))]
            + [once(p.shape) for p in packs],
            out_specs=[row(w) for w in widths]
            + [once((8, count + 32, 256)), whole((1, 1024)), whole((8, 1, 256))],
        ),
        out_shape=[sds((count, w), d) for w, d in zip(widths, dtypes)]
        + [sds((8, count + 32, 256), BF), sds((1, 1024), F32), sds((8, 1, 256), F32)],
        compiler_params=pltpu.CompilerParams(vmem_limit_bytes=58 * 1024 * 1024),
        cost_estimate=SMALL_COST,
        name="row_stage",
    )(bounds, g, h, tokens, gout, mlp_gain, gains, *packs)


def weight_body(two, gout, dmix, dgu, act, gn, *refs):
    a = dot_at(two[...], dgu[...])
    b = jnp.concatenate([dot_at(gout[...], act[...]), dot_at(dmix[...], gn[...])], axis=1)
    if len(refs) == 2:
        refs[0][0] = a.astype(BF)
        refs[1][0] = b.astype(BF)
    else:
        a = (a + refs[0][0].astype(F32)).astype(BF)
        b = (b + refs[1][0].astype(F32)).astype(BF)
        for i in range(4):

            @pl.when(pl.program_id(0) == i)
            def _(i=i):
                refs[2 + i][...] = a
                refs[6 + i][...] = b


def weight_stage(two, gout, dmix, dgu, act, gn, *others):
    count = two.shape[0]
    col = lambda w: pl.BlockSpec((count, w), lambda i: (0, i))
    piece = pl.BlockSpec((1, 1024, 512), lambda i: (i, 0, 0))
    once = pl.BlockSpec((1024, 512), lambda i: (0, 0), pipeline_mode=pl.Buffered(1))
    sds = jax.ShapeDtypeStruct
    return pl.pallas_call(
        weight_body,
        grid=(4,),
        in_specs=[whole((count, 1024))] * 3
        + [col(512), col(256), col(256)]
        + [piece] * len(others),
        out_specs=[once] * 8 if others else [piece] * 2,
        out_shape=[sds((1024, 512), BF)] * 8 if others else [sds((4, 1024, 512), BF)] * 2,
        compiler_params=pltpu.CompilerParams(vmem_limit_bytes=FULL_VMEM),
        cost_estimate=SMALL_COST,
        name="weight_stage",
    )(two, gout, dmix, dgu, act, gn, *others)


def with_steps(da, dt_grad):
    count = da.shape[0]
    cols = jnp.concatenate([dt_grad, jnp.zeros((120, count), F32)], axis=0).T
    last = jnp.where(lanes((1, 128)) < 64, da[:, 256:].astype(F32), pltpu.roll(cols, 64, 1))
    return jnp.concatenate([da[:, :256], last.astype(BF)], axis=1)


def input_grad_body(off, da, ds, dt_grad, weight, out_ref):
    left = with_steps(da[...], dt_grad[...])
    out_ref[...] = (dot_bt(left, weight[:, :384]) + dot_bt(ds[...], weight[:, 384:])).astype(BF)


def input_grad(off, da, ds, dt_grad, weight):
    n = PROJ_ROWS
    own = ds.shape[0] // 2
    at = lambda i, off: (off[0] + i, 0)
    return pl.pallas_call(
        input_grad_body,
        grid_spec=pltpu.PrefetchScalarGridSpec(
            num_scalar_prefetch=1,
            grid=(own // n,),
            in_specs=[
                pl.BlockSpec((n, 384), at),
                pl.BlockSpec((n, 640), at),
                pl.BlockSpec((8, n), lambda i, off: (0, off[0] + i)),
                whole((1024, 1024)),
            ],
            out_specs=pl.BlockSpec((n, 1024), lambda i, off: (i, 0)),
        ),
        out_shape=jax.ShapeDtypeStruct((own, 1024), BF),
        compiler_params=params(),
        cost_estimate=SMALL_COST,
        name="input_grad",
    )(off, da, ds, dt_grad, weight)


def project_grad_body(bounds, normed, da, ds, dt_grad, alone, shared, acc_a, acc_s):
    @pl.when(pl.program_id(0) == 0)
    def _():
        acc_a[...] = jnp.zeros_like(acc_a)
        acc_s[...] = jnp.zeros_like(acc_s)

    acc_a[...] += dot_at(normed[...], with_steps(da[...], dt_grad[...]))
    acc_s[...] += dot_at(normed[...], ds[...])

    @pl.when(pl.program_id(0) == pl.num_programs(0) - 1)
    def _():
        lane = lanes((1, 128))
        left = lane < 64
        turned = acc_a[:, 128:256]
        turned = jnp.where(lane % 64 < 32, pltpu.roll(turned, 96, 1), -pltpu.roll(turned, 32, 1))
        kv = acc_a[:, :128] + jnp.where(left, turned, 0.0)
        q = acc_a[:, 256:] + jnp.where(left, pltpu.roll(turned, 64, 1), 0.0)
        alone[:, :128] = q.astype(BF)
        alone[:, 128:] = acc_s[:, :384].astype(BF)
        low = bounds[2] // 2 == 0
        swapped = pltpu.roll(kv, 64, 1)
        keys = jnp.where(left == low, jnp.where(low, kv, swapped), 0.0)
        values = jnp.where(left == low, jnp.where(low, swapped, kv), 0.0)
        shared[:, :128] = keys.astype(BF)
        shared[:, 128:256] = values.astype(BF)
        shared[:, 256:] = acc_s[:, 384:].astype(BF)


def project_grad(bounds, normed, da, ds, dt_grad):
    full = normed.shape[0]
    n = 512
    row = lambda w: pl.BlockSpec((n, w), lambda i, *_: (i, 0))
    return pl.pallas_call(
        project_grad_body,
        grid_spec=pltpu.PrefetchScalarGridSpec(
            num_scalar_prefetch=1,
            grid=(full // n,),
            in_specs=[
                row(1024),
                row(384),
                row(640),
                pl.BlockSpec((8, n), lambda i, *_: (0, i)),
            ],
            out_specs=[whole((1024, 512))] * 2,
            scratch_shapes=[pltpu.VMEM((1024, 384), F32), pltpu.VMEM((1024, 640), F32)],
        ),
        out_shape=[jax.ShapeDtypeStruct((1024, 512), BF)] * 2,
        compiler_params=params(),
        cost_estimate=SMALL_COST,
        name="project_grad",
    )(bounds, normed, da, ds, dt_grad)


def assemble_body(bounds, p0, p1, p2, l3, r3, out):
    step = pl.program_id(0)
    for r, ref in enumerate((p0, p1, p2)):

        @pl.when(step == r)
        def _(ref=ref):
            out[...] = ref[...]

    @pl.when(step == 3)
    def _():
        out[:, :512] = l3[...]
        out[:, 512:] = r3[...]


def assemble(bounds, parts):
    count = parts[0].shape[0]
    return pl.pallas_call(
        assemble_body,
        grid_spec=pltpu.PrefetchScalarGridSpec(
            num_scalar_prefetch=1,
            grid=(4,),
            in_specs=[whole(p.shape) for p in parts],
            out_specs=pl.BlockSpec((count, 1024), lambda i, b: (i ^ b[2], 0)),
        ),
        out_shape=jax.ShapeDtypeStruct((4 * count, 1024), parts[0].dtype),
        compiler_params=params(),
        cost_estimate=SMALL_COST,
        name="assemble",
    )(bounds, *parts)


def swap(value, step):
    return lax.ppermute(value, "tensor", [(i, i ^ step) for i in range(4)])


def twin(value):
    return lax.ppermute(value, "ctx", [(0, 1), (1, 0)])


def exchange(value):
    return lax.all_to_all(value, ("ctx", "tensor"), 0, 0, tiled=True)


def dp_swap(value, step):
    return lax.ppermute(value, "dp", [(i, i ^ step) for i in range(4)])


class DpSum:
    def __init__(self, value):
        self.four = lax.axis_size("dp") == 4
        place = lax.axis_index("dp")
        self.inner = (place == 1) | (place == 2)
        self.step = 0
        half = value.shape[0] // 2
        first, second = value[:half], value[half:]
        if self.four:
            self.sent = jnp.where(self.inner, second, first)
            self.kept = jnp.where(self.inner, first, second)
        else:
            self.sent = self.kept = value

    def send(self):
        if not self.four:
            self.sent = lax.psum(self.sent, "dp") if self.step == 0 else self.sent
        elif self.step == 1:
            self.sent = lax.ppermute(self.sent, "dp", [(1, 2), (2, 1), (0, 3), (3, 0)])
        else:
            self.sent = dp_swap(self.sent, 1)
        self.step += 1

    def add(self):
        if self.four:
            self.kept = plus(self.kept, self.sent)
            self.sent = self.kept

    def end(self):
        if not self.four:
            return self.sent
        return jnp.concatenate(
            [
                jnp.where(self.inner, self.kept, self.sent),
                jnp.where(self.inner, self.sent, self.kept),
            ],
            axis=0,
        )


def together(*values):
    return lax.optimization_barrier(values)


def after(value, *before):
    return lax.optimization_barrier((value, before))[0]


def plus(a, b):
    return (a.astype(F32) + b.astype(F32)).astype(BF)


def block_at(value, index, count):
    return lax.dynamic_slice_in_dim(value, index * count, count, 0)


def merge_body(bounds, own, got, l0, r0, l2, r1, ls, rs):
    total = (own[...].astype(F32) + got[...].astype(F32)).astype(BF)
    left, right = total[:, :512], total[:, 512:]
    count = total.shape[0]
    low, high = pl.ds(0, count), pl.ds(count, count)
    targets = [
        ((l0, low), (r0, low)),
        ((ls, high), (r1, low)),
        ((l2, low), (rs, high)),
        ((ls, low), (rs, low)),
    ]
    for i, ((a, rows_a), (b, rows_b)) in enumerate(targets):

        @pl.when(pl.program_id(0) == i)
        def _(a=a, b=b, rows_a=rows_a, rows_b=rows_b):
            a[rows_a, :] = left
            b[rows_b, :] = right


def merge(bounds, own, got):
    count = own.shape[0] // 4
    block = pl.BlockSpec((count, 1024), lambda i, b: (i ^ b[2], 0))
    shapes = [(count, 512)] * 4 + [(2 * count, 512)] * 2
    once = lambda shape: pl.BlockSpec(
        shape, lambda i, b: (0, 0), pipeline_mode=pl.Buffered(1)
    )
    return pl.pallas_call(
        merge_body,
        grid_spec=pltpu.PrefetchScalarGridSpec(
            num_scalar_prefetch=1,
            grid=(4,),
            in_specs=[block, block],
            out_specs=[once(v) for v in shapes],
        ),
        out_shape=[jax.ShapeDtypeStruct(v, BF) for v in shapes],
        compiler_params=params(),
        cost_estimate=SMALL_COST,
        name="merge",
    )(bounds, own, got)


def scatter_first(parts):
    return list(parts[:4]) + [swap(parts[4], 1), swap(parts[5], 2)]


def scatter_middle(state):
    left0, right0, left2, right1, left, right = state
    count = left0.shape[0]
    return [left0, right0, left, right, plus(left2, left[:count]), plus(right1, right[:count])]


def scatter_second(state):
    return state[:4] + [swap(state[4], 2), swap(state[5], 1)]


def finish_body(bounds, *refs):
    state, tok, dhid, gain, out, part = refs[:6], *refs[6:]
    total = lambda i: (state[i][...].astype(F32) + state[i + 2][...]) + state[i + 4][...]
    grad = jnp.concatenate([total(0), total(1)], axis=1)
    values = tok[...].astype(F32)
    scale = lax.rsqrt(jnp.mean(values * values, axis=-1, keepdims=True) + EPSILON)
    weighted = grad * gain[...]
    mean = jnp.mean(weighted * values, axis=-1, keepdims=True)
    out[...] = (dhid[...] + scale * weighted - values * (scale * scale * scale * mean)).astype(BF)

    @pl.when(pl.program_id(0) == 0)
    def _():
        part[...] = jnp.zeros_like(part)

    part[...] += jnp.sum(grad * values * scale, axis=0, keepdims=True)


def finish(bounds, state, tokens, dhid, gain):
    count = dhid.shape[0]
    n = count // 2
    half = pl.BlockSpec((n, 512), lambda i, b: (i, 0))
    later = pl.BlockSpec((n, 512), lambda i, b: (2 + i, 0))
    row = pl.BlockSpec((n, 1024), lambda i, b: (i, 0))
    return pl.pallas_call(
        finish_body,
        grid_spec=pltpu.PrefetchScalarGridSpec(
            num_scalar_prefetch=1,
            grid=(2,),
            in_specs=[half, half, later, later, half, half]
            + [pl.BlockSpec((n, 1024), lambda i, b: (2 * b[2] + i, 0)), row, whole((1, 1024))],
            out_specs=[row, whole((1, 1024))],
        ),
        out_shape=[
            jax.ShapeDtypeStruct((count, 1024), BF),
            jax.ShapeDtypeStruct((1, 1024), F32),
        ],
        compiler_params=params(),
        cost_estimate=SMALL_COST,
        name="finish",
    )(bounds, *state, tokens, dhid, gain)


def rope_tables(count):
    exponent = np.arange(0, HEAD_SIZE, 2).astype(np.float32) / np.float32(HEAD_SIZE)
    frequency = (np.float32(ROPE_BASE) ** (-exponent)).astype(np.float32)
    angles = np.arange(count).astype(np.float32)[:, None] * frequency[None, :]
    angles = np.concatenate([angles] * 4, axis=1)
    return (np.cos(angles).astype(np.float32), np.sin(angles).astype(np.float32))


def ordered(own, other, c, axis):
    return jnp.concatenate(
        [jnp.where(c == 0, own, other), jnp.where(c == 0, other, own)], axis=axis
    )


def local(
    tokens, doc_ids, norm_gain, q_proj, key_value_weight, o_proj, z_proj, x_proj, dt_proj,
    bc_proj, conv_x, xconv_bias, conv_bc, bcconv_bias, dt_bias, a_log, skip_gain, gated_gain,
    out_proj, mlp_gain, gate_proj, up_proj, down_proj, out_grad,
):
    t, c = lax.axis_index("tensor"), lax.axis_index("ctx")
    own_tokens, grad_out = tokens[0], out_grad[0]
    own = own_tokens.shape[0]
    full = 2 * own
    mine = own // 4
    other_tokens = twin(own_tokens)

    def cols(w):
        n = w.shape[-1] // 2
        return lax.dynamic_slice_in_dim(w, c * n, n, w.ndim - 1)

    def rows(w):
        return block_at(w, c, w.shape[0] // 2)

    docs = doc_ids[0]
    bounds = jnp.stack([jnp.sum(docs < 1), jnp.sum(docs < 2), t, c]).astype(jnp.int32)
    own_gain = rows(gated_gain)
    gain0 = jnp.concatenate([own_gain, jnp.ones((64,), F32)])
    gains = exchange(jnp.broadcast_to(gain0[None, None], (8, 1, 256)))
    weight, pack0 = prepare(
        bounds, gate_proj, up_proj, down_proj, out_proj, o_proj, key_value_weight, q_proj,
        x_proj, z_proj, dt_proj, bc_proj,
    )
    weight, pack0, gains = together(weight, pack0, gains)
    pack1, pack2 = swap(pack0, 1), swap(pack0, 2)
    cos, sin = rope_tables(full)
    cos, sin = jnp.asarray(cos), jnp.asarray(sin)
    steps = own // PROJ_ROWS
    own_off = jnp.reshape(c * steps, (1,)).astype(jnp.int32)
    other_off = jnp.reshape((1 - c) * steps, (1,)).astype(jnp.int32)
    gain_row = norm_gain[None]
    first = project(own_off, own_tokens, gain_row, weight, cos, sin)
    normed, qp, kv, xbc, z, dt_raw = project(
        other_off, other_tokens, gain_row, weight, cos, sin, before=first
    )

    pad = lambda v: jnp.zeros(v.shape[:-1] + (64,), F32)
    cx, cb = cols(conv_x), cols(xconv_bias)
    taps = jnp.concatenate([cx, pad(cx), conv_bc], axis=1)
    taps = jnp.concatenate([taps, jnp.zeros_like(taps)], axis=0)
    bias = jnp.concatenate([cb, pad(cb), bcconv_bias])[None]
    head = jnp.stack([cols(dt_bias), -jnp.exp(cols(a_log))], axis=1)
    head = jnp.pad(head, ((0, 5), (0, 126)))
    skip = jnp.pad(jnp.repeat(cols(skip_gain), MP), (0, 64))[None]
    g01, g2, y, states = scan_forward(bounds, xbc, z, dt_raw, taps, bias, head, skip)
    g2, g01, pack1, pack2 = together(g2, g01, pack1, pack2)
    left3, right3 = pack1[:, :512], pack2[:, 512:]
    qp, left3, right3, g01 = together(qp, left3, right3, g01)
    left3, right3 = swap(left3, 2), swap(right3, 1)
    near = [pack0, pack1, pack2]
    far = [twin(v) for v in near]
    g_rows = exchange(g01.reshape(8, mine, 128))
    tile, keep = attend(bounds, qp, kv, g2)
    tile, g_rows, far, left3, right3 = together(tile, g_rows, far, left3, right3)
    h_rows = exchange(tile.reshape(8, mine, 128))
    packs = near + [left3, right3] + far + [twin(left3), twin(right3)]

    res = row_stage(bounds, g_rows, h_rows, own_tokens, grad_out, mlp_gain[None], gains, packs)
    layer_rows, two, dmix, dhid = res[0:4]
    act, dgu, gn = list(res[4:6]), list(res[6:8]), list(res[8:10])
    mlp_part, gain_part = res[11:13]
    grad_rows = block_at(grad_out, t, mine)
    dn = exchange(res[10])
    far_w = weight_stage(two, grad_rows, dmix, dgu[1], act[1], gn[1])
    far_w = [twin(v) for v in far_w]
    near_w = weight_stage(two, grad_rows, dmix, dgu[0], act[0], gn[0], *far_w)
    dn, near_w = together(dn, near_w)
    sum_a, sum_b = near_w[:4], near_w[4:]

    a3, b3 = swap(sum_a[3], 1), swap(sum_b[3], 2)
    a1, b2 = swap(sum_a[1], 1), swap(sum_b[2], 2)
    da = attend_back(bounds, qp, kv, keep, dn, cos, sin)
    da, a3, b3 = together(da, a3, b3)
    a_next, b_next = plus(sum_a[2], a3), plus(sum_b[1], b3)
    xbc, a_next, b_next = together(xbc, a_next, b_next)
    a_next, b_next = swap(a_next, 2), swap(b_next, 1)
    own_gain_row = jnp.pad(own_gain, (0, 64))[None]
    zeros = [
        jnp.zeros((256, 128), F32),
        jnp.zeros((8, 512), F32),
        jnp.zeros((8, 512), F32),
        jnp.zeros((16, CHUNK), F32),
    ]
    back = lambda part, carry, made, data: scan_back(
        part, carry, made, bounds, data, z, y, dt_raw, states, dn, taps, bias, head, skip, own_gain_row
    )
    ds, dt_grad, *carry = back(0, zeros, [], xbc)
    ds, a1, b2, a_next, b_next = together(ds, a1, b2, a_next, b_next)
    add3 = lambda a, b, d: (a.astype(F32) + b.astype(F32) + d.astype(F32)).astype(BF)
    sums = DpSum(
        jnp.concatenate([add3(sum_a[0], a1, a_next), add3(sum_b[0], b2, b_next)], axis=1)
    )
    xbc, sums.sent, sums.kept, layer_rows = together(xbc, sums.sent, sums.kept, layer_rows)
    sums.send()
    layer1, layer2 = swap(layer_rows, 1), swap(layer_rows, 2)
    conv_carry = (carry[2], carry[3], carry[0], carry[1])
    ds, dt_grad, conv_acc, head_acc, _, _ = back(1, conv_carry, [ds, dt_grad], xbc)
    ds, sums.sent, layer1, layer2 = together(ds, sums.sent, layer1, layer2)

    sums.add()
    heads = jnp.concatenate(
        [
            jnp.sum(conv_acc[5, :192].reshape(3, 64), axis=1),
            jnp.sum(head_acc[0:3], axis=1),
            jnp.sum(head_acc[8:11], axis=1),
        ]
    )
    place = c * 4 + t
    own_small = jnp.pad(jnp.concatenate([conv_acc[:5, :192].reshape(-1), heads]), (0, 55))
    at_own = lax.dynamic_update_slice_in_dim(
        jnp.zeros((8, 1024), F32), own_small[None], place, 0
    )
    flat = jnp.concatenate(
        [at_own.reshape(-1), gain_part.reshape(-1), conv_acc[:5, 256:].reshape(-1), mlp_part[0]]
    )
    flat = jnp.pad(flat, (0, (-flat.shape[0]) % 1024)).reshape(-1, 128)
    layer3 = [layer1[:, :512], layer2[:, 512:]]
    ds, layer3, flat, sums.sent, sums.kept = together(ds, layer3, flat, sums.sent, sums.kept)
    sums.send()
    flat_got = twin(flat)
    layer3 = [swap(layer3[0], 2), swap(layer3[1], 1)]
    grad_other = input_grad(other_off, da, ds, dt_grad, weight)
    grad_other, flat_got, ds = together(grad_other, flat_got, ds)
    flat = flat + flat_got
    ds, grad_other, flat = together(ds, grad_other, flat)
    sent = twin(grad_other)
    flat_got = swap(flat, 1)
    grad_own = input_grad(own_off, da, ds, dt_grad, weight)
    grad_own, sent, flat_got, layer3 = together(grad_own, sent, flat_got, layer3)
    flat = flat + flat_got
    parts = merge(bounds, grad_own, sent)
    ds, parts, flat = together(ds, parts, flat)
    state = scatter_first(parts)
    flat_got = swap(flat, 2)
    alone, shared = project_grad(bounds, normed, da, ds, dt_grad)
    alone, shared, state, flat_got, sums.sent = together(
        alone, shared, state, flat_got, sums.sent
    )
    flat = flat + flat_got
    sums.add()
    state = scatter_middle(state)
    alone = DpSum(alone)
    (state, flat, sums.sent, sums.kept, alone.sent, alone.kept, shared, layer3) = together(
        state, flat, sums.sent, sums.kept, alone.sent, alone.kept, shared, layer3
    )
    state = scatter_second(state)
    sums.send()
    alone.send()
    shared = exchange(shared.reshape(8, 128, 512))
    layer_out = assemble(bounds, [layer_rows, layer1, layer2, *layer3])
    state, layer_out = together(state, layer_out)
    token_rows, norm_part = finish(bounds, state, own_tokens, dhid, norm_gain[None])
    shared = jnp.sum(shared.astype(F32), axis=0).astype(BF)
    alone.add()
    reduced = sums.end()
    four = lax.axis_size("dp") == 4
    (token_rows, norm_part, alone.sent, alone.kept, reduced, shared, flat) = together(
        token_rows, norm_part, alone.sent, alone.kept, reduced, shared, flat
    )
    tok1, tok2 = swap(token_rows, 1), swap(token_rows, 2)
    alone.send()
    twin_piece = twin(reduced)
    norm_part = jnp.broadcast_to(norm_part.reshape(1, 8, 128), (8, 8, 128))
    norm_part = jnp.sum(exchange(norm_part), axis=0)
    if four:
        every = lambda v: lax.all_to_all(
            jnp.broadcast_to(v[None], (4,) + v.shape), "dp", 0, 0, tiled=True
        )
        shared = jnp.sum(every(shared).astype(F32), axis=0).astype(BF)
        flat = flat + dp_swap(flat, 1)
    else:
        shared, flat = lax.psum(shared, "dp"), lax.psum(flat, "dp")
    tok1, tok2, alone.sent, twin_piece, flat = together(
        tok1, tok2, alone.sent, twin_piece, flat
    )
    alone.add()
    tok3 = [tok1[:, :512], tok2[:, 512:]]
    tok3, alone.sent, alone.kept, flat, norm_part, shared = together(
        tok3, alone.sent, alone.kept, flat, norm_part, shared
    )
    tok3 = [swap(tok3[0], 2), swap(tok3[1], 1)]
    alone.send()
    if four:
        flat = flat + dp_swap(flat, 2)
        norm_sum = jnp.sum(every(norm_part), axis=0).reshape(-1)
    else:
        norm_sum = lax.psum(norm_part, "dp").reshape(-1)
    shared = exchange(jnp.broadcast_to(shared[None], (8, 128, 512)))
    shared = shared.reshape(1024, 512).astype(F32)
    alone = alone.end()
    alone_twin = twin(alone)
    tokens_grad = assemble(bounds, [token_rows, tok1, tok2, *tok3])
    piece_a, piece_b = reduced[:, :512], reduced[:, 512:]
    twin_a, twin_b = twin_piece[:, :512], twin_piece[:, 512:]
    flat = flat.reshape(-1)
    small = flat[:8192].reshape(8, 1024)
    gain_sum = flat[8192:10240].reshape(8, 256)
    bc_sum = flat[10240:11520].reshape(5, 256)
    mlp_sum = flat[11520:12544]
    both_cores = lambda v: jnp.stack([lax.dynamic_index_in_dim(v, k * 4 + t, 0, False) for k in range(2)])
    small = both_cores(small)
    gain_sum = both_cores(gain_sum)[:, :192].reshape(-1)
    conv_small = small[:, :960].reshape(2, 5, 192)
    conv_small = jnp.concatenate([conv_small[0], conv_small[1]], axis=1)
    head_small = small[:, 960:969].reshape(2, 3, 3)
    per_head_sum = lambda i: head_small[:, i].reshape(-1)

    f = lambda lo, hi, own_part, other_part, axis: ordered(
        own_part[:, lo:hi], other_part[:, lo:hi], c, axis
    ).astype(F32)
    flip = lambda lo, hi: ordered(
        piece_b[:, lo:hi].T, twin_b[:, lo:hi].T, c, 0
    ).astype(F32)
    zcols = lambda v: jnp.concatenate([v[:, 384:512], v[:, 320:384]], axis=1)
    return (
        layer_out[None],
        tokens_grad[None],
        norm_sum,
        f(0, 64, alone, alone_twin, 1),
        shared[:, :256],
        flip(448, 512),
        ordered(zcols(alone), zcols(alone_twin), c, 1).astype(F32),
        f(128, 320, alone, alone_twin, 1),
        f(64, 67, alone, alone_twin, 1),
        shared[:, 256:],
        conv_small[:4],
        conv_small[4],
        bc_sum[:4],
        bc_sum[4],
        per_head_sum(2),
        per_head_sum(1),
        per_head_sum(0),
        gain_sum,
        flip(256, 448),
        mlp_sum,
        f(0, 256, piece_a, twin_a, 1),
        f(256, 512, piece_a, twin_a, 1),
        flip(0, 256),
    )


def solution(mesh):
    placed = (
        P("dp", "ctx", None),
        P("dp", None),
        P(),
        P(None, "tensor"),
        P(),
        P("tensor", None),
        P(None, "tensor"),
        P(None, "tensor"),
        P(None, "tensor"),
        P(),
        P(None, "tensor"),
        P("tensor"),
        P(),
        P(),
        P("tensor"),
        P("tensor"),
        P("tensor"),
        P("tensor"),
        P("tensor", None),
        P(),
        P(None, "tensor"),
        P(None, "tensor"),
        P("tensor", None),
        P("dp", "ctx", None),
    )
    return jax.shard_map(
        local,
        mesh=mesh,
        in_specs=placed,
        out_specs=(
            P("dp", "ctx", None),
            P("dp", "ctx", None),
            P(),
            P(None, "tensor"),
            P(),
            P("tensor", None),
            P(None, "tensor"),
            P(None, "tensor"),
            P(None, "tensor"),
            P(),
            P(None, "tensor"),
            P("tensor"),
            P(),
            P(),
            P("tensor"),
            P("tensor"),
            P("tensor"),
            P("tensor"),
            P("tensor", None),
            P(),
            P(None, "tensor"),
            P(None, "tensor"),
            P("tensor", None),
        ),
        check_vma=False,
    )
```

```python
import functools

import jax
import numpy as np
import jax.numpy as jnp
from jax import lax
from jax.experimental import pallas as pl
from jax.experimental.pallas import tpu as pltpu
from jax.sharding import PartitionSpec as P

BF, F32 = jnp.bfloat16, jnp.float32
EPSILON = 1e-05
ROPE_BASE = 100000000000.0
HEAD_SIZE = 64
MP = 64
PROJ_ROWS = 256
BQ = 512
CHUNK = 256
VMEM_LIMIT = 48 * 1024 * 1024
FULL_VMEM = 60 * 1024 * 1024
SMALL_COST = pl.CostEstimate(flops=1000000, bytes_accessed=100000, transcendentals=0)


def dot(left, right, dims=((1,), (0,)), precision=None):
    return lax.dot_general(
        left, right, (dims, ((), ())), precision=precision, preferred_element_type=F32
    )


def dot_bt(left, right):
    return dot(left, right, ((1,), (1,)))


def dot_at(left, right):
    return dot(left, right, ((0,), (0,)))


def lanes(shape):
    return lax.broadcasted_iota(jnp.int32, shape, len(shape) - 1)


def rows_of(shape):
    return lax.broadcasted_iota(jnp.int32, shape, 0)


def doc_start(pos, first, second):
    return jnp.where(pos >= second, second, jnp.where(pos >= first, first, 0))


def halves(low, high):
    return jnp.where(lanes((1, 128)) < 64, low, high)


def params(**kw):
    return pltpu.CompilerParams(vmem_limit_bytes=VMEM_LIMIT, **kw)


def whole(shape):
    return pl.BlockSpec(shape, lambda *_: (0,) * len(shape))


def proj_body(off, tok, gain, weight, cos, sin, *refs):
    normed_ref, qp_ref, kv_ref, xbc_ref, z_ref, dt_ref = refs[-6:]
    values = tok[...].astype(F32)
    scale = lax.rsqrt(jnp.mean(values * values, axis=-1, keepdims=True) + EPSILON)
    normed = (values * scale * gain[...]).astype(BF)
    normed_ref[...] = normed
    c, s = cos[...], sin[...]
    left = lanes((1, 128)) < 64
    att = dot(normed, weight[:, :384])
    kv, turned, qd = att[:, :128], att[:, 128:256], att[:, 256:]
    kv_ref[...] = jnp.where(left, kv * c + turned * s, kv).astype(BF)
    q_rot = qd * c + pltpu.roll(turned, 64, 1) * s
    qp_ref[...] = jnp.where(left, q_rot.astype(BF) * 0.125, 0.0).astype(BF)
    dt_ref[...] = qd.T[64:72, :]
    ssm = dot(normed, weight[:, 384:])
    x2z2 = ssm[:, 128:256]
    xbc_ref[:, :128] = ssm[:, :128].astype(BF)
    xbc_ref[:, 128:256] = jnp.where(left, x2z2, 0.0).astype(BF)
    xbc_ref[:, 256:] = ssm[:, 384:].astype(BF)
    z_ref[:, :128] = ssm[:, 256:384]
    z_ref[:, 128:] = jnp.where(left, pltpu.roll(x2z2, 64, 1), 0.0)


def project(off, tokens, gain, weight, cos, sin, before=None):
    own = tokens.shape[0]
    full = cos.shape[0]
    n = PROJ_ROWS
    outs = [
        jax.ShapeDtypeStruct((full, 1024), BF),
        jax.ShapeDtypeStruct((full, 128), BF),
        jax.ShapeDtypeStruct((full, 128), BF),
        jax.ShapeDtypeStruct((full, 512), BF),
        jax.ShapeDtypeStruct((full, 256), F32),
        jax.ShapeDtypeStruct((8, full), F32),
    ]
    at = lambda i, off: (off[0] + i, 0)
    out_specs = [pl.BlockSpec((n, o.shape[1]), at) for o in outs[:5]]
    out_specs.append(pl.BlockSpec((8, n), lambda i, off: (0, off[0] + i)))
    in_specs = [
        pl.BlockSpec((n, 1024), lambda i, off: (i, 0)),
        whole((1, 1024)),
        whole((1024, 1024)),
        pl.BlockSpec((n, 128), at),
        pl.BlockSpec((n, 128), at),
    ]
    args = [off, tokens, gain, weight, cos, sin]
    alias = {}
    if before is not None:
        in_specs += [pl.BlockSpec(memory_space=pl.ANY)] * 6
        args += list(before)
        alias = {6 + i: i for i in range(6)}
    return pl.pallas_call(
        proj_body,
        grid_spec=pltpu.PrefetchScalarGridSpec(
            num_scalar_prefetch=1, grid=(own // n,), in_specs=in_specs, out_specs=out_specs
        ),
        out_shape=outs,
        input_output_aliases=alias,
        compiler_params=params(),
        cost_estimate=SMALL_COST,
        name="norm_project",
    )(*args)


def turned_lanes(value):
    low = lanes((1, 128)) % 64 < 32
    return jnp.where(low, -pltpu.roll(value, 96, 1), pltpu.roll(value, 32, 1))


def prep_body(bounds, gate, up, down, mix, att, kv, q, x, z, dt, bc, weight, pack):
    n = gate.shape[0]
    pack[:, :256] = gate[...]
    pack[:, 256:512] = up[...]
    pack[:, 512:768] = down[...].T
    pack[:, 768:] = jnp.concatenate([mix[...], att[...]], axis=0).T
    first, low_kv = bounds[3] == 0, bounds[2] // 2 == 0
    lane = lanes((1, 128))
    left = lane < 64
    tile = lambda ref, i: ref[:, 128 * i : 128 * i + 128].astype(F32)
    swapped = lambda v: pltpu.roll(v, 64, 1)
    keys, values = tile(kv, 0), tile(kv, 1)
    keys = jnp.where(low_kv, keys, swapped(keys))
    values = jnp.where(low_kv, swapped(values), values)
    query = tile(q, 0)
    query = jnp.where(first, query, swapped(query))
    steps = jnp.concatenate([dt[...].astype(F32), jnp.zeros((n, 122), F32)], axis=1)
    steps = jnp.where(lane < 3, jnp.where(first, steps, pltpu.roll(steps, 125, 1)), 0.0)

    def heads(ref):
        a, b, d = tile(ref, 0), tile(ref, 1), swapped(tile(ref, 2))
        return jnp.where(first, a, jnp.where(left, swapped(b), d)), jnp.where(first, b, d)

    x01, x2 = heads(x)
    z01, z2 = heads(z)
    tiles = [
        jnp.where(left, keys, values),
        jnp.where(left, turned_lanes(keys), swapped(turned_lanes(query))),
        jnp.where(left, query, swapped(steps)),
        x01,
        jnp.where(left, x2, swapped(z2)),
        z01,
    ]
    for i, value in enumerate(tiles):
        weight[:, 128 * i : 128 * i + 128] = value.astype(BF)
    weight[:, 768:] = bc[...]


def prepare(bounds, gate, up, down, mix, att, kv, q, x, z, dt, bc):
    n = 256
    row = lambda w: pl.BlockSpec((n, w), lambda i, b: (i, 0))
    col = lambda h: pl.BlockSpec((h, n), lambda i, b: (b[3], i))
    mine = pl.BlockSpec((n, 256), lambda i, b: (i, b[3]))
    return pl.pallas_call(
        prep_body,
        grid_spec=pltpu.PrefetchScalarGridSpec(
            num_scalar_prefetch=1,
            grid=(4,),
            in_specs=[mine, mine, col(256), col(192), col(64)]
            + [row(256), row(128), row(384), row(384), row(6), row(256)],
            out_specs=[row(1024), row(1024)],
        ),
        out_shape=[jax.ShapeDtypeStruct((1024, 1024), BF)] * 2,
        compiler_params=pltpu.CompilerParams(vmem_limit_bytes=FULL_VMEM),
        cost_estimate=SMALL_COST,
        name="prepare",
    )(bounds, gate, up, down, mix, att, kv, q, x, z, dt, bc)


def block_range(qi, bounds):
    first, second = bounds[0], bounds[1]
    q0 = qi * BQ
    low = doc_start(q0, first, second) // BQ
    inner = (doc_start(q0 + BQ - 1, first, second) + BQ - 1) // BQ
    return low, jnp.minimum(jnp.maximum(inner, low), qi)


def allowed_keys(qi, kb, bounds):
    q = qi * BQ + rows_of((BQ, 1))
    k = kb * BQ + lanes((1, BQ))
    start = doc_start(q, bounds[0], bounds[1])
    return (k <= q) & (k >= start)


def attend_body(bounds, qp, kv, g2, out_ref, keep_ref):
    qi = pl.program_id(0)
    low, inner = block_range(qi, bounds)
    q = qp[...]

    def step(kb, carry, masked):
        top, total, acc = carry
        k = kv[pl.ds(pl.multiple_of(kb * BQ, BQ), BQ), :]
        s = dot_bt(q, k)
        if masked:
            s = jnp.where(allowed_keys(qi, kb, bounds), s, -1e30)
        new_top = jnp.maximum(top, jnp.max(s, axis=1, keepdims=True))
        p = jnp.exp(s - new_top)
        fade = jnp.exp(top - new_top)
        total = total * fade + jnp.sum(p, axis=1, keepdims=True)
        acc = acc * fade + dot(p.astype(BF), k)
        return new_top, total, acc

    carry = (jnp.full((BQ, 1), -1e30, F32), jnp.zeros((BQ, 1), F32), jnp.zeros((BQ, 128), F32))
    carry = lax.fori_loop(low, inner, lambda kb, c: step(kb, c, True), carry)
    carry = lax.fori_loop(inner, qi, lambda kb, c: step(kb, c, False), carry)
    top, total, acc = step(qi, carry, True)
    out = acc / total
    left = lanes((1, 128)) < 64
    out_ref[...] = jnp.where(left, g2[...], out.astype(BF))
    keep_ref[...] = jnp.where(left, top + jnp.log(total), out)


def attend(bounds, qp, kv, g2):
    full = qp.shape[0]
    block = pl.BlockSpec((BQ, 128), lambda i, *_: (i, 0))
    return pl.pallas_call(
        attend_body,
        grid_spec=pltpu.PrefetchScalarGridSpec(
            num_scalar_prefetch=1,
            grid=(full // BQ,),
            in_specs=[block, whole((full, 128)), block],
            out_specs=[block, block],
        ),
        out_shape=[
            jax.ShapeDtypeStruct((full, 128), BF),
            jax.ShapeDtypeStruct((full, 128), F32),
        ],
        compiler_params=params(),
        cost_estimate=SMALL_COST,
        name="attend",
    )(bounds, qp, kv, g2)


def attend_back_body(bounds, qp, kv, keep, grad, cos, sin, out_ref, acc_ref):
    blocks = pl.num_programs(0)
    qi = blocks - 1 - pl.program_id(0)
    left = lanes((1, 128)) < 64

    @pl.when(pl.program_id(0) == 0)
    def _():
        acc_ref[...] = jnp.zeros_like(acc_ref)

    low, inner = block_range(qi, bounds)
    q = qp[...]
    do = jnp.where(left, 0.0, grad[0].astype(F32))
    delta = jnp.sum(do * keep[...], axis=1, keepdims=True)
    do = do.astype(BF)
    lse = keep[:, :1]

    def step(kb, dq, masked):
        at = pl.ds(pl.multiple_of(kb * BQ, BQ), BQ)
        k = kv[at, :]
        p = jnp.exp(dot_bt(q, k) - lse)
        if masked:
            p = jnp.where(allowed_keys(qi, kb, bounds), p, 0.0)
        ds = (p * (dot_bt(do, k) - delta)).astype(BF)
        acc_ref[at, :] += dot_at(ds, q) + dot_at(p.astype(BF), do)
        return dq + dot(ds, k)

    dq = jnp.zeros((BQ, 128), F32)
    dq = lax.fori_loop(low, inner, lambda kb, c: step(kb, c, True), dq)
    dq = lax.fori_loop(inner, qi, lambda kb, c: step(kb, c, False), dq)
    dq = step(qi, dq, True) * 0.125
    dkv = acc_ref[pl.ds(pl.multiple_of(qi * BQ, BQ), BQ), :]
    c, s = cos[...], sin[...]
    out_ref[:, :128] = jnp.where(left, dkv * c, dkv).astype(BF)
    out_ref[:, 128:256] = (jnp.where(left, dkv, pltpu.roll(dq, 64, 1)) * s).astype(BF)
    out_ref[:, 256:] = jnp.where(left, dq * c, 0.0).astype(BF)


def attend_back(bounds, qp, kv, keep, grad, cos, sin):
    full = qp.shape[0]
    n = full // BQ
    block = pl.BlockSpec((BQ, 128), lambda i, *_: (n - 1 - i, 0))
    return pl.pallas_call(
        attend_back_body,
        grid_spec=pltpu.PrefetchScalarGridSpec(
            num_scalar_prefetch=1,
            grid=(n,),
            in_specs=[
                block,
                whole((full, 128)),
                block,
                pl.BlockSpec((1, BQ, 128), lambda i, *_: (n - 1 - i, 0, 1)),
                block,
                block,
            ],
            out_specs=pl.BlockSpec((BQ, 384), lambda i, *_: (n - 1 - i, 0)),
            scratch_shapes=[pltpu.VMEM((full, 128), F32)],
        ),
        out_shape=jax.ShapeDtypeStruct((full, 384), BF),
        compiler_params=params(),
        cost_estimate=SMALL_COST,
        name="attend_back",
    )(bounds, qp, kv, keep, grad, cos, sin)


def tap_mask(first_row, count, shift, bounds):
    pos = first_row + rows_of((count, 1))
    return (pos - doc_start(pos, bounds[0], bounds[1]) >= shift).astype(F32)


def conv_taps(ext_ref, r0, bounds, taps, bias):
    pre = bias + taps[3:4, :] * ext_ref[pl.ds(8, CHUNK), :]
    for shift in (1, 2, 3):
        mask = tap_mask(r0, CHUNK, shift, bounds)
        pre = pre + taps[3 - shift : 4 - shift, :] * (ext_ref[pl.ds(8 - shift, CHUNK), :] * mask)
    return pre


def chunk_decay(r0, bounds, dt_raw, head, extra=None):
    lane = lanes((1, CHUNK))
    dt = jax.nn.softplus(dt_raw + head[:, 0:1])
    la = dt * head[:, 1:2]
    upper = (rows_of((CHUNK, CHUNK)) <= lanes((CHUNK, CHUNK))).astype(F32)
    cum = dot(la, upper, precision=lax.Precision.HIGHEST)
    rows = [cum, dt] if extra is None else [cum, dt, extra]
    used = 8 * len(rows)
    stacked = jnp.concatenate(rows + [jnp.zeros((CHUNK - used, CHUNK), F32)], axis=0).T
    cum_col, dt_col = stacked[:, 0:8], stacked[:, 8:16]
    pos = r0 + rows_of((CHUNK, 1))
    start = doc_start(pos, bounds[0], bounds[1])
    start_last = doc_start(r0 + CHUNK - 1, bounds[0], bounds[1])
    key = r0 + lane
    mask = (key <= pos) & (key >= start)
    enter = jnp.where(start < r0, jnp.exp(cum_col), 0.0)
    fade = jnp.where(pos >= start_last, jnp.exp(cum_last_row(cum_col) - cum_col), 0.0)
    keep = jnp.where(start_last < r0, jnp.exp(cum_last_row(cum_col)), 0.0)
    return dt, la, cum, dt_col, cum_col, mask, enter, fade, keep, stacked[:, 16:24]


def two_terms(value):
    high = value.astype(BF)
    return high, (value - high.astype(F32)).astype(BF)


def cum_last_row(cum_col):
    return cum_col[CHUNK - 1 : CHUNK, :]


def per_head(col):
    return halves(col[:, 0:1], col[:, 1:2]), col[:, 2:3]


def state_rows(keep):
    row = rows_of((256, 1))
    return jnp.where(row < 64, keep[:, 0:1], jnp.where(row < 128, keep[:, 1:2], keep[:, 2:3]))


def scan_body(bounds, xbc, z, dt_raw, taps, bias, head, skip, g01, g2, y_ref, s_ref, ext, state):
    i = pl.program_id(0)
    r0 = i * CHUNK

    @pl.when(i == 0)
    def _():
        ext[pl.ds(0, 8), :] = jnp.zeros((8, 512), F32)
        state[...] = jnp.zeros_like(state)

    @pl.when(i > 0)
    def _():
        ext[pl.ds(0, 8), :] = ext[pl.ds(CHUNK, 8), :]

    ext[pl.ds(8, CHUNK), :] = xbc[...].astype(F32)
    pre = conv_taps(ext, r0, bounds, taps[...], bias[...])
    conv = pre * jax.nn.sigmoid(pre)
    x01, x2 = conv[:, :128], conv[:, 128:256]
    b, c = conv[:, 256:384].astype(BF), conv[:, 384:].astype(BF)
    dt, la, cum, dt_col, cum_col, mask, enter, fade, keep, _ = chunk_decay(
        r0, bounds, dt_raw[...], head[...]
    )
    inner = dot_bt(c, b)
    x01b, x2b = x01.astype(BF), x2.astype(BF)
    ys = []
    for h in range(3):
        gap = cum_col[:, h : h + 1] - cum[h : h + 1, :]
        decay = jnp.exp(jnp.where(mask, gap, -1e30))
        m = (inner * decay * dt[h : h + 1, :]).astype(BF)
        ys.append(dot(m, x01b if h < 2 else x2b))
    s0 = state[...]
    s_ref[0] = s0
    s0b, s0c = two_terms(s0)
    carried = dot_bt(c, s0b) + dot_bt(c, s0c)
    e01, e2 = per_head(enter)
    y01 = halves(ys[0], ys[1]) + e01 * carried[:, :128] + skip[:, :128] * x01
    y2 = ys[2] + e2 * carried[:, 128:] + skip[:, 128:] * x2
    w01, w2 = per_head(fade * dt_col)
    xw = jnp.concatenate([(x01 * w01).astype(BF), (x2 * w2).astype(BF)], axis=1)
    state[...] = s0 * state_rows(keep) + dot_at(xw, b)
    y_ref[:, :128] = y01
    y_ref[:, 128:] = y2
    z01, z2 = z[:, :128], z[:, 128:]
    g01[...] = (y01 * (z01 * jax.nn.sigmoid(z01))).astype(BF)
    g2[...] = (y2 * (z2 * jax.nn.sigmoid(z2))).astype(BF)


def scan_forward(bounds, xbc, z, dt_raw, taps, bias, head, skip):
    full = xbc.shape[0]
    n = full // CHUNK
    row = lambda width: pl.BlockSpec((CHUNK, width), lambda i, *_: (i, 0))
    return pl.pallas_call(
        scan_body,
        grid_spec=pltpu.PrefetchScalarGridSpec(
            num_scalar_prefetch=1,
            grid=(n,),
            in_specs=[
                row(512),
                row(256),
                pl.BlockSpec((8, CHUNK), lambda i, *_: (0, i)),
                whole((8, 512)),
                whole((1, 512)),
                whole((8, 128)),
                whole((1, 256)),
            ],
            out_specs=[
                row(128),
                row(128),
                row(256),
                pl.BlockSpec((1, 256, 128), lambda i, *_: (i, 0, 0)),
            ],
            scratch_shapes=[pltpu.VMEM((CHUNK + 8, 512), F32), pltpu.VMEM((256, 128), F32)],
        ),
        out_shape=[
            jax.ShapeDtypeStruct((full, 128), BF),
            jax.ShapeDtypeStruct((full, 128), BF),
            jax.ShapeDtypeStruct((full, 256), F32),
            jax.ShapeDtypeStruct((n, 256, 128), F32),
        ],
        compiler_params=params(),
        cost_estimate=SMALL_COST,
        name="scan_forward",
    )(bounds, xbc, z, dt_raw, taps, bias, head, skip)


def scalar_rows(terms):
    total = terms[0:2, :] + terms[2:4, :] + terms[4:6, :]
    return jnp.concatenate([total, jnp.zeros((6, CHUNK), F32)], axis=0)


def scan_back_body(
    last, bounds, xbc, before, z, y, dt_raw, s0_ref, dn01, dn2, scal, taps, bias, head, skip, gain,
    dstate_in, dext_in, acc_in, head_in, *refs,
):
    out_ref, dt_grad, acc, head_acc, dstate_out, dext_out, ext, dext, dstate = refs[-9:]
    step = pl.program_id(0)
    i = last - step
    r0 = i * CHUNK
    left = lanes((1, 128)) < 64

    @pl.when(step == 0)
    def _():
        dext[pl.ds(CHUNK, 8), :] = dext_in[...]
        dstate[...] = dstate_in[...]
        acc[...] = acc_in[...]
        head_acc[...] = head_in[...]

    @pl.when(step > 0)
    def _():
        dext[pl.ds(CHUNK, 8), :] = dext[pl.ds(0, 8), :]

    ext[pl.ds(0, 8), :] = before[...].astype(F32)[8:, :]
    ext[pl.ds(8, CHUNK), :] = xbc[...].astype(F32)
    weights = taps[...]
    pre = conv_taps(ext, r0, bounds, weights, bias[...])
    sig = jax.nn.sigmoid(pre)
    conv = pre * sig
    x01, x2 = conv[:, :128], conv[:, 128:256]
    b, c = conv[:, 256:384].astype(BF), conv[:, 384:].astype(BF)
    dt, la, cum, dt_col, cum_col, mask, enter, fade, keep, scalars = chunk_decay(
        r0, bounds, dt_raw[...], head[...], scalar_rows(scal[0].astype(F32))
    )
    row_scale, row_cross = scalars[:, 0:1], scalars[:, 1:2]

    def gate_back(dn, gain, zz, yy):
        s = jax.nn.sigmoid(zz)
        act = zz * s
        g = yy * act
        sent = g.astype(BF).astype(F32)
        ratio = jnp.where(g == 0.0, 1.0, sent / g)
        dg = (dn * gain * row_scale - sent * row_cross) * ratio
        return dg * act, dg * yy * (s + act * (1.0 - s))

    dy01, dz01 = gate_back(dn01[0].astype(F32), gain[:, :128], z[:, :128], y[:, :128])
    dy2, dz2 = gate_back(dn2[0].astype(F32), gain[:, 128:], z[:, 128:], y[:, 128:])
    dy2, dz2 = jnp.where(left, dy2, 0.0), jnp.where(left, dz2, 0.0)
    inner = dot_bt(c, b)
    x01b, x2b = x01.astype(BF), x2.astype(BF)
    dy01b, dy2b = dy01.astype(BF), dy2.astype(BF)
    zero = jnp.zeros_like(dy01b)
    parts = [(jnp.where(left, dy01b, zero), x01b), (jnp.where(left, zero, dy01b), x01b), (dy2b, x2b)]
    d_inner = jnp.zeros((CHUNK, CHUNK), F32)
    dxs, col_sums, direct, row_sums = [], [], [], []
    for h in range(3):
        gap = cum_col[:, h : h + 1] - cum[h : h + 1, :]
        decay = jnp.exp(jnp.where(mask, gap, -1e30))
        dt_h = dt[h : h + 1, :]
        dyh, xh = parts[h]
        dm = dot_bt(dyh, xh)
        kept = inner * decay
        m = (kept * dt_h).astype(BF)
        dxs.append(dot_at(m, dyh if h == 2 else dy01b))
        pulled = dm * kept
        d_inner = d_inner + dm * (decay * dt_h)
        weighted = pulled * dt_h
        direct.append(jnp.sum(pulled, axis=0, keepdims=True))
        col_sums.append(jnp.sum(weighted, axis=0, keepdims=True))
        row_sums.append(jnp.sum(weighted, axis=1, keepdims=True))
    s0 = s0_ref[0]
    s0b, s0c = two_terms(s0)
    ds1 = dstate[...]
    ds1b, ds1c = two_terms(ds1)
    e01, e2 = per_head(enter)
    ey01, ey2 = dy01 * e01, dy2 * e2
    ey, eyc = two_terms(jnp.concatenate([ey01, ey2], axis=1))
    carried = dot_bt(c, s0b) + dot_bt(c, s0c)
    f01, f2 = per_head(fade)
    d01, d2 = per_head(dt_col)
    back = dot_bt(b, ds1b)
    fb01, fb2 = f01 * back[:, :128], f2 * back[:, 128:]
    xw = jnp.concatenate([(x01 * (f01 * d01)).astype(BF), (x2 * (f2 * d2)).astype(BF)], axis=1)
    d_innerb = d_inner.astype(BF)
    dc = dot(d_innerb, b) + dot(ey, s0b) + dot(eyc, s0b) + dot(ey, s0c)
    db = dot_at(d_innerb, c) + dot(xw, ds1b) + dot(xw, ds1c)
    dx01 = halves(dxs[0], dxs[1]) + d01 * fb01 + skip[:, :128] * dy01
    dx2 = dxs[2] + d2 * fb2 + skip[:, 128:] * dy2
    kept_rows = state_rows(keep)
    crossing = jnp.sum(ds1 * s0 * kept_rows, axis=1, keepdims=True)
    dstate[...] = ds1 * kept_rows + dot_at(ey, c) + dot_at(eyc, c)
    inter01, inter2 = ey01 * carried[:, :128], ey2 * carried[:, 128:]
    u01, u2 = x01 * fb01, x2 * fb2
    pick = lambda v, h: jnp.where(left if h == 0 else ~left, v, 0.0)
    side = lambda v01, v2, h: jnp.sum(pick(v01, h) if h < 2 else v2, axis=1, keepdims=True)
    lane = lanes((1, CHUNK))
    tile = jnp.zeros((CHUNK, CHUNK), F32)
    crossed = jnp.zeros((8, 1), F32)
    head_row = rows_of((8, 1))
    for h in range(3):
        u = side(u01, u2, h)
        moved = row_sums[h] + side(inter01, inter2, h) - u * dt_col[:, h : h + 1]
        tile = jnp.where(lane == h, moved, jnp.where(lane == 8 + h, u, tile))
        total = jnp.sum(crossing[64 * h : 64 * h + 64, :], axis=0, keepdims=True)
        total = total + jnp.sum(u * dt_col[:, h : h + 1], axis=0, keepdims=True)
        crossed = jnp.where(head_row == h, total, crossed)
    tile = tile.T
    stack = lambda items: jnp.concatenate(items + [jnp.zeros((5, CHUNK), F32)], axis=0)
    dcum = tile[0:8, :] - stack(col_sums) + jnp.where(lane == CHUNK - 1, crossed, 0.0)
    lower = (rows_of((CHUNK, CHUNK)) >= lanes((CHUNK, CHUNK))).astype(F32)
    dla = dot(dcum, lower, precision=lax.Precision.HIGHEST)
    ddt = stack(direct) + tile[8:16, :] + dla * head[:, 1:2]
    graw = ddt * jax.nn.sigmoid(dt_raw[...] + head[:, 0:1])
    dt_grad[...] = graw
    head_acc[0:8, :] += dla * la
    head_acc[8:16, :] += graw
    dpre = jnp.concatenate([dx01, dx2, db, dc], axis=1) * (sig + conv * (1.0 - sig))
    dext[pl.ds(0, CHUNK), :] = dpre
    din = weights[3:4, :] * dpre
    acc[3:4, :] += jnp.sum(dpre * ext[pl.ds(8, CHUNK), :], axis=0, keepdims=True)
    acc[4:5, :] += jnp.sum(dpre, axis=0, keepdims=True)
    acc[5:6, :128] += jnp.sum(dy01 * x01, axis=0, keepdims=True)
    acc[5:6, 128:256] += jnp.sum(dy2 * x2, axis=0, keepdims=True)
    for shift in (1, 2, 3):
        tap = 3 - shift
        now = tap_mask(r0, CHUNK, shift, bounds)
        acc[tap : tap + 1, :] += jnp.sum(
            dpre * (ext[pl.ds(8 - shift, CHUNK), :] * now), axis=0, keepdims=True
        )
        later = tap_mask(r0 + shift, CHUNK, shift, bounds)
        din = din + weights[tap : tap + 1, :] * (dext[pl.ds(shift, CHUNK), :] * later)
    out_ref[:, :128] = din[:, :128].astype(BF)
    out_ref[:, 128:256] = jnp.where(left, din[:, 128:256], pltpu.roll(dz2, 64, 1)).astype(BF)
    out_ref[:, 256:384] = dz01.astype(BF)
    out_ref[:, 384:] = din[:, 256:].astype(BF)

    @pl.when(step == pl.num_programs(0) - 1)
    def _():
        dstate_out[...] = dstate[...]
        dext_out[...] = dext[pl.ds(0, 8), :]


def scan_back(part, carry, before, bounds, xbc, z, y, dt_raw, states, dn, taps, bias, head, skip, gain):
    full = xbc.shape[0]
    n = full // CHUNK
    half = n // 2
    last = n - 1 if part == 0 else half - 1
    row = lambda width: pl.BlockSpec((CHUNK, width), lambda i, *_: (last - i, 0))
    tall = CHUNK // 16
    per = n // 8
    sent = lambda col: pl.BlockSpec(
        (1, CHUNK, 128), lambda i, b: ((last - i) // per, (last - i) % per, col)
    )

    def terms(i, b):
        piece, rest = (last - i) // per, (last - i) % per
        each = ROW_BLOCK // CHUNK
        return piece, per * (CHUNK // 16) + rest // each, rest % each

    carried = [whole((256, 128)), whole((8, 512)), whole((8, 512)), whole((16, CHUNK))]
    sds = jax.ShapeDtypeStruct
    args = [bounds, xbc, xbc, z, y, dt_raw, states, dn, dn, dn, taps, bias, head, skip, gain]
    args += list(carry) + list(before)
    alias = {len(args) - 2: 0, len(args) - 1: 1} if before else {}
    return pl.pallas_call(
        functools.partial(scan_back_body, last),
        grid_spec=pltpu.PrefetchScalarGridSpec(
            num_scalar_prefetch=1,
            grid=(half,),
            in_specs=[
                row(512),
                pl.BlockSpec((16, 512), lambda i, *_: (jnp.maximum((last - i) * tall - 1, 0), 0)),
                row(256),
                row(256),
                pl.BlockSpec((8, CHUNK), lambda i, *_: (0, last - i)),
                pl.BlockSpec((1, 256, 128), lambda i, *_: (last - i, 0, 0)),
                sent(0),
                sent(1),
                pl.BlockSpec((1, 16, CHUNK), terms),
                whole((8, 512)),
                whole((1, 512)),
                whole((8, 128)),
                whole((1, 256)),
                whole((1, 256)),
            ]
            + carried
            + [pl.BlockSpec(memory_space=pl.ANY)] * len(before),
            out_specs=[
                row(640),
                pl.BlockSpec((8, CHUNK), lambda i, *_: (0, last - i)),
                whole((8, 512)),
                whole((16, CHUNK)),
                whole((256, 128)),
                whole((8, 512)),
            ],
            scratch_shapes=[
                pltpu.VMEM((CHUNK + 8, 512), F32),
                pltpu.VMEM((CHUNK + 8, 512), F32),
                pltpu.VMEM((256, 128), F32),
            ],
        ),
        out_shape=[
            sds((full, 640), BF),
            sds((8, full), F32),
            sds((8, 512), F32),
            sds((16, CHUNK), F32),
            sds((256, 128), F32),
            sds((8, 512), F32),
        ],
        input_output_aliases=alias,
        compiler_params=params(),
        cost_estimate=SMALL_COST,
        name="scan_back",
    )(*args)


ROW_BLOCK = 256


def row_body(bounds, g, h, tok, gout, mlp_gain, gains, *refs):
    packs, refs = refs[:10], refs[10:]
    pa, pb, slots = [], [], []
    for k, base in enumerate((0, 5)):
        for r in range(4):
            first = packs[base + r]
            second = first.at[:, 512:] if r < 3 else packs[base + 4]
            pa.append(first.at[:, 0:512])
            pb.append(second)
            slots.append((bounds[3] ^ k) * 4 + (bounds[2] ^ r))
    gain_rows = [gains[slot] for slot in slots]
    out_ref, two_ref, dmix_ref, dhid_ref = refs[0:4]
    act_refs, dgu_refs, gn_refs = refs[4:6], refs[6:8], refs[8:10]
    dn, mlp_acc, gain_acc = refs[10:13]
    step = pl.program_id(0)
    left = lanes((1, 128)) < 64
    width = 1536.0

    @pl.when(pl.program_id(0) == 0)
    def _():
        mlp_acc[...] = jnp.zeros_like(mlp_acc)
        gain_acc[...] = jnp.zeros_like(gain_acc)

    pieces = [(r, k) for k in range(2) for r in range(4)]

    def part(ref, s):
        return ref[slots[s]].astype(F32)

    squares = 0.0
    for s in range(8):
        first, second = part(g, s), part(h, s)
        squares = squares + first * first + jnp.where(left, second * second, 0.0)
    rg = lax.rsqrt(jnp.sum(squares, axis=1, keepdims=True) / width + EPSILON)
    mixed = 0.0
    for s, (r, k) in enumerate(pieces):
        gain = gain_rows[s]
        first = part(g, s) * rg * gain[:, :128]
        second = part(h, s)
        second = jnp.where(left, second * rg * gain[:, 128:], second)
        gn = jnp.concatenate([first.astype(BF), second.astype(BF)], axis=1)
        gn_refs[k][:, r * 256 : r * 256 + 256] = gn
        mixed = mixed + dot_bt(gn, pb[s][:, 256:])
    hidden = tok[...].astype(F32) + mixed
    scale = lax.rsqrt(jnp.mean(hidden * hidden, axis=-1, keepdims=True) + EPSILON)
    two = (hidden * scale * mlp_gain[...]).astype(BF)
    two_ref[...] = two
    grad = gout[...]
    ffn = 0.0
    dtwo = 0.0
    for s, (r, k) in enumerate(pieces):
        weight, down = pa[s][...], pb[s][:, :256]
        gu = dot(two, weight)
        gate, up = gu[:, :256], gu[:, 256:]
        sig = jax.nn.sigmoid(gate)
        silu = gate * sig
        act = (silu * up).astype(BF)
        act_refs[k][:, r * 256 : r * 256 + 256] = act
        ffn = ffn + dot_bt(act, down)
        dact = dot(grad, down)
        dgate = (dact * up * (sig + silu * (1.0 - sig))).astype(BF)
        dgu = jnp.concatenate([dgate, (dact * silu).astype(BF)], axis=1)
        dgu_refs[k][:, r * 512 : r * 512 + 512] = dgu
        dtwo = dtwo + dot_bt(dgu, weight)
    out_ref[...] = (hidden + ffn).astype(BF)
    weighted = dtwo * mlp_gain[...]
    mlp_acc[...] += jnp.sum(dtwo * (hidden * scale), axis=0, keepdims=True)
    mean = jnp.mean(weighted * hidden, axis=-1, keepdims=True)
    dhid = grad.astype(F32) + scale * weighted - hidden * (scale * scale * scale * mean)
    dhid_ref[...] = dhid
    dmix = dhid.astype(BF)
    dmix_ref[...] = dmix
    cross = 0.0
    for s, (r, k) in enumerate(pieces):
        dgn = dot(dmix, pb[s][:, 256:]).astype(BF)
        dn[slots[s], pl.ds(pl.multiple_of(step * ROW_BLOCK, ROW_BLOCK), ROW_BLOCK), :] = dgn
        first, second = dgn[:, :128].astype(F32), dgn[:, 128:].astype(F32)
        gain = gain_rows[s]
        own1, own2 = part(g, s), jnp.where(left, part(h, s), 0.0)
        t1, t2 = first * own1, second * own2
        gain_acc[slots[s], :, :128] += jnp.sum(t1 * rg, axis=0, keepdims=True)
        gain_acc[slots[s], :, 128:] += jnp.sum(t2 * rg, axis=0, keepdims=True)
        cross = cross + t1 * gain[:, :128] + t2 * gain[:, 128:]
    cross = jnp.sum(cross, axis=1, keepdims=True) * (rg * rg * rg / width)
    lane = lanes((1, 128))
    tile = jnp.where(lane == 0, rg, jnp.where(lane == 1, cross, 0.0))
    pair = tile.T[0:2, :]
    high = pair.astype(BF)
    rest = pair - high.astype(F32)
    middle = rest.astype(BF)
    low = (rest - middle.astype(F32)).astype(BF)
    block = jnp.concatenate(
        [v.astype(F32) for v in (high, middle, low)] + [jnp.zeros((10, ROW_BLOCK), F32)], axis=0
    ).astype(BF)
    for s in range(8):
        dn[s, pl.ds(pl.multiple_of(2 * ROW_BLOCK + step * 16, 16), 16), :] = block


def row_stage(bounds, g, h, tokens, gout, mlp_gain, gains, packs):
    n = ROW_BLOCK
    count = 2 * n
    row = lambda w: pl.BlockSpec((n, w), lambda i, b: (i, 0))
    part = pl.BlockSpec((n, 1024), lambda i, b: (2 * b[2] + i, 0))
    piece = pl.BlockSpec((8, n, 128), lambda i, b: (0, i, 0))
    once = lambda shape: pl.BlockSpec(
        shape, lambda i, b: (0,) * len(shape), pipeline_mode=pl.Buffered(1)
    )
    sds = jax.ShapeDtypeStruct
    widths = [1024] * 4 + [1024] * 2 + [2048] * 2 + [1024] * 2
    dtypes = [BF] * 3 + [F32] + [BF] * 6
    return pl.pallas_call(
        row_body,
        grid_spec=pltpu.PrefetchScalarGridSpec(
            num_scalar_prefetch=1,
            grid=(2,),
            in_specs=[piece, piece, part, part, whole((1, 1024)), whole((8, 1, 256))]
            + [once(p.shape) for p in packs],
            out_specs=[row(w) for w in widths]
            + [once((8, count + 32, 256)), whole((1, 1024)), whole((8, 1, 256))],
        ),
        out_shape=[sds((count, w), d) for w, d in zip(widths, dtypes)]
        + [sds((8, count + 32, 256), BF), sds((1, 1024), F32), sds((8, 1, 256), F32)],
        compiler_params=pltpu.CompilerParams(vmem_limit_bytes=58 * 1024 * 1024),
        cost_estimate=SMALL_COST,
        name="row_stage",
    )(bounds, g, h, tokens, gout, mlp_gain, gains, *packs)


def weight_body(two, gout, dmix, dgu, act, gn, *refs):
    a = dot_at(two[...], dgu[...])
    b = jnp.concatenate([dot_at(gout[...], act[...]), dot_at(dmix[...], gn[...])], axis=1)
    if len(refs) == 2:
        refs[0][0] = a.astype(BF)
        refs[1][0] = b.astype(BF)
    else:
        a = (a + refs[0][0].astype(F32)).astype(BF)
        b = (b + refs[1][0].astype(F32)).astype(BF)
        for i in range(4):

            @pl.when(pl.program_id(0) == i)
            def _(i=i):
                refs[2 + i][...] = a
                refs[6 + i][...] = b


def weight_stage(two, gout, dmix, dgu, act, gn, *others):
    count = two.shape[0]
    col = lambda w: pl.BlockSpec((count, w), lambda i: (0, i))
    piece = pl.BlockSpec((1, 1024, 512), lambda i: (i, 0, 0))
    once = pl.BlockSpec((1024, 512), lambda i: (0, 0), pipeline_mode=pl.Buffered(1))
    sds = jax.ShapeDtypeStruct
    return pl.pallas_call(
        weight_body,
        grid=(4,),
        in_specs=[whole((count, 1024))] * 3
        + [col(512), col(256), col(256)]
        + [piece] * len(others),
        out_specs=[once] * 8 if others else [piece] * 2,
        out_shape=[sds((1024, 512), BF)] * 8 if others else [sds((4, 1024, 512), BF)] * 2,
        compiler_params=pltpu.CompilerParams(vmem_limit_bytes=FULL_VMEM),
        cost_estimate=SMALL_COST,
        name="weight_stage",
    )(two, gout, dmix, dgu, act, gn, *others)


def with_steps(da, dt_grad):
    count = da.shape[0]
    cols = jnp.concatenate([dt_grad, jnp.zeros((120, count), F32)], axis=0).T
    last = jnp.where(lanes((1, 128)) < 64, da[:, 256:].astype(F32), pltpu.roll(cols, 64, 1))
    return jnp.concatenate([da[:, :256], last.astype(BF)], axis=1)


def input_grad_body(off, da, ds, dt_grad, weight, normed, out_ref, gain_ref):
    left = with_steps(da[...], dt_grad[...])
    grad = dot_bt(left, weight[:, :384]) + dot_bt(ds[...], weight[:, 384:])
    out_ref[...] = grad.astype(BF)

    @pl.when(pl.program_id(0) == 0)
    def _():
        gain_ref[...] = jnp.zeros_like(gain_ref)

    gain_ref[...] += jnp.sum(grad * normed[...].astype(F32), axis=0, keepdims=True)


def input_grad(off, da, ds, dt_grad, weight, normed):
    n = PROJ_ROWS
    own = ds.shape[0] // 2
    at = lambda i, off: (off[0] + i, 0)
    return pl.pallas_call(
        input_grad_body,
        grid_spec=pltpu.PrefetchScalarGridSpec(
            num_scalar_prefetch=1,
            grid=(own // n,),
            in_specs=[
                pl.BlockSpec((n, 384), at),
                pl.BlockSpec((n, 640), at),
                pl.BlockSpec((8, n), lambda i, off: (0, off[0] + i)),
                whole((1024, 1024)),
                pl.BlockSpec((n, 1024), at),
            ],
            out_specs=[pl.BlockSpec((n, 1024), lambda i, off: (i, 0)), whole((1, 1024))],
        ),
        out_shape=[
            jax.ShapeDtypeStruct((own, 1024), BF),
            jax.ShapeDtypeStruct((1, 1024), F32),
        ],
        compiler_params=params(),
        cost_estimate=SMALL_COST,
        name="input_grad",
    )(off, da, ds, dt_grad, weight, normed)


def turned_back(value):
    low = lanes((1, 128)) % 64 < 32
    return jnp.where(low, pltpu.roll(value, 96, 1), -pltpu.roll(value, 32, 1))


def shared_grad_body(bounds, normed, da, ds1, ds2, turned, shared, acc):
    @pl.when(pl.program_id(0) == 0)
    def _():
        acc[...] = jnp.zeros_like(acc)

    cols = jnp.concatenate([da[...], ds1[...], ds2[...]], axis=1)
    acc[...] += dot_at(normed[...], cols)

    @pl.when(pl.program_id(0) == pl.num_programs(0) - 1)
    def _():
        left = lanes((1, 128)) < 64
        kv = acc[:, :128] + jnp.where(left, turned_back(turned[...]), 0.0)
        low = bounds[2] // 2 == 0
        swapped = pltpu.roll(kv, 64, 1)
        keys = jnp.where(left == low, jnp.where(low, kv, swapped), 0.0)
        values = jnp.where(left == low, jnp.where(low, swapped, kv), 0.0)
        shared[:, :128] = keys.astype(BF)
        shared[:, 128:256] = values.astype(BF)
        shared[:, 256:] = acc[:, 128:].astype(BF)


def shared_grad(bounds, normed, da, ds, turned):
    full = normed.shape[0]
    n = 512
    part = lambda w, col: pl.BlockSpec((n, w), lambda i, *_: (i, col))
    return pl.pallas_call(
        shared_grad_body,
        grid_spec=pltpu.PrefetchScalarGridSpec(
            num_scalar_prefetch=1,
            grid=(full // n,),
            in_specs=[part(1024, 0), part(128, 0), part(128, 3), part(128, 4)]
            + [whole((1024, 128))],
            out_specs=whole((1024, 512)),
            scratch_shapes=[pltpu.VMEM((1024, 384), F32)],
        ),
        out_shape=jax.ShapeDtypeStruct((1024, 512), BF),
        compiler_params=params(),
        cost_estimate=SMALL_COST,
        name="shared_grad",
    )(bounds, normed, da, ds, ds, turned)


def alone_grad_body(normed, da1, da2, ds, dt_grad, alone, turned, acc):
    @pl.when(pl.program_id(0) == 0)
    def _():
        acc[...] = jnp.zeros_like(acc)

    count = da1.shape[0]
    cols = jnp.concatenate([dt_grad[...], jnp.zeros((120, count), F32)], axis=0).T
    last = jnp.where(lanes((1, 128)) < 64, da2[...].astype(F32), pltpu.roll(cols, 64, 1))
    acc[...] += dot_at(
        normed[...], jnp.concatenate([last.astype(BF), ds[...], da1[...]], axis=1)
    )

    @pl.when(pl.program_id(0) == pl.num_programs(0) - 1)
    def _():
        left = lanes((1, 128)) < 64
        side = acc[:, 512:]
        turned[...] = side
        query = jnp.where(left, pltpu.roll(turned_back(side), 64, 1), 0.0)
        alone[:, :128] = (acc[:, :128] + query).astype(BF)
        alone[:, 128:] = acc[:, 128:512].astype(BF)


def alone_grad(normed, da, ds, dt_grad):
    full = normed.shape[0]
    n = 512
    part = lambda w, col: pl.BlockSpec((n, w), lambda i: (i, col))
    return pl.pallas_call(
        alone_grad_body,
        grid=(full // n,),
        in_specs=[
            part(1024, 0),
            part(128, 1),
            part(128, 2),
            part(384, 0),
            pl.BlockSpec((8, n), lambda i: (0, i)),
        ],
        out_specs=[whole((1024, 512)), whole((1024, 128))],
        scratch_shapes=[pltpu.VMEM((1024, 640), F32)],
        out_shape=[
            jax.ShapeDtypeStruct((1024, 512), BF),
            jax.ShapeDtypeStruct((1024, 128), F32),
        ],
        compiler_params=params(),
        cost_estimate=SMALL_COST,
        name="alone_grad",
    )(normed, da, da, ds, dt_grad)


def assemble_body(bounds, p0, p1, p2, l3, r3, out):
    step = pl.program_id(0)
    for r, ref in enumerate((p0, p1, p2)):

        @pl.when(step == r)
        def _(ref=ref):
            out[...] = ref[...]

    @pl.when(step == 3)
    def _():
        out[:, :512] = l3[...]
        out[:, 512:] = r3[...]


def assemble(bounds, parts):
    count = parts[0].shape[0]
    return pl.pallas_call(
        assemble_body,
        grid_spec=pltpu.PrefetchScalarGridSpec(
            num_scalar_prefetch=1,
            grid=(4,),
            in_specs=[whole(p.shape) for p in parts],
            out_specs=pl.BlockSpec((count, 1024), lambda i, b: (i ^ b[2], 0)),
        ),
        out_shape=jax.ShapeDtypeStruct((4 * count, 1024), parts[0].dtype),
        compiler_params=params(),
        cost_estimate=SMALL_COST,
        name="assemble",
    )(bounds, *parts)


def piece_out_body(bounds, a, b, other_a, other_b, gate, up, down, mix, att):
    first = bounds[3] == 0

    def pair(own, other):
        own, other = own.astype(F32), other.astype(F32)
        return jnp.where(first, own, other), jnp.where(first, other, own)

    low, high = pair(a[...], other_a[...])
    gate[:, :256], gate[:, 256:] = low[:, :256], high[:, :256]
    up[:, :256], up[:, 256:] = low[:, 256:], high[:, 256:]
    low, high = pair(b[...], other_b[...])
    down[:256, :], down[256:, :] = low[:, :256].T, high[:, :256].T
    low, high = low[:, 256:].T, high[:, 256:].T
    mix[:192, :], mix[192:, :] = low[:192], high[:192]
    att[:64, :], att[64:, :] = low[192:], high[192:]


def piece_out(bounds, a, b, other):
    n = 256
    row = pl.BlockSpec((n, 512), lambda i, *_: (i, 0))
    second = pl.BlockSpec((n, 512), lambda i, *_: (i, 1))
    col = lambda h: pl.BlockSpec((h, n), lambda i, *_: (0, i))
    sds = jax.ShapeDtypeStruct
    return pl.pallas_call(
        piece_out_body,
        grid_spec=pltpu.PrefetchScalarGridSpec(
            num_scalar_prefetch=1,
            grid=(4,),
            in_specs=[row, row, row, second],
            out_specs=[row, row, col(512), col(384), col(128)],
        ),
        out_shape=[
            sds((1024, 512), F32),
            sds((1024, 512), F32),
            sds((512, 1024), F32),
            sds((384, 1024), F32),
            sds((128, 1024), F32),
        ],
        compiler_params=params(),
        cost_estimate=SMALL_COST,
        name="piece_out",
    )(bounds, a, b, other, other)


def alone_out_body(bounds, own, other, q, z, x, dt):
    first = bounds[3] == 0
    lane = lanes((1, 128))
    left = lane < 64
    tile = lambda ref, i: ref[:, 128 * i : 128 * i + 128].astype(F32)
    u = [jnp.where(first, tile(own, i), tile(other, i)) for i in range(4)]
    v = [jnp.where(first, tile(other, i), tile(own, i)) for i in range(4)]
    swapped = lambda value: pltpu.roll(value, 64, 1)
    q[...] = jnp.where(left, u[0], swapped(v[0]))
    x[:, :128] = u[1]
    x[:, 128:256] = jnp.where(left, u[2], swapped(v[1]))
    x[:, 256:] = jnp.where(left, swapped(v[1]), swapped(v[2]))
    z[:, :128] = u[3]
    z[:, 128:256] = jnp.where(left, swapped(u[2]), swapped(v[3]))
    z[:, 256:] = jnp.where(left, swapped(v[3]), v[2])
    dt[...] = jnp.where(lane < 3, swapped(u[0]), pltpu.roll(v[0], 67, 1))[:, :6]


def alone_out(bounds, own, other):
    n = 256
    row = lambda w: pl.BlockSpec((n, w), lambda i, *_: (i, 0))
    widths = [128, 384, 384, 6]
    return pl.pallas_call(
        alone_out_body,
        grid_spec=pltpu.PrefetchScalarGridSpec(
            num_scalar_prefetch=1,
            grid=(4,),
            in_specs=[row(512), row(512)],
            out_specs=[row(w) for w in widths],
        ),
        out_shape=[jax.ShapeDtypeStruct((1024, w), F32) for w in widths],
        compiler_params=params(),
        cost_estimate=SMALL_COST,
        name="alone_out",
    )(bounds, own, other)


def swap(value, step):
    return lax.ppermute(value, "tensor", [(i, i ^ step) for i in range(4)])


def twin(value):
    return lax.ppermute(value, "ctx", [(0, 1), (1, 0)])


def exchange(value):
    return lax.all_to_all(value, ("ctx", "tensor"), 0, 0, tiled=True)


def dp_swap(value, step):
    return lax.ppermute(value, "dp", [(i, i ^ step) for i in range(4)])


MIDDLE = [(1, 2), (2, 1), (0, 3), (3, 0)]
NEAR = [(0, 1), (1, 0), (2, 3), (3, 2)]


class DpSum:
    def __init__(self, value):
        self.four = lax.axis_size("dp") == 4
        place = lax.axis_index("dp")
        self.inner = (place == 1) | (place == 2)
        half = value.shape[0] // 2
        first, second = value[:half], value[half:]
        if self.four:
            self.kept = jnp.where(self.inner, first, second)
            self.out = jnp.where(self.inner, second, first)
        else:
            self.kept = self.out = value

    def first(self, sent):
        return lax.ppermute(sent, "dp", NEAR) if self.four else lax.psum(sent, "dp")

    def middle(self, sent):
        return lax.ppermute(sent, "dp", MIDDLE) if self.four else sent

    def last(self, sent):
        return lax.ppermute(sent, "dp", NEAR) if self.four else sent

    def add(self, kept, got):
        return plus(kept, got) if self.four else got

    def end(self, kept, got):
        if not self.four:
            return got
        return jnp.concatenate(
            [jnp.where(self.inner, kept, got), jnp.where(self.inner, got, kept)], axis=0
        )


def together(*values):
    return lax.optimization_barrier(values)


def after(value, *before):
    return lax.optimization_barrier((value, before))[0]


def plus(a, b):
    return (a.astype(F32) + b.astype(F32)).astype(BF)


def block_at(value, index, count):
    return lax.dynamic_slice_in_dim(value, index * count, count, 0)


def merge_body(bounds, own, got, *outs):
    total = (own[...].astype(F32) + got[...].astype(F32)).astype(BF)
    for i in range(4):

        @pl.when(pl.program_id(0) == i)
        def _(i=i):
            outs[2 * i][...] = total[:, :512]
            outs[2 * i + 1][...] = total[:, 512:]


def merge(bounds, own, got):
    count = own.shape[0] // 4
    block = pl.BlockSpec((count, 1024), lambda i, b: (i ^ b[2], 0))
    once = pl.BlockSpec((count, 512), lambda i, b: (0, 0), pipeline_mode=pl.Buffered(1))
    return pl.pallas_call(
        merge_body,
        grid_spec=pltpu.PrefetchScalarGridSpec(
            num_scalar_prefetch=1,
            grid=(4,),
            in_specs=[block, block],
            out_specs=[once] * 8,
        ),
        out_shape=[jax.ShapeDtypeStruct((count, 512), BF)] * 8,
        compiler_params=params(),
        cost_estimate=SMALL_COST,
        name="merge",
    )(bounds, own, got)


def finish_body(bounds, l0, r0, l1, r1, l2, r2, tok, dhid, gain, out):
    total = lambda a, b, c: (a[...].astype(F32) + b[...]) + c[...]
    grad = jnp.concatenate([total(l0, l1, l2), total(r0, r1, r2)], axis=1)
    values = tok[...].astype(F32)
    scale = lax.rsqrt(jnp.mean(values * values, axis=-1, keepdims=True) + EPSILON)
    weighted = grad * gain[...]
    mean = jnp.mean(weighted * values, axis=-1, keepdims=True)
    out[...] = (dhid[...] + scale * weighted - values * (scale * scale * scale * mean)).astype(BF)


def finish(bounds, state, tokens, dhid, gain):
    count = dhid.shape[0]
    n = count // 2
    half = pl.BlockSpec((n, 512), lambda i, b: (i, 0))
    row = pl.BlockSpec((n, 1024), lambda i, b: (i, 0))
    return pl.pallas_call(
        finish_body,
        grid_spec=pltpu.PrefetchScalarGridSpec(
            num_scalar_prefetch=1,
            grid=(2,),
            in_specs=[half] * 6
            + [pl.BlockSpec((n, 1024), lambda i, b: (2 * b[2] + i, 0)), row, whole((1, 1024))],
            out_specs=row,
        ),
        out_shape=jax.ShapeDtypeStruct((count, 1024), BF),
        compiler_params=params(),
        cost_estimate=SMALL_COST,
        name="finish",
    )(bounds, *state, tokens, dhid, gain)


def rope_tables(count):
    exponent = np.arange(0, HEAD_SIZE, 2).astype(np.float32) / np.float32(HEAD_SIZE)
    frequency = (np.float32(ROPE_BASE) ** (-exponent)).astype(np.float32)
    angles = np.arange(count).astype(np.float32)[:, None] * frequency[None, :]
    angles = np.concatenate([angles] * 4, axis=1)
    return (np.cos(angles).astype(np.float32), np.sin(angles).astype(np.float32))


def local(
    tokens, doc_ids, norm_gain, q_proj, key_value_weight, o_proj, z_proj, x_proj, dt_proj,
    bc_proj, conv_x, xconv_bias, conv_bc, bcconv_bias, dt_bias, a_log, skip_gain, gated_gain,
    out_proj, mlp_gain, gate_proj, up_proj, down_proj, out_grad,
):
    t, c = lax.axis_index("tensor"), lax.axis_index("ctx")
    own_tokens, grad_out = tokens[0], out_grad[0]
    own = own_tokens.shape[0]
    full = 2 * own
    mine = own // 4
    other_tokens = twin(own_tokens)

    def cols(w):
        n = w.shape[-1] // 2
        return lax.dynamic_slice_in_dim(w, c * n, n, w.ndim - 1)

    def rows(w):
        return block_at(w, c, w.shape[0] // 2)

    docs = doc_ids[0]
    bounds = jnp.stack([jnp.sum(docs < 1), jnp.sum(docs < 2), t, c]).astype(jnp.int32)
    own_gain = rows(gated_gain)
    gain0 = jnp.concatenate([own_gain, jnp.ones((64,), F32)])
    gains = exchange(jnp.broadcast_to(gain0[None, None], (8, 1, 256)))
    weight, pack0 = prepare(
        bounds, gate_proj, up_proj, down_proj, out_proj, o_proj, key_value_weight, q_proj,
        x_proj, z_proj, dt_proj, bc_proj,
    )
    weight, pack0, gains = together(weight, pack0, gains)
    pack1, pack2 = swap(pack0, 1), swap(pack0, 2)
    cos, sin = rope_tables(full)
    cos, sin = jnp.asarray(cos), jnp.asarray(sin)
    steps = own // PROJ_ROWS
    own_off = jnp.reshape(c * steps, (1,)).astype(jnp.int32)
    other_off = jnp.reshape((1 - c) * steps, (1,)).astype(jnp.int32)
    gain_row = norm_gain[None]
    first = project(own_off, own_tokens, gain_row, weight, cos, sin)
    normed, qp, kv, xbc, z, dt_raw = project(
        other_off, other_tokens, gain_row, weight, cos, sin, before=first
    )

    pad = lambda v: jnp.zeros(v.shape[:-1] + (64,), F32)
    cx, cb = cols(conv_x), cols(xconv_bias)
    taps = jnp.concatenate([cx, pad(cx), conv_bc], axis=1)
    taps = jnp.concatenate([taps, jnp.zeros_like(taps)], axis=0)
    bias = jnp.concatenate([cb, pad(cb), bcconv_bias])[None]
    head = jnp.stack([cols(dt_bias), -jnp.exp(cols(a_log))], axis=1)
    head = jnp.pad(head, ((0, 5), (0, 126)))
    skip = jnp.pad(jnp.repeat(cols(skip_gain), MP), (0, 64))[None]
    g01, g2, y, states = scan_forward(bounds, xbc, z, dt_raw, taps, bias, head, skip)
    g2, g01, pack1, pack2 = together(g2, g01, pack1, pack2)
    left3, right3 = pack1[:, :512], pack2[:, 512:]
    qp, left3, right3, g01 = together(qp, left3, right3, g01)
    left3, right3 = swap(left3, 2), swap(right3, 1)
    near = [pack0, pack1, pack2]
    far = [twin(v) for v in near]
    g_rows = exchange(g01.reshape(8, mine, 128))
    tile, keep = attend(bounds, qp, kv, g2)
    tile, g_rows, far, left3, right3 = together(tile, g_rows, far, left3, right3)
    h_rows = exchange(tile.reshape(8, mine, 128))
    packs = near + [left3, right3] + far + [twin(left3), twin(right3)]

    res = row_stage(bounds, g_rows, h_rows, own_tokens, grad_out, mlp_gain[None], gains, packs)
    layer_rows, two, dmix, dhid = res[0:4]
    act, dgu, gn = list(res[4:6]), list(res[6:8]), list(res[8:10])
    mlp_part, gain_part = res[11:13]
    grad_rows = block_at(grad_out, t, mine)
    dn = exchange(res[10])
    far_w = weight_stage(two, grad_rows, dmix, dgu[1], act[1], gn[1])
    far_w = [twin(v) for v in far_w]
    near_w = weight_stage(two, grad_rows, dmix, dgu[0], act[0], gn[0], *far_w)
    dn, near_w = together(dn, near_w)
    sum_a, sum_b = near_w[:4], near_w[4:]

    a3, b3 = swap(sum_a[3], 1), swap(sum_b[3], 2)
    a1, b2 = swap(sum_a[1], 1), swap(sum_b[2], 2)
    da = attend_back(bounds, qp, kv, keep, dn, cos, sin)
    da, a3, b3 = together(da, a3, b3)
    a_next, b_next = plus(sum_a[2], a3), plus(sum_b[1], b3)
    xbc, a_next, b_next = together(xbc, a_next, b_next)
    a_next, b_next = swap(a_next, 2), swap(b_next, 1)
    own_gain_row = jnp.pad(own_gain, (0, 64))[None]
    zeros = [
        jnp.zeros((256, 128), F32),
        jnp.zeros((8, 512), F32),
        jnp.zeros((8, 512), F32),
        jnp.zeros((16, CHUNK), F32),
    ]
    back = lambda part, carry, made, data: scan_back(
        part, carry, made, bounds, data, z, y, dt_raw, states, dn, taps, bias, head, skip, own_gain_row
    )
    ds, dt_grad, *carry = back(0, zeros, [], xbc)
    ds, a1, b2, a_next, b_next = together(ds, a1, b2, a_next, b_next)
    add3 = lambda a, b, d: (a.astype(F32) + b.astype(F32) + d.astype(F32)).astype(BF)
    sums = [DpSum(add3(sum_a[0], a1, a_next)), DpSum(add3(sum_b[0], b2, b_next))]
    out = jnp.concatenate([v.out for v in sums], axis=1)
    kept = [v.kept for v in sums]
    half = kept[0].shape[1]
    xbc, out, kept, layer_rows = together(xbc, out, kept, layer_rows)
    got = sums[0].first(out)
    layer1, layer2 = swap(layer_rows, 1), swap(layer_rows, 2)
    conv_carry = (carry[2], carry[3], carry[0], carry[1])
    ds, dt_grad, conv_acc, head_acc, _, _ = back(1, conv_carry, [ds, dt_grad], xbc)
    ds, got, layer1, layer2 = together(ds, got, layer1, layer2)

    kept = [sums[0].add(kept[0], got[:, :half]), sums[1].add(kept[1], got[:, half:])]
    rest = kept[0].shape[0] // 2
    parts = [(v[:rest], v[rest:]) for v in kept]
    layer3 = [layer1[:, :512], layer2[:, 512:]]
    ds, layer3, parts, kept = together(ds, layer3, parts, kept)
    got_a0 = sums[0].middle(parts[0][0])
    layer3 = [swap(layer3[0], 2), swap(layer3[1], 1)]
    grad_other, gain_other = input_grad(other_off, da, ds, dt_grad, weight, normed)
    grad_other, ds, layer3, got_a0 = together(grad_other, ds, layer3, got_a0)
    sent = twin(grad_other)
    got_a1 = sums[0].middle(parts[0][1])
    grad_own, gain_own = input_grad(own_off, da, ds, dt_grad, weight, normed)
    grad_own, sent, got_a1 = together(grad_own, sent, got_a1)
    kept[0] = sums[0].add(kept[0], jnp.concatenate([got_a0, got_a1]))
    grad_own, sent, kept = together(grad_own, sent, kept)
    got_b0 = sums[1].middle(parts[1][0])
    pieces = merge(bounds, grad_own, sent)
    ds, got_b0, pieces = together(ds, got_b0, pieces)
    l0, r0, l1, r1, l2, r2, l3, r3 = pieces
    heads = jnp.concatenate(
        [
            jnp.sum(conv_acc[5, :192].reshape(3, 64), axis=1),
            jnp.sum(head_acc[0:3], axis=1),
            jnp.sum(head_acc[8:11], axis=1),
        ]
    )
    place = c * 4 + t
    own_small = jnp.pad(jnp.concatenate([conv_acc[:5, :192].reshape(-1), heads]), (0, 55))
    at_own = lax.dynamic_update_slice_in_dim(
        jnp.zeros((8, 1024), F32), own_small[None], place, 0
    )
    norm_part = (gain_other[0] + gain_own[0]) / norm_gain
    flat = jnp.concatenate(
        [at_own.reshape(-1), gain_part.reshape(-1), conv_acc[:5, 256:].reshape(-1), mlp_part[0]]
        + [norm_part]
    )
    flat = jnp.pad(flat, (0, (-flat.shape[0]) % 1024)).reshape(1, -1, 128)
    flat = jnp.broadcast_to(flat, (8,) + flat.shape[1:])
    ds, l0, r0, l1, r1, l2, r2, l3, r3, flat, kept = together(
        ds, l0, r0, l1, r1, l2, r2, l3, r3, flat, kept
    )
    l3, r3 = swap(l3, 1), swap(r3, 2)
    got_b1 = sums[1].middle(parts[1][1])
    got_a = sums[0].last(kept[0])
    flat = exchange(flat)
    alone, turned = alone_grad(normed, da, ds, dt_grad)
    alone, turned, l3, r3, got_b1, got_a, flat = together(
        alone, turned, l3, r3, got_b1, got_a, flat
    )
    l2, r1 = plus(l2, l3), plus(r1, r3)
    flat = jnp.sum(flat, axis=0)
    kept[1] = sums[1].add(kept[1], jnp.concatenate([got_b0, got_b1]))
    single = DpSum(alone)
    out, alone = single.out, single.kept
    count = out.shape[0]
    out = jnp.concatenate([out, kept[1]])
    turned, l1, r2, l2, r1, flat, out, alone, kept = together(
        turned, l1, r2, l2, r1, flat, out, alone, kept
    )
    l2, r1 = swap(l2, 2), swap(r1, 1)
    l1, r2 = swap(l1, 1), swap(r2, 2)
    got = single.first(out)
    shared = shared_grad(bounds, normed, da, ds, turned)
    shared, l1, r2, l2, r1, got = together(shared, l1, r2, l2, r1, got)
    state = [l0, r0, l1, r1, l2, r2]
    token_rows = finish(bounds, state, own_tokens, dhid, norm_gain[None])
    alone = single.add(alone, got[:count])
    reduced = [sums[0].end(kept[0], got_a), sums[1].end(kept[1], got[count:])]
    both = jnp.concatenate(reduced, axis=1)
    layer_rows, layer1, layer2, layer3, token_rows, alone, reduced, both, flat, shared = together(
        layer_rows, layer1, layer2, layer3, token_rows, alone, reduced, both, flat, shared
    )
    four = lax.axis_size("dp") == 4
    tok1, tok2 = swap(token_rows, 1), swap(token_rows, 2)
    got = single.middle(alone)
    twin_piece = twin(both)
    flat_got = dp_swap(flat, 1) if four else lax.psum(flat, "dp")
    shared = exchange(shared.reshape(8, 128, 512))
    layer_out = assemble(bounds, [layer_rows, layer1, layer2, *layer3])
    tok1, tok2, got, flat_got, layer_out, twin_piece, shared = together(
        tok1, tok2, got, flat_got, layer_out, twin_piece, shared
    )
    flat = flat + flat_got if four else flat_got
    alone = single.add(alone, got)
    tok3 = [tok1[:, :512], tok2[:, 512:]]
    shared = jnp.sum(shared.astype(F32), axis=0).astype(BF)
    if four:
        shared = jnp.broadcast_to(shared[None], (4, 128, 512))
    tok3, alone, flat, reduced, twin_piece, shared = together(
        tok3, alone, flat, reduced, twin_piece, shared
    )
    tok3 = [swap(tok3[0], 2), swap(tok3[1], 1)]
    got = single.last(alone)
    flat_got = dp_swap(flat, 2) if four else flat
    if four:
        shared = lax.all_to_all(shared, "dp", 0, 0, tiled=True)
    else:
        shared = lax.psum(shared.astype(F32), "dp")
    outs = piece_out(bounds, reduced[0], reduced[1], twin_piece)
    tok3, got, flat_got, outs, shared = together(tok3, got, flat_got, outs, shared)
    if four:
        shared = jnp.sum(shared.astype(F32), axis=0)
    shared = jnp.broadcast_to(shared.astype(BF)[None], (8, 128, 512))
    alone = single.end(alone, got)
    alone, shared, tok3 = together(alone, shared, tok3)
    alone_twin = twin(alone)
    shared = exchange(shared)
    tokens_grad = assemble(bounds, [token_rows, tok1, tok2, *tok3])
    alone, alone_twin, shared, tokens_grad = together(alone, alone_twin, shared, tokens_grad)
    q_out, z_out, x_out, dt_out = alone_out(bounds, alone, alone_twin)
    shared = shared.reshape(1024, 512).astype(F32)
    flat = flat + flat_got if four else flat_got
    flat = flat.reshape(-1)
    norm_sum = flat[12544:13568]
    small = flat[:8192].reshape(8, 1024)
    gain_sum = flat[8192:10240].reshape(8, 256)
    bc_sum = flat[10240:11520].reshape(5, 256)
    mlp_sum = flat[11520:12544]
    both_cores = lambda v: jnp.stack([lax.dynamic_index_in_dim(v, k * 4 + t, 0, False) for k in range(2)])
    small = both_cores(small)
    gain_sum = both_cores(gain_sum)[:, :192].reshape(-1)
    conv_small = small[:, :960].reshape(2, 5, 192)
    conv_small = jnp.concatenate([conv_small[0], conv_small[1]], axis=1)
    head_small = small[:, 960:969].reshape(2, 3, 3)
    per_head_sum = lambda i: head_small[:, i].reshape(-1)

    gate_out, up_out, down_out, mix_out, att_out = outs
    return (
        layer_out[None],
        tokens_grad[None],
        norm_sum,
        q_out,
        shared[:, :256],
        att_out,
        z_out,
        x_out,
        dt_out,
        shared[:, 256:],
        conv_small[:4],
        conv_small[4],
        bc_sum[:4],
        bc_sum[4],
        per_head_sum(2),
        per_head_sum(1),
        per_head_sum(0),
        gain_sum,
        mix_out,
        mlp_sum,
        gate_out,
        up_out,
        down_out,
    )


def solution(mesh):
    placed = (
        P("dp", "ctx", None),
        P("dp", None),
        P(),
        P(None, "tensor"),
        P(),
        P("tensor", None),
        P(None, "tensor"),
        P(None, "tensor"),
        P(None, "tensor"),
        P(),
        P(None, "tensor"),
        P("tensor"),
        P(),
        P(),
        P("tensor"),
        P("tensor"),
        P("tensor"),
        P("tensor"),
        P("tensor", None),
        P(),
        P(None, "tensor"),
        P(None, "tensor"),
        P("tensor", None),
        P("dp", "ctx", None),
    )
    return jax.shard_map(
        local,
        mesh=mesh,
        in_specs=placed,
        out_specs=(
            P("dp", "ctx", None),
            P("dp", "ctx", None),
            P(),
            P(None, "tensor"),
            P(),
            P("tensor", None),
            P(None, "tensor"),
            P(None, "tensor"),
            P(None, "tensor"),
            P(),
            P(None, "tensor"),
            P("tensor"),
            P(),
            P(),
            P("tensor"),
            P("tensor"),
            P("tensor"),
            P("tensor"),
            P("tensor", None),
            P(),
            P(None, "tensor"),
            P(None, "tensor"),
            P("tensor", None),
        ),
        check_vma=False,
    )
```

```python
import functools

import jax
import numpy as np
import jax.numpy as jnp
from jax import lax
from jax.experimental import pallas as pl
from jax.experimental.pallas import tpu as pltpu
from jax.sharding import PartitionSpec as P

BF, F32 = jnp.bfloat16, jnp.float32
EPSILON = 1e-05
ROPE_BASE = 100000000000.0
HEAD_SIZE = 64
MP = 64
PROJ_ROWS = 256
BQ = 512
CHUNK = 256
VMEM_LIMIT = 48 * 1024 * 1024
FULL_VMEM = 60 * 1024 * 1024
SMALL_COST = pl.CostEstimate(flops=1000000, bytes_accessed=100000, transcendentals=0)


def dot(left, right, dims=((1,), (0,)), precision=None):
    return lax.dot_general(
        left, right, (dims, ((), ())), precision=precision, preferred_element_type=F32
    )


def dot_bt(left, right):
    return dot(left, right, ((1,), (1,)))


def dot_at(left, right):
    return dot(left, right, ((0,), (0,)))


def lanes(shape):
    return lax.broadcasted_iota(jnp.int32, shape, len(shape) - 1)


def rows_of(shape):
    return lax.broadcasted_iota(jnp.int32, shape, 0)


def doc_start(pos, first, second):
    return jnp.where(pos >= second, second, jnp.where(pos >= first, first, 0))


def halves(low, high):
    return jnp.where(lanes((1, 128)) < 64, low, high)


def params(**kw):
    return pltpu.CompilerParams(vmem_limit_bytes=VMEM_LIMIT, **kw)


def whole(shape):
    return pl.BlockSpec(shape, lambda *_: (0,) * len(shape))


def proj_body(off, tok, gain, weight, cos, sin, *refs):
    normed_ref, qp_ref, kv_ref, xbc_ref, z_ref, dt_ref = refs[-6:]
    values = tok[...].astype(F32)
    scale = lax.rsqrt(jnp.mean(values * values, axis=-1, keepdims=True) + EPSILON)
    normed = (values * scale * gain[...]).astype(BF)
    normed_ref[...] = normed
    c, s = cos[...], sin[...]
    left = lanes((1, 128)) < 64
    att = dot(normed, weight[:, :384])
    kv, turned, qd = att[:, :128], att[:, 128:256], att[:, 256:]
    kv_ref[...] = jnp.where(left, kv * c + turned * s, kv).astype(BF)
    q_rot = qd * c + pltpu.roll(turned, 64, 1) * s
    qp_ref[...] = jnp.where(left, q_rot.astype(BF) * 0.125, 0.0).astype(BF)
    dt_ref[...] = qd.T[64:72, :]
    ssm = dot(normed, weight[:, 384:])
    x2z2 = ssm[:, 128:256]
    xbc_ref[:, :128] = ssm[:, :128].astype(BF)
    xbc_ref[:, 128:256] = jnp.where(left, x2z2, 0.0).astype(BF)
    xbc_ref[:, 256:] = ssm[:, 384:].astype(BF)
    z_ref[:, :128] = ssm[:, 256:384]
    z_ref[:, 128:] = jnp.where(left, pltpu.roll(x2z2, 64, 1), 0.0)


def project(off, tokens, gain, weight, cos, sin, before=None):
    own = tokens.shape[0]
    full = cos.shape[0]
    n = PROJ_ROWS
    outs = [
        jax.ShapeDtypeStruct((full, 1024), BF),
        jax.ShapeDtypeStruct((full, 128), BF),
        jax.ShapeDtypeStruct((full, 128), BF),
        jax.ShapeDtypeStruct((full, 512), BF),
        jax.ShapeDtypeStruct((full, 256), F32),
        jax.ShapeDtypeStruct((8, full), F32),
    ]
    at = lambda i, off: (off[0] + i, 0)
    out_specs = [pl.BlockSpec((n, o.shape[1]), at) for o in outs[:5]]
    out_specs.append(pl.BlockSpec((8, n), lambda i, off: (0, off[0] + i)))
    in_specs = [
        pl.BlockSpec((n, 1024), lambda i, off: (i, 0)),
        whole((1, 1024)),
        whole((1024, 1024)),
        pl.BlockSpec((n, 128), at),
        pl.BlockSpec((n, 128), at),
    ]
    args = [off, tokens, gain, weight, cos, sin]
    alias = {}
    if before is not None:
        in_specs += [pl.BlockSpec(memory_space=pl.ANY)] * 6
        args += list(before)
        alias = {6 + i: i for i in range(6)}
    return pl.pallas_call(
        proj_body,
        grid_spec=pltpu.PrefetchScalarGridSpec(
            num_scalar_prefetch=1, grid=(own // n,), in_specs=in_specs, out_specs=out_specs
        ),
        out_shape=outs,
        input_output_aliases=alias,
        compiler_params=params(),
        cost_estimate=SMALL_COST,
        name="norm_project",
    )(*args)


def turned_lanes(value):
    low = lanes((1, 128)) % 64 < 32
    return jnp.where(low, -pltpu.roll(value, 96, 1), pltpu.roll(value, 32, 1))


def prep_body(bounds, gate, up, down, mix, att, kv, q, x, z, dt, bc, weight, pack):
    n = gate.shape[0]
    pack[:, :256] = gate[...]
    pack[:, 256:512] = up[...]
    pack[:, 512:768] = down[...].T
    pack[:, 768:] = jnp.concatenate([mix[...], att[...]], axis=0).T
    first, low_kv = bounds[3] == 0, bounds[2] // 2 == 0
    lane = lanes((1, 128))
    left = lane < 64
    tile = lambda ref, i: ref[:, 128 * i : 128 * i + 128].astype(F32)
    swapped = lambda v: pltpu.roll(v, 64, 1)
    keys, values = tile(kv, 0), tile(kv, 1)
    keys = jnp.where(low_kv, keys, swapped(keys))
    values = jnp.where(low_kv, swapped(values), values)
    query = tile(q, 0)
    query = jnp.where(first, query, swapped(query))
    steps = jnp.concatenate([dt[...].astype(F32), jnp.zeros((n, 122), F32)], axis=1)
    steps = jnp.where(lane < 3, jnp.where(first, steps, pltpu.roll(steps, 125, 1)), 0.0)

    def heads(ref):
        a, b, d = tile(ref, 0), tile(ref, 1), swapped(tile(ref, 2))
        return jnp.where(first, a, jnp.where(left, swapped(b), d)), jnp.where(first, b, d)

    x01, x2 = heads(x)
    z01, z2 = heads(z)
    tiles = [
        jnp.where(left, keys, values),
        jnp.where(left, turned_lanes(keys), swapped(turned_lanes(query))),
        jnp.where(left, query, swapped(steps)),
        x01,
        jnp.where(left, x2, swapped(z2)),
        z01,
    ]
    for i, value in enumerate(tiles):
        weight[:, 128 * i : 128 * i + 128] = value.astype(BF)
    weight[:, 768:] = bc[...]


def prepare(bounds, gate, up, down, mix, att, kv, q, x, z, dt, bc):
    n = 256
    row = lambda w: pl.BlockSpec((n, w), lambda i, b: (i, 0))
    col = lambda h: pl.BlockSpec((h, n), lambda i, b: (b[3], i))
    mine = pl.BlockSpec((n, 256), lambda i, b: (i, b[3]))
    return pl.pallas_call(
        prep_body,
        grid_spec=pltpu.PrefetchScalarGridSpec(
            num_scalar_prefetch=1,
            grid=(4,),
            in_specs=[mine, mine, col(256), col(192), col(64)]
            + [row(256), row(128), row(384), row(384), row(6), row(256)],
            out_specs=[row(1024), row(1024)],
        ),
        out_shape=[jax.ShapeDtypeStruct((1024, 1024), BF)] * 2,
        compiler_params=pltpu.CompilerParams(vmem_limit_bytes=FULL_VMEM),
        cost_estimate=SMALL_COST,
        name="prepare",
    )(bounds, gate, up, down, mix, att, kv, q, x, z, dt, bc)


def block_range(qi, bounds):
    first, second = bounds[0], bounds[1]
    q0 = qi * BQ
    low = doc_start(q0, first, second) // BQ
    inner = (doc_start(q0 + BQ - 1, first, second) + BQ - 1) // BQ
    return low, jnp.minimum(jnp.maximum(inner, low), qi)


def allowed_keys(qi, kb, bounds):
    q = qi * BQ + rows_of((BQ, 1))
    k = kb * BQ + lanes((1, BQ))
    start = doc_start(q, bounds[0], bounds[1])
    return (k <= q) & (k >= start)


def attend_body(bounds, qp, kv, g2, out_ref, keep_ref):
    qi = pl.program_id(0)
    low, inner = block_range(qi, bounds)
    q = qp[...]

    def step(kb, carry, masked):
        top, total, acc = carry
        k = kv[pl.ds(pl.multiple_of(kb * BQ, BQ), BQ), :]
        s = dot_bt(q, k)
        if masked:
            s = jnp.where(allowed_keys(qi, kb, bounds), s, -1e30)
        new_top = jnp.maximum(top, jnp.max(s, axis=1, keepdims=True))
        p = jnp.exp(s - new_top)
        fade = jnp.exp(top - new_top)
        total = total * fade + jnp.sum(p, axis=1, keepdims=True)
        acc = acc * fade + dot(p.astype(BF), k)
        return new_top, total, acc

    carry = (jnp.full((BQ, 1), -1e30, F32), jnp.zeros((BQ, 1), F32), jnp.zeros((BQ, 128), F32))
    carry = lax.fori_loop(low, inner, lambda kb, c: step(kb, c, True), carry)
    carry = lax.fori_loop(inner, qi, lambda kb, c: step(kb, c, False), carry)
    top, total, acc = step(qi, carry, True)
    out = acc / total
    left = lanes((1, 128)) < 64
    out_ref[...] = jnp.where(left, g2[...], out.astype(BF))
    keep_ref[...] = jnp.where(left, top + jnp.log(total), out)


def attend(bounds, qp, kv, g2):
    full = qp.shape[0]
    block = pl.BlockSpec((BQ, 128), lambda i, *_: (i, 0))
    return pl.pallas_call(
        attend_body,
        grid_spec=pltpu.PrefetchScalarGridSpec(
            num_scalar_prefetch=1,
            grid=(full // BQ,),
            in_specs=[block, whole((full, 128)), block],
            out_specs=[block, block],
        ),
        out_shape=[
            jax.ShapeDtypeStruct((full, 128), BF),
            jax.ShapeDtypeStruct((full, 128), F32),
        ],
        compiler_params=params(),
        cost_estimate=SMALL_COST,
        name="attend",
    )(bounds, qp, kv, g2)


def attend_back_body(bounds, qp, kv, keep, grad, cos, sin, out_ref, acc_ref):
    blocks = pl.num_programs(0)
    qi = blocks - 1 - pl.program_id(0)
    left = lanes((1, 128)) < 64

    @pl.when(pl.program_id(0) == 0)
    def _():
        acc_ref[...] = jnp.zeros_like(acc_ref)

    low, inner = block_range(qi, bounds)
    q = qp[...]
    do = jnp.where(left, 0.0, grad[0].astype(F32))
    delta = jnp.sum(do * keep[...], axis=1, keepdims=True)
    do = do.astype(BF)
    lse = keep[:, :1]

    def step(kb, dq, masked):
        at = pl.ds(pl.multiple_of(kb * BQ, BQ), BQ)
        k = kv[at, :]
        p = jnp.exp(dot_bt(q, k) - lse)
        if masked:
            p = jnp.where(allowed_keys(qi, kb, bounds), p, 0.0)
        ds = (p * (dot_bt(do, k) - delta)).astype(BF)
        acc_ref[at, :] += dot_at(ds, q) + dot_at(p.astype(BF), do)
        return dq + dot(ds, k)

    dq = jnp.zeros((BQ, 128), F32)
    dq = lax.fori_loop(low, inner, lambda kb, c: step(kb, c, True), dq)
    dq = lax.fori_loop(inner, qi, lambda kb, c: step(kb, c, False), dq)
    dq = step(qi, dq, True) * 0.125
    dkv = acc_ref[pl.ds(pl.multiple_of(qi * BQ, BQ), BQ), :]
    c, s = cos[...], sin[...]
    out_ref[:, :128] = jnp.where(left, dkv * c, dkv).astype(BF)
    out_ref[:, 128:256] = (jnp.where(left, dkv, pltpu.roll(dq, 64, 1)) * s).astype(BF)
    out_ref[:, 256:] = jnp.where(left, dq * c, 0.0).astype(BF)


def attend_back(bounds, qp, kv, keep, grad, cos, sin):
    full = qp.shape[0]
    n = full // BQ
    block = pl.BlockSpec((BQ, 128), lambda i, *_: (n - 1 - i, 0))
    return pl.pallas_call(
        attend_back_body,
        grid_spec=pltpu.PrefetchScalarGridSpec(
            num_scalar_prefetch=1,
            grid=(n,),
            in_specs=[
                block,
                whole((full, 128)),
                block,
                pl.BlockSpec((1, BQ, 128), lambda i, *_: (n - 1 - i, 0, 0)),
                block,
                block,
            ],
            out_specs=pl.BlockSpec((BQ, 384), lambda i, *_: (n - 1 - i, 0)),
            scratch_shapes=[pltpu.VMEM((full, 128), F32)],
        ),
        out_shape=jax.ShapeDtypeStruct((full, 384), BF),
        compiler_params=params(),
        cost_estimate=SMALL_COST,
        name="attend_back",
    )(bounds, qp, kv, keep, grad, cos, sin)


def tap_mask(first_row, count, shift, bounds):
    pos = first_row + rows_of((count, 1))
    return (pos - doc_start(pos, bounds[0], bounds[1]) >= shift).astype(F32)


def conv_taps(ext_ref, r0, bounds, taps, bias):
    pre = bias + taps[3:4, :] * ext_ref[pl.ds(8, CHUNK), :]
    for shift in (1, 2, 3):
        mask = tap_mask(r0, CHUNK, shift, bounds)
        pre = pre + taps[3 - shift : 4 - shift, :] * (ext_ref[pl.ds(8 - shift, CHUNK), :] * mask)
    return pre


def chunk_decay(r0, bounds, dt_raw, head, extra=None):
    lane = lanes((1, CHUNK))
    dt = jax.nn.softplus(dt_raw + head[:, 0:1])
    la = dt * head[:, 1:2]
    upper = (rows_of((CHUNK, CHUNK)) <= lanes((CHUNK, CHUNK))).astype(F32)
    cum = dot(la, upper, precision=lax.Precision.HIGHEST)
    rows = [cum, dt] if extra is None else [cum, dt, extra]
    used = 8 * len(rows)
    stacked = jnp.concatenate(rows + [jnp.zeros((CHUNK - used, CHUNK), F32)], axis=0).T
    cum_col, dt_col = stacked[:, 0:8], stacked[:, 8:16]
    pos = r0 + rows_of((CHUNK, 1))
    start = doc_start(pos, bounds[0], bounds[1])
    start_last = doc_start(r0 + CHUNK - 1, bounds[0], bounds[1])
    key = r0 + lane
    mask = (key <= pos) & (key >= start)
    enter = jnp.where(start < r0, jnp.exp(cum_col), 0.0)
    fade = jnp.where(pos >= start_last, jnp.exp(cum_last_row(cum_col) - cum_col), 0.0)
    keep = jnp.where(start_last < r0, jnp.exp(cum_last_row(cum_col)), 0.0)
    return dt, la, cum, dt_col, cum_col, mask, enter, fade, keep, stacked[:, 16:24]


def two_terms(value):
    high = value.astype(BF)
    return high, (value - high.astype(F32)).astype(BF)


def cum_last_row(cum_col):
    return cum_col[CHUNK - 1 : CHUNK, :]


def per_head(col):
    return halves(col[:, 0:1], col[:, 1:2]), col[:, 2:3]


def state_rows(keep):
    row = rows_of((256, 1))
    return jnp.where(row < 64, keep[:, 0:1], jnp.where(row < 128, keep[:, 1:2], keep[:, 2:3]))


def scan_body(bounds, xbc, z, dt_raw, taps, bias, head, skip, g01, g2, y_ref, s_ref, ext, state):
    i = pl.program_id(0)
    r0 = i * CHUNK

    @pl.when(i == 0)
    def _():
        ext[pl.ds(0, 8), :] = jnp.zeros((8, 512), F32)
        state[...] = jnp.zeros_like(state)

    @pl.when(i > 0)
    def _():
        ext[pl.ds(0, 8), :] = ext[pl.ds(CHUNK, 8), :]

    ext[pl.ds(8, CHUNK), :] = xbc[...].astype(F32)
    pre = conv_taps(ext, r0, bounds, taps[...], bias[...])
    conv = pre * jax.nn.sigmoid(pre)
    x01, x2 = conv[:, :128], conv[:, 128:256]
    b, c = conv[:, 256:384].astype(BF), conv[:, 384:].astype(BF)
    dt, la, cum, dt_col, cum_col, mask, enter, fade, keep, _ = chunk_decay(
        r0, bounds, dt_raw[...], head[...]
    )
    inner = dot_bt(c, b)
    x01b, x2b = x01.astype(BF), x2.astype(BF)
    ys = []
    for h in range(3):
        gap = cum_col[:, h : h + 1] - cum[h : h + 1, :]
        decay = jnp.exp(jnp.where(mask, gap, -1e30))
        m = (inner * decay * dt[h : h + 1, :]).astype(BF)
        ys.append(dot(m, x01b if h < 2 else x2b))
    s0 = state[...]
    s_ref[0] = s0
    s0b, s0c = two_terms(s0)
    carried = dot_bt(c, s0b) + dot_bt(c, s0c)
    e01, e2 = per_head(enter)
    y01 = halves(ys[0], ys[1]) + e01 * carried[:, :128] + skip[:, :128] * x01
    y2 = ys[2] + e2 * carried[:, 128:] + skip[:, 128:] * x2
    w01, w2 = per_head(fade * dt_col)
    xw = jnp.concatenate([(x01 * w01).astype(BF), (x2 * w2).astype(BF)], axis=1)
    state[...] = s0 * state_rows(keep) + dot_at(xw, b)
    y_ref[:, :128] = y01
    y_ref[:, 128:] = y2
    z01, z2 = z[:, :128], z[:, 128:]
    g01[...] = (y01 * (z01 * jax.nn.sigmoid(z01))).astype(BF)
    g2[...] = (y2 * (z2 * jax.nn.sigmoid(z2))).astype(BF)


def scan_forward(bounds, xbc, z, dt_raw, taps, bias, head, skip):
    full = xbc.shape[0]
    n = full // CHUNK
    row = lambda width: pl.BlockSpec((CHUNK, width), lambda i, *_: (i, 0))
    return pl.pallas_call(
        scan_body,
        grid_spec=pltpu.PrefetchScalarGridSpec(
            num_scalar_prefetch=1,
            grid=(n,),
            in_specs=[
                row(512),
                row(256),
                pl.BlockSpec((8, CHUNK), lambda i, *_: (0, i)),
                whole((8, 512)),
                whole((1, 512)),
                whole((8, 128)),
                whole((1, 256)),
            ],
            out_specs=[
                row(128),
                row(128),
                row(256),
                pl.BlockSpec((1, 256, 128), lambda i, *_: (i, 0, 0)),
            ],
            scratch_shapes=[pltpu.VMEM((CHUNK + 8, 512), F32), pltpu.VMEM((256, 128), F32)],
        ),
        out_shape=[
            jax.ShapeDtypeStruct((full, 128), BF),
            jax.ShapeDtypeStruct((full, 128), BF),
            jax.ShapeDtypeStruct((full, 256), F32),
            jax.ShapeDtypeStruct((n, 256, 128), F32),
        ],
        compiler_params=params(),
        cost_estimate=SMALL_COST,
        name="scan_forward",
    )(bounds, xbc, z, dt_raw, taps, bias, head, skip)


def scalar_rows(terms):
    low = terms[0:2, :] + terms[2:4, :] + terms[4:6, :]
    high = terms[6:8, :] + terms[8:10, :] + terms[10:12, :]
    total = jnp.concatenate([low, high], axis=1)
    return jnp.concatenate([total, jnp.zeros((6, CHUNK), F32)], axis=0)


def scan_back_body(
    last, bounds, xbc, before, z, y, dt_raw, s0_ref, dn01, dn2, scal, taps, bias, head, skip, gain,
    dstate_in, dext_in, acc_in, head_in, *refs,
):
    out_ref, dt_grad, acc, head_acc, dstate_out, dext_out, ext, dext, dstate = refs[-9:]
    step = pl.program_id(0)
    i = last - step
    r0 = i * CHUNK
    left = lanes((1, 128)) < 64

    @pl.when(step == 0)
    def _():
        dext[pl.ds(CHUNK, 8), :] = dext_in[...]
        dstate[...] = dstate_in[...]
        acc[...] = acc_in[...]
        head_acc[...] = head_in[...]

    @pl.when(step > 0)
    def _():
        dext[pl.ds(CHUNK, 8), :] = dext[pl.ds(0, 8), :]

    ext[pl.ds(0, 8), :] = before[...].astype(F32)[8:, :]
    ext[pl.ds(8, CHUNK), :] = xbc[...].astype(F32)
    weights = taps[...]
    pre = conv_taps(ext, r0, bounds, weights, bias[...])
    sig = jax.nn.sigmoid(pre)
    conv = pre * sig
    x01, x2 = conv[:, :128], conv[:, 128:256]
    b, c = conv[:, 256:384].astype(BF), conv[:, 384:].astype(BF)
    dt, la, cum, dt_col, cum_col, mask, enter, fade, keep, scalars = chunk_decay(
        r0, bounds, dt_raw[...], head[...], scalar_rows(scal[0].astype(F32))
    )
    row_scale, row_cross = scalars[:, 0:1], scalars[:, 1:2]

    def gate_back(dn, gain, zz, yy):
        s = jax.nn.sigmoid(zz)
        act = zz * s
        g = yy * act
        sent = g.astype(BF).astype(F32)
        ratio = jnp.where(g == 0.0, 1.0, sent / g)
        dg = (dn * gain * row_scale - sent * row_cross) * ratio
        return dg * act, dg * yy * (s + act * (1.0 - s))

    dy01, dz01 = gate_back(dn01[0].astype(F32), gain[:, :128], z[:, :128], y[:, :128])
    dy2, dz2 = gate_back(dn2[0].astype(F32), gain[:, 128:], z[:, 128:], y[:, 128:])
    dy2, dz2 = jnp.where(left, dy2, 0.0), jnp.where(left, dz2, 0.0)
    inner = dot_bt(c, b)
    x01b, x2b = x01.astype(BF), x2.astype(BF)
    dy01b, dy2b = dy01.astype(BF), dy2.astype(BF)
    zero = jnp.zeros_like(dy01b)
    parts = [(jnp.where(left, dy01b, zero), x01b), (jnp.where(left, zero, dy01b), x01b), (dy2b, x2b)]
    d_inner = jnp.zeros((CHUNK, CHUNK), F32)
    dxs, col_sums, direct, row_sums = [], [], [], []
    for h in range(3):
        gap = cum_col[:, h : h + 1] - cum[h : h + 1, :]
        decay = jnp.exp(jnp.where(mask, gap, -1e30))
        dt_h = dt[h : h + 1, :]
        dyh, xh = parts[h]
        dm = dot_bt(dyh, xh)
        kept = inner * decay
        m = (kept * dt_h).astype(BF)
        dxs.append(dot_at(m, dyh if h == 2 else dy01b))
        pulled = dm * kept
        d_inner = d_inner + dm * (decay * dt_h)
        weighted = pulled * dt_h
        direct.append(jnp.sum(pulled, axis=0, keepdims=True))
        col_sums.append(jnp.sum(weighted, axis=0, keepdims=True))
        row_sums.append(jnp.sum(weighted, axis=1, keepdims=True))
    s0 = s0_ref[0]
    s0b, s0c = two_terms(s0)
    ds1 = dstate[...]
    ds1b, ds1c = two_terms(ds1)
    e01, e2 = per_head(enter)
    ey01, ey2 = dy01 * e01, dy2 * e2
    ey, eyc = two_terms(jnp.concatenate([ey01, ey2], axis=1))
    carried = dot_bt(c, s0b) + dot_bt(c, s0c)
    f01, f2 = per_head(fade)
    d01, d2 = per_head(dt_col)
    back = dot_bt(b, ds1b)
    fb01, fb2 = f01 * back[:, :128], f2 * back[:, 128:]
    xw = jnp.concatenate([(x01 * (f01 * d01)).astype(BF), (x2 * (f2 * d2)).astype(BF)], axis=1)
    d_innerb = d_inner.astype(BF)
    dc = dot(d_innerb, b) + dot(ey, s0b) + dot(eyc, s0b) + dot(ey, s0c)
    db = dot_at(d_innerb, c) + dot(xw, ds1b) + dot(xw, ds1c)
    dx01 = halves(dxs[0], dxs[1]) + d01 * fb01 + skip[:, :128] * dy01
    dx2 = dxs[2] + d2 * fb2 + skip[:, 128:] * dy2
    kept_rows = state_rows(keep)
    crossing = jnp.sum(ds1 * s0 * kept_rows, axis=1, keepdims=True)
    dstate[...] = ds1 * kept_rows + dot_at(ey, c) + dot_at(eyc, c)
    inter01, inter2 = ey01 * carried[:, :128], ey2 * carried[:, 128:]
    u01, u2 = x01 * fb01, x2 * fb2
    pick = lambda v, h: jnp.where(left if h == 0 else ~left, v, 0.0)
    side = lambda v01, v2, h: jnp.sum(pick(v01, h) if h < 2 else v2, axis=1, keepdims=True)
    lane = lanes((1, CHUNK))
    tile = jnp.zeros((CHUNK, CHUNK), F32)
    crossed = jnp.zeros((8, 1), F32)
    head_row = rows_of((8, 1))
    for h in range(3):
        u = side(u01, u2, h)
        moved = row_sums[h] + side(inter01, inter2, h) - u * dt_col[:, h : h + 1]
        tile = jnp.where(lane == h, moved, jnp.where(lane == 8 + h, u, tile))
        total = jnp.sum(crossing[64 * h : 64 * h + 64, :], axis=0, keepdims=True)
        total = total + jnp.sum(u * dt_col[:, h : h + 1], axis=0, keepdims=True)
        crossed = jnp.where(head_row == h, total, crossed)
    tile = tile.T
    stack = lambda items: jnp.concatenate(items + [jnp.zeros((5, CHUNK), F32)], axis=0)
    dcum = tile[0:8, :] - stack(col_sums) + jnp.where(lane == CHUNK - 1, crossed, 0.0)
    lower = (rows_of((CHUNK, CHUNK)) >= lanes((CHUNK, CHUNK))).astype(F32)
    dla = dot(dcum, lower, precision=lax.Precision.HIGHEST)
    ddt = stack(direct) + tile[8:16, :] + dla * head[:, 1:2]
    graw = ddt * jax.nn.sigmoid(dt_raw[...] + head[:, 0:1])
    dt_grad[...] = graw
    head_acc[0:8, :] += dla * la
    head_acc[8:16, :] += graw
    dpre = jnp.concatenate([dx01, dx2, db, dc], axis=1) * (sig + conv * (1.0 - sig))
    dext[pl.ds(0, CHUNK), :] = dpre
    din = weights[3:4, :] * dpre
    acc[3:4, :] += jnp.sum(dpre * ext[pl.ds(8, CHUNK), :], axis=0, keepdims=True)
    acc[4:5, :] += jnp.sum(dpre, axis=0, keepdims=True)
    acc[5:6, :128] += jnp.sum(dy01 * x01, axis=0, keepdims=True)
    acc[5:6, 128:256] += jnp.sum(dy2 * x2, axis=0, keepdims=True)
    for shift in (1, 2, 3):
        tap = 3 - shift
        now = tap_mask(r0, CHUNK, shift, bounds)
        acc[tap : tap + 1, :] += jnp.sum(
            dpre * (ext[pl.ds(8 - shift, CHUNK), :] * now), axis=0, keepdims=True
        )
        later = tap_mask(r0 + shift, CHUNK, shift, bounds)
        din = din + weights[tap : tap + 1, :] * (dext[pl.ds(shift, CHUNK), :] * later)
    out_ref[:, :128] = din[:, :128].astype(BF)
    out_ref[:, 128:256] = jnp.where(left, din[:, 128:256], pltpu.roll(dz2, 64, 1)).astype(BF)
    out_ref[:, 256:384] = dz01.astype(BF)
    out_ref[:, 384:] = din[:, 256:].astype(BF)

    @pl.when(step == pl.num_programs(0) - 1)
    def _():
        dstate_out[...] = dstate[...]
        dext_out[...] = dext[pl.ds(0, 8), :]


def scan_back(part, carry, before, bounds, xbc, z, y, dt_raw, states, late, dn, taps, bias, head, skip, gain):
    full = xbc.shape[0]
    n = full // CHUNK
    half = n // 2
    last = n - 1 if part == 0 else half - 1
    row = lambda width: pl.BlockSpec((CHUNK, width), lambda i, *_: (last - i, 0))
    tall = CHUNK // 16
    per = n // 8
    sent = pl.BlockSpec((1, CHUNK, 128), lambda i, b: ((last - i) // per, (last - i) % per, 0))

    def terms(i, b):
        piece, rest = (last - i) // per, (last - i) % per
        return piece, per * (CHUNK // 16) + rest, 0

    carried = [whole((256, 128)), whole((8, 512)), whole((8, 512)), whole((16, CHUNK))]
    sds = jax.ShapeDtypeStruct
    args = [bounds, xbc, xbc, z, y, dt_raw, states, late, dn, late, taps, bias, head, skip, gain]
    args += list(carry) + list(before)
    alias = {len(args) - 2: 0, len(args) - 1: 1} if before else {}
    return pl.pallas_call(
        functools.partial(scan_back_body, last),
        grid_spec=pltpu.PrefetchScalarGridSpec(
            num_scalar_prefetch=1,
            grid=(half,),
            in_specs=[
                row(512),
                pl.BlockSpec((16, 512), lambda i, *_: (jnp.maximum((last - i) * tall - 1, 0), 0)),
                row(256),
                row(256),
                pl.BlockSpec((8, CHUNK), lambda i, *_: (0, last - i)),
                pl.BlockSpec((1, 256, 128), lambda i, *_: (last - i, 0, 0)),
                sent,
                sent,
                pl.BlockSpec((1, 16, 128), terms),
                whole((8, 512)),
                whole((1, 512)),
                whole((8, 128)),
                whole((1, 256)),
                whole((1, 256)),
            ]
            + carried
            + [pl.BlockSpec(memory_space=pl.ANY)] * len(before),
            out_specs=[
                row(640),
                pl.BlockSpec((8, CHUNK), lambda i, *_: (0, last - i)),
                whole((8, 512)),
                whole((16, CHUNK)),
                whole((256, 128)),
                whole((8, 512)),
            ],
            scratch_shapes=[
                pltpu.VMEM((CHUNK + 8, 512), F32),
                pltpu.VMEM((CHUNK + 8, 512), F32),
                pltpu.VMEM((256, 128), F32),
            ],
        ),
        out_shape=[
            sds((full, 640), BF),
            sds((8, full), F32),
            sds((8, 512), F32),
            sds((16, CHUNK), F32),
            sds((256, 128), F32),
            sds((8, 512), F32),
        ],
        input_output_aliases=alias,
        compiler_params=params(),
        cost_estimate=SMALL_COST,
        name="scan_back",
    )(*args)


ROW_BLOCK = 256


def row_body(bounds, g, h, tok, gout, mlp_gain, gains, *refs):
    packs, refs = refs[:10], refs[10:]
    pa, pb, slots = [], [], []
    for k, base in enumerate((0, 5)):
        for r in range(4):
            first = packs[base + r]
            second = first.at[:, 512:] if r < 3 else packs[base + 4]
            pa.append(first.at[:, 0:512])
            pb.append(second)
            slots.append((bounds[3] ^ k) * 4 + (bounds[2] ^ r))
    gain_rows = [gains[slot] for slot in slots]
    out_ref, two_ref, dmix_ref, dhid_ref = refs[0:4]
    act_refs, dgu_refs, gn_refs = refs[4:6], refs[6:8], refs[8:10]
    dn, dn_late, mlp_acc, gain_acc = refs[10:14]
    step = pl.program_id(0)
    left = lanes((1, 128)) < 64
    width = 1536.0

    @pl.when(pl.program_id(0) == 0)
    def _():
        mlp_acc[...] = jnp.zeros_like(mlp_acc)
        gain_acc[...] = jnp.zeros_like(gain_acc)

    pieces = [(r, k) for k in range(2) for r in range(4)]

    def part(ref, s):
        return ref[slots[s]].astype(F32)

    squares = 0.0
    for s in range(8):
        first, second = part(g, s), part(h, s)
        squares = squares + first * first + jnp.where(left, second * second, 0.0)
    rg = lax.rsqrt(jnp.sum(squares, axis=1, keepdims=True) / width + EPSILON)
    mixed = 0.0
    for s, (r, k) in enumerate(pieces):
        gain = gain_rows[s]
        first = part(g, s) * rg * gain[:, :128]
        second = part(h, s)
        second = jnp.where(left, second * rg * gain[:, 128:], second)
        gn = jnp.concatenate([first.astype(BF), second.astype(BF)], axis=1)
        gn_refs[k][:, r * 256 : r * 256 + 256] = gn
        mixed = mixed + dot_bt(gn, pb[s][:, 256:])
    hidden = tok[...].astype(F32) + mixed
    scale = lax.rsqrt(jnp.mean(hidden * hidden, axis=-1, keepdims=True) + EPSILON)
    two = (hidden * scale * mlp_gain[...]).astype(BF)
    two_ref[...] = two
    grad = gout[...]
    ffn = 0.0
    dtwo = 0.0
    for s, (r, k) in enumerate(pieces):
        weight, down = pa[s][...], pb[s][:, :256]
        gu = dot(two, weight)
        gate, up = gu[:, :256], gu[:, 256:]
        sig = jax.nn.sigmoid(gate)
        silu = gate * sig
        act = (silu * up).astype(BF)
        act_refs[k][:, r * 256 : r * 256 + 256] = act
        ffn = ffn + dot_bt(act, down)
        dact = dot(grad, down)
        dgate = (dact * up * (sig + silu * (1.0 - sig))).astype(BF)
        dgu = jnp.concatenate([dgate, (dact * silu).astype(BF)], axis=1)
        dgu_refs[k][:, r * 512 : r * 512 + 512] = dgu
        dtwo = dtwo + dot_bt(dgu, weight)
    whole_out = (hidden + ffn).astype(BF)
    out_ref[0] = whole_out[:, :512]
    out_ref[1] = whole_out[:, 512:]
    weighted = dtwo * mlp_gain[...]
    mlp_acc[...] += jnp.sum(dtwo * (hidden * scale), axis=0, keepdims=True)
    mean = jnp.mean(weighted * hidden, axis=-1, keepdims=True)
    dhid = grad.astype(F32) + scale * weighted - hidden * (scale * scale * scale * mean)
    dhid_ref[...] = dhid
    dmix = dhid.astype(BF)
    dmix_ref[...] = dmix
    cross = 0.0
    for s, (r, k) in enumerate(pieces):
        dgn = dot(dmix, pb[s][:, 256:]).astype(BF)
        at = pl.ds(pl.multiple_of(step * ROW_BLOCK, ROW_BLOCK), ROW_BLOCK)
        dn[slots[s], at, :] = dgn[:, 128:]
        dn_late[slots[s], at, :] = dgn[:, :128]
        first, second = dgn[:, :128].astype(F32), dgn[:, 128:].astype(F32)
        gain = gain_rows[s]
        own1, own2 = part(g, s), jnp.where(left, part(h, s), 0.0)
        t1, t2 = first * own1, second * own2
        gain_acc[slots[s], :, :128] += jnp.sum(t1 * rg, axis=0, keepdims=True)
        gain_acc[slots[s], :, 128:] += jnp.sum(t2 * rg, axis=0, keepdims=True)
        cross = cross + t1 * gain[:, :128] + t2 * gain[:, 128:]
    cross = jnp.sum(cross, axis=1, keepdims=True) * (rg * rg * rg / width)
    lane = lanes((1, 128))
    tile = jnp.where(lane == 0, rg, jnp.where(lane == 1, cross, 0.0))
    pair = tile.T[0:2, :]
    high = pair.astype(BF)
    rest = pair - high.astype(F32)
    middle = rest.astype(BF)
    low = (rest - middle.astype(F32)).astype(BF)
    terms = [v.astype(F32) for v in (high, middle, low)]
    block = jnp.concatenate(
        [v[:, :128] for v in terms] + [v[:, 128:] for v in terms] + [jnp.zeros((4, 128), F32)],
        axis=0,
    ).astype(BF)
    for s in range(8):
        dn_late[s, pl.ds(pl.multiple_of(2 * ROW_BLOCK + step * 16, 16), 16), :] = block


def row_stage(bounds, g, h, tokens, gout, mlp_gain, gains, packs):
    n = ROW_BLOCK
    count = 2 * n
    row = lambda w: pl.BlockSpec((n, w), lambda i, b: (i, 0))
    part = pl.BlockSpec((n, 1024), lambda i, b: (2 * b[2] + i, 0))
    piece = pl.BlockSpec((8, n, 128), lambda i, b: (0, i, 0))
    once = lambda shape: pl.BlockSpec(
        shape, lambda i, b: (0,) * len(shape), pipeline_mode=pl.Buffered(1)
    )
    sds = jax.ShapeDtypeStruct
    widths = [1024] * 4 + [1024] * 2 + [2048] * 2 + [1024] * 2
    dtypes = [BF] * 3 + [F32] + [BF] * 6
    return pl.pallas_call(
        row_body,
        grid_spec=pltpu.PrefetchScalarGridSpec(
            num_scalar_prefetch=1,
            grid=(2,),
            in_specs=[piece, piece, part, part, whole((1, 1024)), whole((8, 1, 256))]
            + [once(p.shape) for p in packs],
            out_specs=[pl.BlockSpec((2, n, 512), lambda i, b: (0, i, 0))]
            + [row(w) for w in widths[1:]]
            + [once((8, count, 128)), once((8, count + 32, 128))]
            + [whole((1, 1024)), whole((8, 1, 256))],
        ),
        out_shape=[sds((2, count, 512), BF)]
        + [sds((count, w), d) for w, d in zip(widths[1:], dtypes[1:])]
        + [sds((8, count, 128), BF), sds((8, count + 32, 128), BF)]
        + [sds((1, 1024), F32), sds((8, 1, 256), F32)],
        compiler_params=pltpu.CompilerParams(vmem_limit_bytes=58 * 1024 * 1024),
        cost_estimate=SMALL_COST,
        name="row_stage",
    )(bounds, g, h, tokens, gout, mlp_gain, gains, *packs)


def weight_body(two, gout, dmix, dgu, act, gn, *refs):
    a = dot_at(two[...], dgu[...])
    b = jnp.concatenate([dot_at(gout[...], act[...]), dot_at(dmix[...], gn[...])], axis=1)
    if len(refs) == 2:
        refs[0][0] = a.astype(BF)
        refs[1][0] = b.astype(BF)
    else:
        a = (a + refs[0][0].astype(F32)).astype(BF)
        b = (b + refs[1][0].astype(F32)).astype(BF)
        for i in range(2):

            @pl.when(pl.program_id(0) == i)
            def _(i=i):
                refs[2 + i][...] = a
                refs[4 + i][...] = b


def weight_stage(start, two, gout, dmix, dgu, act, gn, *others):
    count = two.shape[0]
    col = lambda w: pl.BlockSpec((count, w), lambda i: (0, start - 2 * i))
    piece = pl.BlockSpec((1, 1024, 512), lambda i: (i, 0, 0))
    once = pl.BlockSpec((1024, 512), lambda i: (0, 0), pipeline_mode=pl.Buffered(1))
    sds = jax.ShapeDtypeStruct
    return pl.pallas_call(
        weight_body,
        grid=(2,),
        in_specs=[whole((count, 1024))] * 3
        + [col(512), col(256), col(256)]
        + [piece] * len(others),
        out_specs=[once] * 4 if others else [piece] * 2,
        out_shape=[sds((1024, 512), BF)] * 4 if others else [sds((2, 1024, 512), BF)] * 2,
        compiler_params=pltpu.CompilerParams(vmem_limit_bytes=FULL_VMEM),
        cost_estimate=SMALL_COST,
        name="weight_stage",
    )(two, gout, dmix, dgu, act, gn, *others)


def with_steps(da, dt_grad):
    count = da.shape[0]
    cols = jnp.concatenate([dt_grad, jnp.zeros((120, count), F32)], axis=0).T
    last = jnp.where(lanes((1, 128)) < 64, da[:, 256:].astype(F32), pltpu.roll(cols, 64, 1))
    return jnp.concatenate([da[:, :256], last.astype(BF)], axis=1)


def input_grad_body(off, da, ds, dt_grad, weight, normed, out_ref, gain_ref):
    left = with_steps(da[...], dt_grad[...])
    grad = dot_bt(left, weight[:, :384]) + dot_bt(ds[...], weight[:, 384:])
    out_ref[...] = grad.astype(BF)

    @pl.when(pl.program_id(0) == 0)
    def _():
        gain_ref[...] = jnp.zeros_like(gain_ref)

    gain_ref[...] += jnp.sum(grad * normed[...].astype(F32), axis=0, keepdims=True)


def input_grad(off, da, ds, dt_grad, weight, normed):
    n = PROJ_ROWS
    own = ds.shape[0] // 2
    at = lambda i, off: (off[0] + i, 0)
    return pl.pallas_call(
        input_grad_body,
        grid_spec=pltpu.PrefetchScalarGridSpec(
            num_scalar_prefetch=1,
            grid=(own // n,),
            in_specs=[
                pl.BlockSpec((n, 384), at),
                pl.BlockSpec((n, 640), at),
                pl.BlockSpec((8, n), lambda i, off: (0, off[0] + i)),
                whole((1024, 1024)),
                pl.BlockSpec((n, 1024), at),
            ],
            out_specs=[pl.BlockSpec((n, 1024), lambda i, off: (i, 0)), whole((1, 1024))],
        ),
        out_shape=[
            jax.ShapeDtypeStruct((own, 1024), BF),
            jax.ShapeDtypeStruct((1, 1024), F32),
        ],
        compiler_params=params(),
        cost_estimate=SMALL_COST,
        name="input_grad",
    )(off, da, ds, dt_grad, weight, normed)


def turned_back(value):
    low = lanes((1, 128)) % 64 < 32
    return jnp.where(low, pltpu.roll(value, 96, 1), -pltpu.roll(value, 32, 1))


def shared_grad_body(bounds, normed, da, ds1, ds2, turned, shared, acc):
    @pl.when(pl.program_id(0) == 0)
    def _():
        acc[...] = jnp.zeros_like(acc)

    cols = jnp.concatenate([da[...], ds1[...], ds2[...]], axis=1)
    acc[...] += dot_at(normed[...], cols)

    @pl.when(pl.program_id(0) == pl.num_programs(0) - 1)
    def _():
        left = lanes((1, 128)) < 64
        kv = acc[:, :128] + jnp.where(left, turned_back(turned[...]), 0.0)
        low = bounds[2] // 2 == 0
        swapped = pltpu.roll(kv, 64, 1)
        keys = jnp.where(left == low, jnp.where(low, kv, swapped), 0.0)
        values = jnp.where(left == low, jnp.where(low, swapped, kv), 0.0)
        shared[:, :128] = keys.astype(BF)
        shared[:, 128:256] = values.astype(BF)
        shared[:, 256:] = acc[:, 128:].astype(BF)


def shared_grad(bounds, normed, da, ds, turned):
    full = normed.shape[0]
    n = 512
    part = lambda w, col: pl.BlockSpec((n, w), lambda i, *_: (i, col))
    return pl.pallas_call(
        shared_grad_body,
        grid_spec=pltpu.PrefetchScalarGridSpec(
            num_scalar_prefetch=1,
            grid=(full // n,),
            in_specs=[part(1024, 0), part(128, 0), part(128, 3), part(128, 4)]
            + [whole((1024, 128))],
            out_specs=whole((1024, 512)),
            scratch_shapes=[pltpu.VMEM((1024, 384), F32)],
        ),
        out_shape=jax.ShapeDtypeStruct((1024, 512), BF),
        compiler_params=params(),
        cost_estimate=SMALL_COST,
        name="shared_grad",
    )(bounds, normed, da, ds, ds, turned)


def alone_grad_body(bounds, normed, da1, da2, ds, dt_grad, kept, sent, turned, acc):
    @pl.when(pl.program_id(0) == 0)
    def _():
        acc[...] = jnp.zeros_like(acc)

    count = da1.shape[0]
    cols = jnp.concatenate([dt_grad[...], jnp.zeros((120, count), F32)], axis=0).T
    last = jnp.where(lanes((1, 128)) < 64, da2[...].astype(F32), pltpu.roll(cols, 64, 1))
    acc[...] += dot_at(
        normed[...], jnp.concatenate([last.astype(BF), ds[...], da1[...]], axis=1)
    )

    @pl.when(pl.program_id(0) == pl.num_programs(0) - 1)
    def _():
        left = lanes((1, 128)) < 64
        side = acc[:, 512:]
        turned[...] = side
        query = jnp.where(left, pltpu.roll(turned_back(side), 64, 1), 0.0)
        first = (acc[:, :128] + query).astype(BF)
        half = first.shape[0] // 2

        def write(ref, low):
            ref[:, :128] = first[low : low + half]
            ref[:, 128:] = acc[pl.ds(low, half), 128:512].astype(BF)

        @pl.when(bounds[4] == 1)
        def _():
            write(kept, 0)
            write(sent, half)

        @pl.when(bounds[4] == 0)
        def _():
            write(kept, half)
            write(sent, 0)


def alone_grad(bounds, normed, da, ds, dt_grad):
    full = normed.shape[0]
    n = 512
    part = lambda w, col: pl.BlockSpec((n, w), lambda i, *_: (i, col))
    return pl.pallas_call(
        alone_grad_body,
        grid_spec=pltpu.PrefetchScalarGridSpec(
            num_scalar_prefetch=1,
            grid=(full // n,),
            in_specs=[
                part(1024, 0),
                part(128, 1),
                part(128, 2),
                part(384, 0),
                pl.BlockSpec((8, n), lambda i, *_: (0, i)),
            ],
            out_specs=[whole((512, 512))] * 2 + [whole((1024, 128))],
            scratch_shapes=[pltpu.VMEM((1024, 640), F32)],
        ),
        out_shape=[
            jax.ShapeDtypeStruct((512, 512), BF),
            jax.ShapeDtypeStruct((512, 512), BF),
            jax.ShapeDtypeStruct((1024, 128), F32),
        ],
        compiler_params=params(),
        cost_estimate=SMALL_COST,
        name="alone_grad",
    )(bounds, normed, da, da, ds, dt_grad)


def assemble_body(bounds, p0, p1, p2, l3, r3, out):
    step = pl.program_id(0)
    for r, ref in enumerate((p0, p1, p2)):

        @pl.when(step == r)
        def _(ref=ref):
            out[:, :512] = ref[0]
            out[:, 512:] = ref[1]

    @pl.when(step == 3)
    def _():
        out[:, :512] = l3[...]
        out[:, 512:] = r3[...]


def assemble(bounds, parts):
    count = parts[0].shape[1]
    return pl.pallas_call(
        assemble_body,
        grid_spec=pltpu.PrefetchScalarGridSpec(
            num_scalar_prefetch=1,
            grid=(4,),
            in_specs=[whole(p.shape) for p in parts],
            out_specs=pl.BlockSpec((count, 1024), lambda i, b: (i ^ b[2], 0)),
        ),
        out_shape=jax.ShapeDtypeStruct((4 * count, 1024), parts[0].dtype),
        compiler_params=pltpu.CompilerParams(vmem_limit_bytes=FULL_VMEM),
        cost_estimate=SMALL_COST,
        name="assemble",
    )(bounds, *parts)


def piece_out_body(bounds, a, b, other_a, other_b, gate, up, down, mix, att):
    first = bounds[3] == 0

    def pair(own, other):
        own, other = own.astype(F32), other.astype(F32)
        return jnp.where(first, own, other), jnp.where(first, other, own)

    low, high = pair(a[...], other_a[...])
    gate[:, :256], gate[:, 256:] = low[:, :256], high[:, :256]
    up[:, :256], up[:, 256:] = low[:, 256:], high[:, 256:]
    low, high = pair(b[...], other_b[...])
    down[:256, :], down[256:, :] = low[:, :256].T, high[:, :256].T
    low, high = low[:, 256:].T, high[:, 256:].T
    mix[:192, :], mix[192:, :] = low[:192], high[:192]
    att[:64, :], att[64:, :] = low[192:], high[192:]


def piece_out(bounds, both, other):
    n = 256
    row = pl.BlockSpec((n, 512), lambda i, *_: (i, 0))
    second = pl.BlockSpec((n, 512), lambda i, *_: (i, 1))
    col = lambda h: pl.BlockSpec((h, n), lambda i, *_: (0, i))
    sds = jax.ShapeDtypeStruct
    return pl.pallas_call(
        piece_out_body,
        grid_spec=pltpu.PrefetchScalarGridSpec(
            num_scalar_prefetch=1,
            grid=(4,),
            in_specs=[row, second, row, second],
            out_specs=[row, row, col(512), col(384), col(128)],
        ),
        out_shape=[
            sds((1024, 512), F32),
            sds((1024, 512), F32),
            sds((512, 1024), F32),
            sds((384, 1024), F32),
            sds((128, 1024), F32),
        ],
        compiler_params=params(),
        cost_estimate=SMALL_COST,
        name="piece_out",
    )(bounds, both, both, other, other)


def alone_out_body(bounds, own, other, q, z, x, dt):
    first = bounds[3] == 0
    lane = lanes((1, 128))
    left = lane < 64
    tile = lambda ref, i: ref[:, 128 * i : 128 * i + 128].astype(F32)
    u = [jnp.where(first, tile(own, i), tile(other, i)) for i in range(4)]
    v = [jnp.where(first, tile(other, i), tile(own, i)) for i in range(4)]
    swapped = lambda value: pltpu.roll(value, 64, 1)
    q[...] = jnp.where(left, u[0], swapped(v[0]))
    x[:, :128] = u[1]
    x[:, 128:256] = jnp.where(left, u[2], swapped(v[1]))
    x[:, 256:] = jnp.where(left, swapped(v[1]), swapped(v[2]))
    z[:, :128] = u[3]
    z[:, 128:256] = jnp.where(left, swapped(u[2]), swapped(v[3]))
    z[:, 256:] = jnp.where(left, swapped(v[3]), v[2])
    dt[...] = jnp.where(lane < 3, swapped(u[0]), pltpu.roll(v[0], 67, 1))[:, :6]


def alone_out(bounds, own, other):
    n = 256
    row = lambda w: pl.BlockSpec((n, w), lambda i, *_: (i, 0))
    widths = [128, 384, 384, 6]
    return pl.pallas_call(
        alone_out_body,
        grid_spec=pltpu.PrefetchScalarGridSpec(
            num_scalar_prefetch=1,
            grid=(4,),
            in_specs=[row(512), row(512)],
            out_specs=[row(w) for w in widths],
        ),
        out_shape=[jax.ShapeDtypeStruct((1024, w), F32) for w in widths],
        compiler_params=params(),
        cost_estimate=SMALL_COST,
        name="alone_out",
    )(bounds, own, other)


def piece_sum_body(bounds, *refs):
    total = lambda i: (
        refs[i][...].astype(F32) + refs[i + 1][...] + refs[i + 2][...]
    ).astype(BF)
    kept, out = refs[12:]
    for group, ref in ((0, kept), (6, out)):
        ref[:, :512] = total(group)
        ref[:, 512:] = total(group + 3)


def piece_sum(bounds, a, b):
    n = 256
    keep = pl.BlockSpec((n, 512), lambda i, s: (i + 2 - 2 * s[4], 0))
    send = pl.BlockSpec((n, 512), lambda i, s: (i + 2 * s[4], 0))
    row = pl.BlockSpec((n, 1024), lambda i, s: (i, 0))
    return pl.pallas_call(
        piece_sum_body,
        grid_spec=pltpu.PrefetchScalarGridSpec(
            num_scalar_prefetch=1,
            grid=(2,),
            in_specs=[keep] * 6 + [send] * 6,
            out_specs=[row, row],
        ),
        out_shape=[jax.ShapeDtypeStruct((512, 1024), BF)] * 2,
        compiler_params=params(),
        cost_estimate=SMALL_COST,
        name="piece_sum",
    )(bounds, *a, *b, *a, *b)


def relay_body(first, second, kept, got, left, right, total):
    left[...] = first[0]
    right[...] = second[0]
    total[...] = (kept[...].astype(F32) + got[...]).astype(BF)


def relay(first, second, kept, got):
    n = first.shape[1] // 2
    row = pl.BlockSpec((n, 512), lambda i: (i, 0))
    half = lambda k: pl.BlockSpec((1, n, 512), lambda i: (k, i, 0))
    return pl.pallas_call(
        relay_body,
        grid=(2,),
        in_specs=[half(0), half(1), row, row],
        out_specs=[row] * 3,
        out_shape=[jax.ShapeDtypeStruct((2 * n, 512), BF)] * 3,
        compiler_params=pltpu.CompilerParams(vmem_limit_bytes=FULL_VMEM),
        cost_estimate=SMALL_COST,
        name="relay",
    )(first, second, kept, got)


def pair_sum_body(a, b, c, d, first, second):
    first[...] = (a[...].astype(F32) + b[...]).astype(BF)
    second[...] = (c[...].astype(F32) + d[...]).astype(BF)


def pair_sum(a, b, c, d):
    n = a.shape[0] // 2
    row = pl.BlockSpec((n, a.shape[1]), lambda i: (i, 0))
    return pl.pallas_call(
        pair_sum_body,
        grid=(2,),
        in_specs=[row] * 4,
        out_specs=[row, row],
        out_shape=[jax.ShapeDtypeStruct(a.shape, BF)] * 2,
        compiler_params=pltpu.CompilerParams(vmem_limit_bytes=FULL_VMEM),
        cost_estimate=SMALL_COST,
        name="pair_sum",
    )(a, b, c, d)


def swap(value, step):
    return lax.ppermute(value, "tensor", [(i, i ^ step) for i in range(4)])


def twin(value):
    return lax.ppermute(value, "ctx", [(0, 1), (1, 0)])


def exchange(value):
    return lax.all_to_all(value, ("ctx", "tensor"), 0, 0, tiled=True)


def dp_swap(value, step):
    return lax.ppermute(value, "dp", [(i, i ^ step) for i in range(4)])


MIDDLE = [(1, 2), (2, 1), (0, 3), (3, 0)]
NEAR = [(0, 1), (1, 0), (2, 3), (3, 2)]


class DpSum:
    def __init__(self):
        self.four = lax.axis_size("dp") == 4
        place = lax.axis_index("dp")
        self.inner = (place == 1) | (place == 2)

    def first(self, kept, sent):
        if self.four:
            return lax.ppermute(sent, "dp", NEAR)
        self.rest = lax.psum(sent, "dp")
        return lax.psum(kept, "dp")

    def middle(self, value):
        return lax.ppermute(value, "dp", MIDDLE) if self.four else value

    def last(self, value):
        return lax.ppermute(value, "dp", NEAR) if self.four else value

    def add(self, kept, got):
        return plus(kept, got) if self.four else got

    def end(self, kept, got):
        if not self.four:
            return jnp.concatenate([kept, self.rest], axis=0)
        return jnp.concatenate(
            [jnp.where(self.inner, kept, got), jnp.where(self.inner, got, kept)], axis=0
        )


def together(*values):
    return lax.optimization_barrier(values)


def after(value, *before):
    return lax.optimization_barrier((value, before))[0]


def plus(a, b):
    return (a.astype(F32) + b.astype(F32)).astype(BF)


def block_at(value, index, count):
    return lax.dynamic_slice_in_dim(value, index * count, count, 0)


def merge_body(bounds, own, got, *outs):
    total = (own[...].astype(F32) + got[...].astype(F32)).astype(BF)
    for i in range(4):

        @pl.when(pl.program_id(0) == i)
        def _(i=i):
            outs[2 * i][...] = total[:, :512]
            outs[2 * i + 1][...] = total[:, 512:]


def merge(bounds, own, got):
    count = own.shape[0] // 4
    block = pl.BlockSpec((count, 1024), lambda i, b: (i ^ b[2], 0))
    once = pl.BlockSpec((count, 512), lambda i, b: (0, 0), pipeline_mode=pl.Buffered(1))
    return pl.pallas_call(
        merge_body,
        grid_spec=pltpu.PrefetchScalarGridSpec(
            num_scalar_prefetch=1,
            grid=(4,),
            in_specs=[block, block],
            out_specs=[once] * 8,
        ),
        out_shape=[jax.ShapeDtypeStruct((count, 512), BF)] * 8,
        compiler_params=params(),
        cost_estimate=SMALL_COST,
        name="merge",
    )(bounds, own, got)


def finish_body(bounds, l0, r0, l1, r1, l2, r2, tok, dhid, gain, out):
    three = lambda a, b, c: (a[...].astype(F32) + b[...]) + c[...]
    grad = jnp.concatenate([three(l0, l1, l2), three(r0, r1, r2)], axis=1)
    values = tok[...].astype(F32)
    scale = lax.rsqrt(jnp.mean(values * values, axis=-1, keepdims=True) + EPSILON)
    weighted = grad * gain[...]
    mean = jnp.mean(weighted * values, axis=-1, keepdims=True)
    total = dhid[...] + scale * weighted - values * (scale * scale * scale * mean)
    out[0] = total[:, :512].astype(BF)
    out[1] = total[:, 512:].astype(BF)


def finish(bounds, state, tokens, dhid, gain):
    count = dhid.shape[0]
    n = count // 2
    half = pl.BlockSpec((n, 512), lambda i, b: (i, 0))
    row = pl.BlockSpec((n, 1024), lambda i, b: (i, 0))
    return pl.pallas_call(
        finish_body,
        grid_spec=pltpu.PrefetchScalarGridSpec(
            num_scalar_prefetch=1,
            grid=(2,),
            in_specs=[half] * 6
            + [pl.BlockSpec((n, 1024), lambda i, b: (2 * b[2] + i, 0)), row, whole((1, 1024))],
            out_specs=pl.BlockSpec((2, n, 512), lambda i, b: (0, i, 0)),
        ),
        out_shape=jax.ShapeDtypeStruct((2, count, 512), BF),
        compiler_params=params(),
        cost_estimate=SMALL_COST,
        name="finish",
    )(bounds, *state, tokens, dhid, gain)


def rope_tables(count):
    exponent = np.arange(0, HEAD_SIZE, 2).astype(np.float32) / np.float32(HEAD_SIZE)
    frequency = (np.float32(ROPE_BASE) ** (-exponent)).astype(np.float32)
    angles = np.arange(count).astype(np.float32)[:, None] * frequency[None, :]
    angles = np.concatenate([angles] * 4, axis=1)
    return (np.cos(angles).astype(np.float32), np.sin(angles).astype(np.float32))


def local(
    tokens, doc_ids, norm_gain, q_proj, key_value_weight, o_proj, z_proj, x_proj, dt_proj,
    bc_proj, conv_x, xconv_bias, conv_bc, bcconv_bias, dt_bias, a_log, skip_gain, gated_gain,
    out_proj, mlp_gain, gate_proj, up_proj, down_proj, out_grad,
):
    t, c = lax.axis_index("tensor"), lax.axis_index("ctx")
    own_tokens, grad_out = tokens[0], out_grad[0]
    own = own_tokens.shape[0]
    full = 2 * own
    mine = own // 4
    other_tokens = twin(own_tokens)

    def cols(w):
        n = w.shape[-1] // 2
        return lax.dynamic_slice_in_dim(w, c * n, n, w.ndim - 1)

    def rows(w):
        return block_at(w, c, w.shape[0] // 2)

    here = jnp.stack([jnp.zeros((), jnp.int32), jnp.zeros((), jnp.int32), t, c]).astype(jnp.int32)
    weight, pack0 = prepare(
        here, gate_proj, up_proj, down_proj, out_proj, o_proj, key_value_weight, q_proj,
        x_proj, z_proj, dt_proj, bc_proj,
    )
    weight, pack0, doc_ids = together(weight, pack0, doc_ids)
    pack1, pack2 = swap(pack0, 1), swap(pack0, 2)
    docs = doc_ids[0]
    place_dp = lax.axis_index("dp")
    inner = (place_dp == 1) | (place_dp == 2) | (lax.axis_size("dp") != 4)
    bounds = jnp.stack([jnp.sum(docs < 1), jnp.sum(docs < 2), t, c, inner]).astype(jnp.int32)
    own_gain = rows(gated_gain)
    gain0 = jnp.concatenate([own_gain, jnp.ones((64,), F32)])
    gain0 = jnp.broadcast_to(gain0[None, None], (8, 1, 256))

    cos, sin = rope_tables(full)
    cos, sin = jnp.asarray(cos), jnp.asarray(sin)
    steps = own // PROJ_ROWS
    own_off = jnp.reshape(c * steps, (1,)).astype(jnp.int32)
    other_off = jnp.reshape((1 - c) * steps, (1,)).astype(jnp.int32)
    gain_row = norm_gain[None]
    first = project(own_off, own_tokens, gain_row, weight, cos, sin)
    normed, qp, kv, xbc, z, dt_raw = project(
        other_off, other_tokens, gain_row, weight, cos, sin, before=first
    )

    pad = lambda v: jnp.zeros(v.shape[:-1] + (64,), F32)
    cx, cb = cols(conv_x), cols(xconv_bias)
    taps = jnp.concatenate([cx, pad(cx), conv_bc], axis=1)
    taps = jnp.concatenate([taps, jnp.zeros_like(taps)], axis=0)
    bias = jnp.concatenate([cb, pad(cb), bcconv_bias])[None]
    head = jnp.stack([cols(dt_bias), -jnp.exp(cols(a_log))], axis=1)
    head = jnp.pad(head, ((0, 5), (0, 126)))
    skip = jnp.pad(jnp.repeat(cols(skip_gain), MP), (0, 64))[None]
    xbc, gain0 = together(xbc, gain0)
    gains = exchange(gain0)
    g01, g2, y, states = scan_forward(bounds, xbc, z, dt_raw, taps, bias, head, skip)
    g2, g01, pack1, pack2, gains = together(g2, g01, pack1, pack2, gains)
    left3, right3 = pack1[:, :512], pack2[:, 512:]
    qp, left3, right3, g01 = together(qp, left3, right3, g01)
    left3, right3 = swap(left3, 2), swap(right3, 1)
    near = [pack0, pack1, pack2]
    far = [twin(v) for v in near]
    g_rows = exchange(g01.reshape(8, mine, 128))
    tile, keep = attend(bounds, qp, kv, g2)
    tile, g_rows, far, left3, right3 = together(tile, g_rows, far, left3, right3)
    h_rows = exchange(tile.reshape(8, mine, 128))
    packs = near + [left3, right3] + far + [twin(left3), twin(right3)]

    res = row_stage(bounds, g_rows, h_rows, own_tokens, grad_out, mlp_gain[None], gains, packs)
    layer_rows, two, dmix, dhid = res[0:4]
    act, dgu, gn = list(res[4:6]), list(res[6:8]), list(res[8:10])
    mlp_part, gain_part = res[12:14]
    grad_rows = block_at(grad_out, t, mine)
    dn, late = exchange(res[10]), res[11]
    far_w = weight_stage(3, two, grad_rows, dmix, dgu[1], act[1], gn[1])
    far_v = weight_stage(2, two, grad_rows, dmix, dgu[1], act[1], gn[1])
    far_w, far_v = [twin(v) for v in far_w], [twin(v) for v in far_v]
    near_w = weight_stage(3, two, grad_rows, dmix, dgu[0], act[0], gn[0], *far_w)
    near_v = weight_stage(2, two, grad_rows, dmix, dgu[0], act[0], gn[0], *far_v)
    dn, near_w, near_v, late = together(dn, near_w, near_v, late)
    sum_a = [near_v[1], near_w[1], near_v[0], near_w[0]]
    sum_b = [near_v[3], near_w[3], near_v[2], near_w[2]]
    late = exchange(late)

    a3, b3 = swap(sum_a[3], 1), swap(sum_b[3], 2)
    a1, b2 = swap(sum_a[1], 1), swap(sum_b[2], 2)
    da = attend_back(bounds, qp, kv, keep, dn, cos, sin)
    da, a3, b3, late = together(da, a3, b3, late)
    a_next, b_next = pair_sum(sum_a[2], a3, sum_b[1], b3)
    xbc, a_next, b_next = together(xbc, a_next, b_next)
    a_next, b_next = swap(a_next, 2), swap(b_next, 1)
    own_gain_row = jnp.pad(own_gain, (0, 64))[None]
    zeros = [
        jnp.zeros((256, 128), F32),
        jnp.zeros((8, 512), F32),
        jnp.zeros((8, 512), F32),
        jnp.zeros((16, CHUNK), F32),
    ]
    back = lambda part, carry, made, data: scan_back(
        part, carry, made, bounds, data, z, y, dt_raw, states, late, dn, taps, bias, head, skip,
        own_gain_row,
    )
    ds, dt_grad, *carry = back(0, zeros, [], xbc)
    ds, a1, b2, a_next, b_next = together(ds, a1, b2, a_next, b_next)
    kept, out = piece_sum(bounds, (sum_a[0], a1, a_next), (sum_b[0], b2, b_next))
    sums, single = DpSum(), DpSum()
    xbc, out, kept, layer_rows = together(xbc, out, kept, layer_rows)
    got = sums.first(kept, out)
    layer1, layer2 = swap(layer_rows, 1), swap(layer_rows, 2)
    conv_carry = (carry[2], carry[3], carry[0], carry[1])
    ds, dt_grad, conv_acc, head_acc, _, _ = back(1, conv_carry, [ds, dt_grad], xbc)
    ds, got, layer1, layer2 = together(ds, got, layer1, layer2)

    kept = sums.add(kept, got)
    parts = [block_at(kept, i, kept.shape[0] // 4) for i in range(4)]
    layer3 = [layer1[0], layer2[1]]
    ds, layer3, parts, kept = together(ds, layer3, parts, kept)
    got0 = sums.middle(parts[0])
    layer3 = [swap(layer3[0], 2), swap(layer3[1], 1)]
    grad_other, gain_other = input_grad(other_off, da, ds, dt_grad, weight, normed)
    grad_other, ds, layer3, got0 = together(grad_other, ds, layer3, got0)
    four = lax.axis_size("dp") == 4
    sent = twin(grad_other)
    got1 = sums.middle(parts[1])
    grad_own, gain_own = input_grad(own_off, da, ds, dt_grad, weight, normed)
    grad_own, sent, got1 = together(grad_own, sent, got1)
    got2 = sums.middle(parts[2])
    pieces = merge(bounds, grad_own, sent)
    ds, got2, pieces = together(ds, got2, pieces)
    l0, r0, l1, r1, l2, r2, l3, r3 = pieces
    low_rows = sums.add(jnp.concatenate(parts[:2]), jnp.concatenate([got0, got1]))
    heads = jnp.concatenate(
        [
            jnp.sum(conv_acc[5, :192].reshape(3, 64), axis=1),
            jnp.sum(head_acc[0:3], axis=1),
            jnp.sum(head_acc[8:11], axis=1),
        ]
    )
    place = c * 4 + t
    own_small = jnp.pad(jnp.concatenate([conv_acc[:5, :192].reshape(-1), heads]), (0, 55))
    at_own = lax.dynamic_update_slice_in_dim(
        jnp.zeros((8, 1024), F32), own_small[None], place, 0
    )
    norm_part = (gain_other[0] + gain_own[0]) / norm_gain
    flat = jnp.concatenate(
        [at_own.reshape(-1), gain_part.reshape(-1), conv_acc[:5, 256:].reshape(-1), mlp_part[0]]
        + [norm_part]
    )
    flat = jnp.pad(flat, (0, (-flat.shape[0]) % 1024)).reshape(1, -1, 128)
    flat = jnp.broadcast_to(flat, (8,) + flat.shape[1:])
    ds, l0, r0, l1, r1, l2, r2, l3, r3, flat, low_rows = together(
        ds, l0, r0, l1, r1, l2, r2, l3, r3, flat, low_rows
    )
    l3, r3 = swap(l3, 1), swap(r3, 2)
    got3 = sums.middle(parts[3])
    got_low = sums.last(low_rows)
    flat = exchange(flat)
    alone, out, turned = alone_grad(bounds, normed, da, ds, dt_grad)
    alone, out, turned, l3, r3, got3, got_low, flat = together(
        alone, out, turned, l3, r3, got3, got_low, flat
    )
    l2, r1 = pair_sum(l2, l3, r1, r3)
    flat = jnp.sum(flat, axis=0)
    high_rows = sums.add(jnp.concatenate(parts[2:]), jnp.concatenate([got2, got3]))
    count = alone.shape[0]
    if four:
        out = jnp.concatenate([out, high_rows[:, :512], high_rows[:, 512:]])
    l1, r2, l2, r1, flat, out, alone, high_rows, turned = together(
        l1, r2, l2, r1, flat, out, alone, high_rows, turned
    )
    l2, r1 = swap(l2, 2), swap(r1, 1)
    l1, r2 = swap(l1, 1), swap(r2, 2)
    got = single.first(alone, out)
    shared = shared_grad(bounds, normed, da, ds, turned)
    l1, r2, l2, r1, got, shared = together(l1, r2, l2, r1, got, shared)
    if four:
        half = count + high_rows.shape[0]
        got_high = jnp.concatenate([got[count:half], got[half:]], axis=1)
    else:
        got_high = high_rows
    both = sums.end(
        jnp.concatenate([low_rows, high_rows]), jnp.concatenate([got_low, got_high])
    )
    got_alone = got[:count]
    token_rows = finish(bounds, [l0, r0, l1, r1, l2, r2], own_tokens, dhid, norm_gain[None])
    alone = single.add(alone, got_alone)
    shared = shared.reshape(8, 128, 512)
    token_rows, alone, both, flat, shared, layer_rows, layer1, layer2, layer3 = together(
        token_rows, alone, both, flat, shared, layer_rows, layer1, layer2, layer3
    )
    tok1, tok2 = swap(token_rows, 1), swap(token_rows, 2)
    got = single.middle(alone)
    twin_piece = twin(both)
    flat_got = dp_swap(flat, 1) if four else lax.psum(flat, "dp")
    shared = exchange(shared)
    layer_out = assemble(bounds, [layer_rows, layer1, layer2, *layer3])
    tok1, tok2, got, flat_got, twin_piece, shared, layer_out = together(
        tok1, tok2, got, flat_got, twin_piece, shared, layer_out
    )
    shared = jnp.sum(shared.astype(F32), axis=0).astype(BF)
    if four:
        shared = jnp.broadcast_to(shared[None], (4, 128, 512))
    flat = flat + flat_got if four else flat_got
    *tok3, total = relay(tok1, tok2, alone, got)
    alone = total if four else single.add(alone, got)
    tok3, alone, flat, twin_piece, shared = together(tok3, alone, flat, twin_piece, shared)
    tok3 = [swap(tok3[0], 2), swap(tok3[1], 1)]
    got = single.last(alone)
    flat_got = dp_swap(flat, 2) if four else flat
    if four:
        shared = lax.all_to_all(shared, "dp", 0, 0, tiled=True)
    else:
        shared = lax.psum(shared.astype(F32), "dp")[None]
    outs = piece_out(bounds, both, twin_piece)
    tok3, got, flat_got, outs, shared = together(tok3, got, flat_got, outs, shared)
    alone = single.end(alone, got)
    shared = jnp.sum(shared.astype(F32), axis=0).astype(BF)
    shared = jnp.broadcast_to(shared[None], (8, 128, 512))
    alone, tok3, shared = together(alone, tok3, shared)
    alone_twin = twin(alone)
    shared = exchange(shared)
    tokens_grad = assemble(bounds, [token_rows, tok1, tok2, *tok3])
    alone, alone_twin, tokens_grad = together(alone, alone_twin, tokens_grad)
    shared = shared.reshape(1024, 512).astype(F32)
    kv_out, bc_out = shared[:, :256], shared[:, 256:]
    q_out, z_out, x_out, dt_out = alone_out(bounds, alone, alone_twin)
    flat = flat + flat_got if four else flat_got
    flat = flat.reshape(-1)
    norm_sum = flat[12544:13568]
    small = flat[:8192].reshape(8, 1024)
    gain_sum = flat[8192:10240].reshape(8, 256)
    bc_sum = flat[10240:11520].reshape(5, 256)
    mlp_sum = flat[11520:12544]
    both_cores = lambda v: jnp.stack([lax.dynamic_index_in_dim(v, k * 4 + t, 0, False) for k in range(2)])
    small = both_cores(small)
    gain_sum = both_cores(gain_sum)[:, :192].reshape(-1)
    conv_small = small[:, :960].reshape(2, 5, 192)
    conv_small = jnp.concatenate([conv_small[0], conv_small[1]], axis=1)
    head_small = small[:, 960:969].reshape(2, 3, 3)
    per_head_sum = lambda i: head_small[:, i].reshape(-1)

    gate_out, up_out, down_out, mix_out, att_out = outs
    return (
        layer_out[None],
        tokens_grad[None],
        norm_sum,
        q_out,
        kv_out,
        att_out,
        z_out,
        x_out,
        dt_out,
        bc_out,
        conv_small[:4],
        conv_small[4],
        bc_sum[:4],
        bc_sum[4],
        per_head_sum(2),
        per_head_sum(1),
        per_head_sum(0),
        gain_sum,
        mix_out,
        mlp_sum,
        gate_out,
        up_out,
        down_out,
    )


def solution(mesh):
    placed = (
        P("dp", "ctx", None),
        P("dp", None),
        P(),
        P(None, "tensor"),
        P(),
        P("tensor", None),
        P(None, "tensor"),
        P(None, "tensor"),
        P(None, "tensor"),
        P(),
        P(None, "tensor"),
        P("tensor"),
        P(),
        P(),
        P("tensor"),
        P("tensor"),
        P("tensor"),
        P("tensor"),
        P("tensor", None),
        P(),
        P(None, "tensor"),
        P(None, "tensor"),
        P("tensor", None),
        P("dp", "ctx", None),
    )
    return jax.shard_map(
        local,
        mesh=mesh,
        in_specs=placed,
        out_specs=(
            P("dp", "ctx", None),
            P("dp", "ctx", None),
            P(),
            P(None, "tensor"),
            P(),
            P("tensor", None),
            P(None, "tensor"),
            P(None, "tensor"),
            P(None, "tensor"),
            P(),
            P(None, "tensor"),
            P("tensor"),
            P(),
            P(),
            P("tensor"),
            P("tensor"),
            P("tensor"),
            P("tensor"),
            P("tensor", None),
            P(),
            P(None, "tensor"),
            P(None, "tensor"),
            P("tensor", None),
        ),
        check_vma=False,
    )
```

```python
import functools

import jax
import numpy as np
import jax.numpy as jnp
from jax import lax
from jax.experimental import pallas as pl
from jax.experimental.pallas import tpu as pltpu
from jax.sharding import PartitionSpec as P

BF, F32 = jnp.bfloat16, jnp.float32
EPSILON = 1e-05
ROPE_BASE = 100000000000.0
HEAD_SIZE = 64
MP = 64
PROJ_ROWS = 256
BQ = 512
CHUNK = 256
VMEM_LIMIT = 48 * 1024 * 1024
FULL_VMEM = 60 * 1024 * 1024
SMALL_COST = pl.CostEstimate(flops=1000000, bytes_accessed=100000, transcendentals=0)


def dot(left, right, dims=((1,), (0,)), precision=None):
    return lax.dot_general(
        left, right, (dims, ((), ())), precision=precision, preferred_element_type=F32
    )


def dot_bt(left, right):
    return dot(left, right, ((1,), (1,)))


def dot_at(left, right):
    return dot(left, right, ((0,), (0,)))


def lanes(shape):
    return lax.broadcasted_iota(jnp.int32, shape, len(shape) - 1)


def rows_of(shape):
    return lax.broadcasted_iota(jnp.int32, shape, 0)


def doc_start(pos, first, second):
    return jnp.where(pos >= second, second, jnp.where(pos >= first, first, 0))


def halves(low, high):
    return jnp.where(lanes((1, 128)) < 64, low, high)


def params(**kw):
    return pltpu.CompilerParams(vmem_limit_bytes=VMEM_LIMIT, **kw)


def whole(shape):
    return pl.BlockSpec(shape, lambda *_: (0,) * len(shape))


def proj_body(off, tok, gain, weight, cos, sin, *refs):
    normed_ref, qp_ref, kv_ref, xbc_ref, z_ref, dt_ref = refs[-6:]
    values = tok[...].astype(F32)
    scale = lax.rsqrt(jnp.mean(values * values, axis=-1, keepdims=True) + EPSILON)
    normed = (values * scale * gain[...]).astype(BF)
    normed_ref[...] = normed
    c, s = cos[...], sin[...]
    left = lanes((1, 128)) < 64
    att = dot(normed, weight[:, :384])
    kv, turned, qd = att[:, :128], att[:, 128:256], att[:, 256:]
    kv_ref[...] = jnp.where(left, kv * c + turned * s, kv).astype(BF)
    q_rot = qd * c + pltpu.roll(turned, 64, 1) * s
    qp_ref[...] = jnp.where(left, q_rot.astype(BF) * 0.125, 0.0).astype(BF)
    dt_ref[...] = qd.T[64:72, :]
    ssm = dot(normed, weight[:, 384:])
    x2z2 = ssm[:, 128:256]
    xbc_ref[:, :128] = ssm[:, :128].astype(BF)
    xbc_ref[:, 128:256] = jnp.where(left, x2z2, 0.0).astype(BF)
    xbc_ref[:, 256:] = ssm[:, 384:].astype(BF)
    z_ref[:, :128] = ssm[:, 256:384]
    z_ref[:, 128:] = jnp.where(left, pltpu.roll(x2z2, 64, 1), 0.0)


def project(off, tokens, gain, weight, cos, sin, before=None):
    own = tokens.shape[0]
    full = cos.shape[0]
    n = PROJ_ROWS
    outs = [
        jax.ShapeDtypeStruct((full, 1024), BF),
        jax.ShapeDtypeStruct((full, 128), BF),
        jax.ShapeDtypeStruct((full, 128), BF),
        jax.ShapeDtypeStruct((full, 512), BF),
        jax.ShapeDtypeStruct((full, 256), F32),
        jax.ShapeDtypeStruct((8, full), F32),
    ]
    at = lambda i, off: (off[0] + i, 0)
    out_specs = [pl.BlockSpec((n, o.shape[1]), at) for o in outs[:5]]
    out_specs.append(pl.BlockSpec((8, n), lambda i, off: (0, off[0] + i)))
    in_specs = [
        pl.BlockSpec((n, 1024), lambda i, off: (i, 0)),
        whole((1, 1024)),
        whole((1024, 1024)),
        pl.BlockSpec((n, 128), at),
        pl.BlockSpec((n, 128), at),
    ]
    args = [off, tokens, gain, weight, cos, sin]
    alias = {}
    if before is not None:
        in_specs += [pl.BlockSpec(memory_space=pl.ANY)] * 6
        args += list(before)
        alias = {6 + i: i for i in range(6)}
    return pl.pallas_call(
        proj_body,
        grid_spec=pltpu.PrefetchScalarGridSpec(
            num_scalar_prefetch=1, grid=(own // n,), in_specs=in_specs, out_specs=out_specs
        ),
        out_shape=outs,
        input_output_aliases=alias,
        compiler_params=params(),
        cost_estimate=SMALL_COST,
        name="norm_project",
    )(*args)


def turned_lanes(value):
    low = lanes((1, 128)) % 64 < 32
    return jnp.where(low, -pltpu.roll(value, 96, 1), pltpu.roll(value, 32, 1))


def prep_body(bounds, gate, up, down, mix, att, kv, q, x, z, dt, bc, weight, pack):
    n = gate.shape[0]
    pack[:, :256] = gate[...]
    pack[:, 256:512] = up[...]
    pack[:, 512:768] = down[...].T
    pack[:, 768:] = jnp.concatenate([mix[...], att[...]], axis=0).T
    first, low_kv = bounds[3] == 0, bounds[2] // 2 == 0
    lane = lanes((1, 128))
    left = lane < 64
    tile = lambda ref, i: ref[:, 128 * i : 128 * i + 128].astype(F32)
    swapped = lambda v: pltpu.roll(v, 64, 1)
    keys, values = tile(kv, 0), tile(kv, 1)
    keys = jnp.where(low_kv, keys, swapped(keys))
    values = jnp.where(low_kv, swapped(values), values)
    query = tile(q, 0)
    query = jnp.where(first, query, swapped(query))
    steps = jnp.concatenate([dt[...].astype(F32), jnp.zeros((n, 122), F32)], axis=1)
    steps = jnp.where(lane < 3, jnp.where(first, steps, pltpu.roll(steps, 125, 1)), 0.0)

    def heads(ref):
        a, b, d = tile(ref, 0), tile(ref, 1), swapped(tile(ref, 2))
        return jnp.where(first, a, jnp.where(left, swapped(b), d)), jnp.where(first, b, d)

    x01, x2 = heads(x)
    z01, z2 = heads(z)
    tiles = [
        jnp.where(left, keys, values),
        jnp.where(left, turned_lanes(keys), swapped(turned_lanes(query))),
        jnp.where(left, query, swapped(steps)),
        x01,
        jnp.where(left, x2, swapped(z2)),
        z01,
    ]
    for i, value in enumerate(tiles):
        weight[:, 128 * i : 128 * i + 128] = value.astype(BF)
    weight[:, 768:] = bc[...]


def prepare(bounds, gate, up, down, mix, att, kv, q, x, z, dt, bc):
    n = 256
    row = lambda w: pl.BlockSpec((n, w), lambda i, b: (i, 0))
    col = lambda h: pl.BlockSpec((h, n), lambda i, b: (b[3], i))
    mine = pl.BlockSpec((n, 256), lambda i, b: (i, b[3]))
    return pl.pallas_call(
        prep_body,
        grid_spec=pltpu.PrefetchScalarGridSpec(
            num_scalar_prefetch=1,
            grid=(4,),
            in_specs=[mine, mine, col(256), col(192), col(64)]
            + [row(256), row(128), row(384), row(384), row(6), row(256)],
            out_specs=[row(1024), row(1024)],
        ),
        out_shape=[jax.ShapeDtypeStruct((1024, 1024), BF)] * 2,
        compiler_params=pltpu.CompilerParams(vmem_limit_bytes=FULL_VMEM),
        cost_estimate=SMALL_COST,
        name="prepare",
    )(bounds, gate, up, down, mix, att, kv, q, x, z, dt, bc)


def block_range(qi, bounds):
    first, second = bounds[0], bounds[1]
    q0 = qi * BQ
    low = doc_start(q0, first, second) // BQ
    inner = (doc_start(q0 + BQ - 1, first, second) + BQ - 1) // BQ
    return low, jnp.minimum(jnp.maximum(inner, low), qi)


def allowed_rows(qi, kb, bounds):
    q = qi * BQ + lanes((1, BQ))
    k = kb * BQ + rows_of((BQ, 1))
    return (k <= q) & (k >= doc_start(q, bounds[0], bounds[1]))


def allowed_keys(qi, kb, bounds):
    q = qi * BQ + rows_of((BQ, 1))
    k = kb * BQ + lanes((1, BQ))
    start = doc_start(q, bounds[0], bounds[1])
    return (k <= q) & (k >= start)


def attend_body(bounds, qp, kv, g2, out_ref, keep_ref):
    qi = pl.program_id(0)
    low, inner = block_range(qi, bounds)
    q = qp[...]

    def step(kb, carry, masked):
        top, total, acc = carry
        k = kv[pl.ds(pl.multiple_of(kb * BQ, BQ), BQ), :]
        s = dot_bt(q, k)
        if masked:
            s = jnp.where(allowed_keys(qi, kb, bounds), s, -1e30)
        new_top = jnp.maximum(top, jnp.max(s, axis=1, keepdims=True))
        p = jnp.exp(s - new_top)
        fade = jnp.exp(top - new_top)
        total = total * fade + jnp.sum(p, axis=1, keepdims=True)
        acc = acc * fade + dot(p.astype(BF), k)
        return new_top, total, acc

    carry = (jnp.full((BQ, 1), -1e30, F32), jnp.zeros((BQ, 1), F32), jnp.zeros((BQ, 128), F32))
    carry = lax.fori_loop(low, inner, lambda kb, c: step(kb, c, True), carry)
    carry = lax.fori_loop(inner, qi, lambda kb, c: step(kb, c, False), carry)
    top, total, acc = step(qi, carry, True)
    out = acc / total
    left = lanes((1, 128)) < 64
    out_ref[...] = jnp.where(left, g2[...], out.astype(BF))
    keep_ref[...] = jnp.where(left, top + jnp.log(total), out)


def attend(bounds, qp, kv, g2):
    full = qp.shape[0]
    block = pl.BlockSpec((BQ, 128), lambda i, *_: (i, 0))
    return pl.pallas_call(
        attend_body,
        grid_spec=pltpu.PrefetchScalarGridSpec(
            num_scalar_prefetch=1,
            grid=(full // BQ,),
            in_specs=[block, whole((full, 128)), block],
            out_specs=[block, block],
        ),
        out_shape=[
            jax.ShapeDtypeStruct((full, 128), BF),
            jax.ShapeDtypeStruct((full, 128), F32),
        ],
        compiler_params=params(),
        cost_estimate=SMALL_COST,
        name="attend",
    )(bounds, qp, kv, g2)


def attend_back_body(bounds, qp, kv, keep, grad, cos, sin, out_ref, acc_ref):
    blocks = pl.num_programs(0)
    qi = blocks - 1 - pl.program_id(0)
    left = lanes((1, 128)) < 64

    @pl.when(pl.program_id(0) == 0)
    def _():
        acc_ref[...] = jnp.zeros_like(acc_ref)

    low, inner = block_range(qi, bounds)
    q = qp[...]
    do = jnp.where(left, 0.0, grad[0].astype(F32))
    delta = jnp.sum(do * keep[...], axis=1, keepdims=True)
    do = do.astype(BF)
    stats = jnp.where(lanes((1, 128)) == 0, keep[...], delta).T
    lse, delta = stats[0:1, :], stats[1:2, :]

    def step(kb, dq, masked):
        at = pl.ds(pl.multiple_of(kb * BQ, BQ), BQ)
        k = kv[at, :]
        p = jnp.exp(dot_bt(k, q) - lse)
        if masked:
            p = jnp.where(allowed_rows(qi, kb, bounds), p, 0.0)
        ds = (p * (dot_bt(k, do) - delta)).astype(BF)
        acc_ref[at, :] += dot(ds, q) + dot(p.astype(BF), do)
        return dq + dot_at(ds, k)

    dq = jnp.zeros((BQ, 128), F32)
    dq = lax.fori_loop(low, inner, lambda kb, c: step(kb, c, True), dq)
    dq = lax.fori_loop(inner, qi, lambda kb, c: step(kb, c, False), dq)
    dq = step(qi, dq, True) * 0.125
    dkv = acc_ref[pl.ds(pl.multiple_of(qi * BQ, BQ), BQ), :]
    c, s = cos[...], sin[...]
    out_ref[:, :128] = jnp.where(left, dkv * c, dkv).astype(BF)
    out_ref[:, 128:256] = (jnp.where(left, dkv, pltpu.roll(dq, 64, 1)) * s).astype(BF)
    out_ref[:, 256:] = jnp.where(left, dq * c, 0.0).astype(BF)


def attend_back(bounds, qp, kv, keep, grad, cos, sin):
    full = qp.shape[0]
    n = full // BQ
    block = pl.BlockSpec((BQ, 128), lambda i, *_: (n - 1 - i, 0))
    return pl.pallas_call(
        attend_back_body,
        grid_spec=pltpu.PrefetchScalarGridSpec(
            num_scalar_prefetch=1,
            grid=(n,),
            in_specs=[
                block,
                whole((full, 128)),
                block,
                pl.BlockSpec((1, BQ, 128), lambda i, *_: (n - 1 - i, 0, 0)),
                block,
                block,
            ],
            out_specs=pl.BlockSpec((BQ, 384), lambda i, *_: (n - 1 - i, 0)),
            scratch_shapes=[pltpu.VMEM((full, 128), F32)],
        ),
        out_shape=jax.ShapeDtypeStruct((full, 384), BF),
        compiler_params=params(),
        cost_estimate=SMALL_COST,
        name="attend_back",
    )(bounds, qp, kv, keep, grad, cos, sin)


def tap_mask(first_row, count, shift, bounds):
    pos = first_row + rows_of((count, 1))
    return (pos - doc_start(pos, bounds[0], bounds[1]) >= shift).astype(F32)


def conv_taps(ext_ref, r0, bounds, taps, bias):
    pre = bias + taps[3:4, :] * ext_ref[pl.ds(8, CHUNK), :]
    for shift in (1, 2, 3):
        mask = tap_mask(r0, CHUNK, shift, bounds)
        pre = pre + taps[3 - shift : 4 - shift, :] * (ext_ref[pl.ds(8 - shift, CHUNK), :] * mask)
    return pre


def chunk_decay(r0, bounds, dt_raw, head, extra=None):
    lane = lanes((1, CHUNK))
    dt = jax.nn.softplus(dt_raw + head[:, 0:1])
    la = dt * head[:, 1:2]
    upper = (rows_of((CHUNK, CHUNK)) <= lanes((CHUNK, CHUNK))).astype(F32)
    cum = dot(la, upper, precision=lax.Precision.HIGHEST)
    rows = [cum, dt] if extra is None else [cum, dt, extra]
    used = 8 * len(rows)
    stacked = jnp.concatenate(rows + [jnp.zeros((CHUNK - used, CHUNK), F32)], axis=0).T
    cum_col, dt_col = stacked[:, 0:8], stacked[:, 8:16]
    pos = r0 + rows_of((CHUNK, 1))
    start = doc_start(pos, bounds[0], bounds[1])
    start_last = doc_start(r0 + CHUNK - 1, bounds[0], bounds[1])
    key = r0 + lane
    mask = (key <= pos) & (key >= start)
    enter = jnp.where(start < r0, jnp.exp(cum_col), 0.0)
    fade = jnp.where(pos >= start_last, jnp.exp(cum_last_row(cum_col) - cum_col), 0.0)
    keep = jnp.where(start_last < r0, jnp.exp(cum_last_row(cum_col)), 0.0)
    return dt, la, cum, dt_col, cum_col, mask, enter, fade, keep, stacked[:, 16:24]


def two_terms(value):
    high = value.astype(BF)
    return high, (value - high.astype(F32)).astype(BF)


def cum_last_row(cum_col):
    return cum_col[CHUNK - 1 : CHUNK, :]


def per_head(col):
    return halves(col[:, 0:1], col[:, 1:2]), col[:, 2:3]


def state_rows(keep):
    row = rows_of((256, 1))
    return jnp.where(row < 64, keep[:, 0:1], jnp.where(row < 128, keep[:, 1:2], keep[:, 2:3]))


def scan_body(
    bounds, xbc, z, dt_raw, taps, bias, head, skip, g01, g2, y_ref, s_ref, pre_ref, ext, state
):
    i = pl.program_id(0)
    r0 = i * CHUNK

    @pl.when(i == 0)
    def _():
        ext[pl.ds(0, 8), :] = jnp.zeros((8, 512), F32)
        state[...] = jnp.zeros_like(state)

    @pl.when(i > 0)
    def _():
        ext[pl.ds(0, 8), :] = ext[pl.ds(CHUNK, 8), :]

    ext[pl.ds(8, CHUNK), :] = xbc[...].astype(F32)
    pre = conv_taps(ext, r0, bounds, taps[...], bias[...])
    pre_ref[...] = pre
    conv = pre * jax.nn.sigmoid(pre)
    x01, x2 = conv[:, :128], conv[:, 128:256]
    b, c = conv[:, 256:384].astype(BF), conv[:, 384:].astype(BF)
    dt, la, cum, dt_col, cum_col, mask, enter, fade, keep, _ = chunk_decay(
        r0, bounds, dt_raw[...], head[...]
    )
    inner = dot_bt(c, b)
    x01b, x2b = x01.astype(BF), x2.astype(BF)
    ys = []
    for h in range(3):
        gap = cum_col[:, h : h + 1] - cum[h : h + 1, :]
        decay = jnp.exp(jnp.where(mask, gap, -1e30))
        m = (inner * decay * dt[h : h + 1, :]).astype(BF)
        ys.append(dot(m, x01b if h < 2 else x2b))
    s0 = state[...]
    s_ref[0] = s0
    s0b, s0c = two_terms(s0)
    carried = dot_bt(c, s0b) + dot_bt(c, s0c)
    e01, e2 = per_head(enter)
    y01 = halves(ys[0], ys[1]) + e01 * carried[:, :128] + skip[:, :128] * x01
    y2 = ys[2] + e2 * carried[:, 128:] + skip[:, 128:] * x2
    w01, w2 = per_head(fade * dt_col)
    xw = jnp.concatenate([(x01 * w01).astype(BF), (x2 * w2).astype(BF)], axis=1)
    state[...] = s0 * state_rows(keep) + dot_at(xw, b)
    y_ref[:, :128] = y01
    y_ref[:, 128:] = y2
    z01, z2 = z[:, :128], z[:, 128:]
    g01[...] = (y01 * (z01 * jax.nn.sigmoid(z01))).astype(BF)
    g2[...] = (y2 * (z2 * jax.nn.sigmoid(z2))).astype(BF)


def scan_forward(bounds, xbc, z, dt_raw, taps, bias, head, skip):
    full = xbc.shape[0]
    n = full // CHUNK
    row = lambda width: pl.BlockSpec((CHUNK, width), lambda i, *_: (i, 0))
    return pl.pallas_call(
        scan_body,
        grid_spec=pltpu.PrefetchScalarGridSpec(
            num_scalar_prefetch=1,
            grid=(n,),
            in_specs=[
                row(512),
                row(256),
                pl.BlockSpec((8, CHUNK), lambda i, *_: (0, i)),
                whole((8, 512)),
                whole((1, 512)),
                whole((8, 128)),
                whole((1, 256)),
            ],
            out_specs=[
                row(128),
                row(128),
                row(256),
                pl.BlockSpec((1, 256, 128), lambda i, *_: (i, 0, 0)),
                row(512),
            ],
            scratch_shapes=[pltpu.VMEM((CHUNK + 8, 512), F32), pltpu.VMEM((256, 128), F32)],
        ),
        out_shape=[
            jax.ShapeDtypeStruct((full, 128), BF),
            jax.ShapeDtypeStruct((full, 128), BF),
            jax.ShapeDtypeStruct((full, 256), F32),
            jax.ShapeDtypeStruct((n, 256, 128), F32),
            jax.ShapeDtypeStruct((full, 512), F32),
        ],
        compiler_params=params(),
        cost_estimate=SMALL_COST,
        name="scan_forward",
    )(bounds, xbc, z, dt_raw, taps, bias, head, skip)


def scalar_rows(terms):
    low = terms[0:2, :] + terms[2:4, :] + terms[4:6, :]
    high = terms[6:8, :] + terms[8:10, :] + terms[10:12, :]
    total = jnp.concatenate([low, high], axis=1)
    return jnp.concatenate([total, jnp.zeros((6, CHUNK), F32)], axis=0)


def scan_back_body(
    last, bounds, xbc, before, pre_ref, z, y, dt_raw, s0_ref, dn01, dn2, scal, taps, head, skip,
    gain,
    dstate_in, dext_in, acc_in, head_in, *refs,
):
    out_ref, dt_grad, acc, head_acc, dstate_out, dext_out, ext, dext, dstate = refs[-9:]
    step = pl.program_id(0)
    i = last - step
    r0 = i * CHUNK
    left = lanes((1, 128)) < 64

    @pl.when(step == 0)
    def _():
        dext[pl.ds(CHUNK, 8), :] = dext_in[...]
        dstate[...] = dstate_in[...]
        acc[...] = acc_in[...]
        head_acc[...] = head_in[...]

    @pl.when(step > 0)
    def _():
        dext[pl.ds(CHUNK, 8), :] = dext[pl.ds(0, 8), :]

    ext[pl.ds(0, 8), :] = before[...].astype(F32)[8:, :]
    ext[pl.ds(8, CHUNK), :] = xbc[...].astype(F32)
    weights = taps[...]
    pre = pre_ref[...]
    sig = jax.nn.sigmoid(pre)
    conv = pre * sig
    x01, x2 = conv[:, :128], conv[:, 128:256]
    b, c = conv[:, 256:384].astype(BF), conv[:, 384:].astype(BF)
    dt, la, cum, dt_col, cum_col, mask, enter, fade, keep, scalars = chunk_decay(
        r0, bounds, dt_raw[...], head[...], scalar_rows(scal[0].astype(F32))
    )
    row_scale, row_cross = scalars[:, 0:1], scalars[:, 1:2]

    def gate_back(dn, gain, zz, yy):
        s = jax.nn.sigmoid(zz)
        act = zz * s
        g = yy * act
        sent = g.astype(BF).astype(F32)
        ratio = jnp.where(g == 0.0, 1.0, sent / g)
        dg = (dn * gain * row_scale - sent * row_cross) * ratio
        return dg * act, dg * yy * (s + act * (1.0 - s))

    dy01, dz01 = gate_back(dn01[0].astype(F32), gain[:, :128], z[:, :128], y[:, :128])
    dy2, dz2 = gate_back(dn2[0].astype(F32), gain[:, 128:], z[:, 128:], y[:, 128:])
    dy2, dz2 = jnp.where(left, dy2, 0.0), jnp.where(left, dz2, 0.0)
    inner = dot_bt(b, c)
    x01b, x2b = x01.astype(BF), x2.astype(BF)
    dy01b, dy2b = dy01.astype(BF), dy2.astype(BF)
    zero = jnp.zeros_like(dy01b)
    parts = [(jnp.where(left, dy01b, zero), x01b), (jnp.where(left, zero, dy01b), x01b), (dy2b, x2b)]
    query = r0 + lanes((1, CHUNK))
    key = r0 + rows_of((CHUNK, 1))
    mask = (key <= query) & (key >= doc_start(query, bounds[0], bounds[1]))
    d_inner = jnp.zeros((CHUNK, CHUNK), F32)
    dxs, direct, row_sums = [], [], []
    for h in range(3):
        gap = cum[h : h + 1, :] - cum_col[:, h : h + 1]
        decay = jnp.exp(jnp.where(mask, gap, -1e30))
        dt_h = dt_col[:, h : h + 1]
        dyh, xh = parts[h]
        dm = dot_bt(xh, dyh)
        kept = inner * decay
        dxs.append(dot((kept * dt_h).astype(BF), dyh if h == 2 else dy01b))
        pulled = dm * kept
        d_inner = d_inner + dm * (decay * dt_h)
        direct.append(jnp.sum(pulled, axis=1, keepdims=True))
        row_sums.append(jnp.sum(pulled * dt_h, axis=0, keepdims=True))
    s0 = s0_ref[0]
    s0b, s0c = two_terms(s0)
    ds1 = dstate[...]
    ds1b, ds1c = two_terms(ds1)
    e01, e2 = per_head(enter)
    ey01, ey2 = dy01 * e01, dy2 * e2
    ey, eyc = two_terms(jnp.concatenate([ey01, ey2], axis=1))
    carried = dot_bt(c, s0b) + dot_bt(c, s0c)
    f01, f2 = per_head(fade)
    d01, d2 = per_head(dt_col)
    back = dot_bt(b, ds1b)
    fb01, fb2 = f01 * back[:, :128], f2 * back[:, 128:]
    xw = jnp.concatenate([(x01 * (f01 * d01)).astype(BF), (x2 * (f2 * d2)).astype(BF)], axis=1)
    d_innerb = d_inner.astype(BF)
    dc = dot_at(d_innerb, b) + dot(ey, s0b) + dot(eyc, s0b) + dot(ey, s0c)
    db = dot(d_innerb, c) + dot(xw, ds1b) + dot(xw, ds1c)
    dx01 = halves(dxs[0], dxs[1]) + d01 * fb01 + skip[:, :128] * dy01
    dx2 = dxs[2] + d2 * fb2 + skip[:, 128:] * dy2
    kept_rows = state_rows(keep)
    crossing = jnp.sum(ds1 * s0 * kept_rows, axis=1, keepdims=True)
    dstate[...] = ds1 * kept_rows + dot_at(ey, c) + dot_at(eyc, c)
    inter01, inter2 = ey01 * carried[:, :128], ey2 * carried[:, 128:]
    u01, u2 = x01 * fb01, x2 * fb2
    pick = lambda v, h: jnp.where(left if h == 0 else ~left, v, 0.0)
    side = lambda v01, v2, h: jnp.sum(pick(v01, h) if h < 2 else v2, axis=1, keepdims=True)
    lane = lanes((1, CHUNK))
    tile = jnp.zeros((CHUNK, CHUNK), F32)
    crossed = jnp.zeros((8, 1), F32)
    head_row = rows_of((8, 1))
    for h in range(3):
        u = side(u01, u2, h)
        pulled = u + direct[h]
        moved = side(inter01, inter2, h) - pulled * dt_col[:, h : h + 1]
        tile = jnp.where(lane == h, moved, jnp.where(lane == 8 + h, pulled, tile))
        total = jnp.sum(crossing[64 * h : 64 * h + 64, :], axis=0, keepdims=True)
        total = total + jnp.sum(u * dt_col[:, h : h + 1], axis=0, keepdims=True)
        crossed = jnp.where(head_row == h, total, crossed)
    tile = tile.T
    stack = lambda items: jnp.concatenate(items + [jnp.zeros((5, CHUNK), F32)], axis=0)
    dcum = tile[0:8, :] + stack(row_sums) + jnp.where(lane == CHUNK - 1, crossed, 0.0)
    lower = (rows_of((CHUNK, CHUNK)) >= lanes((CHUNK, CHUNK))).astype(F32)
    dla = dot(dcum, lower, precision=lax.Precision.HIGHEST)
    ddt = tile[8:16, :] + dla * head[:, 1:2]
    graw = ddt * jax.nn.sigmoid(dt_raw[...] + head[:, 0:1])
    dt_grad[...] = graw
    head_acc[0:8, :] += dla * la
    head_acc[8:16, :] += graw
    dpre = jnp.concatenate([dx01, dx2, db, dc], axis=1) * (sig + conv * (1.0 - sig))
    dext[pl.ds(0, CHUNK), :] = dpre
    din = weights[3:4, :] * dpre
    acc[3:4, :] += jnp.sum(dpre * ext[pl.ds(8, CHUNK), :], axis=0, keepdims=True)
    acc[4:5, :] += jnp.sum(dpre, axis=0, keepdims=True)
    acc[5:6, :128] += jnp.sum(dy01 * x01, axis=0, keepdims=True)
    acc[5:6, 128:256] += jnp.sum(dy2 * x2, axis=0, keepdims=True)
    for shift in (1, 2, 3):
        tap = 3 - shift
        now = tap_mask(r0, CHUNK, shift, bounds)
        acc[tap : tap + 1, :] += jnp.sum(
            dpre * (ext[pl.ds(8 - shift, CHUNK), :] * now), axis=0, keepdims=True
        )
        later = tap_mask(r0 + shift, CHUNK, shift, bounds)
        din = din + weights[tap : tap + 1, :] * (dext[pl.ds(shift, CHUNK), :] * later)
    out_ref[:, :128] = din[:, :128].astype(BF)
    out_ref[:, 128:256] = jnp.where(left, din[:, 128:256], pltpu.roll(dz2, 64, 1)).astype(BF)
    out_ref[:, 256:384] = dz01.astype(BF)
    out_ref[:, 384:] = din[:, 256:].astype(BF)

    @pl.when(step == pl.num_programs(0) - 1)
    def _():
        dstate_out[...] = dstate[...]
        dext_out[...] = dext[pl.ds(0, 8), :]


def scan_back(
    part, carry, before, bounds, xbc, pre, z, y, dt_raw, states, late, dn, taps, head, skip, gain
):
    full = xbc.shape[0]
    n = full // CHUNK
    half = n // 2
    last = n - 1 if part == 0 else half - 1
    row = lambda width: pl.BlockSpec((CHUNK, width), lambda i, *_: (last - i, 0))
    tall = CHUNK // 16
    per = n // 8
    sent = pl.BlockSpec((1, CHUNK, 128), lambda i, b: ((last - i) // per, (last - i) % per, 0))

    def terms(i, b):
        piece, rest = (last - i) // per, (last - i) % per
        return piece, per * (CHUNK // 16) + rest, 0

    carried = [whole((256, 128)), whole((8, 512)), whole((8, 512)), whole((16, CHUNK))]
    sds = jax.ShapeDtypeStruct
    args = [bounds, xbc, xbc, pre, z, y, dt_raw, states, late, dn, late, taps, head, skip, gain]
    args += list(carry) + list(before)
    alias = {len(args) - 2: 0, len(args) - 1: 1} if before else {}
    return pl.pallas_call(
        functools.partial(scan_back_body, last),
        grid_spec=pltpu.PrefetchScalarGridSpec(
            num_scalar_prefetch=1,
            grid=(half,),
            in_specs=[
                row(512),
                pl.BlockSpec((16, 512), lambda i, *_: (jnp.maximum((last - i) * tall - 1, 0), 0)),
                row(512),
                row(256),
                row(256),
                pl.BlockSpec((8, CHUNK), lambda i, *_: (0, last - i)),
                pl.BlockSpec((1, 256, 128), lambda i, *_: (last - i, 0, 0)),
                sent,
                sent,
                pl.BlockSpec((1, 16, 128), terms),
                whole((8, 512)),
                whole((8, 128)),
                whole((1, 256)),
                whole((1, 256)),
            ]
            + carried
            + [pl.BlockSpec(memory_space=pl.ANY)] * len(before),
            out_specs=[
                row(640),
                pl.BlockSpec((8, CHUNK), lambda i, *_: (0, last - i)),
                whole((8, 512)),
                whole((16, CHUNK)),
                whole((256, 128)),
                whole((8, 512)),
            ],
            scratch_shapes=[
                pltpu.VMEM((CHUNK + 8, 512), F32),
                pltpu.VMEM((CHUNK + 8, 512), F32),
                pltpu.VMEM((256, 128), F32),
            ],
        ),
        out_shape=[
            sds((full, 640), BF),
            sds((8, full), F32),
            sds((8, 512), F32),
            sds((16, CHUNK), F32),
            sds((256, 128), F32),
            sds((8, 512), F32),
        ],
        input_output_aliases=alias,
        compiler_params=params(),
        cost_estimate=SMALL_COST,
        name="scan_back",
    )(*args)


ROW_BLOCK = 256


def row_body(bounds, g, h, tok, gout, mlp_gain, gains, *refs):
    packs, refs = refs[:10], refs[10:]
    pa, pb, slots = [], [], []
    for k, base in enumerate((0, 5)):
        for r in range(4):
            first = packs[base + r]
            second = first.at[:, 512:] if r < 3 else packs[base + 4]
            pa.append(first.at[:, 0:512])
            pb.append(second)
            slots.append((bounds[3] ^ k) * 4 + (bounds[2] ^ r))
    gain_rows = [gains[slot] for slot in slots]
    out_ref, two_ref, dmix_ref, dhid_ref = refs[0:4]
    act_refs, dgu_refs, gn_refs = refs[4:6], refs[6:8], refs[8:10]
    dn, dn_late, mlp_acc, gain_acc = refs[10:14]
    step = pl.program_id(0)
    left = lanes((1, 128)) < 64
    width = 1536.0

    @pl.when(pl.program_id(0) == 0)
    def _():
        mlp_acc[...] = jnp.zeros_like(mlp_acc)
        gain_acc[...] = jnp.zeros_like(gain_acc)

    pieces = [(r, k) for k in range(2) for r in range(4)]

    def part(ref, s):
        return ref[slots[s]].astype(F32)

    squares = 0.0
    for s in range(8):
        first, second = part(g, s), part(h, s)
        squares = squares + first * first + jnp.where(left, second * second, 0.0)
    rg = lax.rsqrt(jnp.sum(squares, axis=1, keepdims=True) / width + EPSILON)
    mixed = 0.0
    for s, (r, k) in enumerate(pieces):
        gain = gain_rows[s]
        first = part(g, s) * rg * gain[:, :128]
        second = part(h, s)
        second = jnp.where(left, second * rg * gain[:, 128:], second)
        gn = jnp.concatenate([first.astype(BF), second.astype(BF)], axis=1)
        gn_refs[k][:, r * 256 : r * 256 + 256] = gn
        mixed = mixed + dot_bt(gn, pb[s][:, 256:])
    hidden = tok[...].astype(F32) + mixed
    scale = lax.rsqrt(jnp.mean(hidden * hidden, axis=-1, keepdims=True) + EPSILON)
    two = (hidden * scale * mlp_gain[...]).astype(BF)
    two_ref[...] = two
    grad = gout[...]
    ffn = 0.0
    dtwo = 0.0
    for s, (r, k) in enumerate(pieces):
        weight, down = pa[s][...], pb[s][:, :256]
        gu = dot(two, weight)
        gate, up = gu[:, :256], gu[:, 256:]
        sig = jax.nn.sigmoid(gate)
        silu = gate * sig
        act = (silu * up).astype(BF)
        act_refs[k][:, r * 256 : r * 256 + 256] = act
        ffn = ffn + dot_bt(act, down)
        dact = dot(grad, down)
        dgate = (dact * up * (sig + silu * (1.0 - sig))).astype(BF)
        dgu = jnp.concatenate([dgate, (dact * silu).astype(BF)], axis=1)
        dgu_refs[k][:, r * 512 : r * 512 + 512] = dgu
        dtwo = dtwo + dot_bt(dgu, weight)
    whole_out = (hidden + ffn).astype(BF)
    out_ref[0] = whole_out[:, :512]
    out_ref[1] = whole_out[:, 512:]
    weighted = dtwo * mlp_gain[...]
    mlp_acc[...] += jnp.sum(dtwo * (hidden * scale), axis=0, keepdims=True)
    mean = jnp.mean(weighted * hidden, axis=-1, keepdims=True)
    dhid = grad.astype(F32) + scale * weighted - hidden * (scale * scale * scale * mean)
    dhid_ref[...] = dhid
    dmix = dhid.astype(BF)
    dmix_ref[...] = dmix
    cross = 0.0
    for s, (r, k) in enumerate(pieces):
        dgn = dot(dmix, pb[s][:, 256:]).astype(BF)
        at = pl.ds(pl.multiple_of(step * ROW_BLOCK, ROW_BLOCK), ROW_BLOCK)
        dn[slots[s], at, :] = dgn[:, 128:]
        dn_late[slots[s], at, :] = dgn[:, :128]
        first, second = dgn[:, :128].astype(F32), dgn[:, 128:].astype(F32)
        gain = gain_rows[s]
        own1, own2 = part(g, s), jnp.where(left, part(h, s), 0.0)
        t1, t2 = first * own1, second * own2
        gain_acc[slots[s], :, :128] += jnp.sum(t1 * rg, axis=0, keepdims=True)
        gain_acc[slots[s], :, 128:] += jnp.sum(t2 * rg, axis=0, keepdims=True)
        cross = cross + t1 * gain[:, :128] + t2 * gain[:, 128:]
    cross = jnp.sum(cross, axis=1, keepdims=True) * (rg * rg * rg / width)
    lane = lanes((1, 128))
    tile = jnp.where(lane == 0, rg, jnp.where(lane == 1, cross, 0.0))
    pair = tile.T[0:2, :]
    high = pair.astype(BF)
    rest = pair - high.astype(F32)
    middle = rest.astype(BF)
    low = (rest - middle.astype(F32)).astype(BF)
    terms = [v.astype(F32) for v in (high, middle, low)]
    block = jnp.concatenate(
        [v[:, :128] for v in terms] + [v[:, 128:] for v in terms] + [jnp.zeros((4, 128), F32)],
        axis=0,
    ).astype(BF)
    for s in range(8):
        dn_late[s, pl.ds(pl.multiple_of(2 * ROW_BLOCK + step * 16, 16), 16), :] = block


def row_stage(bounds, g, h, tokens, gout, mlp_gain, gains, packs):
    n = ROW_BLOCK
    count = 2 * n
    row = lambda w: pl.BlockSpec((n, w), lambda i, b: (i, 0))
    part = pl.BlockSpec((n, 1024), lambda i, b: (2 * b[2] + i, 0))
    piece = pl.BlockSpec((8, n, 128), lambda i, b: (0, i, 0))
    once = lambda shape: pl.BlockSpec(
        shape, lambda i, b: (0,) * len(shape), pipeline_mode=pl.Buffered(1)
    )
    sds = jax.ShapeDtypeStruct
    widths = [1024] * 4 + [1024] * 2 + [2048] * 2 + [1024] * 2
    dtypes = [BF] * 3 + [F32] + [BF] * 6
    return pl.pallas_call(
        row_body,
        grid_spec=pltpu.PrefetchScalarGridSpec(
            num_scalar_prefetch=1,
            grid=(2,),
            in_specs=[piece, piece, part, part, whole((1, 1024)), whole((8, 1, 256))]
            + [once(p.shape) for p in packs],
            out_specs=[pl.BlockSpec((2, n, 512), lambda i, b: (0, i, 0))]
            + [row(w) for w in widths[1:]]
            + [once((8, count, 128)), once((8, count + 32, 128))]
            + [whole((1, 1024)), whole((8, 1, 256))],
        ),
        out_shape=[sds((2, count, 512), BF)]
        + [sds((count, w), d) for w, d in zip(widths[1:], dtypes[1:])]
        + [sds((8, count, 128), BF), sds((8, count + 32, 128), BF)]
        + [sds((1, 1024), F32), sds((8, 1, 256), F32)],
        compiler_params=pltpu.CompilerParams(vmem_limit_bytes=58 * 1024 * 1024),
        cost_estimate=SMALL_COST,
        name="row_stage",
    )(bounds, g, h, tokens, gout, mlp_gain, gains, *packs)


def weight_body(two, gout, dmix, dgu, act, gn, *refs):
    a = dot_at(two[...], dgu[...])
    b = jnp.concatenate([dot_at(gout[...], act[...]), dot_at(dmix[...], gn[...])], axis=1)
    if len(refs) == 2:
        refs[0][0] = a.astype(BF)
        refs[1][0] = b.astype(BF)
    else:
        a = (a + refs[0][0].astype(F32)).astype(BF)
        b = (b + refs[1][0].astype(F32)).astype(BF)
        for i in range(4):

            @pl.when(pl.program_id(0) == i)
            def _(i=i):
                refs[2 + i][...] = a
                refs[6 + i][...] = b


def weight_stage(two, gout, dmix, dgu, act, gn, *others):
    count = two.shape[0]
    col = lambda w: pl.BlockSpec((count, w), lambda i: (0, i))
    piece = pl.BlockSpec((1, 1024, 512), lambda i: (i, 0, 0))
    once = pl.BlockSpec((1024, 512), lambda i: (0, 0), pipeline_mode=pl.Buffered(1))
    sds = jax.ShapeDtypeStruct
    return pl.pallas_call(
        weight_body,
        grid=(4,),
        in_specs=[whole((count, 1024))] * 3
        + [col(512), col(256), col(256)]
        + [piece] * len(others),
        out_specs=[once] * 8 if others else [piece] * 2,
        out_shape=[sds((1024, 512), BF)] * 8 if others else [sds((4, 1024, 512), BF)] * 2,
        compiler_params=pltpu.CompilerParams(vmem_limit_bytes=FULL_VMEM),
        cost_estimate=SMALL_COST,
        name="weight_stage",
    )(two, gout, dmix, dgu, act, gn, *others)


def with_steps(da, dt_grad):
    count = da.shape[0]
    cols = jnp.concatenate([dt_grad, jnp.zeros((120, count), F32)], axis=0).T
    last = jnp.where(lanes((1, 128)) < 64, da[:, 256:].astype(F32), pltpu.roll(cols, 64, 1))
    return jnp.concatenate([da[:, :256], last.astype(BF)], axis=1)


def input_grad_body(off, da, ds, dt_grad, weight, normed, out_ref, gain_ref):
    left = with_steps(da[...], dt_grad[...])
    grad = dot_bt(left, weight[:, :384]) + dot_bt(ds[...], weight[:, 384:])
    out_ref[...] = grad.astype(BF)

    @pl.when(pl.program_id(0) == 0)
    def _():
        gain_ref[...] = jnp.zeros_like(gain_ref)

    gain_ref[...] += jnp.sum(grad * normed[...].astype(F32), axis=0, keepdims=True)


def input_grad(off, da, ds, dt_grad, weight, normed):
    n = PROJ_ROWS
    own = ds.shape[0] // 2
    at = lambda i, off: (off[0] + i, 0)
    return pl.pallas_call(
        input_grad_body,
        grid_spec=pltpu.PrefetchScalarGridSpec(
            num_scalar_prefetch=1,
            grid=(own // n,),
            in_specs=[
                pl.BlockSpec((n, 384), at),
                pl.BlockSpec((n, 640), at),
                pl.BlockSpec((8, n), lambda i, off: (0, off[0] + i)),
                whole((1024, 1024)),
                pl.BlockSpec((n, 1024), at),
            ],
            out_specs=[pl.BlockSpec((n, 1024), lambda i, off: (i, 0)), whole((1, 1024))],
        ),
        out_shape=[
            jax.ShapeDtypeStruct((own, 1024), BF),
            jax.ShapeDtypeStruct((1, 1024), F32),
        ],
        compiler_params=params(),
        cost_estimate=SMALL_COST,
        name="input_grad",
    )(off, da, ds, dt_grad, weight, normed)


def turned_back(value):
    low = lanes((1, 128)) % 64 < 32
    return jnp.where(low, pltpu.roll(value, 96, 1), -pltpu.roll(value, 32, 1))


def shared_grad_body(bounds, normed, da, ds1, ds2, turned, shared, acc):
    @pl.when(pl.program_id(0) == 0)
    def _():
        acc[...] = jnp.zeros_like(acc)

    cols = jnp.concatenate([da[...], ds1[...], ds2[...]], axis=1)
    acc[...] += dot_at(normed[...], cols)

    @pl.when(pl.program_id(0) == pl.num_programs(0) - 1)
    def _():
        left = lanes((1, 128)) < 64
        kv = acc[:, :128] + jnp.where(left, turned_back(turned[...]), 0.0)
        low = bounds[2] // 2 == 0
        swapped = pltpu.roll(kv, 64, 1)
        keys = jnp.where(left == low, jnp.where(low, kv, swapped), 0.0)
        values = jnp.where(left == low, jnp.where(low, swapped, kv), 0.0)
        shared[:, :128] = keys.astype(BF)
        shared[:, 128:256] = values.astype(BF)
        shared[:, 256:] = acc[:, 128:].astype(BF)


def shared_grad(bounds, normed, da, ds, turned):
    full = normed.shape[0]
    n = 512
    part = lambda w, col: pl.BlockSpec((n, w), lambda i, *_: (i, col))
    return pl.pallas_call(
        shared_grad_body,
        grid_spec=pltpu.PrefetchScalarGridSpec(
            num_scalar_prefetch=1,
            grid=(full // n,),
            in_specs=[part(1024, 0), part(128, 0), part(128, 3), part(128, 4)]
            + [whole((1024, 128))],
            out_specs=whole((1024, 512)),
            scratch_shapes=[pltpu.VMEM((1024, 384), F32)],
        ),
        out_shape=jax.ShapeDtypeStruct((1024, 512), BF),
        compiler_params=params(),
        cost_estimate=SMALL_COST,
        name="shared_grad",
    )(bounds, normed, da, ds, ds, turned)


def alone_grad_body(bounds, normed, da1, da2, ds, dt_grad, kept, sent, turned, acc):
    @pl.when(pl.program_id(0) == 0)
    def _():
        acc[...] = jnp.zeros_like(acc)

    count = da1.shape[0]
    cols = jnp.concatenate([dt_grad[...], jnp.zeros((120, count), F32)], axis=0).T
    last = jnp.where(lanes((1, 128)) < 64, da2[...].astype(F32), pltpu.roll(cols, 64, 1))
    acc[...] += dot_at(
        normed[...], jnp.concatenate([last.astype(BF), ds[...], da1[...]], axis=1)
    )

    @pl.when(pl.program_id(0) == pl.num_programs(0) - 1)
    def _():
        left = lanes((1, 128)) < 64
        side = acc[:, 512:]
        turned[...] = side
        query = jnp.where(left, pltpu.roll(turned_back(side), 64, 1), 0.0)
        first = (acc[:, :128] + query).astype(BF)
        half = first.shape[0] // 2

        def write(ref, low):
            ref[:, :128] = first[low : low + half]
            ref[:, 128:] = acc[pl.ds(low, half), 128:512].astype(BF)

        @pl.when(bounds[4] == 1)
        def _():
            write(kept, 0)
            write(sent, half)

        @pl.when(bounds[4] == 0)
        def _():
            write(kept, half)
            write(sent, 0)


def alone_grad(bounds, normed, da, ds, dt_grad):
    full = normed.shape[0]
    n = 512
    part = lambda w, col: pl.BlockSpec((n, w), lambda i, *_: (i, col))
    return pl.pallas_call(
        alone_grad_body,
        grid_spec=pltpu.PrefetchScalarGridSpec(
            num_scalar_prefetch=1,
            grid=(full // n,),
            in_specs=[
                part(1024, 0),
                part(128, 1),
                part(128, 2),
                part(384, 0),
                pl.BlockSpec((8, n), lambda i, *_: (0, i)),
            ],
            out_specs=[whole((512, 512))] * 2 + [whole((1024, 128))],
            scratch_shapes=[pltpu.VMEM((1024, 640), F32)],
        ),
        out_shape=[
            jax.ShapeDtypeStruct((512, 512), BF),
            jax.ShapeDtypeStruct((512, 512), BF),
            jax.ShapeDtypeStruct((1024, 128), F32),
        ],
        compiler_params=params(),
        cost_estimate=SMALL_COST,
        name="alone_grad",
    )(bounds, normed, da, da, ds, dt_grad)


def assemble_body(bounds, p0, p1, p2, l3, r3, out):
    step = pl.program_id(0)
    for r, ref in enumerate((p0, p1, p2)):

        @pl.when(step == r)
        def _(ref=ref):
            out[:, :512] = ref[0]
            out[:, 512:] = ref[1]

    @pl.when(step == 3)
    def _():
        out[:, :512] = l3[...]
        out[:, 512:] = r3[...]


def assemble(bounds, parts):
    count = parts[0].shape[1]
    return pl.pallas_call(
        assemble_body,
        grid_spec=pltpu.PrefetchScalarGridSpec(
            num_scalar_prefetch=1,
            grid=(4,),
            in_specs=[whole(p.shape) for p in parts],
            out_specs=pl.BlockSpec((count, 1024), lambda i, b: (i ^ b[2], 0)),
        ),
        out_shape=jax.ShapeDtypeStruct((4 * count, 1024), parts[0].dtype),
        compiler_params=pltpu.CompilerParams(vmem_limit_bytes=FULL_VMEM),
        cost_estimate=SMALL_COST,
        name="assemble",
    )(bounds, *parts)


def piece_out_body(bounds, a, b, other_a, other_b, gate, up, down, mix, att):
    first = bounds[3] == 0

    def pair(own, other):
        own, other = own.astype(F32), other.astype(F32)
        return jnp.where(first, own, other), jnp.where(first, other, own)

    low, high = pair(a[...], other_a[...])
    gate[:, :256], gate[:, 256:] = low[:, :256], high[:, :256]
    up[:, :256], up[:, 256:] = low[:, 256:], high[:, 256:]
    low, high = pair(b[...], other_b[...])
    down[:256, :], down[256:, :] = low[:, :256].T, high[:, :256].T
    low, high = low[:, 256:].T, high[:, 256:].T
    mix[:192, :], mix[192:, :] = low[:192], high[:192]
    att[:64, :], att[64:, :] = low[192:], high[192:]


def piece_out(bounds, both, other):
    n = 256
    row = pl.BlockSpec((n, 512), lambda i, *_: (i, 0))
    second = pl.BlockSpec((n, 512), lambda i, *_: (i, 1))
    col = lambda h: pl.BlockSpec((h, n), lambda i, *_: (0, i))
    sds = jax.ShapeDtypeStruct
    return pl.pallas_call(
        piece_out_body,
        grid_spec=pltpu.PrefetchScalarGridSpec(
            num_scalar_prefetch=1,
            grid=(4,),
            in_specs=[row, second, row, second],
            out_specs=[row, row, col(512), col(384), col(128)],
        ),
        out_shape=[
            sds((1024, 512), F32),
            sds((1024, 512), F32),
            sds((512, 1024), F32),
            sds((384, 1024), F32),
            sds((128, 1024), F32),
        ],
        compiler_params=params(),
        cost_estimate=SMALL_COST,
        name="piece_out",
    )(bounds, both, both, other, other)


def alone_out_body(bounds, own, other, q, z, x, dt):
    first = bounds[3] == 0
    lane = lanes((1, 128))
    left = lane < 64
    tile = lambda ref, i: ref[:, 128 * i : 128 * i + 128].astype(F32)
    u = [jnp.where(first, tile(own, i), tile(other, i)) for i in range(4)]
    v = [jnp.where(first, tile(other, i), tile(own, i)) for i in range(4)]
    swapped = lambda value: pltpu.roll(value, 64, 1)
    q[...] = jnp.where(left, u[0], swapped(v[0]))
    x[:, :128] = u[1]
    x[:, 128:256] = jnp.where(left, u[2], swapped(v[1]))
    x[:, 256:] = jnp.where(left, swapped(v[1]), swapped(v[2]))
    z[:, :128] = u[3]
    z[:, 128:256] = jnp.where(left, swapped(u[2]), swapped(v[3]))
    z[:, 256:] = jnp.where(left, swapped(v[3]), v[2])
    dt[...] = jnp.where(lane < 3, swapped(u[0]), pltpu.roll(v[0], 67, 1))[:, :6]


def alone_out(bounds, own, other):
    n = 256
    row = lambda w: pl.BlockSpec((n, w), lambda i, *_: (i, 0))
    widths = [128, 384, 384, 6]
    return pl.pallas_call(
        alone_out_body,
        grid_spec=pltpu.PrefetchScalarGridSpec(
            num_scalar_prefetch=1,
            grid=(4,),
            in_specs=[row(512), row(512)],
            out_specs=[row(w) for w in widths],
        ),
        out_shape=[jax.ShapeDtypeStruct((1024, w), F32) for w in widths],
        compiler_params=params(),
        cost_estimate=SMALL_COST,
        name="alone_out",
    )(bounds, own, other)


def piece_sum_body(bounds, *refs):
    total = lambda i: (
        refs[i][...].astype(F32) + refs[i + 1][...] + refs[i + 2][...]
    ).astype(BF)
    kept, out = refs[12:]
    for group, ref in ((0, kept), (6, out)):
        ref[:, :512] = total(group)
        ref[:, 512:] = total(group + 3)


def piece_sum(bounds, a, b):
    n = 256
    keep = pl.BlockSpec((n, 512), lambda i, s: (i + 2 - 2 * s[4], 0))
    send = pl.BlockSpec((n, 512), lambda i, s: (i + 2 * s[4], 0))
    row = pl.BlockSpec((n, 1024), lambda i, s: (i, 0))
    return pl.pallas_call(
        piece_sum_body,
        grid_spec=pltpu.PrefetchScalarGridSpec(
            num_scalar_prefetch=1,
            grid=(2,),
            in_specs=[keep] * 6 + [send] * 6,
            out_specs=[row, row],
        ),
        out_shape=[jax.ShapeDtypeStruct((512, 1024), BF)] * 2,
        compiler_params=params(),
        cost_estimate=SMALL_COST,
        name="piece_sum",
    )(bounds, *a, *b, *a, *b)


def relay_body(first, second, kept, got, left, right, total):
    left[...] = first[0]
    right[...] = second[0]
    total[...] = (kept[...].astype(F32) + got[...]).astype(BF)


def relay(first, second, kept, got):
    n = first.shape[1] // 2
    row = pl.BlockSpec((n, 512), lambda i: (i, 0))
    half = lambda k: pl.BlockSpec((1, n, 512), lambda i: (k, i, 0))
    return pl.pallas_call(
        relay_body,
        grid=(2,),
        in_specs=[half(0), half(1), row, row],
        out_specs=[row] * 3,
        out_shape=[jax.ShapeDtypeStruct((2 * n, 512), BF)] * 3,
        compiler_params=pltpu.CompilerParams(vmem_limit_bytes=FULL_VMEM),
        cost_estimate=SMALL_COST,
        name="relay",
    )(first, second, kept, got)


def halves_body(first, second, left, right):
    left[...] = first[...]
    right[...] = second[...]


def pack_halves(first, second):
    n = 256
    out = pl.BlockSpec((n, 512), lambda i: (i, 0))
    return pl.pallas_call(
        halves_body,
        grid=(4,),
        in_specs=[out, pl.BlockSpec((n, 512), lambda i: (i, 1))],
        out_specs=[out, out],
        out_shape=[jax.ShapeDtypeStruct((1024, 512), BF)] * 2,
        compiler_params=pltpu.CompilerParams(vmem_limit_bytes=FULL_VMEM),
        cost_estimate=SMALL_COST,
        name="pack_halves",
    )(first, second)


def pair_sum_body(a, b, c, d, first, second):
    first[...] = (a[...].astype(F32) + b[...]).astype(BF)
    second[...] = (c[...].astype(F32) + d[...]).astype(BF)


def pair_sum(a, b, c, d):
    n = a.shape[0] // 2
    row = pl.BlockSpec((n, a.shape[1]), lambda i: (i, 0))
    return pl.pallas_call(
        pair_sum_body,
        grid=(2,),
        in_specs=[row] * 4,
        out_specs=[row, row],
        out_shape=[jax.ShapeDtypeStruct(a.shape, BF)] * 2,
        compiler_params=pltpu.CompilerParams(vmem_limit_bytes=FULL_VMEM),
        cost_estimate=SMALL_COST,
        name="pair_sum",
    )(a, b, c, d)


def swap(value, step):
    return lax.ppermute(value, "tensor", [(i, i ^ step) for i in range(4)])


def twin(value):
    return lax.ppermute(value, "ctx", [(0, 1), (1, 0)])


def exchange(value):
    return lax.all_to_all(value, ("ctx", "tensor"), 0, 0, tiled=True)


def dp_swap(value, step):
    return lax.ppermute(value, "dp", [(i, i ^ step) for i in range(4)])


MIDDLE = [(1, 2), (2, 1), (0, 3), (3, 0)]
NEAR = [(0, 1), (1, 0), (2, 3), (3, 2)]


class DpSum:
    def __init__(self):
        self.four = lax.axis_size("dp") == 4
        place = lax.axis_index("dp")
        self.inner = (place == 1) | (place == 2)

    def first(self, kept, sent):
        if self.four:
            return lax.ppermute(sent, "dp", NEAR)
        self.rest = lax.psum(sent, "dp")
        return lax.psum(kept, "dp")

    def middle(self, value):
        return lax.ppermute(value, "dp", MIDDLE) if self.four else value

    def last(self, value):
        return lax.ppermute(value, "dp", NEAR) if self.four else value

    def add(self, kept, got):
        return plus(kept, got) if self.four else got

    def end(self, kept, got):
        if not self.four:
            return jnp.concatenate([kept, self.rest], axis=0)
        return jnp.concatenate(
            [jnp.where(self.inner, kept, got), jnp.where(self.inner, got, kept)], axis=0
        )


def together(*values):
    return lax.optimization_barrier(values)


def after(value, *before):
    return lax.optimization_barrier((value, before))[0]


def plus(a, b):
    return (a.astype(F32) + b.astype(F32)).astype(BF)


def block_at(value, index, count):
    return lax.dynamic_slice_in_dim(value, index * count, count, 0)


def merge_body(bounds, own, got, *outs):
    total = (own[...].astype(F32) + got[...].astype(F32)).astype(BF)
    for i in range(4):

        @pl.when(pl.program_id(0) == i)
        def _(i=i):
            outs[2 * i][...] = total[:, :512]
            outs[2 * i + 1][...] = total[:, 512:]


def merge(bounds, own, got):
    count = own.shape[0] // 4
    block = pl.BlockSpec((count, 1024), lambda i, b: (i ^ b[2], 0))
    once = pl.BlockSpec((count, 512), lambda i, b: (0, 0), pipeline_mode=pl.Buffered(1))
    return pl.pallas_call(
        merge_body,
        grid_spec=pltpu.PrefetchScalarGridSpec(
            num_scalar_prefetch=1,
            grid=(4,),
            in_specs=[block, block],
            out_specs=[once] * 8,
        ),
        out_shape=[jax.ShapeDtypeStruct((count, 512), BF)] * 8,
        compiler_params=params(),
        cost_estimate=SMALL_COST,
        name="merge",
    )(bounds, own, got)


def finish_body(bounds, l0, r0, l1, r1, l2, r2, tok, dhid, gain, out):
    three = lambda a, b, c: (a[...].astype(F32) + b[...]) + c[...]
    grad = jnp.concatenate([three(l0, l1, l2), three(r0, r1, r2)], axis=1)
    values = tok[...].astype(F32)
    scale = lax.rsqrt(jnp.mean(values * values, axis=-1, keepdims=True) + EPSILON)
    weighted = grad * gain[...]
    mean = jnp.mean(weighted * values, axis=-1, keepdims=True)
    total = dhid[...] + scale * weighted - values * (scale * scale * scale * mean)
    out[0] = total[:, :512].astype(BF)
    out[1] = total[:, 512:].astype(BF)


def finish(bounds, state, tokens, dhid, gain):
    count = dhid.shape[0]
    n = count // 2
    half = pl.BlockSpec((n, 512), lambda i, b: (i, 0))
    row = pl.BlockSpec((n, 1024), lambda i, b: (i, 0))
    return pl.pallas_call(
        finish_body,
        grid_spec=pltpu.PrefetchScalarGridSpec(
            num_scalar_prefetch=1,
            grid=(2,),
            in_specs=[half] * 6
            + [pl.BlockSpec((n, 1024), lambda i, b: (2 * b[2] + i, 0)), row, whole((1, 1024))],
            out_specs=pl.BlockSpec((2, n, 512), lambda i, b: (0, i, 0)),
        ),
        out_shape=jax.ShapeDtypeStruct((2, count, 512), BF),
        compiler_params=params(),
        cost_estimate=SMALL_COST,
        name="finish",
    )(bounds, *state, tokens, dhid, gain)


def rope_tables(count):
    exponent = np.arange(0, HEAD_SIZE, 2).astype(np.float32) / np.float32(HEAD_SIZE)
    frequency = (np.float32(ROPE_BASE) ** (-exponent)).astype(np.float32)
    angles = np.arange(count).astype(np.float32)[:, None] * frequency[None, :]
    angles = np.concatenate([angles] * 4, axis=1)
    return (np.cos(angles).astype(np.float32), np.sin(angles).astype(np.float32))


def local(
    tokens, doc_ids, norm_gain, q_proj, key_value_weight, o_proj, z_proj, x_proj, dt_proj,
    bc_proj, conv_x, xconv_bias, conv_bc, bcconv_bias, dt_bias, a_log, skip_gain, gated_gain,
    out_proj, mlp_gain, gate_proj, up_proj, down_proj, out_grad,
):
    t, c = lax.axis_index("tensor"), lax.axis_index("ctx")
    own_tokens, grad_out = tokens[0], out_grad[0]
    own = own_tokens.shape[0]
    full = 2 * own
    mine = own // 4
    other_tokens = twin(own_tokens)

    def cols(w):
        n = w.shape[-1] // 2
        return lax.dynamic_slice_in_dim(w, c * n, n, w.ndim - 1)

    def rows(w):
        return block_at(w, c, w.shape[0] // 2)

    here = jnp.stack([jnp.zeros((), jnp.int32), jnp.zeros((), jnp.int32), t, c]).astype(jnp.int32)
    weight, pack0 = prepare(
        here, gate_proj, up_proj, down_proj, out_proj, o_proj, key_value_weight, q_proj,
        x_proj, z_proj, dt_proj, bc_proj,
    )
    weight, pack0, doc_ids = together(weight, pack0, doc_ids)
    pack1, pack2 = swap(pack0, 1), swap(pack0, 2)
    docs = doc_ids[0]
    place_dp = lax.axis_index("dp")
    inner = (place_dp == 1) | (place_dp == 2) | (lax.axis_size("dp") != 4)
    bounds = jnp.stack([jnp.sum(docs < 1), jnp.sum(docs < 2), t, c, inner]).astype(jnp.int32)
    own_gain = rows(gated_gain)
    gain0 = jnp.concatenate([own_gain, jnp.ones((64,), F32)])
    gain0 = jnp.broadcast_to(gain0[None, None], (8, 1, 256))

    cos, sin = rope_tables(full)
    cos, sin = jnp.asarray(cos), jnp.asarray(sin)
    steps = own // PROJ_ROWS
    own_off = jnp.reshape(c * steps, (1,)).astype(jnp.int32)
    other_off = jnp.reshape((1 - c) * steps, (1,)).astype(jnp.int32)
    gain_row = norm_gain[None]
    first = project(own_off, own_tokens, gain_row, weight, cos, sin)
    normed, qp, kv, xbc, z, dt_raw = project(
        other_off, other_tokens, gain_row, weight, cos, sin, before=first
    )

    pad = lambda v: jnp.zeros(v.shape[:-1] + (64,), F32)
    cx, cb = cols(conv_x), cols(xconv_bias)
    taps = jnp.concatenate([cx, pad(cx), conv_bc], axis=1)
    taps = jnp.concatenate([taps, jnp.zeros_like(taps)], axis=0)
    bias = jnp.concatenate([cb, pad(cb), bcconv_bias])[None]
    head = jnp.stack([cols(dt_bias), -jnp.exp(cols(a_log))], axis=1)
    head = jnp.pad(head, ((0, 5), (0, 126)))
    skip = jnp.pad(jnp.repeat(cols(skip_gain), MP), (0, 64))[None]
    xbc, gain0 = together(xbc, gain0)
    gains = exchange(gain0)
    g01, g2, y, states, pre = scan_forward(bounds, xbc, z, dt_raw, taps, bias, head, skip)
    g2, g01, pack1, pack2, gains = together(g2, g01, pack1, pack2, gains)
    left3, right3 = pack_halves(pack1, pack2)
    qp, left3, right3, g01 = together(qp, left3, right3, g01)
    left3, right3 = swap(left3, 2), swap(right3, 1)
    near = [pack0, pack1, pack2]
    far = [twin(v) for v in near]
    g_rows = exchange(g01.reshape(8, mine, 128))
    tile, keep = attend(bounds, qp, kv, g2)
    tile, g_rows, far, left3, right3 = together(tile, g_rows, far, left3, right3)
    h_rows = exchange(tile.reshape(8, mine, 128))
    packs = near + [left3, right3] + far + [twin(left3), twin(right3)]

    res = row_stage(bounds, g_rows, h_rows, own_tokens, grad_out, mlp_gain[None], gains, packs)
    layer_rows, two, dmix, dhid = res[0:4]
    act, dgu, gn = list(res[4:6]), list(res[6:8]), list(res[8:10])
    mlp_part, gain_part = res[12:14]
    grad_rows = block_at(grad_out, t, mine)
    dn, late = exchange(res[10]), res[11]
    far_w = weight_stage(two, grad_rows, dmix, dgu[1], act[1], gn[1])
    far_w = [twin(v) for v in far_w]
    near_w = weight_stage(two, grad_rows, dmix, dgu[0], act[0], gn[0], *far_w)
    dn, near_w, late = together(dn, near_w, late)
    sum_a, sum_b = near_w[:4], near_w[4:]
    late = exchange(late)

    a3, b3 = swap(sum_a[3], 1), swap(sum_b[3], 2)
    a1, b2 = swap(sum_a[1], 1), swap(sum_b[2], 2)
    da = attend_back(bounds, qp, kv, keep, dn, cos, sin)
    da, a3, b3, late = together(da, a3, b3, late)
    a_next, b_next = pair_sum(sum_a[2], a3, sum_b[1], b3)
    xbc, a_next, b_next = together(xbc, a_next, b_next)
    a_next, b_next = swap(a_next, 2), swap(b_next, 1)
    own_gain_row = jnp.pad(own_gain, (0, 64))[None]
    zeros = [
        jnp.zeros((256, 128), F32),
        jnp.zeros((8, 512), F32),
        jnp.zeros((8, 512), F32),
        jnp.zeros((16, CHUNK), F32),
    ]
    back = lambda part, carry, made, data: scan_back(
        part, carry, made, bounds, data, pre, z, y, dt_raw, states, late, dn, taps, head, skip,
        own_gain_row,
    )
    ds, dt_grad, *carry = back(0, zeros, [], xbc)
    ds, a1, b2, a_next, b_next = together(ds, a1, b2, a_next, b_next)
    kept, out = piece_sum(bounds, (sum_a[0], a1, a_next), (sum_b[0], b2, b_next))
    sums, single = DpSum(), DpSum()
    xbc, out, kept, layer_rows = together(xbc, out, kept, layer_rows)
    got = sums.first(kept, out)
    layer1, layer2 = swap(layer_rows, 1), swap(layer_rows, 2)
    conv_carry = (carry[2], carry[3], carry[0], carry[1])
    ds, dt_grad, conv_acc, head_acc, _, _ = back(1, conv_carry, [ds, dt_grad], xbc)
    ds, got, layer1, layer2 = together(ds, got, layer1, layer2)

    kept = sums.add(kept, got)
    parts = [block_at(kept, i, kept.shape[0] // 4) for i in range(4)]
    layer3 = [layer1[0], layer2[1]]
    ds, layer3, parts, kept = together(ds, layer3, parts, kept)
    got0 = sums.middle(parts[0])
    layer3 = [swap(layer3[0], 2), swap(layer3[1], 1)]
    grad_other, gain_other = input_grad(other_off, da, ds, dt_grad, weight, normed)
    grad_other, ds, layer3, got0 = together(grad_other, ds, layer3, got0)
    four = lax.axis_size("dp") == 4
    sent = twin(grad_other)
    got1 = sums.middle(parts[1])
    grad_own, gain_own = input_grad(own_off, da, ds, dt_grad, weight, normed)
    grad_own, sent, got1 = together(grad_own, sent, got1)
    got2 = sums.middle(parts[2])
    pieces = merge(bounds, grad_own, sent)
    ds, got2, pieces = together(ds, got2, pieces)
    l0, r0, l1, r1, l2, r2, l3, r3 = pieces
    low_rows = sums.add(jnp.concatenate(parts[:2]), jnp.concatenate([got0, got1]))
    heads = jnp.concatenate(
        [
            jnp.sum(conv_acc[5, :192].reshape(3, 64), axis=1),
            jnp.sum(head_acc[0:3], axis=1),
            jnp.sum(head_acc[8:11], axis=1),
        ]
    )
    place = c * 4 + t
    own_small = jnp.pad(jnp.concatenate([conv_acc[:5, :192].reshape(-1), heads]), (0, 55))
    at_own = lax.dynamic_update_slice_in_dim(
        jnp.zeros((8, 1024), F32), own_small[None], place, 0
    )
    norm_part = (gain_other[0] + gain_own[0]) / norm_gain
    flat = jnp.concatenate(
        [at_own.reshape(-1), gain_part.reshape(-1), conv_acc[:5, 256:].reshape(-1), mlp_part[0]]
        + [norm_part]
    )
    flat = jnp.pad(flat, (0, (-flat.shape[0]) % 1024)).reshape(1, -1, 128)
    flat = jnp.broadcast_to(flat, (8,) + flat.shape[1:])
    ds, l0, r0, l1, r1, l2, r2, l3, r3, flat, low_rows = together(
        ds, l0, r0, l1, r1, l2, r2, l3, r3, flat, low_rows
    )
    l3, r3 = swap(l3, 1), swap(r3, 2)
    got3 = sums.middle(parts[3])
    got_low = sums.last(low_rows)
    flat = exchange(flat)
    alone, out, turned = alone_grad(bounds, normed, da, ds, dt_grad)
    alone, out, turned, l3, r3, got3, got_low, flat = together(
        alone, out, turned, l3, r3, got3, got_low, flat
    )
    l2, r1 = pair_sum(l2, l3, r1, r3)
    flat = jnp.sum(flat, axis=0)
    high_rows = sums.add(jnp.concatenate(parts[2:]), jnp.concatenate([got2, got3]))
    count = alone.shape[0]
    if four:
        out = jnp.concatenate([out, high_rows[:, :512], high_rows[:, 512:]])
    l1, r2, l2, r1, flat, out, alone, high_rows, turned = together(
        l1, r2, l2, r1, flat, out, alone, high_rows, turned
    )
    l2, r1 = swap(l2, 2), swap(r1, 1)
    l1, r2 = swap(l1, 1), swap(r2, 2)
    got = single.first(alone, out)
    shared = shared_grad(bounds, normed, da, ds, turned)
    l1, r2, l2, r1, got, shared = together(l1, r2, l2, r1, got, shared)
    if four:
        half = count + high_rows.shape[0]
        got_high = jnp.concatenate([got[count:half], got[half:]], axis=1)
    else:
        got_high = high_rows
    both = sums.end(
        jnp.concatenate([low_rows, high_rows]), jnp.concatenate([got_low, got_high])
    )
    got_alone = got[:count]
    token_rows = finish(bounds, [l0, r0, l1, r1, l2, r2], own_tokens, dhid, norm_gain[None])
    alone = single.add(alone, got_alone)
    shared = shared.reshape(8, 128, 512)
    token_rows, alone, both, flat, shared, layer_rows, layer1, layer2, layer3 = together(
        token_rows, alone, both, flat, shared, layer_rows, layer1, layer2, layer3
    )
    tok1, tok2 = swap(token_rows, 1), swap(token_rows, 2)
    got = single.middle(alone)
    twin_piece = twin(both)
    flat_got = dp_swap(flat, 1) if four else lax.psum(flat, "dp")
    shared = exchange(shared)
    layer_out = assemble(bounds, [layer_rows, layer1, layer2, *layer3])
    tok1, tok2, got, flat_got, twin_piece, shared, layer_out = together(
        tok1, tok2, got, flat_got, twin_piece, shared, layer_out
    )
    shared = jnp.sum(shared.astype(F32), axis=0).astype(BF)
    if four:
        shared = jnp.broadcast_to(shared[None], (4, 128, 512))
    flat = flat + flat_got if four else flat_got
    *tok3, total = relay(tok1, tok2, alone, got)
    alone = total if four else single.add(alone, got)
    tok3, alone, flat, twin_piece, shared = together(tok3, alone, flat, twin_piece, shared)
    tok3 = [swap(tok3[0], 2), swap(tok3[1], 1)]
    got = single.last(alone)
    flat_got = dp_swap(flat, 2) if four else flat
    if four:
        shared = lax.all_to_all(shared, "dp", 0, 0, tiled=True)
    else:
        shared = lax.psum(shared.astype(F32), "dp")[None]
    outs = piece_out(bounds, both, twin_piece)
    tok3, got, flat_got, outs, shared = together(tok3, got, flat_got, outs, shared)
    alone = single.end(alone, got)
    shared = jnp.sum(shared.astype(F32), axis=0).astype(BF)
    shared = jnp.broadcast_to(shared[None], (8, 128, 512))
    alone, tok3, shared = together(alone, tok3, shared)
    alone_twin = twin(alone)
    shared = exchange(shared)
    tokens_grad = assemble(bounds, [token_rows, tok1, tok2, *tok3])
    alone, alone_twin, tokens_grad = together(alone, alone_twin, tokens_grad)
    shared = shared.reshape(1024, 512).astype(F32)
    kv_out, bc_out = shared[:, :256], shared[:, 256:]
    q_out, z_out, x_out, dt_out = alone_out(bounds, alone, alone_twin)
    flat = flat + flat_got if four else flat_got
    flat = flat.reshape(-1)
    norm_sum = flat[12544:13568]
    small = flat[:8192].reshape(8, 1024)
    gain_sum = flat[8192:10240].reshape(8, 256)
    bc_sum = flat[10240:11520].reshape(5, 256)
    mlp_sum = flat[11520:12544]
    both_cores = lambda v: jnp.stack([lax.dynamic_index_in_dim(v, k * 4 + t, 0, False) for k in range(2)])
    small = both_cores(small)
    gain_sum = both_cores(gain_sum)[:, :192].reshape(-1)
    conv_small = small[:, :960].reshape(2, 5, 192)
    conv_small = jnp.concatenate([conv_small[0], conv_small[1]], axis=1)
    head_small = small[:, 960:969].reshape(2, 3, 3)
    per_head_sum = lambda i: head_small[:, i].reshape(-1)

    gate_out, up_out, down_out, mix_out, att_out = outs
    return (
        layer_out[None],
        tokens_grad[None],
        norm_sum,
        q_out,
        kv_out,
        att_out,
        z_out,
        x_out,
        dt_out,
        bc_out,
        conv_small[:4],
        conv_small[4],
        bc_sum[:4],
        bc_sum[4],
        per_head_sum(2),
        per_head_sum(1),
        per_head_sum(0),
        gain_sum,
        mix_out,
        mlp_sum,
        gate_out,
        up_out,
        down_out,
    )


def solution(mesh):
    placed = (
        P("dp", "ctx", None),
        P("dp", None),
        P(),
        P(None, "tensor"),
        P(),
        P("tensor", None),
        P(None, "tensor"),
        P(None, "tensor"),
        P(None, "tensor"),
        P(),
        P(None, "tensor"),
        P("tensor"),
        P(),
        P(),
        P("tensor"),
        P("tensor"),
        P("tensor"),
        P("tensor"),
        P("tensor", None),
        P(),
        P(None, "tensor"),
        P(None, "tensor"),
        P("tensor", None),
        P("dp", "ctx", None),
    )
    return jax.shard_map(
        local,
        mesh=mesh,
        in_specs=placed,
        out_specs=(
            P("dp", "ctx", None),
            P("dp", "ctx", None),
            P(),
            P(None, "tensor"),
            P(),
            P("tensor", None),
            P(None, "tensor"),
            P(None, "tensor"),
            P(None, "tensor"),
            P(),
            P(None, "tensor"),
            P("tensor"),
            P(),
            P(),
            P("tensor"),
            P("tensor"),
            P("tensor"),
            P("tensor"),
            P("tensor", None),
            P(),
            P(None, "tensor"),
            P(None, "tensor"),
            P("tensor", None),
        ),
        check_vma=False,
    )
```

```python
import functools

import jax
import numpy as np
import jax.numpy as jnp
from jax import lax
from jax.experimental import pallas as pl
from jax.experimental.pallas import tpu as pltpu
from jax.sharding import PartitionSpec as P

BF, F32 = jnp.bfloat16, jnp.float32
EPSILON = 1e-05
ROPE_BASE = 100000000000.0
HEAD_SIZE = 64
MP = 64
PROJ_ROWS = 256
BQ = 512
CHUNK = 256
VMEM_LIMIT = 48 * 1024 * 1024
FULL_VMEM = 60 * 1024 * 1024
SMALL_COST = pl.CostEstimate(flops=1000000, bytes_accessed=100000, transcendentals=0)


def dot(left, right, dims=((1,), (0,)), precision=None):
    return lax.dot_general(
        left, right, (dims, ((), ())), precision=precision, preferred_element_type=F32
    )


def dot_bt(left, right):
    return dot(left, right, ((1,), (1,)))


def dot_at(left, right):
    return dot(left, right, ((0,), (0,)))


def lanes(shape):
    return lax.broadcasted_iota(jnp.int32, shape, len(shape) - 1)


def rows_of(shape):
    return lax.broadcasted_iota(jnp.int32, shape, 0)


def doc_start(pos, first, second):
    return jnp.where(pos >= second, second, jnp.where(pos >= first, first, 0))


def halves(low, high):
    return jnp.where(lanes((1, 128)) < 64, low, high)


def params(**kw):
    return pltpu.CompilerParams(vmem_limit_bytes=VMEM_LIMIT, **kw)


def whole(shape):
    return pl.BlockSpec(shape, lambda *_: (0,) * len(shape))


def proj_body(off, tok, gain, weight, cos, sin, *refs):
    normed_ref, qp_ref, kv_ref, xbc_ref, z_ref, dt_ref = refs[-6:]
    values = tok[...].astype(F32)
    scale = lax.rsqrt(jnp.mean(values * values, axis=-1, keepdims=True) + EPSILON)
    normed = (values * scale * gain[...]).astype(BF)
    normed_ref[...] = normed
    c, s = cos[...], sin[...]
    left = lanes((1, 128)) < 64
    att = dot(normed, weight[:, :384])
    kv, turned, qd = att[:, :128], att[:, 128:256], att[:, 256:]
    kv_ref[...] = jnp.where(left, kv * c + turned * s, kv).astype(BF)
    q_rot = qd * c + pltpu.roll(turned, 64, 1) * s
    qp_ref[...] = jnp.where(left, q_rot.astype(BF) * 0.125, 0.0).astype(BF)
    dt_ref[...] = qd.T[64:72, :]
    ssm = dot(normed, weight[:, 384:])
    x2z2 = ssm[:, 128:256]
    xbc_ref[:, :128] = ssm[:, :128].astype(BF)
    xbc_ref[:, 128:256] = jnp.where(left, x2z2, 0.0).astype(BF)
    xbc_ref[:, 256:] = ssm[:, 384:].astype(BF)
    z_ref[:, :128] = ssm[:, 256:384]
    z_ref[:, 128:] = jnp.where(left, pltpu.roll(x2z2, 64, 1), 0.0)


def project(off, tokens, gain, weight, cos, sin, before=None):
    own = tokens.shape[0]
    full = cos.shape[0]
    n = PROJ_ROWS
    outs = [
        jax.ShapeDtypeStruct((full, 1024), BF),
        jax.ShapeDtypeStruct((full, 128), BF),
        jax.ShapeDtypeStruct((full, 128), BF),
        jax.ShapeDtypeStruct((full, 512), BF),
        jax.ShapeDtypeStruct((full, 256), F32),
        jax.ShapeDtypeStruct((8, full), F32),
    ]
    at = lambda i, off: (off[0] + i, 0)
    out_specs = [pl.BlockSpec((n, o.shape[1]), at) for o in outs[:5]]
    out_specs.append(pl.BlockSpec((8, n), lambda i, off: (0, off[0] + i)))
    in_specs = [
        pl.BlockSpec((n, 1024), lambda i, off: (i, 0)),
        whole((1, 1024)),
        whole((1024, 1024)),
        pl.BlockSpec((n, 128), at),
        pl.BlockSpec((n, 128), at),
    ]
    args = [off, tokens, gain, weight, cos, sin]
    alias = {}
    if before is not None:
        in_specs += [pl.BlockSpec(memory_space=pl.ANY)] * 6
        args += list(before)
        alias = {6 + i: i for i in range(6)}
    return pl.pallas_call(
        proj_body,
        grid_spec=pltpu.PrefetchScalarGridSpec(
            num_scalar_prefetch=1, grid=(own // n,), in_specs=in_specs, out_specs=out_specs
        ),
        out_shape=outs,
        input_output_aliases=alias,
        compiler_params=params(),
        cost_estimate=SMALL_COST,
        name="norm_project",
    )(*args)


def turned_lanes(value):
    low = lanes((1, 128)) % 64 < 32
    return jnp.where(low, -pltpu.roll(value, 96, 1), pltpu.roll(value, 32, 1))


def prep_body(bounds, gate, up, down, mix, att, kv, q, x, z, dt, bc, weight, pack):
    n = gate.shape[0]
    pack[:, :256] = gate[...]
    pack[:, 256:512] = up[...]
    pack[:, 512:768] = down[...].T
    pack[:, 768:] = jnp.concatenate([mix[...], att[...]], axis=0).T
    first, low_kv = bounds[3] == 0, bounds[2] // 2 == 0
    lane = lanes((1, 128))
    left = lane < 64
    tile = lambda ref, i: ref[:, 128 * i : 128 * i + 128].astype(F32)
    swapped = lambda v: pltpu.roll(v, 64, 1)
    keys, values = tile(kv, 0), tile(kv, 1)
    keys = jnp.where(low_kv, keys, swapped(keys))
    values = jnp.where(low_kv, swapped(values), values)
    query = tile(q, 0)
    query = jnp.where(first, query, swapped(query))
    steps = jnp.concatenate([dt[...].astype(F32), jnp.zeros((n, 122), F32)], axis=1)
    steps = jnp.where(lane < 3, jnp.where(first, steps, pltpu.roll(steps, 125, 1)), 0.0)

    def heads(ref):
        a, b, d = tile(ref, 0), tile(ref, 1), swapped(tile(ref, 2))
        return jnp.where(first, a, jnp.where(left, swapped(b), d)), jnp.where(first, b, d)

    x01, x2 = heads(x)
    z01, z2 = heads(z)
    tiles = [
        jnp.where(left, keys, values),
        jnp.where(left, turned_lanes(keys), swapped(turned_lanes(query))),
        jnp.where(left, query, swapped(steps)),
        x01,
        jnp.where(left, x2, swapped(z2)),
        z01,
    ]
    for i, value in enumerate(tiles):
        weight[:, 128 * i : 128 * i + 128] = value.astype(BF)
    weight[:, 768:] = bc[...]


def prepare(bounds, gate, up, down, mix, att, kv, q, x, z, dt, bc):
    n = 256
    row = lambda w: pl.BlockSpec((n, w), lambda i, b: (i, 0))
    col = lambda h: pl.BlockSpec((h, n), lambda i, b: (b[3], i))
    mine = pl.BlockSpec((n, 256), lambda i, b: (i, b[3]))
    return pl.pallas_call(
        prep_body,
        grid_spec=pltpu.PrefetchScalarGridSpec(
            num_scalar_prefetch=1,
            grid=(4,),
            in_specs=[mine, mine, col(256), col(192), col(64)]
            + [row(256), row(128), row(384), row(384), row(6), row(256)],
            out_specs=[row(1024), row(1024)],
        ),
        out_shape=[jax.ShapeDtypeStruct((1024, 1024), BF)] * 2,
        compiler_params=pltpu.CompilerParams(vmem_limit_bytes=FULL_VMEM),
        cost_estimate=SMALL_COST,
        name="prepare",
    )(bounds, gate, up, down, mix, att, kv, q, x, z, dt, bc)


def block_range(qi, bounds):
    first, second = bounds[0], bounds[1]
    q0 = qi * BQ
    low = doc_start(q0, first, second) // BQ
    inner = (doc_start(q0 + BQ - 1, first, second) + BQ - 1) // BQ
    return low, jnp.minimum(jnp.maximum(inner, low), qi)


def allowed_rows(qi, kb, bounds):
    q = qi * BQ + lanes((1, BQ))
    k = kb * BQ + rows_of((BQ, 1))
    return (k <= q) & (k >= doc_start(q, bounds[0], bounds[1]))


def allowed_keys(qi, kb, bounds):
    q = qi * BQ + rows_of((BQ, 1))
    k = kb * BQ + lanes((1, BQ))
    start = doc_start(q, bounds[0], bounds[1])
    return (k <= q) & (k >= start)


def attend_body(bounds, qp, kv, g2, out_ref, keep_ref):
    qi = pl.program_id(0)
    low, inner = block_range(qi, bounds)
    q = qp[...]

    def step(kb, carry, masked):
        top, total, acc = carry
        k = kv[pl.ds(pl.multiple_of(kb * BQ, BQ), BQ), :]
        s = dot_bt(q, k)
        if masked:
            s = jnp.where(allowed_keys(qi, kb, bounds), s, -1e30)
        new_top = jnp.maximum(top, jnp.max(s, axis=1, keepdims=True))
        p = jnp.exp(s - new_top)
        fade = jnp.exp(top - new_top)
        total = total * fade + jnp.sum(p, axis=1, keepdims=True)
        acc = acc * fade + dot(p.astype(BF), k)
        return new_top, total, acc

    carry = (jnp.full((BQ, 1), -1e30, F32), jnp.zeros((BQ, 1), F32), jnp.zeros((BQ, 128), F32))
    carry = lax.fori_loop(low, inner, lambda kb, c: step(kb, c, True), carry)
    carry = lax.fori_loop(inner, qi, lambda kb, c: step(kb, c, False), carry)
    top, total, acc = step(qi, carry, True)
    out = acc / total
    left = lanes((1, 128)) < 64
    out_ref[...] = jnp.where(left, g2[...], out.astype(BF))
    keep_ref[...] = jnp.where(left, top + jnp.log(total), out)


def attend(bounds, qp, kv, g2):
    full = qp.shape[0]
    block = pl.BlockSpec((BQ, 128), lambda i, *_: (i, 0))
    return pl.pallas_call(
        attend_body,
        grid_spec=pltpu.PrefetchScalarGridSpec(
            num_scalar_prefetch=1,
            grid=(full // BQ,),
            in_specs=[block, whole((full, 128)), block],
            out_specs=[block, block],
        ),
        out_shape=[
            jax.ShapeDtypeStruct((full, 128), BF),
            jax.ShapeDtypeStruct((full, 128), F32),
        ],
        compiler_params=params(),
        cost_estimate=SMALL_COST,
        name="attend",
    )(bounds, qp, kv, g2)


def attend_back_body(bounds, qp, kv, keep, grad, cos, sin, out_ref, acc_ref):
    blocks = pl.num_programs(0)
    qi = blocks - 1 - pl.program_id(0)
    left = lanes((1, 128)) < 64

    @pl.when(pl.program_id(0) == 0)
    def _():
        acc_ref[...] = jnp.zeros_like(acc_ref)

    low, inner = block_range(qi, bounds)
    q = qp[...]
    do = jnp.where(left, 0.0, grad[0].astype(F32))
    delta = jnp.sum(do * keep[...], axis=1, keepdims=True)
    do = do.astype(BF)
    stats = jnp.where(lanes((1, 128)) == 0, keep[...], delta).T
    lse, delta = stats[0:1, :], stats[1:2, :]

    def step(kb, dq, masked):
        at = pl.ds(pl.multiple_of(kb * BQ, BQ), BQ)
        k = kv[at, :]
        p = jnp.exp(dot_bt(k, q) - lse)
        if masked:
            p = jnp.where(allowed_rows(qi, kb, bounds), p, 0.0)
        ds = (p * (dot_bt(k, do) - delta)).astype(BF)
        acc_ref[at, :] += dot(ds, q) + dot(p.astype(BF), do)
        return dq + dot_at(ds, k)

    dq = jnp.zeros((BQ, 128), F32)
    dq = lax.fori_loop(low, inner, lambda kb, c: step(kb, c, True), dq)
    dq = lax.fori_loop(inner, qi, lambda kb, c: step(kb, c, False), dq)
    dq = step(qi, dq, True) * 0.125
    dkv = acc_ref[pl.ds(pl.multiple_of(qi * BQ, BQ), BQ), :]
    c, s = cos[...], sin[...]
    out_ref[:, :128] = jnp.where(left, dkv * c, dkv).astype(BF)
    out_ref[:, 128:256] = (jnp.where(left, dkv, pltpu.roll(dq, 64, 1)) * s).astype(BF)
    out_ref[:, 256:] = jnp.where(left, dq * c, 0.0).astype(BF)


def attend_back(bounds, qp, kv, keep, grad, cos, sin):
    full = qp.shape[0]
    n = full // BQ
    block = pl.BlockSpec((BQ, 128), lambda i, *_: (n - 1 - i, 0))
    return pl.pallas_call(
        attend_back_body,
        grid_spec=pltpu.PrefetchScalarGridSpec(
            num_scalar_prefetch=1,
            grid=(n,),
            in_specs=[
                block,
                whole((full, 128)),
                block,
                pl.BlockSpec((1, BQ, 128), lambda i, *_: (n - 1 - i, 0, 0)),
                block,
                block,
            ],
            out_specs=pl.BlockSpec((BQ, 384), lambda i, *_: (n - 1 - i, 0)),
            scratch_shapes=[pltpu.VMEM((full, 128), F32)],
        ),
        out_shape=jax.ShapeDtypeStruct((full, 384), BF),
        compiler_params=params(),
        cost_estimate=SMALL_COST,
        name="attend_back",
    )(bounds, qp, kv, keep, grad, cos, sin)


def tap_mask(first_row, count, shift, bounds):
    pos = first_row + rows_of((count, 1))
    return (pos - doc_start(pos, bounds[0], bounds[1]) >= shift).astype(F32)


def conv_taps(ext_ref, r0, bounds, taps, bias):
    pre = bias + taps[3:4, :] * ext_ref[pl.ds(8, CHUNK), :]
    for shift in (1, 2, 3):
        mask = tap_mask(r0, CHUNK, shift, bounds)
        pre = pre + taps[3 - shift : 4 - shift, :] * (ext_ref[pl.ds(8 - shift, CHUNK), :] * mask)
    return pre


def chunk_decay(r0, bounds, dt_raw, head, extra=None):
    lane = lanes((1, CHUNK))
    dt = jax.nn.softplus(dt_raw + head[:, 0:1])
    la = dt * head[:, 1:2]
    upper = (rows_of((CHUNK, CHUNK)) <= lanes((CHUNK, CHUNK))).astype(F32)
    cum = dot(la, upper, precision=lax.Precision.HIGHEST)
    rows = [cum, dt] if extra is None else [cum, dt, extra]
    used = 8 * len(rows)
    stacked = jnp.concatenate(rows + [jnp.zeros((CHUNK - used, CHUNK), F32)], axis=0).T
    cum_col, dt_col = stacked[:, 0:8], stacked[:, 8:16]
    pos = r0 + rows_of((CHUNK, 1))
    start = doc_start(pos, bounds[0], bounds[1])
    start_last = doc_start(r0 + CHUNK - 1, bounds[0], bounds[1])
    key = r0 + lane
    mask = (key <= pos) & (key >= start)
    enter = jnp.where(start < r0, jnp.exp(cum_col), 0.0)
    fade = jnp.where(pos >= start_last, jnp.exp(cum_last_row(cum_col) - cum_col), 0.0)
    keep = jnp.where(start_last < r0, jnp.exp(cum_last_row(cum_col)), 0.0)
    return dt, la, cum, dt_col, cum_col, mask, enter, fade, keep, stacked[:, 16:24]


def two_terms(value):
    high = value.astype(BF)
    return high, (value - high.astype(F32)).astype(BF)


def cum_last_row(cum_col):
    return cum_col[CHUNK - 1 : CHUNK, :]


def per_head(col):
    return halves(col[:, 0:1], col[:, 1:2]), col[:, 2:3]


def state_rows(keep):
    row = rows_of((256, 1))
    return jnp.where(row < 64, keep[:, 0:1], jnp.where(row < 128, keep[:, 1:2], keep[:, 2:3]))


def scan_body(
    bounds, xbc, z, dt_raw, taps, bias, head, skip, g01, g2, y_ref, s_ref, pre_ref, ext, state
):
    i = pl.program_id(0)
    r0 = i * CHUNK

    @pl.when(i == 0)
    def _():
        ext[pl.ds(0, 8), :] = jnp.zeros((8, 512), F32)
        state[...] = jnp.zeros_like(state)

    @pl.when(i > 0)
    def _():
        ext[pl.ds(0, 8), :] = ext[pl.ds(CHUNK, 8), :]

    ext[pl.ds(8, CHUNK), :] = xbc[...].astype(F32)
    pre = conv_taps(ext, r0, bounds, taps[...], bias[...])
    pre_ref[...] = pre
    conv = pre * jax.nn.sigmoid(pre)
    x01, x2 = conv[:, :128], conv[:, 128:256]
    b, c = conv[:, 256:384].astype(BF), conv[:, 384:].astype(BF)
    dt, la, cum, dt_col, cum_col, mask, enter, fade, keep, _ = chunk_decay(
        r0, bounds, dt_raw[...], head[...]
    )
    inner = dot_bt(c, b)
    x01b, x2b = x01.astype(BF), x2.astype(BF)
    ys = []
    for h in range(3):
        gap = cum_col[:, h : h + 1] - cum[h : h + 1, :]
        decay = jnp.exp(jnp.where(mask, gap, -1e30))
        m = (inner * decay * dt[h : h + 1, :]).astype(BF)
        ys.append(dot(m, x01b if h < 2 else x2b))
    s0 = state[...]
    s_ref[0] = s0
    s0b, s0c = two_terms(s0)
    carried = dot_bt(c, s0b) + dot_bt(c, s0c)
    e01, e2 = per_head(enter)
    y01 = halves(ys[0], ys[1]) + e01 * carried[:, :128] + skip[:, :128] * x01
    y2 = ys[2] + e2 * carried[:, 128:] + skip[:, 128:] * x2
    w01, w2 = per_head(fade * dt_col)
    xw = jnp.concatenate([(x01 * w01).astype(BF), (x2 * w2).astype(BF)], axis=1)
    state[...] = s0 * state_rows(keep) + dot_at(xw, b)
    y_ref[:, :128] = y01
    y_ref[:, 128:] = y2
    z01, z2 = z[:, :128], z[:, 128:]
    g01[...] = (y01 * (z01 * jax.nn.sigmoid(z01))).astype(BF)
    g2[...] = (y2 * (z2 * jax.nn.sigmoid(z2))).astype(BF)


def scan_forward(bounds, xbc, z, dt_raw, taps, bias, head, skip):
    full = xbc.shape[0]
    n = full // CHUNK
    row = lambda width: pl.BlockSpec((CHUNK, width), lambda i, *_: (i, 0))
    return pl.pallas_call(
        scan_body,
        grid_spec=pltpu.PrefetchScalarGridSpec(
            num_scalar_prefetch=1,
            grid=(n,),
            in_specs=[
                row(512),
                row(256),
                pl.BlockSpec((8, CHUNK), lambda i, *_: (0, i)),
                whole((8, 512)),
                whole((1, 512)),
                whole((8, 128)),
                whole((1, 256)),
            ],
            out_specs=[
                row(128),
                row(128),
                row(256),
                pl.BlockSpec((1, 256, 128), lambda i, *_: (i, 0, 0)),
                row(512),
            ],
            scratch_shapes=[pltpu.VMEM((CHUNK + 8, 512), F32), pltpu.VMEM((256, 128), F32)],
        ),
        out_shape=[
            jax.ShapeDtypeStruct((full, 128), BF),
            jax.ShapeDtypeStruct((full, 128), BF),
            jax.ShapeDtypeStruct((full, 256), F32),
            jax.ShapeDtypeStruct((n, 256, 128), F32),
            jax.ShapeDtypeStruct((full, 512), F32),
        ],
        compiler_params=params(),
        cost_estimate=SMALL_COST,
        name="scan_forward",
    )(bounds, xbc, z, dt_raw, taps, bias, head, skip)


def scalar_rows(terms):
    low = terms[0:2, :] + terms[2:4, :] + terms[4:6, :]
    high = terms[6:8, :] + terms[8:10, :] + terms[10:12, :]
    total = jnp.concatenate([low, high], axis=1)
    return jnp.concatenate([total, jnp.zeros((6, CHUNK), F32)], axis=0)


def scan_back_body(
    last, bounds, xbc, before, pre_ref, z, y, dt_raw, s0_ref, dn01, dn2, scal, taps, head, skip,
    gain,
    dstate_in, dext_in, acc_in, head_in, *refs,
):
    out_ref, dt_grad, acc, head_acc, dstate_out, dext_out, ext, dext, dstate = refs[-9:]
    step = pl.program_id(0)
    i = last - step
    r0 = i * CHUNK
    left = lanes((1, 128)) < 64

    @pl.when(step == 0)
    def _():
        dext[pl.ds(CHUNK, 8), :] = dext_in[...]
        dstate[...] = dstate_in[...]
        acc[...] = acc_in[...]
        head_acc[...] = head_in[...]

    @pl.when(step > 0)
    def _():
        dext[pl.ds(CHUNK, 8), :] = dext[pl.ds(0, 8), :]

    ext[pl.ds(0, 8), :] = before[...].astype(F32)[8:, :]
    ext[pl.ds(8, CHUNK), :] = xbc[...].astype(F32)
    weights = taps[...]
    pre = pre_ref[...]
    sig = jax.nn.sigmoid(pre)
    conv = pre * sig
    x01, x2 = conv[:, :128], conv[:, 128:256]
    b, c = conv[:, 256:384].astype(BF), conv[:, 384:].astype(BF)
    dt, la, cum, dt_col, cum_col, mask, enter, fade, keep, scalars = chunk_decay(
        r0, bounds, dt_raw[...], head[...], scalar_rows(scal[0].astype(F32))
    )
    row_scale, row_cross = scalars[:, 0:1], scalars[:, 1:2]

    def gate_back(dn, gain, zz, yy):
        s = jax.nn.sigmoid(zz)
        act = zz * s
        g = yy * act
        sent = g.astype(BF).astype(F32)
        ratio = jnp.where(g == 0.0, 1.0, sent / g)
        dg = (dn * gain * row_scale - sent * row_cross) * ratio
        return dg * act, dg * yy * (s + act * (1.0 - s))

    dy01, dz01 = gate_back(dn01[0].astype(F32), gain[:, :128], z[:, :128], y[:, :128])
    dy2, dz2 = gate_back(dn2[0].astype(F32), gain[:, 128:], z[:, 128:], y[:, 128:])
    dy2, dz2 = jnp.where(left, dy2, 0.0), jnp.where(left, dz2, 0.0)
    inner = dot_bt(b, c)
    x01b, x2b = x01.astype(BF), x2.astype(BF)
    dy01b, dy2b = dy01.astype(BF), dy2.astype(BF)
    zero = jnp.zeros_like(dy01b)
    parts = [(jnp.where(left, dy01b, zero), x01b), (jnp.where(left, zero, dy01b), x01b), (dy2b, x2b)]
    query = r0 + lanes((1, CHUNK))
    key = r0 + rows_of((CHUNK, 1))
    mask = (key <= query) & (key >= doc_start(query, bounds[0], bounds[1]))
    d_inner = jnp.zeros((CHUNK, CHUNK), F32)
    dxs, direct, row_sums = [], [], []
    for h in range(3):
        gap = cum[h : h + 1, :] - cum_col[:, h : h + 1]
        decay = jnp.exp(jnp.where(mask, gap, -1e30))
        dt_h = dt_col[:, h : h + 1]
        dyh, xh = parts[h]
        dm = dot_bt(xh, dyh)
        kept = inner * decay
        dxs.append(dot((kept * dt_h).astype(BF), dyh if h == 2 else dy01b))
        pulled = dm * kept
        d_inner = d_inner + dm * (decay * dt_h)
        direct.append(jnp.sum(pulled, axis=1, keepdims=True))
        row_sums.append(jnp.sum(pulled * dt_h, axis=0, keepdims=True))
    s0 = s0_ref[0]
    s0b, s0c = two_terms(s0)
    ds1 = dstate[...]
    ds1b, ds1c = two_terms(ds1)
    e01, e2 = per_head(enter)
    ey01, ey2 = dy01 * e01, dy2 * e2
    ey, eyc = two_terms(jnp.concatenate([ey01, ey2], axis=1))
    carried = dot_bt(c, s0b) + dot_bt(c, s0c)
    f01, f2 = per_head(fade)
    d01, d2 = per_head(dt_col)
    back = dot_bt(b, ds1b)
    fb01, fb2 = f01 * back[:, :128], f2 * back[:, 128:]
    xw = jnp.concatenate([(x01 * (f01 * d01)).astype(BF), (x2 * (f2 * d2)).astype(BF)], axis=1)
    d_innerb = d_inner.astype(BF)
    dc = dot_at(d_innerb, b) + dot(ey, s0b) + dot(eyc, s0b) + dot(ey, s0c)
    db = dot(d_innerb, c) + dot(xw, ds1b) + dot(xw, ds1c)
    dx01 = halves(dxs[0], dxs[1]) + d01 * fb01 + skip[:, :128] * dy01
    dx2 = dxs[2] + d2 * fb2 + skip[:, 128:] * dy2
    kept_rows = state_rows(keep)
    crossing = jnp.sum(ds1 * s0 * kept_rows, axis=1, keepdims=True)
    dstate[...] = ds1 * kept_rows + dot_at(ey, c) + dot_at(eyc, c)
    inter01, inter2 = ey01 * carried[:, :128], ey2 * carried[:, 128:]
    u01, u2 = x01 * fb01, x2 * fb2
    pick = lambda v, h: jnp.where(left if h == 0 else ~left, v, 0.0)
    side = lambda v01, v2, h: jnp.sum(pick(v01, h) if h < 2 else v2, axis=1, keepdims=True)
    lane = lanes((1, CHUNK))
    tile = jnp.zeros((CHUNK, CHUNK), F32)
    crossed = jnp.zeros((8, 1), F32)
    head_row = rows_of((8, 1))
    for h in range(3):
        u = side(u01, u2, h)
        pulled = u + direct[h]
        moved = side(inter01, inter2, h) - pulled * dt_col[:, h : h + 1]
        tile = jnp.where(lane == h, moved, jnp.where(lane == 8 + h, pulled, tile))
        total = jnp.sum(crossing[64 * h : 64 * h + 64, :], axis=0, keepdims=True)
        total = total + jnp.sum(u * dt_col[:, h : h + 1], axis=0, keepdims=True)
        crossed = jnp.where(head_row == h, total, crossed)
    tile = tile.T
    stack = lambda items: jnp.concatenate(items + [jnp.zeros((5, CHUNK), F32)], axis=0)
    dcum = tile[0:8, :] + stack(row_sums) + jnp.where(lane == CHUNK - 1, crossed, 0.0)
    lower = (rows_of((CHUNK, CHUNK)) >= lanes((CHUNK, CHUNK))).astype(F32)
    dla = dot(dcum, lower, precision=lax.Precision.HIGHEST)
    ddt = tile[8:16, :] + dla * head[:, 1:2]
    graw = ddt * jax.nn.sigmoid(dt_raw[...] + head[:, 0:1])
    dt_grad[...] = graw
    head_acc[0:8, :] += dla * la
    head_acc[8:16, :] += graw
    dpre = jnp.concatenate([dx01, dx2, db, dc], axis=1) * (sig + conv * (1.0 - sig))
    dext[pl.ds(0, CHUNK), :] = dpre
    din = weights[3:4, :] * dpre
    acc[3:4, :] += jnp.sum(dpre * ext[pl.ds(8, CHUNK), :], axis=0, keepdims=True)
    acc[4:5, :] += jnp.sum(dpre, axis=0, keepdims=True)
    acc[5:6, :128] += jnp.sum(dy01 * x01, axis=0, keepdims=True)
    acc[5:6, 128:256] += jnp.sum(dy2 * x2, axis=0, keepdims=True)
    for shift in (1, 2, 3):
        tap = 3 - shift
        now = tap_mask(r0, CHUNK, shift, bounds)
        acc[tap : tap + 1, :] += jnp.sum(
            dpre * (ext[pl.ds(8 - shift, CHUNK), :] * now), axis=0, keepdims=True
        )
        later = tap_mask(r0 + shift, CHUNK, shift, bounds)
        din = din + weights[tap : tap + 1, :] * (dext[pl.ds(shift, CHUNK), :] * later)
    out_ref[:, :128] = din[:, :128].astype(BF)
    out_ref[:, 128:256] = jnp.where(left, din[:, 128:256], pltpu.roll(dz2, 64, 1)).astype(BF)
    out_ref[:, 256:384] = dz01.astype(BF)
    out_ref[:, 384:] = din[:, 256:].astype(BF)

    @pl.when(step == pl.num_programs(0) - 1)
    def _():
        dstate_out[...] = dstate[...]
        dext_out[...] = dext[pl.ds(0, 8), :]


def scan_back(
    part, carry, before, bounds, xbc, pre, z, y, dt_raw, states, late, dn, taps, head, skip, gain
):
    full = xbc.shape[0]
    n = full // CHUNK
    half = n // 2
    last = n - 1 if part == 0 else half - 1
    row = lambda width: pl.BlockSpec((CHUNK, width), lambda i, *_: (last - i, 0))
    tall = CHUNK // 16
    per = n // 8
    sent = pl.BlockSpec((1, CHUNK, 128), lambda i, b: ((last - i) // per, (last - i) % per, 0))

    def terms(i, b):
        piece, rest = (last - i) // per, (last - i) % per
        return piece, per * (CHUNK // 16) + rest, 0

    carried = [whole((256, 128)), whole((8, 512)), whole((8, 512)), whole((16, CHUNK))]
    sds = jax.ShapeDtypeStruct
    args = [bounds, xbc, xbc, pre, z, y, dt_raw, states, late, dn, late, taps, head, skip, gain]
    args += list(carry) + list(before)
    alias = {len(args) - 2: 0, len(args) - 1: 1} if before else {}
    return pl.pallas_call(
        functools.partial(scan_back_body, last),
        grid_spec=pltpu.PrefetchScalarGridSpec(
            num_scalar_prefetch=1,
            grid=(half,),
            in_specs=[
                row(512),
                pl.BlockSpec((16, 512), lambda i, *_: (jnp.maximum((last - i) * tall - 1, 0), 0)),
                row(512),
                row(256),
                row(256),
                pl.BlockSpec((8, CHUNK), lambda i, *_: (0, last - i)),
                pl.BlockSpec((1, 256, 128), lambda i, *_: (last - i, 0, 0)),
                sent,
                sent,
                pl.BlockSpec((1, 16, 128), terms),
                whole((8, 512)),
                whole((8, 128)),
                whole((1, 256)),
                whole((1, 256)),
            ]
            + carried
            + [pl.BlockSpec(memory_space=pl.ANY)] * len(before),
            out_specs=[
                row(640),
                pl.BlockSpec((8, CHUNK), lambda i, *_: (0, last - i)),
                whole((8, 512)),
                whole((16, CHUNK)),
                whole((256, 128)),
                whole((8, 512)),
            ],
            scratch_shapes=[
                pltpu.VMEM((CHUNK + 8, 512), F32),
                pltpu.VMEM((CHUNK + 8, 512), F32),
                pltpu.VMEM((256, 128), F32),
            ],
        ),
        out_shape=[
            sds((full, 640), BF),
            sds((8, full), F32),
            sds((8, 512), F32),
            sds((16, CHUNK), F32),
            sds((256, 128), F32),
            sds((8, 512), F32),
        ],
        input_output_aliases=alias,
        compiler_params=params(),
        cost_estimate=SMALL_COST,
        name="scan_back",
    )(*args)


ROW_BLOCK = 256


def row_body(bounds, g, h, tok, gout, mlp_gain, gains, *refs):
    packs, refs = refs[:10], refs[10:]
    pa, pb, slots = [], [], []
    for k, base in enumerate((0, 5)):
        for r in range(4):
            first = packs[base + r]
            second = first.at[:, 512:] if r < 3 else packs[base + 4]
            pa.append(first.at[:, 0:512])
            pb.append(second)
            slots.append((bounds[3] ^ k) * 4 + (bounds[2] ^ r))
    gain_rows = [gains[slot] for slot in slots]
    out_ref, two_ref, dmix_ref, dhid_ref = refs[0:4]
    act_refs, dgu_refs, gn_refs = refs[4:6], refs[6:8], refs[8:10]
    dn, dn_late, mlp_acc, gain_acc = refs[10:14]
    step = pl.program_id(0)
    left = lanes((1, 128)) < 64
    width = 1536.0

    @pl.when(pl.program_id(0) == 0)
    def _():
        mlp_acc[...] = jnp.zeros_like(mlp_acc)
        gain_acc[...] = jnp.zeros_like(gain_acc)

    pieces = [(r, k) for k in range(2) for r in range(4)]

    def part(ref, s):
        return ref[slots[s]].astype(F32)

    squares = 0.0
    for s in range(8):
        first, second = part(g, s), part(h, s)
        squares = squares + first * first + jnp.where(left, second * second, 0.0)
    rg = lax.rsqrt(jnp.sum(squares, axis=1, keepdims=True) / width + EPSILON)
    mixed = 0.0
    for s, (r, k) in enumerate(pieces):
        gain = gain_rows[s]
        first = part(g, s) * rg * gain[:, :128]
        second = part(h, s)
        second = jnp.where(left, second * rg * gain[:, 128:], second)
        gn = jnp.concatenate([first.astype(BF), second.astype(BF)], axis=1)
        gn_refs[k][:, r * 256 : r * 256 + 256] = gn
        mixed = mixed + dot_bt(gn, pb[s][:, 256:])
    hidden = tok[...].astype(F32) + mixed
    scale = lax.rsqrt(jnp.mean(hidden * hidden, axis=-1, keepdims=True) + EPSILON)
    two = (hidden * scale * mlp_gain[...]).astype(BF)
    two_ref[...] = two
    grad = gout[...]
    ffn = 0.0
    dtwo = 0.0
    for s, (r, k) in enumerate(pieces):
        weight, down = pa[s][...], pb[s][:, :256]
        gu = dot(two, weight)
        gate, up = gu[:, :256], gu[:, 256:]
        sig = jax.nn.sigmoid(gate)
        silu = gate * sig
        act = (silu * up).astype(BF)
        act_refs[k][:, r * 256 : r * 256 + 256] = act
        ffn = ffn + dot_bt(act, down)
        dact = dot(grad, down)
        dgate = (dact * up * (sig + silu * (1.0 - sig))).astype(BF)
        dgu = jnp.concatenate([dgate, (dact * silu).astype(BF)], axis=1)
        dgu_refs[k][:, r * 512 : r * 512 + 512] = dgu
        dtwo = dtwo + dot_bt(dgu, weight)
    whole_out = (hidden + ffn).astype(BF)
    out_ref[0] = whole_out[:, :512]
    out_ref[1] = whole_out[:, 512:]
    weighted = dtwo * mlp_gain[...]
    mlp_acc[...] += jnp.sum(dtwo * (hidden * scale), axis=0, keepdims=True)
    mean = jnp.mean(weighted * hidden, axis=-1, keepdims=True)
    dhid = grad.astype(F32) + scale * weighted - hidden * (scale * scale * scale * mean)
    dhid_ref[...] = dhid
    dmix = dhid.astype(BF)
    dmix_ref[...] = dmix
    cross = 0.0
    for s, (r, k) in enumerate(pieces):
        dgn = dot(dmix, pb[s][:, 256:]).astype(BF)
        at = pl.ds(pl.multiple_of(step * ROW_BLOCK, ROW_BLOCK), ROW_BLOCK)
        dn[slots[s], at, :] = dgn[:, 128:]
        dn_late[slots[s], at, :] = dgn[:, :128]
        first, second = dgn[:, :128].astype(F32), dgn[:, 128:].astype(F32)
        gain = gain_rows[s]
        own1, own2 = part(g, s), jnp.where(left, part(h, s), 0.0)
        t1, t2 = first * own1, second * own2
        gain_acc[slots[s], :, :128] += jnp.sum(t1 * rg, axis=0, keepdims=True)
        gain_acc[slots[s], :, 128:] += jnp.sum(t2 * rg, axis=0, keepdims=True)
        cross = cross + t1 * gain[:, :128] + t2 * gain[:, 128:]
    cross = jnp.sum(cross, axis=1, keepdims=True) * (rg * rg * rg / width)
    lane = lanes((1, 128))
    tile = jnp.where(lane == 0, rg, jnp.where(lane == 1, cross, 0.0))
    pair = tile.T[0:2, :]
    high = pair.astype(BF)
    rest = pair - high.astype(F32)
    middle = rest.astype(BF)
    low = (rest - middle.astype(F32)).astype(BF)
    terms = [v.astype(F32) for v in (high, middle, low)]
    block = jnp.concatenate(
        [v[:, :128] for v in terms] + [v[:, 128:] for v in terms] + [jnp.zeros((4, 128), F32)],
        axis=0,
    ).astype(BF)
    for s in range(8):
        dn_late[s, pl.ds(pl.multiple_of(2 * ROW_BLOCK + step * 16, 16), 16), :] = block


def row_stage(bounds, g, h, tokens, gout, mlp_gain, gains, packs):
    n = ROW_BLOCK
    count = 2 * n
    row = lambda w: pl.BlockSpec((n, w), lambda i, b: (i, 0))
    part = pl.BlockSpec((n, 1024), lambda i, b: (2 * b[2] + i, 0))
    piece = pl.BlockSpec((8, n, 128), lambda i, b: (0, i, 0))
    once = lambda shape: pl.BlockSpec(
        shape, lambda i, b: (0,) * len(shape), pipeline_mode=pl.Buffered(1)
    )
    sds = jax.ShapeDtypeStruct
    widths = [1024] * 4 + [1024] * 2 + [2048] * 2 + [1024] * 2
    dtypes = [BF] * 3 + [F32] + [BF] * 6
    return pl.pallas_call(
        row_body,
        grid_spec=pltpu.PrefetchScalarGridSpec(
            num_scalar_prefetch=1,
            grid=(2,),
            in_specs=[piece, piece, part, part, whole((1, 1024)), whole((8, 1, 256))]
            + [once(p.shape) for p in packs],
            out_specs=[pl.BlockSpec((2, n, 512), lambda i, b: (0, i, 0))]
            + [row(w) for w in widths[1:]]
            + [once((8, count, 128)), once((8, count + 32, 128))]
            + [whole((1, 1024)), whole((8, 1, 256))],
        ),
        out_shape=[sds((2, count, 512), BF)]
        + [sds((count, w), d) for w, d in zip(widths[1:], dtypes[1:])]
        + [sds((8, count, 128), BF), sds((8, count + 32, 128), BF)]
        + [sds((1, 1024), F32), sds((8, 1, 256), F32)],
        compiler_params=pltpu.CompilerParams(vmem_limit_bytes=58 * 1024 * 1024),
        cost_estimate=SMALL_COST,
        name="row_stage",
    )(bounds, g, h, tokens, gout, mlp_gain, gains, *packs)


def weight_body(two, gout, dmix, dgu, act, gn, *refs):
    a = dot_at(two[...], dgu[...])
    b = jnp.concatenate([dot_at(gout[...], act[...]), dot_at(dmix[...], gn[...])], axis=1)
    if len(refs) == 2:
        refs[0][0] = a.astype(BF)
        refs[1][0] = b.astype(BF)
    else:
        a = (a + refs[0][0].astype(F32)).astype(BF)
        b = (b + refs[1][0].astype(F32)).astype(BF)
        for i in range(4):

            @pl.when(pl.program_id(0) == i)
            def _(i=i):
                refs[2 + i][...] = a
                refs[6 + i][...] = b


def weight_stage(two, gout, dmix, dgu, act, gn, *others):
    count = two.shape[0]
    col = lambda w: pl.BlockSpec((count, w), lambda i: (0, i))
    piece = pl.BlockSpec((1, 1024, 512), lambda i: (i, 0, 0))
    once = pl.BlockSpec((1024, 512), lambda i: (0, 0), pipeline_mode=pl.Buffered(1))
    sds = jax.ShapeDtypeStruct
    return pl.pallas_call(
        weight_body,
        grid=(4,),
        in_specs=[whole((count, 1024))] * 3
        + [col(512), col(256), col(256)]
        + [piece] * len(others),
        out_specs=[once] * 8 if others else [piece] * 2,
        out_shape=[sds((1024, 512), BF)] * 8 if others else [sds((4, 1024, 512), BF)] * 2,
        compiler_params=pltpu.CompilerParams(vmem_limit_bytes=FULL_VMEM),
        cost_estimate=SMALL_COST,
        name="weight_stage",
    )(two, gout, dmix, dgu, act, gn, *others)


def with_steps(da, dt_grad):
    count = da.shape[0]
    cols = jnp.concatenate([dt_grad, jnp.zeros((120, count), F32)], axis=0).T
    last = jnp.where(lanes((1, 128)) < 64, da[:, 256:].astype(F32), pltpu.roll(cols, 64, 1))
    return jnp.concatenate([da[:, :256], last.astype(BF)], axis=1)


def input_grad_body(off, da, ds, dt_grad, weight, normed, out_ref, gain_ref):
    left = with_steps(da[...], dt_grad[...])
    grad = dot_bt(left, weight[:, :384]) + dot_bt(ds[...], weight[:, 384:])
    out_ref[...] = grad.astype(BF)

    @pl.when(pl.program_id(0) == 0)
    def _():
        gain_ref[...] = jnp.zeros_like(gain_ref)

    gain_ref[...] += jnp.sum(grad * normed[...].astype(F32), axis=0, keepdims=True)


def input_grad(off, da, ds, dt_grad, weight, normed):
    n = PROJ_ROWS
    own = ds.shape[0] // 2
    at = lambda i, off: (off[0] + i, 0)
    return pl.pallas_call(
        input_grad_body,
        grid_spec=pltpu.PrefetchScalarGridSpec(
            num_scalar_prefetch=1,
            grid=(own // n,),
            in_specs=[
                pl.BlockSpec((n, 384), at),
                pl.BlockSpec((n, 640), at),
                pl.BlockSpec((8, n), lambda i, off: (0, off[0] + i)),
                whole((1024, 1024)),
                pl.BlockSpec((n, 1024), at),
            ],
            out_specs=[pl.BlockSpec((n, 1024), lambda i, off: (i, 0)), whole((1, 1024))],
        ),
        out_shape=[
            jax.ShapeDtypeStruct((own, 1024), BF),
            jax.ShapeDtypeStruct((1, 1024), F32),
        ],
        compiler_params=params(),
        cost_estimate=SMALL_COST,
        name="input_grad",
    )(off, da, ds, dt_grad, weight, normed)


def turned_back(value):
    low = lanes((1, 128)) % 64 < 32
    return jnp.where(low, pltpu.roll(value, 96, 1), -pltpu.roll(value, 32, 1))


def shared_grad_body(bounds, normed, da, ds1, ds2, turned, shared, acc):
    @pl.when(pl.program_id(0) == 0)
    def _():
        acc[...] = jnp.zeros_like(acc)

    cols = jnp.concatenate([da[...], ds1[...], ds2[...]], axis=1)
    acc[...] += dot_at(normed[...], cols)

    @pl.when(pl.program_id(0) == pl.num_programs(0) - 1)
    def _():
        left = lanes((1, 128)) < 64
        kv = acc[:, :128] + jnp.where(left, turned_back(turned[...]), 0.0)
        low = bounds[2] // 2 == 0
        swapped = pltpu.roll(kv, 64, 1)
        keys = jnp.where(left == low, jnp.where(low, kv, swapped), 0.0)
        values = jnp.where(left == low, jnp.where(low, swapped, kv), 0.0)
        shared[:, :128] = keys.astype(BF)
        shared[:, 128:256] = values.astype(BF)
        shared[:, 256:] = acc[:, 128:].astype(BF)


def shared_grad(bounds, normed, da, ds, turned):
    full = normed.shape[0]
    n = 512
    part = lambda w, col: pl.BlockSpec((n, w), lambda i, *_: (i, col))
    return pl.pallas_call(
        shared_grad_body,
        grid_spec=pltpu.PrefetchScalarGridSpec(
            num_scalar_prefetch=1,
            grid=(full // n,),
            in_specs=[part(1024, 0), part(128, 0), part(128, 3), part(128, 4)]
            + [whole((1024, 128))],
            out_specs=whole((1024, 512)),
            scratch_shapes=[pltpu.VMEM((1024, 384), F32)],
        ),
        out_shape=jax.ShapeDtypeStruct((1024, 512), BF),
        compiler_params=params(),
        cost_estimate=SMALL_COST,
        name="shared_grad",
    )(bounds, normed, da, ds, ds, turned)


def alone_grad_body(bounds, normed, da1, da2, ds, dt_grad, kept, sent, turned, acc):
    @pl.when(pl.program_id(0) == 0)
    def _():
        acc[...] = jnp.zeros_like(acc)

    count = da1.shape[0]
    cols = jnp.concatenate([dt_grad[...], jnp.zeros((120, count), F32)], axis=0).T
    last = jnp.where(lanes((1, 128)) < 64, da2[...].astype(F32), pltpu.roll(cols, 64, 1))
    acc[...] += dot_at(
        normed[...], jnp.concatenate([last.astype(BF), ds[...], da1[...]], axis=1)
    )

    @pl.when(pl.program_id(0) == pl.num_programs(0) - 1)
    def _():
        left = lanes((1, 128)) < 64
        side = acc[:, 512:]
        turned[...] = side
        query = jnp.where(left, pltpu.roll(turned_back(side), 64, 1), 0.0)
        first = (acc[:, :128] + query).astype(BF)
        half = first.shape[0] // 2

        def write(ref, low):
            ref[:, :128] = first[low : low + half]
            ref[:, 128:] = acc[pl.ds(low, half), 128:512].astype(BF)

        @pl.when(bounds[4] == 1)
        def _():
            write(kept, 0)
            write(sent, half)

        @pl.when(bounds[4] == 0)
        def _():
            write(kept, half)
            write(sent, 0)


def alone_grad(bounds, normed, da, ds, dt_grad):
    full = normed.shape[0]
    n = 512
    part = lambda w, col: pl.BlockSpec((n, w), lambda i, *_: (i, col))
    return pl.pallas_call(
        alone_grad_body,
        grid_spec=pltpu.PrefetchScalarGridSpec(
            num_scalar_prefetch=1,
            grid=(full // n,),
            in_specs=[
                part(1024, 0),
                part(128, 1),
                part(128, 2),
                part(384, 0),
                pl.BlockSpec((8, n), lambda i, *_: (0, i)),
            ],
            out_specs=[whole((512, 512))] * 2 + [whole((1024, 128))],
            scratch_shapes=[pltpu.VMEM((1024, 640), F32)],
        ),
        out_shape=[
            jax.ShapeDtypeStruct((512, 512), BF),
            jax.ShapeDtypeStruct((512, 512), BF),
            jax.ShapeDtypeStruct((1024, 128), F32),
        ],
        compiler_params=params(),
        cost_estimate=SMALL_COST,
        name="alone_grad",
    )(bounds, normed, da, da, ds, dt_grad)


def assemble_body(bounds, p0, p1, p2, l3, r3, out):
    step = pl.program_id(0)
    for r, ref in enumerate((p0, p1, p2)):

        @pl.when(step == r)
        def _(ref=ref):
            out[:, :512] = ref[0]
            out[:, 512:] = ref[1]

    @pl.when(step == 3)
    def _():
        out[:, :512] = l3[...]
        out[:, 512:] = r3[...]


def assemble(bounds, parts):
    count = parts[0].shape[1]
    return pl.pallas_call(
        assemble_body,
        grid_spec=pltpu.PrefetchScalarGridSpec(
            num_scalar_prefetch=1,
            grid=(4,),
            in_specs=[whole(p.shape) for p in parts],
            out_specs=pl.BlockSpec((count, 1024), lambda i, b: (i ^ b[2], 0)),
        ),
        out_shape=jax.ShapeDtypeStruct((4 * count, 1024), parts[0].dtype),
        compiler_params=pltpu.CompilerParams(vmem_limit_bytes=FULL_VMEM),
        cost_estimate=SMALL_COST,
        name="assemble",
    )(bounds, *parts)


def piece_out_body(bounds, a, b, other_a, other_b, gate, up, down, mix, att):
    first = bounds[3] == 0

    def pair(own, other):
        own, other = own.astype(F32), other.astype(F32)
        return jnp.where(first, own, other), jnp.where(first, other, own)

    low, high = pair(a[...], other_a[...])
    gate[:, :256], gate[:, 256:] = low[:, :256], high[:, :256]
    up[:, :256], up[:, 256:] = low[:, 256:], high[:, 256:]
    low, high = pair(b[...], other_b[...])
    down[:256, :], down[256:, :] = low[:, :256].T, high[:, :256].T
    low, high = low[:, 256:].T, high[:, 256:].T
    mix[:192, :], mix[192:, :] = low[:192], high[:192]
    att[:64, :], att[64:, :] = low[192:], high[192:]


def piece_out(bounds, both, other):
    n = 256
    row = pl.BlockSpec((n, 512), lambda i, *_: (i, 0))
    second = pl.BlockSpec((n, 512), lambda i, *_: (i, 1))
    col = lambda h: pl.BlockSpec((h, n), lambda i, *_: (0, i))
    sds = jax.ShapeDtypeStruct
    return pl.pallas_call(
        piece_out_body,
        grid_spec=pltpu.PrefetchScalarGridSpec(
            num_scalar_prefetch=1,
            grid=(4,),
            in_specs=[row, second, row, second],
            out_specs=[row, row, col(512), col(384), col(128)],
        ),
        out_shape=[
            sds((1024, 512), F32),
            sds((1024, 512), F32),
            sds((512, 1024), F32),
            sds((384, 1024), F32),
            sds((128, 1024), F32),
        ],
        compiler_params=params(),
        cost_estimate=SMALL_COST,
        name="piece_out",
    )(bounds, both, both, other, other)


def alone_out_body(bounds, own, other, q, z, x, dt):
    first = bounds[3] == 0
    lane = lanes((1, 128))
    left = lane < 64
    tile = lambda ref, i: ref[:, 128 * i : 128 * i + 128].astype(F32)
    u = [jnp.where(first, tile(own, i), tile(other, i)) for i in range(4)]
    v = [jnp.where(first, tile(other, i), tile(own, i)) for i in range(4)]
    swapped = lambda value: pltpu.roll(value, 64, 1)
    q[...] = jnp.where(left, u[0], swapped(v[0]))
    x[:, :128] = u[1]
    x[:, 128:256] = jnp.where(left, u[2], swapped(v[1]))
    x[:, 256:] = jnp.where(left, swapped(v[1]), swapped(v[2]))
    z[:, :128] = u[3]
    z[:, 128:256] = jnp.where(left, swapped(u[2]), swapped(v[3]))
    z[:, 256:] = jnp.where(left, swapped(v[3]), v[2])
    dt[...] = jnp.where(lane < 3, swapped(u[0]), pltpu.roll(v[0], 67, 1))[:, :6]


def alone_out(bounds, own, other):
    n = 256
    row = lambda w: pl.BlockSpec((n, w), lambda i, *_: (i, 0))
    widths = [128, 384, 384, 6]
    return pl.pallas_call(
        alone_out_body,
        grid_spec=pltpu.PrefetchScalarGridSpec(
            num_scalar_prefetch=1,
            grid=(4,),
            in_specs=[row(512), row(512)],
            out_specs=[row(w) for w in widths],
        ),
        out_shape=[jax.ShapeDtypeStruct((1024, w), F32) for w in widths],
        compiler_params=params(),
        cost_estimate=SMALL_COST,
        name="alone_out",
    )(bounds, own, other)


def piece_sum_body(bounds, *refs):
    total = lambda i: (
        refs[i][...].astype(F32) + refs[i + 1][...] + refs[i + 2][...]
    ).astype(BF)
    kept, out = refs[12:]
    for group, ref in ((0, kept), (6, out)):
        ref[:, :512] = total(group)
        ref[:, 512:] = total(group + 3)


def piece_sum(bounds, a, b):
    n = 256
    keep = pl.BlockSpec((n, 512), lambda i, s: (i + 2 - 2 * s[4], 0))
    send = pl.BlockSpec((n, 512), lambda i, s: (i + 2 * s[4], 0))
    row = pl.BlockSpec((n, 1024), lambda i, s: (i, 0))
    return pl.pallas_call(
        piece_sum_body,
        grid_spec=pltpu.PrefetchScalarGridSpec(
            num_scalar_prefetch=1,
            grid=(2,),
            in_specs=[keep] * 6 + [send] * 6,
            out_specs=[row, row],
        ),
        out_shape=[jax.ShapeDtypeStruct((512, 1024), BF)] * 2,
        compiler_params=params(),
        cost_estimate=SMALL_COST,
        name="piece_sum",
    )(bounds, *a, *b, *a, *b)


def relay_body(first, second, kept, got, left, right, total):
    left[...] = first[0]
    right[...] = second[0]
    total[...] = (kept[...].astype(F32) + got[...]).astype(BF)


def relay(first, second, kept, got):
    n = first.shape[1] // 2
    row = pl.BlockSpec((n, 512), lambda i: (i, 0))
    half = lambda k: pl.BlockSpec((1, n, 512), lambda i: (k, i, 0))
    return pl.pallas_call(
        relay_body,
        grid=(2,),
        in_specs=[half(0), half(1), row, row],
        out_specs=[row] * 3,
        out_shape=[jax.ShapeDtypeStruct((2 * n, 512), BF)] * 3,
        compiler_params=pltpu.CompilerParams(vmem_limit_bytes=FULL_VMEM),
        cost_estimate=SMALL_COST,
        name="relay",
    )(first, second, kept, got)


def halves_body(first, second, left, right):
    left[...] = first[...]
    right[...] = second[...]


def pack_halves(first, second):
    n = 256
    out = pl.BlockSpec((n, 512), lambda i: (i, 0))
    return pl.pallas_call(
        halves_body,
        grid=(4,),
        in_specs=[out, pl.BlockSpec((n, 512), lambda i: (i, 1))],
        out_specs=[out, out],
        out_shape=[jax.ShapeDtypeStruct((1024, 512), BF)] * 2,
        compiler_params=pltpu.CompilerParams(vmem_limit_bytes=FULL_VMEM),
        cost_estimate=SMALL_COST,
        name="pack_halves",
    )(first, second)


def pair_sum_body(a, b, c, d, first, second):
    first[...] = (a[...].astype(F32) + b[...]).astype(BF)
    second[...] = (c[...].astype(F32) + d[...]).astype(BF)


def pair_sum(a, b, c, d):
    n = a.shape[0] // 2
    row = pl.BlockSpec((n, a.shape[1]), lambda i: (i, 0))
    return pl.pallas_call(
        pair_sum_body,
        grid=(2,),
        in_specs=[row] * 4,
        out_specs=[row, row],
        out_shape=[jax.ShapeDtypeStruct(a.shape, BF)] * 2,
        compiler_params=pltpu.CompilerParams(vmem_limit_bytes=FULL_VMEM),
        cost_estimate=SMALL_COST,
        name="pair_sum",
    )(a, b, c, d)


def swap(value, step):
    return lax.ppermute(value, "tensor", [(i, i ^ step) for i in range(4)])


def twin(value):
    return lax.ppermute(value, "ctx", [(0, 1), (1, 0)])


def exchange(value):
    return lax.all_to_all(value, ("ctx", "tensor"), 0, 0, tiled=True)


def dp_swap(value, step):
    return lax.ppermute(value, "dp", [(i, i ^ step) for i in range(4)])


MIDDLE = [(1, 2), (2, 1), (0, 3), (3, 0)]
NEAR = [(0, 1), (1, 0), (2, 3), (3, 2)]


class DpSum:
    def __init__(self):
        self.four = lax.axis_size("dp") == 4
        place = lax.axis_index("dp")
        self.inner = (place == 1) | (place == 2)

    def first(self, kept, sent):
        if self.four:
            return lax.ppermute(sent, "dp", NEAR)
        self.rest = lax.psum(sent, "dp")
        return lax.psum(kept, "dp")

    def middle(self, value):
        return lax.ppermute(value, "dp", MIDDLE) if self.four else value

    def last(self, value):
        return lax.ppermute(value, "dp", NEAR) if self.four else value

    def add(self, kept, got):
        return plus(kept, got) if self.four else got

    def end(self, kept, got):
        if not self.four:
            return jnp.concatenate([kept, self.rest], axis=0)
        return jnp.concatenate(
            [jnp.where(self.inner, kept, got), jnp.where(self.inner, got, kept)], axis=0
        )


def together(*values):
    return lax.optimization_barrier(values)


def after(value, *before):
    return lax.optimization_barrier((value, before))[0]


def plus(a, b):
    return (a.astype(F32) + b.astype(F32)).astype(BF)


def block_at(value, index, count):
    return lax.dynamic_slice_in_dim(value, index * count, count, 0)


def merge_body(bounds, own, got, *outs):
    total = (own[...].astype(F32) + got[...].astype(F32)).astype(BF)
    for i in range(4):

        @pl.when(pl.program_id(0) == i)
        def _(i=i):
            outs[2 * i][...] = total[:, :512]
            outs[2 * i + 1][...] = total[:, 512:]


def merge(bounds, own, got):
    count = own.shape[0] // 4
    block = pl.BlockSpec((count, 1024), lambda i, b: (i ^ b[2], 0))
    once = pl.BlockSpec((count, 512), lambda i, b: (0, 0), pipeline_mode=pl.Buffered(1))
    return pl.pallas_call(
        merge_body,
        grid_spec=pltpu.PrefetchScalarGridSpec(
            num_scalar_prefetch=1,
            grid=(4,),
            in_specs=[block, block],
            out_specs=[once] * 8,
        ),
        out_shape=[jax.ShapeDtypeStruct((count, 512), BF)] * 8,
        compiler_params=params(),
        cost_estimate=SMALL_COST,
        name="merge",
    )(bounds, own, got)


def finish_body(bounds, l0, r0, l1, r1, l2, r2, tok, dhid, gain, out):
    three = lambda a, b, c: (a[...].astype(F32) + b[...]) + c[...]
    grad = jnp.concatenate([three(l0, l1, l2), three(r0, r1, r2)], axis=1)
    values = tok[...].astype(F32)
    scale = lax.rsqrt(jnp.mean(values * values, axis=-1, keepdims=True) + EPSILON)
    weighted = grad * gain[...]
    mean = jnp.mean(weighted * values, axis=-1, keepdims=True)
    total = dhid[...] + scale * weighted - values * (scale * scale * scale * mean)
    out[0] = total[:, :512].astype(BF)
    out[1] = total[:, 512:].astype(BF)


def finish(bounds, state, tokens, dhid, gain):
    count = dhid.shape[0]
    n = count // 2
    half = pl.BlockSpec((n, 512), lambda i, b: (i, 0))
    row = pl.BlockSpec((n, 1024), lambda i, b: (i, 0))
    return pl.pallas_call(
        finish_body,
        grid_spec=pltpu.PrefetchScalarGridSpec(
            num_scalar_prefetch=1,
            grid=(2,),
            in_specs=[half] * 6
            + [pl.BlockSpec((n, 1024), lambda i, b: (2 * b[2] + i, 0)), row, whole((1, 1024))],
            out_specs=pl.BlockSpec((2, n, 512), lambda i, b: (0, i, 0)),
        ),
        out_shape=jax.ShapeDtypeStruct((2, count, 512), BF),
        compiler_params=params(),
        cost_estimate=SMALL_COST,
        name="finish",
    )(bounds, *state, tokens, dhid, gain)


def rope_tables(count):
    exponent = np.arange(0, HEAD_SIZE, 2).astype(np.float32) / np.float32(HEAD_SIZE)
    frequency = (np.float32(ROPE_BASE) ** (-exponent)).astype(np.float32)
    angles = np.arange(count).astype(np.float32)[:, None] * frequency[None, :]
    angles = np.concatenate([angles] * 4, axis=1)
    return (np.cos(angles).astype(np.float32), np.sin(angles).astype(np.float32))


def local(
    tokens, doc_ids, norm_gain, q_proj, key_value_weight, o_proj, z_proj, x_proj, dt_proj,
    bc_proj, conv_x, xconv_bias, conv_bc, bcconv_bias, dt_bias, a_log, skip_gain, gated_gain,
    out_proj, mlp_gain, gate_proj, up_proj, down_proj, out_grad,
):
    t, c = lax.axis_index("tensor"), lax.axis_index("ctx")
    own_tokens, grad_out = tokens[0], out_grad[0]
    own = own_tokens.shape[0]
    full = 2 * own
    mine = own // 4
    other_tokens = twin(own_tokens)

    def cols(w):
        n = w.shape[-1] // 2
        return lax.dynamic_slice_in_dim(w, c * n, n, w.ndim - 1)

    def rows(w):
        return block_at(w, c, w.shape[0] // 2)

    here = jnp.stack([jnp.zeros((), jnp.int32), jnp.zeros((), jnp.int32), t, c]).astype(jnp.int32)
    weight, pack0 = prepare(
        here, gate_proj, up_proj, down_proj, out_proj, o_proj, key_value_weight, q_proj,
        x_proj, z_proj, dt_proj, bc_proj,
    )
    weight, pack0, doc_ids = together(weight, pack0, doc_ids)
    pack1, pack2 = swap(pack0, 1), swap(pack0, 2)
    docs = doc_ids[0]
    place_dp = lax.axis_index("dp")
    inner = (place_dp == 1) | (place_dp == 2) | (lax.axis_size("dp") != 4)
    bounds = jnp.stack([jnp.sum(docs < 1), jnp.sum(docs < 2), t, c, inner]).astype(jnp.int32)
    own_gain = rows(gated_gain)
    gain0 = jnp.concatenate([own_gain, jnp.ones((64,), F32)])
    gain0 = jnp.broadcast_to(gain0[None, None], (8, 1, 256))

    cos, sin = rope_tables(full)
    cos, sin = jnp.asarray(cos), jnp.asarray(sin)
    steps = own // PROJ_ROWS
    own_off = jnp.reshape(c * steps, (1,)).astype(jnp.int32)
    other_off = jnp.reshape((1 - c) * steps, (1,)).astype(jnp.int32)
    gain_row = norm_gain[None]
    first = project(own_off, own_tokens, gain_row, weight, cos, sin)
    normed, qp, kv, xbc, z, dt_raw = project(
        other_off, other_tokens, gain_row, weight, cos, sin, before=first
    )

    pad = lambda v: jnp.zeros(v.shape[:-1] + (64,), F32)
    cx, cb = cols(conv_x), cols(xconv_bias)
    taps = jnp.concatenate([cx, pad(cx), conv_bc], axis=1)
    taps = jnp.concatenate([taps, jnp.zeros_like(taps)], axis=0)
    bias = jnp.concatenate([cb, pad(cb), bcconv_bias])[None]
    head = jnp.stack([cols(dt_bias), -jnp.exp(cols(a_log))], axis=1)
    head = jnp.pad(head, ((0, 5), (0, 126)))
    skip = jnp.pad(jnp.repeat(cols(skip_gain), MP), (0, 64))[None]
    xbc, gain0 = together(xbc, gain0)
    gains = exchange(gain0)
    g01, g2, y, states, pre = scan_forward(bounds, xbc, z, dt_raw, taps, bias, head, skip)
    g2, g01, pack1, pack2, gains = together(g2, g01, pack1, pack2, gains)
    left3, right3 = pack_halves(pack1, pack2)
    qp, left3, right3, g01 = together(qp, left3, right3, g01)
    left3, right3 = swap(left3, 2), swap(right3, 1)
    near = [pack0, pack1, pack2]
    far = [twin(v) for v in near]
    g_rows = exchange(g01.reshape(8, mine, 128))
    tile, keep = attend(bounds, qp, kv, g2)
    tile, g_rows, far, left3, right3 = together(tile, g_rows, far, left3, right3)
    h_rows = exchange(tile.reshape(8, mine, 128))
    packs = near + [left3, right3] + far + [twin(left3), twin(right3)]

    res = row_stage(bounds, g_rows, h_rows, own_tokens, grad_out, mlp_gain[None], gains, packs)
    layer_rows, two, dmix, dhid = res[0:4]
    act, dgu, gn = list(res[4:6]), list(res[6:8]), list(res[8:10])
    mlp_part, gain_part = res[12:14]
    grad_rows = block_at(grad_out, t, mine)
    dn, late = exchange(res[10]), res[11]
    far_w = weight_stage(two, grad_rows, dmix, dgu[1], act[1], gn[1])
    far_w = [twin(v) for v in far_w]
    near_w = weight_stage(two, grad_rows, dmix, dgu[0], act[0], gn[0], *far_w)
    dn, near_w, late = together(dn, near_w, late)
    sum_a, sum_b = near_w[:4], near_w[4:]
    late = exchange(late)

    a3, b3 = swap(sum_a[3], 1), swap(sum_b[3], 2)
    a1, b2 = swap(sum_a[1], 1), swap(sum_b[2], 2)
    da = attend_back(bounds, qp, kv, keep, dn, cos, sin)
    da, a3, b3, late = together(da, a3, b3, late)
    a_next, b_next = pair_sum(sum_a[2], a3, sum_b[1], b3)
    xbc, a_next, b_next = together(xbc, a_next, b_next)
    a_next, b_next = swap(a_next, 2), swap(b_next, 1)
    own_gain_row = jnp.pad(own_gain, (0, 64))[None]
    zeros = [
        jnp.zeros((256, 128), F32),
        jnp.zeros((8, 512), F32),
        jnp.zeros((8, 512), F32),
        jnp.zeros((16, CHUNK), F32),
    ]
    back = lambda part, carry, made, data: scan_back(
        part, carry, made, bounds, data, pre, z, y, dt_raw, states, late, dn, taps, head, skip,
        own_gain_row,
    )
    ds, dt_grad, *carry = back(0, zeros, [], xbc)
    ds, a1, b2, a_next, b_next = together(ds, a1, b2, a_next, b_next)
    kept, out = piece_sum(bounds, (sum_a[0], a1, a_next), (sum_b[0], b2, b_next))
    sums, single = DpSum(), DpSum()
    xbc, out, kept, layer_rows = together(xbc, out, kept, layer_rows)
    got = sums.first(kept, out)
    layer1, layer2 = swap(layer_rows, 1), swap(layer_rows, 2)
    conv_carry = (carry[2], carry[3], carry[0], carry[1])
    ds, dt_grad, conv_acc, head_acc, _, _ = back(1, conv_carry, [ds, dt_grad], xbc)
    ds, got, layer1, layer2 = together(ds, got, layer1, layer2)

    kept = sums.add(kept, got)
    parts = [block_at(kept, i, kept.shape[0] // 4) for i in range(4)]
    layer3 = [layer1[0], layer2[1]]
    ds, layer3, parts, kept = together(ds, layer3, parts, kept)
    got0 = sums.middle(parts[0])
    layer3 = [swap(layer3[0], 2), swap(layer3[1], 1)]
    grad_other, gain_other = input_grad(other_off, da, ds, dt_grad, weight, normed)
    grad_other, ds, layer3, got0 = together(grad_other, ds, layer3, got0)
    four = lax.axis_size("dp") == 4
    sent = twin(grad_other)
    got1 = sums.middle(parts[1])
    grad_own, gain_own = input_grad(own_off, da, ds, dt_grad, weight, normed)
    grad_own, sent, got1 = together(grad_own, sent, got1)
    got2 = sums.middle(parts[2])
    pieces = merge(bounds, grad_own, sent)
    ds, pieces = together(ds, pieces)
    l0, r0, l1, r1, l2, r2, l3, r3 = pieces
    low_rows = sums.add(jnp.concatenate(parts[:2]), jnp.concatenate([got0, got1]))
    heads = jnp.concatenate(
        [
            jnp.sum(conv_acc[5, :192].reshape(3, 64), axis=1),
            jnp.sum(head_acc[0:3], axis=1),
            jnp.sum(head_acc[8:11], axis=1),
        ]
    )
    place = c * 4 + t
    own_small = jnp.pad(jnp.concatenate([conv_acc[:5, :192].reshape(-1), heads]), (0, 55))
    at_own = lax.dynamic_update_slice_in_dim(
        jnp.zeros((8, 1024), F32), own_small[None], place, 0
    )
    norm_part = (gain_other[0] + gain_own[0]) / norm_gain
    flat = jnp.concatenate(
        [at_own.reshape(-1), gain_part.reshape(-1), conv_acc[:5, 256:].reshape(-1), mlp_part[0]]
        + [norm_part]
    )
    flat = jnp.pad(flat, (0, (-flat.shape[0]) % 1024)).reshape(1, -1, 128)
    flat = jnp.broadcast_to(flat, (8,) + flat.shape[1:])
    ds, l0, r0, l1, r1, l2, r2, l3, r3, flat, low_rows, got2 = together(
        ds, l0, r0, l1, r1, l2, r2, l3, r3, flat, low_rows, got2
    )
    l3, r3 = swap(l3, 1), swap(r3, 2)
    got3 = sums.middle(parts[3])
    flat = exchange(flat)
    alone, out, turned = alone_grad(bounds, normed, da, ds, dt_grad)
    alone, out, turned, l3, r3, got3, flat = together(alone, out, turned, l3, r3, got3, flat)
    l2, r1 = pair_sum(l2, l3, r1, r3)
    flat = jnp.sum(flat, axis=0)
    high_rows = sums.add(jnp.concatenate(parts[2:]), jnp.concatenate([got2, got3]))
    count = alone.shape[0]
    if four:
        out = jnp.concatenate([out, low_rows[:, :512], low_rows[:, 512:]])
    l1, r2, l2, r1, flat, out, alone, high_rows, turned = together(
        l1, r2, l2, r1, flat, out, alone, high_rows, turned
    )
    l2, r1 = swap(l2, 2), swap(r1, 1)
    l1, r2 = swap(l1, 1), swap(r2, 2)
    got = single.first(alone, out)
    shared = shared_grad(bounds, normed, da, ds, turned)
    l1, r2, l2, r1, got, shared = together(l1, r2, l2, r1, got, shared)
    if four:
        half = count + low_rows.shape[0]
        got_low = jnp.concatenate([got[count:half], got[half:]], axis=1)
    else:
        got_low = low_rows
    got_alone = got[:count]
    token_rows = finish(bounds, [l0, r0, l1, r1, l2, r2], own_tokens, dhid, norm_gain[None])
    alone = single.add(alone, got_alone)
    shared = shared.reshape(8, 128, 512)
    token_rows, alone, high_rows, flat, shared, layer_rows, layer1, layer2, layer3 = together(
        token_rows, alone, high_rows, flat, shared, layer_rows, layer1, layer2, layer3
    )
    tok1, tok2 = swap(token_rows, 1), swap(token_rows, 2)
    got = single.middle(alone)
    got_high = sums.last(high_rows)
    flat_got = dp_swap(flat, 1) if four else lax.psum(flat, "dp")
    shared = exchange(shared)
    layer_out = assemble(bounds, [layer_rows, layer1, layer2, *layer3])
    tok1, tok2, got, flat_got, got_high, shared, layer_out = together(
        tok1, tok2, got, flat_got, got_high, shared, layer_out
    )
    both = sums.end(
        jnp.concatenate([low_rows, high_rows]), jnp.concatenate([got_low, got_high])
    )
    shared = jnp.sum(shared.astype(F32), axis=0).astype(BF)
    if four:
        shared = jnp.broadcast_to(shared[None], (4, 128, 512))
    flat = flat + flat_got if four else flat_got
    *tok3, total = relay(tok1, tok2, alone, got)
    alone = total if four else single.add(alone, got)
    tok3, alone, flat, both, shared = together(tok3, alone, flat, both, shared)
    twin_piece = twin(both)
    tok3 = [swap(tok3[0], 2), swap(tok3[1], 1)]
    got = single.last(alone)
    flat_got = dp_swap(flat, 2) if four else flat
    if four:
        shared = lax.all_to_all(shared, "dp", 0, 0, tiled=True)
    else:
        shared = lax.psum(shared.astype(F32), "dp")[None]
    outs = piece_out(bounds, both, twin_piece)
    tok3, got, flat_got, outs, shared = together(tok3, got, flat_got, outs, shared)
    alone = single.end(alone, got)
    shared = jnp.sum(shared.astype(F32), axis=0).astype(BF)
    shared = jnp.broadcast_to(shared[None], (8, 128, 512))
    alone, tok3, shared = together(alone, tok3, shared)
    alone_twin = twin(alone)
    shared = exchange(shared)
    tokens_grad = assemble(bounds, [token_rows, tok1, tok2, *tok3])
    alone, alone_twin, tokens_grad = together(alone, alone_twin, tokens_grad)
    shared = shared.reshape(1024, 512).astype(F32)
    kv_out, bc_out = shared[:, :256], shared[:, 256:]
    q_out, z_out, x_out, dt_out = alone_out(bounds, alone, alone_twin)
    flat = flat + flat_got if four else flat_got
    flat = flat.reshape(-1)
    norm_sum = flat[12544:13568]
    small = flat[:8192].reshape(8, 1024)
    gain_sum = flat[8192:10240].reshape(8, 256)
    bc_sum = flat[10240:11520].reshape(5, 256)
    mlp_sum = flat[11520:12544]
    both_cores = lambda v: jnp.stack([lax.dynamic_index_in_dim(v, k * 4 + t, 0, False) for k in range(2)])
    small = both_cores(small)
    gain_sum = both_cores(gain_sum)[:, :192].reshape(-1)
    conv_small = small[:, :960].reshape(2, 5, 192)
    conv_small = jnp.concatenate([conv_small[0], conv_small[1]], axis=1)
    head_small = small[:, 960:969].reshape(2, 3, 3)
    per_head_sum = lambda i: head_small[:, i].reshape(-1)

    gate_out, up_out, down_out, mix_out, att_out = outs
    return (
        layer_out[None],
        tokens_grad[None],
        norm_sum,
        q_out,
        kv_out,
        att_out,
        z_out,
        x_out,
        dt_out,
        bc_out,
        conv_small[:4],
        conv_small[4],
        bc_sum[:4],
        bc_sum[4],
        per_head_sum(2),
        per_head_sum(1),
        per_head_sum(0),
        gain_sum,
        mix_out,
        mlp_sum,
        gate_out,
        up_out,
        down_out,
    )


def solution(mesh):
    placed = (
        P("dp", "ctx", None),
        P("dp", None),
        P(),
        P(None, "tensor"),
        P(),
        P("tensor", None),
        P(None, "tensor"),
        P(None, "tensor"),
        P(None, "tensor"),
        P(),
        P(None, "tensor"),
        P("tensor"),
        P(),
        P(),
        P("tensor"),
        P("tensor"),
        P("tensor"),
        P("tensor"),
        P("tensor", None),
        P(),
        P(None, "tensor"),
        P(None, "tensor"),
        P("tensor", None),
        P("dp", "ctx", None),
    )
    return jax.shard_map(
        local,
        mesh=mesh,
        in_specs=placed,
        out_specs=(
            P("dp", "ctx", None),
            P("dp", "ctx", None),
            P(),
            P(None, "tensor"),
            P(),
            P("tensor", None),
            P(None, "tensor"),
            P(None, "tensor"),
            P(None, "tensor"),
            P(),
            P(None, "tensor"),
            P("tensor"),
            P(),
            P(),
            P("tensor"),
            P("tensor"),
            P("tensor"),
            P("tensor"),
            P("tensor", None),
            P(),
            P(None, "tensor"),
            P(None, "tensor"),
            P("tensor", None),
        ),
        check_vma=False,
    )
```

```python
import functools

import jax
import numpy as np
import jax.numpy as jnp
from jax import lax
from jax.experimental import pallas as pl
from jax.experimental.pallas import tpu as pltpu
from jax.sharding import PartitionSpec as P

BF, F32 = jnp.bfloat16, jnp.float32
EPSILON = 1e-05
ROPE_BASE = 100000000000.0
HEAD_SIZE = 64
MP = 64
PROJ_ROWS = 256
BQ = 512
CHUNK = 256
VMEM_LIMIT = 48 * 1024 * 1024
FULL_VMEM = 60 * 1024 * 1024
SMALL_COST = pl.CostEstimate(flops=1000000, bytes_accessed=100000, transcendentals=0)


def dot(left, right, dims=((1,), (0,)), precision=None):
    return lax.dot_general(
        left, right, (dims, ((), ())), precision=precision, preferred_element_type=F32
    )


def dot_bt(left, right):
    return dot(left, right, ((1,), (1,)))


def dot_at(left, right):
    return dot(left, right, ((0,), (0,)))


def lanes(shape):
    return lax.broadcasted_iota(jnp.int32, shape, len(shape) - 1)


def rows_of(shape):
    return lax.broadcasted_iota(jnp.int32, shape, 0)


def doc_start(pos, first, second):
    return jnp.where(pos >= second, second, jnp.where(pos >= first, first, 0))


def halves(low, high):
    return jnp.where(lanes((1, 128)) < 64, low, high)


def params(**kw):
    return pltpu.CompilerParams(vmem_limit_bytes=VMEM_LIMIT, **kw)


def whole(shape):
    return pl.BlockSpec(shape, lambda *_: (0,) * len(shape))


def proj_body(off, tok, gain, weight, cos, sin, *refs):
    normed_ref, qp_ref, kv_ref, xbc_ref, z_ref, dt_ref = refs[-6:]
    values = tok[...].astype(F32)
    scale = lax.rsqrt(jnp.mean(values * values, axis=-1, keepdims=True) + EPSILON)
    normed = (values * scale * gain[...]).astype(BF)
    normed_ref[...] = normed
    c, s = cos[...], sin[...]
    left = lanes((1, 128)) < 64
    att = dot(normed, weight[:, :384])
    kv, turned, qd = att[:, :128], att[:, 128:256], att[:, 256:]
    kv_ref[...] = jnp.where(left, kv * c + turned * s, kv).astype(BF)
    q_rot = qd * c + pltpu.roll(turned, 64, 1) * s
    qp_ref[...] = jnp.where(left, q_rot.astype(BF) * 0.125, 0.0).astype(BF)
    dt_ref[...] = qd.T[64:72, :]
    ssm = dot(normed, weight[:, 384:])
    x2z2 = ssm[:, 128:256]
    xbc_ref[:, :128] = ssm[:, :128].astype(BF)
    xbc_ref[:, 128:256] = jnp.where(left, x2z2, 0.0).astype(BF)
    xbc_ref[:, 256:] = ssm[:, 384:].astype(BF)
    z_ref[:, :128] = ssm[:, 256:384]
    z_ref[:, 128:] = jnp.where(left, pltpu.roll(x2z2, 64, 1), 0.0)


def project(off, tokens, gain, weight, cos, sin, before=None):
    own = tokens.shape[0]
    full = cos.shape[0]
    n = PROJ_ROWS
    outs = [
        jax.ShapeDtypeStruct((full, 1024), BF),
        jax.ShapeDtypeStruct((full, 128), BF),
        jax.ShapeDtypeStruct((full, 128), BF),
        jax.ShapeDtypeStruct((full, 512), BF),
        jax.ShapeDtypeStruct((full, 256), F32),
        jax.ShapeDtypeStruct((8, full), F32),
    ]
    at = lambda i, off: (off[0] + i, 0)
    out_specs = [pl.BlockSpec((n, o.shape[1]), at) for o in outs[:5]]
    out_specs.append(pl.BlockSpec((8, n), lambda i, off: (0, off[0] + i)))
    in_specs = [
        pl.BlockSpec((n, 1024), lambda i, off: (i, 0)),
        whole((1, 1024)),
        whole((1024, 1024)),
        pl.BlockSpec((n, 128), at),
        pl.BlockSpec((n, 128), at),
    ]
    args = [off, tokens, gain, weight, cos, sin]
    alias = {}
    if before is not None:
        in_specs += [pl.BlockSpec(memory_space=pl.ANY)] * 6
        args += list(before)
        alias = {6 + i: i for i in range(6)}
    return pl.pallas_call(
        proj_body,
        grid_spec=pltpu.PrefetchScalarGridSpec(
            num_scalar_prefetch=1, grid=(own // n,), in_specs=in_specs, out_specs=out_specs
        ),
        out_shape=outs,
        input_output_aliases=alias,
        compiler_params=params(),
        cost_estimate=SMALL_COST,
        name="norm_project",
    )(*args)


def turned_lanes(value):
    low = lanes((1, 128)) % 64 < 32
    return jnp.where(low, -pltpu.roll(value, 96, 1), pltpu.roll(value, 32, 1))


def prep_body(bounds, gate, up, down, mix, att, kv, q, x, z, dt, bc, weight, pack):
    n = gate.shape[0]
    pack[:, :256] = gate[...]
    pack[:, 256:512] = up[...]
    pack[:, 512:768] = down[...].T
    pack[:, 768:] = jnp.concatenate([mix[...], att[...]], axis=0).T
    first, low_kv = bounds[3] == 0, bounds[2] // 2 == 0
    lane = lanes((1, 128))
    left = lane < 64
    tile = lambda ref, i: ref[:, 128 * i : 128 * i + 128].astype(F32)
    swapped = lambda v: pltpu.roll(v, 64, 1)
    keys, values = tile(kv, 0), tile(kv, 1)
    keys = jnp.where(low_kv, keys, swapped(keys))
    values = jnp.where(low_kv, swapped(values), values)
    query = tile(q, 0)
    query = jnp.where(first, query, swapped(query))
    steps = jnp.concatenate([dt[...].astype(F32), jnp.zeros((122, n), F32)], axis=0).T
    steps = jnp.where(lane < 3, jnp.where(first, steps, pltpu.roll(steps, 125, 1)), 0.0)

    def heads(ref):
        a, b, d = tile(ref, 0), tile(ref, 1), swapped(tile(ref, 2))
        return jnp.where(first, a, jnp.where(left, swapped(b), d)), jnp.where(first, b, d)

    x01, x2 = heads(x)
    z01, z2 = heads(z)
    tiles = [
        jnp.where(left, keys, values),
        jnp.where(left, turned_lanes(keys), swapped(turned_lanes(query))),
        jnp.where(left, query, swapped(steps)),
        x01,
        jnp.where(left, x2, swapped(z2)),
        z01,
    ]
    for i, value in enumerate(tiles):
        weight[:, 128 * i : 128 * i + 128] = value.astype(BF)
    weight[:, 768:] = bc[...]


def prepare(bounds, gate, up, down, mix, att, kv, q, x, z, dt, bc):
    n = 256
    row = lambda w: pl.BlockSpec((n, w), lambda i, b: (i, 0))
    col = lambda h: pl.BlockSpec((h, n), lambda i, b: (b[3], i))
    mine = pl.BlockSpec((n, 256), lambda i, b: (i, b[3]))
    return pl.pallas_call(
        prep_body,
        grid_spec=pltpu.PrefetchScalarGridSpec(
            num_scalar_prefetch=1,
            grid=(4,),
            in_specs=[mine, mine, col(256), col(192), col(64)]
            + [row(256), row(128), row(384), row(384)]
            + [pl.BlockSpec((6, n), lambda i, b: (0, i)), row(256)],
            out_specs=[row(1024), row(1024)],
        ),
        out_shape=[jax.ShapeDtypeStruct((1024, 1024), BF)] * 2,
        compiler_params=pltpu.CompilerParams(vmem_limit_bytes=FULL_VMEM),
        cost_estimate=SMALL_COST,
        name="prepare",
    )(bounds, gate, up, down, mix, att, kv, q, x, z, dt, bc)


def block_range(qi, bounds):
    first, second = bounds[0], bounds[1]
    q0 = qi * BQ
    low = doc_start(q0, first, second) // BQ
    inner = (doc_start(q0 + BQ - 1, first, second) + BQ - 1) // BQ
    return low, jnp.minimum(jnp.maximum(inner, low), qi)


def allowed_rows(qi, kb, bounds):
    q = qi * BQ + lanes((1, BQ))
    k = kb * BQ + rows_of((BQ, 1))
    return (k <= q) & (k >= doc_start(q, bounds[0], bounds[1]))


def allowed_keys(qi, kb, bounds):
    q = qi * BQ + rows_of((BQ, 1))
    k = kb * BQ + lanes((1, BQ))
    start = doc_start(q, bounds[0], bounds[1])
    return (k <= q) & (k >= start)


def attend_body(bounds, qp, kv, g2, out_ref, keep_ref):
    qi = pl.program_id(0)
    low, inner = block_range(qi, bounds)
    q = qp[...]

    def step(kb, carry, masked):
        top, total, acc = carry
        k = kv[pl.ds(pl.multiple_of(kb * BQ, BQ), BQ), :]
        s = dot_bt(q, k)
        if masked:
            s = jnp.where(allowed_keys(qi, kb, bounds), s, -1e30)
        new_top = jnp.maximum(top, jnp.max(s, axis=1, keepdims=True))
        p = jnp.exp(s - new_top)
        fade = jnp.exp(top - new_top)
        total = total * fade + jnp.sum(p, axis=1, keepdims=True)
        acc = acc * fade + dot(p.astype(BF), k)
        return new_top, total, acc

    carry = (jnp.full((BQ, 1), -1e30, F32), jnp.zeros((BQ, 1), F32), jnp.zeros((BQ, 128), F32))
    carry = lax.fori_loop(low, inner, lambda kb, c: step(kb, c, True), carry)
    carry = lax.fori_loop(inner, qi, lambda kb, c: step(kb, c, False), carry)
    top, total, acc = step(qi, carry, True)
    out = acc / total
    left = lanes((1, 128)) < 64
    out_ref[...] = jnp.where(left, g2[...], out.astype(BF))
    keep_ref[...] = jnp.where(left, top + jnp.log(total), out)


def attend(bounds, qp, kv, g2):
    full = qp.shape[0]
    block = pl.BlockSpec((BQ, 128), lambda i, *_: (i, 0))
    return pl.pallas_call(
        attend_body,
        grid_spec=pltpu.PrefetchScalarGridSpec(
            num_scalar_prefetch=1,
            grid=(full // BQ,),
            in_specs=[block, whole((full, 128)), block],
            out_specs=[block, block],
        ),
        out_shape=[
            jax.ShapeDtypeStruct((full, 128), BF),
            jax.ShapeDtypeStruct((full, 128), F32),
        ],
        compiler_params=params(),
        cost_estimate=SMALL_COST,
        name="attend",
    )(bounds, qp, kv, g2)


def attend_back_body(bounds, qp, kv, keep, grad, cos, sin, out_ref, acc_ref):
    blocks = pl.num_programs(0)
    qi = blocks - 1 - pl.program_id(0)
    left = lanes((1, 128)) < 64

    @pl.when(pl.program_id(0) == 0)
    def _():
        acc_ref[...] = jnp.zeros_like(acc_ref)

    low, inner = block_range(qi, bounds)
    q = qp[...]
    do = jnp.where(left, 0.0, grad[0].astype(F32))
    delta = jnp.sum(do * keep[...], axis=1, keepdims=True)
    do = do.astype(BF)
    stats = jnp.where(lanes((1, 128)) == 0, keep[...], delta).T
    lse, delta = stats[0:1, :], stats[1:2, :]

    def step(kb, dq, masked):
        at = pl.ds(pl.multiple_of(kb * BQ, BQ), BQ)
        k = kv[at, :]
        p = jnp.exp(dot_bt(k, q) - lse)
        if masked:
            p = jnp.where(allowed_rows(qi, kb, bounds), p, 0.0)
        ds = (p * (dot_bt(k, do) - delta)).astype(BF)
        acc_ref[at, :] += dot(ds, q) + dot(p.astype(BF), do)
        return dq + dot_at(ds, k)

    dq = jnp.zeros((BQ, 128), F32)
    dq = lax.fori_loop(low, inner, lambda kb, c: step(kb, c, True), dq)
    dq = lax.fori_loop(inner, qi, lambda kb, c: step(kb, c, False), dq)
    dq = step(qi, dq, True) * 0.125
    dkv = acc_ref[pl.ds(pl.multiple_of(qi * BQ, BQ), BQ), :]
    c, s = cos[...], sin[...]
    out_ref[:, :128] = jnp.where(left, dkv * c, dkv).astype(BF)
    out_ref[:, 128:256] = (jnp.where(left, dkv, pltpu.roll(dq, 64, 1)) * s).astype(BF)
    out_ref[:, 256:] = jnp.where(left, dq * c, 0.0).astype(BF)


def attend_back(bounds, qp, kv, keep, grad, cos, sin):
    full = qp.shape[0]
    n = full // BQ
    block = pl.BlockSpec((BQ, 128), lambda i, *_: (n - 1 - i, 0))
    return pl.pallas_call(
        attend_back_body,
        grid_spec=pltpu.PrefetchScalarGridSpec(
            num_scalar_prefetch=1,
            grid=(n,),
            in_specs=[
                block,
                whole((full, 128)),
                block,
                pl.BlockSpec((1, BQ, 128), lambda i, *_: (n - 1 - i, 0, 0)),
                block,
                block,
            ],
            out_specs=pl.BlockSpec((BQ, 384), lambda i, *_: (n - 1 - i, 0)),
            scratch_shapes=[pltpu.VMEM((full, 128), F32)],
        ),
        out_shape=jax.ShapeDtypeStruct((full, 384), BF),
        compiler_params=params(),
        cost_estimate=SMALL_COST,
        name="attend_back",
    )(bounds, qp, kv, keep, grad, cos, sin)


def tap_mask(first_row, count, shift, bounds):
    pos = first_row + rows_of((count, 1))
    return (pos - doc_start(pos, bounds[0], bounds[1]) >= shift).astype(F32)


def conv_taps(ext_ref, r0, bounds, taps, bias):
    pre = bias + taps[3:4, :] * ext_ref[pl.ds(8, CHUNK), :]
    for shift in (1, 2, 3):
        mask = tap_mask(r0, CHUNK, shift, bounds)
        pre = pre + taps[3 - shift : 4 - shift, :] * (ext_ref[pl.ds(8 - shift, CHUNK), :] * mask)
    return pre


def chunk_decay(r0, bounds, dt_raw, head, extra=None):
    lane = lanes((1, CHUNK))
    dt = jax.nn.softplus(dt_raw + head[:, 0:1])
    la = dt * head[:, 1:2]
    upper = (rows_of((CHUNK, CHUNK)) <= lanes((CHUNK, CHUNK))).astype(F32)
    cum = dot(la, upper, precision=lax.Precision.HIGHEST)
    rows = [cum, dt] if extra is None else [cum, dt, extra]
    used = 8 * len(rows)
    stacked = jnp.concatenate(rows + [jnp.zeros((CHUNK - used, CHUNK), F32)], axis=0).T
    cum_col, dt_col = stacked[:, 0:8], stacked[:, 8:16]
    pos = r0 + rows_of((CHUNK, 1))
    start = doc_start(pos, bounds[0], bounds[1])
    start_last = doc_start(r0 + CHUNK - 1, bounds[0], bounds[1])
    key = r0 + lane
    mask = (key <= pos) & (key >= start)
    enter = jnp.where(start < r0, jnp.exp(cum_col), 0.0)
    fade = jnp.where(pos >= start_last, jnp.exp(cum_last_row(cum_col) - cum_col), 0.0)
    keep = jnp.where(start_last < r0, jnp.exp(cum_last_row(cum_col)), 0.0)
    return dt, la, cum, dt_col, cum_col, mask, enter, fade, keep, stacked[:, 16:24]


def two_terms(value):
    high = value.astype(BF)
    return high, (value - high.astype(F32)).astype(BF)


def cum_last_row(cum_col):
    return cum_col[CHUNK - 1 : CHUNK, :]


def per_head(col):
    return halves(col[:, 0:1], col[:, 1:2]), col[:, 2:3]


def state_rows(keep):
    row = rows_of((256, 1))
    return jnp.where(row < 64, keep[:, 0:1], jnp.where(row < 128, keep[:, 1:2], keep[:, 2:3]))


def scan_body(
    bounds, xbc, z, dt_raw, taps, bias, head, skip, g01, g2, y_ref, s_ref, pre_ref, ext, state
):
    i = pl.program_id(0)
    r0 = i * CHUNK

    @pl.when(i == 0)
    def _():
        ext[pl.ds(0, 8), :] = jnp.zeros((8, 512), F32)
        state[...] = jnp.zeros_like(state)

    @pl.when(i > 0)
    def _():
        ext[pl.ds(0, 8), :] = ext[pl.ds(CHUNK, 8), :]

    ext[pl.ds(8, CHUNK), :] = xbc[...].astype(F32)
    pre = conv_taps(ext, r0, bounds, taps[...], bias[...])
    pre_ref[...] = pre
    conv = pre * jax.nn.sigmoid(pre)
    x01, x2 = conv[:, :128], conv[:, 128:256]
    b, c = conv[:, 256:384].astype(BF), conv[:, 384:].astype(BF)
    dt, la, cum, dt_col, cum_col, mask, enter, fade, keep, _ = chunk_decay(
        r0, bounds, dt_raw[...], head[...]
    )
    inner = dot_bt(c, b)
    x01b, x2b = x01.astype(BF), x2.astype(BF)
    ys = []
    for h in range(3):
        gap = cum_col[:, h : h + 1] - cum[h : h + 1, :]
        decay = jnp.exp(jnp.where(mask, gap, -1e30))
        m = (inner * decay * dt[h : h + 1, :]).astype(BF)
        ys.append(dot(m, x01b if h < 2 else x2b))
    s0 = state[...]
    s_ref[0] = s0
    s0b, s0c = two_terms(s0)
    carried = dot_bt(c, s0b) + dot_bt(c, s0c)
    e01, e2 = per_head(enter)
    y01 = halves(ys[0], ys[1]) + e01 * carried[:, :128] + skip[:, :128] * x01
    y2 = ys[2] + e2 * carried[:, 128:] + skip[:, 128:] * x2
    w01, w2 = per_head(fade * dt_col)
    xw = jnp.concatenate([(x01 * w01).astype(BF), (x2 * w2).astype(BF)], axis=1)
    state[...] = s0 * state_rows(keep) + dot_at(xw, b)
    y_ref[:, :128] = y01
    y_ref[:, 128:] = y2
    z01, z2 = z[:, :128], z[:, 128:]
    g01[...] = (y01 * (z01 * jax.nn.sigmoid(z01))).astype(BF)
    g2[...] = (y2 * (z2 * jax.nn.sigmoid(z2))).astype(BF)


def scan_forward(bounds, xbc, z, dt_raw, taps, bias, head, skip):
    full = xbc.shape[0]
    n = full // CHUNK
    row = lambda width: pl.BlockSpec((CHUNK, width), lambda i, *_: (i, 0))
    return pl.pallas_call(
        scan_body,
        grid_spec=pltpu.PrefetchScalarGridSpec(
            num_scalar_prefetch=1,
            grid=(n,),
            in_specs=[
                row(512),
                row(256),
                pl.BlockSpec((8, CHUNK), lambda i, *_: (0, i)),
                whole((8, 512)),
                whole((1, 512)),
                whole((8, 128)),
                whole((1, 256)),
            ],
            out_specs=[
                row(128),
                row(128),
                row(256),
                pl.BlockSpec((1, 256, 128), lambda i, *_: (i, 0, 0)),
                row(512),
            ],
            scratch_shapes=[pltpu.VMEM((CHUNK + 8, 512), F32), pltpu.VMEM((256, 128), F32)],
        ),
        out_shape=[
            jax.ShapeDtypeStruct((full, 128), BF),
            jax.ShapeDtypeStruct((full, 128), BF),
            jax.ShapeDtypeStruct((full, 256), F32),
            jax.ShapeDtypeStruct((n, 256, 128), F32),
            jax.ShapeDtypeStruct((full, 512), F32),
        ],
        compiler_params=params(),
        cost_estimate=SMALL_COST,
        name="scan_forward",
    )(bounds, xbc, z, dt_raw, taps, bias, head, skip)


def scalar_rows(terms):
    low = terms[0:2, :] + terms[2:4, :] + terms[4:6, :]
    high = terms[6:8, :] + terms[8:10, :] + terms[10:12, :]
    total = jnp.concatenate([low, high], axis=1)
    return jnp.concatenate([total, jnp.zeros((6, CHUNK), F32)], axis=0)


def scan_back_body(
    last, bounds, xbc, before, pre_ref, z, y, dt_raw, s0_ref, dn01, dn2, scal, taps, head, skip,
    gain,
    dstate_in, dext_in, acc_in, head_in, *refs,
):
    out_ref, dt_grad, acc, head_acc, dstate_out, dext_out, ext, dext, dstate = refs[-9:]
    step = pl.program_id(0)
    i = last - step
    r0 = i * CHUNK
    left = lanes((1, 128)) < 64

    @pl.when(step == 0)
    def _():
        dext[pl.ds(CHUNK, 8), :] = dext_in[...]
        dstate[...] = dstate_in[...]
        acc[...] = acc_in[...]
        head_acc[...] = head_in[...]

    @pl.when(step > 0)
    def _():
        dext[pl.ds(CHUNK, 8), :] = dext[pl.ds(0, 8), :]

    ext[pl.ds(0, 8), :] = before[...].astype(F32)[8:, :]
    ext[pl.ds(8, CHUNK), :] = xbc[...].astype(F32)
    weights = taps[...]
    pre = pre_ref[...]
    sig = jax.nn.sigmoid(pre)
    conv = pre * sig
    x01, x2 = conv[:, :128], conv[:, 128:256]
    b, c = conv[:, 256:384].astype(BF), conv[:, 384:].astype(BF)
    dt, la, cum, dt_col, cum_col, mask, enter, fade, keep, scalars = chunk_decay(
        r0, bounds, dt_raw[...], head[...], scalar_rows(scal[0].astype(F32))
    )
    row_scale, row_cross = scalars[:, 0:1], scalars[:, 1:2]

    def gate_back(dn, gain, zz, yy):
        s = jax.nn.sigmoid(zz)
        act = zz * s
        g = yy * act
        sent = g.astype(BF).astype(F32)
        ratio = jnp.where(g == 0.0, 1.0, sent / g)
        dg = (dn * gain * row_scale - sent * row_cross) * ratio
        return dg * act, dg * yy * (s + act * (1.0 - s))

    dy01, dz01 = gate_back(dn01[0].astype(F32), gain[:, :128], z[:, :128], y[:, :128])
    dy2, dz2 = gate_back(dn2[0].astype(F32), gain[:, 128:], z[:, 128:], y[:, 128:])
    dy2, dz2 = jnp.where(left, dy2, 0.0), jnp.where(left, dz2, 0.0)
    inner = dot_bt(b, c)
    x01b, x2b = x01.astype(BF), x2.astype(BF)
    dy01b, dy2b = dy01.astype(BF), dy2.astype(BF)
    zero = jnp.zeros_like(dy01b)
    parts = [(jnp.where(left, dy01b, zero), x01b), (jnp.where(left, zero, dy01b), x01b), (dy2b, x2b)]
    query = r0 + lanes((1, CHUNK))
    key = r0 + rows_of((CHUNK, 1))
    mask = (key <= query) & (key >= doc_start(query, bounds[0], bounds[1]))
    d_inner = jnp.zeros((CHUNK, CHUNK), F32)
    dxs, direct, row_sums = [], [], []
    for h in range(3):
        gap = cum[h : h + 1, :] - cum_col[:, h : h + 1]
        decay = jnp.exp(jnp.where(mask, gap, -1e30))
        dt_h = dt_col[:, h : h + 1]
        dyh, xh = parts[h]
        dm = dot_bt(xh, dyh)
        kept = inner * decay
        dxs.append(dot((kept * dt_h).astype(BF), dyh if h == 2 else dy01b))
        pulled = dm * kept
        d_inner = d_inner + dm * (decay * dt_h)
        direct.append(jnp.sum(pulled, axis=1, keepdims=True))
        row_sums.append(jnp.sum(pulled * dt_h, axis=0, keepdims=True))
    s0 = s0_ref[0]
    s0b, s0c = two_terms(s0)
    ds1 = dstate[...]
    ds1b, ds1c = two_terms(ds1)
    e01, e2 = per_head(enter)
    ey01, ey2 = dy01 * e01, dy2 * e2
    ey, eyc = two_terms(jnp.concatenate([ey01, ey2], axis=1))
    carried = dot_bt(c, s0b) + dot_bt(c, s0c)
    f01, f2 = per_head(fade)
    d01, d2 = per_head(dt_col)
    back = dot_bt(b, ds1b)
    fb01, fb2 = f01 * back[:, :128], f2 * back[:, 128:]
    xw = jnp.concatenate([(x01 * (f01 * d01)).astype(BF), (x2 * (f2 * d2)).astype(BF)], axis=1)
    d_innerb = d_inner.astype(BF)
    dc = dot_at(d_innerb, b) + dot(ey, s0b) + dot(eyc, s0b) + dot(ey, s0c)
    db = dot(d_innerb, c) + dot(xw, ds1b) + dot(xw, ds1c)
    dx01 = halves(dxs[0], dxs[1]) + d01 * fb01 + skip[:, :128] * dy01
    dx2 = dxs[2] + d2 * fb2 + skip[:, 128:] * dy2
    kept_rows = state_rows(keep)
    crossing = jnp.sum(ds1 * s0 * kept_rows, axis=1, keepdims=True)
    dstate[...] = ds1 * kept_rows + dot_at(ey, c) + dot_at(eyc, c)
    inter01, inter2 = ey01 * carried[:, :128], ey2 * carried[:, 128:]
    u01, u2 = x01 * fb01, x2 * fb2
    pick = lambda v, h: jnp.where(left if h == 0 else ~left, v, 0.0)
    side = lambda v01, v2, h: jnp.sum(pick(v01, h) if h < 2 else v2, axis=1, keepdims=True)
    lane = lanes((1, CHUNK))
    tile = jnp.zeros((CHUNK, CHUNK), F32)
    crossed = jnp.zeros((8, 1), F32)
    head_row = rows_of((8, 1))
    for h in range(3):
        u = side(u01, u2, h)
        pulled = u + direct[h]
        moved = side(inter01, inter2, h) - pulled * dt_col[:, h : h + 1]
        tile = jnp.where(lane == h, moved, jnp.where(lane == 8 + h, pulled, tile))
        total = jnp.sum(crossing[64 * h : 64 * h + 64, :], axis=0, keepdims=True)
        total = total + jnp.sum(u * dt_col[:, h : h + 1], axis=0, keepdims=True)
        crossed = jnp.where(head_row == h, total, crossed)
    tile = tile.T
    stack = lambda items: jnp.concatenate(items + [jnp.zeros((5, CHUNK), F32)], axis=0)
    dcum = tile[0:8, :] + stack(row_sums) + jnp.where(lane == CHUNK - 1, crossed, 0.0)
    lower = (rows_of((CHUNK, CHUNK)) >= lanes((CHUNK, CHUNK))).astype(F32)
    dla = dot(dcum, lower, precision=lax.Precision.HIGHEST)
    ddt = tile[8:16, :] + dla * head[:, 1:2]
    graw = ddt * jax.nn.sigmoid(dt_raw[...] + head[:, 0:1])
    dt_grad[...] = graw
    head_acc[0:8, :] += dla * la
    head_acc[8:16, :] += graw
    dpre = jnp.concatenate([dx01, dx2, db, dc], axis=1) * (sig + conv * (1.0 - sig))
    dext[pl.ds(0, CHUNK), :] = dpre
    din = weights[3:4, :] * dpre
    acc[3:4, :] += jnp.sum(dpre * ext[pl.ds(8, CHUNK), :], axis=0, keepdims=True)
    acc[4:5, :] += jnp.sum(dpre, axis=0, keepdims=True)
    acc[5:6, :128] += jnp.sum(dy01 * x01, axis=0, keepdims=True)
    acc[5:6, 128:256] += jnp.sum(dy2 * x2, axis=0, keepdims=True)
    for shift in (1, 2, 3):
        tap = 3 - shift
        now = tap_mask(r0, CHUNK, shift, bounds)
        acc[tap : tap + 1, :] += jnp.sum(
            dpre * (ext[pl.ds(8 - shift, CHUNK), :] * now), axis=0, keepdims=True
        )
        later = tap_mask(r0 + shift, CHUNK, shift, bounds)
        din = din + weights[tap : tap + 1, :] * (dext[pl.ds(shift, CHUNK), :] * later)
    out_ref[:, :128] = din[:, :128].astype(BF)
    out_ref[:, 128:256] = jnp.where(left, din[:, 128:256], pltpu.roll(dz2, 64, 1)).astype(BF)
    out_ref[:, 256:384] = dz01.astype(BF)
    out_ref[:, 384:] = din[:, 256:].astype(BF)

    @pl.when(step == pl.num_programs(0) - 1)
    def _():
        dstate_out[...] = dstate[...]
        dext_out[...] = dext[pl.ds(0, 8), :]


def scan_back(
    part, carry, before, bounds, xbc, pre, z, y, dt_raw, states, late, dn, taps, head, skip, gain
):
    full = xbc.shape[0]
    n = full // CHUNK
    half = n // 2
    last = n - 1 if part == 0 else half - 1
    row = lambda width: pl.BlockSpec((CHUNK, width), lambda i, *_: (last - i, 0))
    tall = CHUNK // 16
    per = n // 8
    sent = pl.BlockSpec((1, CHUNK, 128), lambda i, b: ((last - i) // per, (last - i) % per, 0))

    def terms(i, b):
        piece, rest = (last - i) // per, (last - i) % per
        return piece, per * (CHUNK // 16) + rest, 0

    carried = [whole((256, 128)), whole((8, 512)), whole((8, 512)), whole((16, CHUNK))]
    sds = jax.ShapeDtypeStruct
    args = [bounds, xbc, xbc, pre, z, y, dt_raw, states, late, dn, late, taps, head, skip, gain]
    args += list(carry) + list(before)
    alias = {len(args) - 2: 0, len(args) - 1: 1} if before else {}
    return pl.pallas_call(
        functools.partial(scan_back_body, last),
        grid_spec=pltpu.PrefetchScalarGridSpec(
            num_scalar_prefetch=1,
            grid=(half,),
            in_specs=[
                row(512),
                pl.BlockSpec((16, 512), lambda i, *_: (jnp.maximum((last - i) * tall - 1, 0), 0)),
                row(512),
                row(256),
                row(256),
                pl.BlockSpec((8, CHUNK), lambda i, *_: (0, last - i)),
                pl.BlockSpec((1, 256, 128), lambda i, *_: (last - i, 0, 0)),
                sent,
                sent,
                pl.BlockSpec((1, 16, 128), terms),
                whole((8, 512)),
                whole((8, 128)),
                whole((1, 256)),
                whole((1, 256)),
            ]
            + carried
            + [pl.BlockSpec(memory_space=pl.ANY)] * len(before),
            out_specs=[
                row(640),
                pl.BlockSpec((8, CHUNK), lambda i, *_: (0, last - i)),
                whole((8, 512)),
                whole((16, CHUNK)),
                whole((256, 128)),
                whole((8, 512)),
            ],
            scratch_shapes=[
                pltpu.VMEM((CHUNK + 8, 512), F32),
                pltpu.VMEM((CHUNK + 8, 512), F32),
                pltpu.VMEM((256, 128), F32),
            ],
        ),
        out_shape=[
            sds((full, 640), BF),
            sds((8, full), F32),
            sds((8, 512), F32),
            sds((16, CHUNK), F32),
            sds((256, 128), F32),
            sds((8, 512), F32),
        ],
        input_output_aliases=alias,
        compiler_params=params(),
        cost_estimate=SMALL_COST,
        name="scan_back",
    )(*args)


ROW_BLOCK = 256


def row_body(bounds, g, h, tok, gout, mlp_gain, gains, *refs):
    packs, refs = refs[:10], refs[10:]
    pa, pb, slots = [], [], []
    for k, base in enumerate((0, 5)):
        for r in range(4):
            first = packs[base + r]
            second = first.at[:, 512:] if r < 3 else packs[base + 4]
            pa.append(first.at[:, 0:512])
            pb.append(second)
            slots.append((bounds[3] ^ k) * 4 + (bounds[2] ^ r))
    gain_rows = [gains[slot] for slot in slots]
    out_ref, two_ref, dmix_ref, dhid_ref = refs[0:4]
    act_refs, dgu_refs, gn_refs = refs[4:6], refs[6:8], refs[8:10]
    dn, dn_late, mlp_acc, gain_acc = refs[10:14]
    step = pl.program_id(0)
    left = lanes((1, 128)) < 64
    width = 1536.0

    @pl.when(pl.program_id(0) == 0)
    def _():
        mlp_acc[...] = jnp.zeros_like(mlp_acc)
        gain_acc[...] = jnp.zeros_like(gain_acc)

    pieces = [(r, k) for k in range(2) for r in range(4)]

    def part(ref, s):
        return ref[slots[s]].astype(F32)

    squares = 0.0
    for s in range(8):
        first, second = part(g, s), part(h, s)
        squares = squares + first * first + jnp.where(left, second * second, 0.0)
    rg = lax.rsqrt(jnp.sum(squares, axis=1, keepdims=True) / width + EPSILON)
    mixed = 0.0
    for s, (r, k) in enumerate(pieces):
        gain = gain_rows[s]
        first = part(g, s) * rg * gain[:, :128]
        second = part(h, s)
        second = jnp.where(left, second * rg * gain[:, 128:], second)
        gn = jnp.concatenate([first.astype(BF), second.astype(BF)], axis=1)
        gn_refs[k][:, r * 256 : r * 256 + 256] = gn
        mixed = mixed + dot_bt(gn, pb[s][:, 256:])
    hidden = tok[...].astype(F32) + mixed
    scale = lax.rsqrt(jnp.mean(hidden * hidden, axis=-1, keepdims=True) + EPSILON)
    two = (hidden * scale * mlp_gain[...]).astype(BF)
    two_ref[...] = two
    grad = gout[...]
    ffn = 0.0
    dtwo = 0.0
    for s, (r, k) in enumerate(pieces):
        weight, down = pa[s][...], pb[s][:, :256]
        gu = dot(two, weight)
        gate, up = gu[:, :256], gu[:, 256:]
        sig = jax.nn.sigmoid(gate)
        silu = gate * sig
        act = (silu * up).astype(BF)
        act_refs[k][:, r * 256 : r * 256 + 256] = act
        ffn = ffn + dot_bt(act, down)
        dact = dot(grad, down)
        dgate = (dact * up * (sig + silu * (1.0 - sig))).astype(BF)
        dgu = jnp.concatenate([dgate, (dact * silu).astype(BF)], axis=1)
        dgu_refs[k][:, r * 512 : r * 512 + 512] = dgu
        dtwo = dtwo + dot_bt(dgu, weight)
    whole_out = (hidden + ffn).astype(BF)
    out_ref[0] = whole_out[:, :512]
    out_ref[1] = whole_out[:, 512:]
    weighted = dtwo * mlp_gain[...]
    mlp_acc[...] += jnp.sum(dtwo * (hidden * scale), axis=0, keepdims=True)
    mean = jnp.mean(weighted * hidden, axis=-1, keepdims=True)
    dhid = grad.astype(F32) + scale * weighted - hidden * (scale * scale * scale * mean)
    dhid_ref[...] = dhid
    dmix = dhid.astype(BF)
    dmix_ref[...] = dmix
    cross = 0.0
    for s, (r, k) in enumerate(pieces):
        dgn = dot(dmix, pb[s][:, 256:]).astype(BF)
        at = pl.ds(pl.multiple_of(step * ROW_BLOCK, ROW_BLOCK), ROW_BLOCK)
        dn[slots[s], at, :] = dgn[:, 128:]
        dn_late[slots[s], at, :] = dgn[:, :128]
        first, second = dgn[:, :128].astype(F32), dgn[:, 128:].astype(F32)
        gain = gain_rows[s]
        own1, own2 = part(g, s), jnp.where(left, part(h, s), 0.0)
        t1, t2 = first * own1, second * own2
        gain_acc[slots[s], :, :128] += jnp.sum(t1 * rg, axis=0, keepdims=True)
        gain_acc[slots[s], :, 128:] += jnp.sum(t2 * rg, axis=0, keepdims=True)
        cross = cross + t1 * gain[:, :128] + t2 * gain[:, 128:]
    cross = jnp.sum(cross, axis=1, keepdims=True) * (rg * rg * rg / width)
    lane = lanes((1, 128))
    tile = jnp.where(lane == 0, rg, jnp.where(lane == 1, cross, 0.0))
    pair = tile.T[0:2, :]
    high = pair.astype(BF)
    rest = pair - high.astype(F32)
    middle = rest.astype(BF)
    low = (rest - middle.astype(F32)).astype(BF)
    terms = [v.astype(F32) for v in (high, middle, low)]
    block = jnp.concatenate(
        [v[:, :128] for v in terms] + [v[:, 128:] for v in terms] + [jnp.zeros((4, 128), F32)],
        axis=0,
    ).astype(BF)
    for s in range(8):
        dn_late[s, pl.ds(pl.multiple_of(2 * ROW_BLOCK + step * 16, 16), 16), :] = block


def row_stage(bounds, g, h, tokens, gout, mlp_gain, gains, packs):
    n = ROW_BLOCK
    count = 2 * n
    row = lambda w: pl.BlockSpec((n, w), lambda i, b: (i, 0))
    part = pl.BlockSpec((n, 1024), lambda i, b: (2 * b[2] + i, 0))
    piece = pl.BlockSpec((8, n, 128), lambda i, b: (0, i, 0))
    once = lambda shape: pl.BlockSpec(
        shape, lambda i, b: (0,) * len(shape), pipeline_mode=pl.Buffered(1)
    )
    sds = jax.ShapeDtypeStruct
    widths = [1024] * 4 + [1024] * 2 + [2048] * 2 + [1024] * 2
    dtypes = [BF] * 3 + [F32] + [BF] * 6
    return pl.pallas_call(
        row_body,
        grid_spec=pltpu.PrefetchScalarGridSpec(
            num_scalar_prefetch=1,
            grid=(2,),
            in_specs=[piece, piece, part, part, whole((1, 1024)), whole((8, 1, 256))]
            + [once(p.shape) for p in packs],
            out_specs=[pl.BlockSpec((2, n, 512), lambda i, b: (0, i, 0))]
            + [row(w) for w in widths[1:]]
            + [once((8, count, 128)), once((8, count + 32, 128))]
            + [whole((1, 1024)), whole((8, 1, 256))],
        ),
        out_shape=[sds((2, count, 512), BF)]
        + [sds((count, w), d) for w, d in zip(widths[1:], dtypes[1:])]
        + [sds((8, count, 128), BF), sds((8, count + 32, 128), BF)]
        + [sds((1, 1024), F32), sds((8, 1, 256), F32)],
        compiler_params=pltpu.CompilerParams(vmem_limit_bytes=58 * 1024 * 1024),
        cost_estimate=SMALL_COST,
        name="row_stage",
    )(bounds, g, h, tokens, gout, mlp_gain, gains, *packs)


def weight_body(two, gout, dmix, dgu, act, gn, *refs):
    a = dot_at(two[...], dgu[...])
    b = jnp.concatenate([dot_at(gout[...], act[...]), dot_at(dmix[...], gn[...])], axis=1)
    if len(refs) == 2:
        refs[0][0] = a.astype(BF)
        refs[1][0] = b.astype(BF)
    else:
        a = (a + refs[0][0].astype(F32)).astype(BF)
        b = (b + refs[1][0].astype(F32)).astype(BF)
        for i in range(4):

            @pl.when(pl.program_id(0) == i)
            def _(i=i):
                refs[2 + i][...] = a
                refs[6 + i][...] = b


def weight_stage(two, gout, dmix, dgu, act, gn, *others):
    count = two.shape[0]
    col = lambda w: pl.BlockSpec((count, w), lambda i: (0, i))
    piece = pl.BlockSpec((1, 1024, 512), lambda i: (i, 0, 0))
    once = pl.BlockSpec((1024, 512), lambda i: (0, 0), pipeline_mode=pl.Buffered(1))
    sds = jax.ShapeDtypeStruct
    return pl.pallas_call(
        weight_body,
        grid=(4,),
        in_specs=[whole((count, 1024))] * 3
        + [col(512), col(256), col(256)]
        + [piece] * len(others),
        out_specs=[once] * 8 if others else [piece] * 2,
        out_shape=[sds((1024, 512), BF)] * 8 if others else [sds((4, 1024, 512), BF)] * 2,
        compiler_params=pltpu.CompilerParams(vmem_limit_bytes=FULL_VMEM),
        cost_estimate=SMALL_COST,
        name="weight_stage",
    )(two, gout, dmix, dgu, act, gn, *others)


def with_steps(da, dt_grad):
    count = da.shape[0]
    cols = jnp.concatenate([dt_grad, jnp.zeros((120, count), F32)], axis=0).T
    last = jnp.where(lanes((1, 128)) < 64, da[:, 256:].astype(F32), pltpu.roll(cols, 64, 1))
    return jnp.concatenate([da[:, :256], last.astype(BF)], axis=1)


def input_grad_body(off, da, ds, dt_grad, weight, normed, out_ref, gain_ref):
    left = with_steps(da[...], dt_grad[...])
    grad = dot_bt(left, weight[:, :384]) + dot_bt(ds[...], weight[:, 384:])
    out_ref[...] = grad.astype(BF)

    @pl.when(pl.program_id(0) == 0)
    def _():
        gain_ref[...] = jnp.zeros_like(gain_ref)

    gain_ref[...] += jnp.sum(grad * normed[...].astype(F32), axis=0, keepdims=True)


def input_grad(off, da, ds, dt_grad, weight, normed):
    n = PROJ_ROWS
    own = ds.shape[0] // 2
    at = lambda i, off: (off[0] + i, 0)
    return pl.pallas_call(
        input_grad_body,
        grid_spec=pltpu.PrefetchScalarGridSpec(
            num_scalar_prefetch=1,
            grid=(own // n,),
            in_specs=[
                pl.BlockSpec((n, 384), at),
                pl.BlockSpec((n, 640), at),
                pl.BlockSpec((8, n), lambda i, off: (0, off[0] + i)),
                whole((1024, 1024)),
                pl.BlockSpec((n, 1024), at),
            ],
            out_specs=[pl.BlockSpec((n, 1024), lambda i, off: (i, 0)), whole((1, 1024))],
        ),
        out_shape=[
            jax.ShapeDtypeStruct((own, 1024), BF),
            jax.ShapeDtypeStruct((1, 1024), F32),
        ],
        compiler_params=params(),
        cost_estimate=SMALL_COST,
        name="input_grad",
    )(off, da, ds, dt_grad, weight, normed)


def turned_back(value):
    low = lanes((1, 128)) % 64 < 32
    return jnp.where(low, pltpu.roll(value, 96, 1), -pltpu.roll(value, 32, 1))


def shared_grad_body(bounds, normed, da, ds1, ds2, turned, shared, acc):
    @pl.when(pl.program_id(0) == 0)
    def _():
        acc[...] = jnp.zeros_like(acc)

    cols = jnp.concatenate([da[...], ds1[...], ds2[...]], axis=1)
    acc[...] += dot_at(normed[...], cols)

    @pl.when(pl.program_id(0) == pl.num_programs(0) - 1)
    def _():
        left = lanes((1, 128)) < 64
        kv = acc[:, :128] + jnp.where(left, turned_back(turned[...]), 0.0)
        low = bounds[2] // 2 == 0
        swapped = pltpu.roll(kv, 64, 1)
        keys = jnp.where(left == low, jnp.where(low, kv, swapped), 0.0)
        values = jnp.where(left == low, jnp.where(low, swapped, kv), 0.0)
        shared[:, :128] = keys.astype(BF)
        shared[:, 128:256] = values.astype(BF)
        shared[:, 256:] = acc[:, 128:].astype(BF)


def shared_grad(bounds, normed, da, ds, turned):
    full = normed.shape[0]
    n = 512
    part = lambda w, col: pl.BlockSpec((n, w), lambda i, *_: (i, col))
    return pl.pallas_call(
        shared_grad_body,
        grid_spec=pltpu.PrefetchScalarGridSpec(
            num_scalar_prefetch=1,
            grid=(full // n,),
            in_specs=[part(1024, 0), part(128, 0), part(128, 3), part(128, 4)]
            + [whole((1024, 128))],
            out_specs=whole((1024, 512)),
            scratch_shapes=[pltpu.VMEM((1024, 384), F32)],
        ),
        out_shape=jax.ShapeDtypeStruct((1024, 512), BF),
        compiler_params=params(),
        cost_estimate=SMALL_COST,
        name="shared_grad",
    )(bounds, normed, da, ds, ds, turned)


def alone_grad_body(bounds, normed, da1, da2, ds, dt_grad, kept, sent, turned, acc):
    @pl.when(pl.program_id(0) == 0)
    def _():
        acc[...] = jnp.zeros_like(acc)

    count = da1.shape[0]
    cols = jnp.concatenate([dt_grad[...], jnp.zeros((120, count), F32)], axis=0).T
    last = jnp.where(lanes((1, 128)) < 64, da2[...].astype(F32), pltpu.roll(cols, 64, 1))
    acc[...] += dot_at(
        normed[...], jnp.concatenate([last.astype(BF), ds[...], da1[...]], axis=1)
    )

    @pl.when(pl.program_id(0) == pl.num_programs(0) - 1)
    def _():
        left = lanes((1, 128)) < 64
        side = acc[:, 512:]
        turned[...] = side
        query = jnp.where(left, pltpu.roll(turned_back(side), 64, 1), 0.0)
        first = (acc[:, :128] + query).astype(BF)
        half = first.shape[0] // 2

        def write(ref, low):
            ref[:, :128] = first[low : low + half]
            ref[:, 128:] = acc[pl.ds(low, half), 128:512].astype(BF)

        @pl.when(bounds[4] == 1)
        def _():
            write(kept, 0)
            write(sent, half)

        @pl.when(bounds[4] == 0)
        def _():
            write(kept, half)
            write(sent, 0)


def alone_grad(bounds, normed, da, ds, dt_grad):
    full = normed.shape[0]
    n = 512
    part = lambda w, col: pl.BlockSpec((n, w), lambda i, *_: (i, col))
    return pl.pallas_call(
        alone_grad_body,
        grid_spec=pltpu.PrefetchScalarGridSpec(
            num_scalar_prefetch=1,
            grid=(full // n,),
            in_specs=[
                part(1024, 0),
                part(128, 1),
                part(128, 2),
                part(384, 0),
                pl.BlockSpec((8, n), lambda i, *_: (0, i)),
            ],
            out_specs=[whole((512, 512))] * 2 + [whole((1024, 128))],
            scratch_shapes=[pltpu.VMEM((1024, 640), F32)],
        ),
        out_shape=[
            jax.ShapeDtypeStruct((512, 512), BF),
            jax.ShapeDtypeStruct((512, 512), BF),
            jax.ShapeDtypeStruct((1024, 128), F32),
        ],
        compiler_params=params(),
        cost_estimate=SMALL_COST,
        name="alone_grad",
    )(bounds, normed, da, da, ds, dt_grad)


def assemble_body(bounds, p0, p1, p2, l3, r3, out):
    step = pl.program_id(0)
    for r, ref in enumerate((p0, p1, p2)):

        @pl.when(step == r)
        def _(ref=ref):
            out[:, :512] = ref[0]
            out[:, 512:] = ref[1]

    @pl.when(step == 3)
    def _():
        out[:, :512] = l3[...]
        out[:, 512:] = r3[...]


def assemble(bounds, parts):
    count = parts[0].shape[1]
    return pl.pallas_call(
        assemble_body,
        grid_spec=pltpu.PrefetchScalarGridSpec(
            num_scalar_prefetch=1,
            grid=(4,),
            in_specs=[whole(p.shape) for p in parts],
            out_specs=pl.BlockSpec((count, 1024), lambda i, b: (i ^ b[2], 0)),
        ),
        out_shape=jax.ShapeDtypeStruct((4 * count, 1024), parts[0].dtype),
        compiler_params=pltpu.CompilerParams(vmem_limit_bytes=FULL_VMEM),
        cost_estimate=SMALL_COST,
        name="assemble",
    )(bounds, *parts)


def piece_out_body(bounds, a, b, other_a, other_b, gate, up, down, mix, att):
    first = bounds[3] == 0

    def pair(own, other):
        own, other = own.astype(F32), other.astype(F32)
        return jnp.where(first, own, other), jnp.where(first, other, own)

    low, high = pair(a[...], other_a[...])
    gate[:, :256], gate[:, 256:] = low[:, :256], high[:, :256]
    up[:, :256], up[:, 256:] = low[:, 256:], high[:, 256:]
    low, high = pair(b[...], other_b[...])
    down[:256, :], down[256:, :] = low[:, :256].T, high[:, :256].T
    low, high = low[:, 256:].T, high[:, 256:].T
    mix[:192, :], mix[192:, :] = low[:192], high[:192]
    att[:64, :], att[64:, :] = low[192:], high[192:]


def piece_out(bounds, both, other):
    n = 256
    row = pl.BlockSpec((n, 512), lambda i, *_: (i, 0))
    second = pl.BlockSpec((n, 512), lambda i, *_: (i, 1))
    col = lambda h: pl.BlockSpec((h, n), lambda i, *_: (0, i))
    sds = jax.ShapeDtypeStruct
    return pl.pallas_call(
        piece_out_body,
        grid_spec=pltpu.PrefetchScalarGridSpec(
            num_scalar_prefetch=1,
            grid=(4,),
            in_specs=[row, second, row, second],
            out_specs=[row, row, col(512), col(384), col(128)],
        ),
        out_shape=[
            sds((1024, 512), F32),
            sds((1024, 512), F32),
            sds((512, 1024), F32),
            sds((384, 1024), F32),
            sds((128, 1024), F32),
        ],
        compiler_params=params(),
        cost_estimate=SMALL_COST,
        name="piece_out",
    )(bounds, both, both, other, other)


def alone_out_body(bounds, own, other, q, z, x, dt):
    first = bounds[3] == 0
    lane = lanes((1, 128))
    left = lane < 64
    tile = lambda ref, i: ref[:, 128 * i : 128 * i + 128].astype(F32)
    u = [jnp.where(first, tile(own, i), tile(other, i)) for i in range(4)]
    v = [jnp.where(first, tile(other, i), tile(own, i)) for i in range(4)]
    swapped = lambda value: pltpu.roll(value, 64, 1)
    q[...] = jnp.where(left, u[0], swapped(v[0]))
    x[:, :128] = u[1]
    x[:, 128:256] = jnp.where(left, u[2], swapped(v[1]))
    x[:, 256:] = jnp.where(left, swapped(v[1]), swapped(v[2]))
    z[:, :128] = u[3]
    z[:, 128:256] = jnp.where(left, swapped(u[2]), swapped(v[3]))
    z[:, 256:] = jnp.where(left, swapped(v[3]), v[2])
    dt[...] = jnp.where(lane < 3, swapped(u[0]), pltpu.roll(v[0], 67, 1)).T[:6, :]


def alone_out(bounds, own, other):
    n = 256
    row = lambda w: pl.BlockSpec((n, w), lambda i, *_: (i, 0))
    widths = [128, 384, 384]
    return pl.pallas_call(
        alone_out_body,
        grid_spec=pltpu.PrefetchScalarGridSpec(
            num_scalar_prefetch=1,
            grid=(4,),
            in_specs=[row(512), row(512)],
            out_specs=[row(w) for w in widths] + [pl.BlockSpec((6, n), lambda i, *_: (0, i))],
        ),
        out_shape=[jax.ShapeDtypeStruct((1024, w), F32) for w in widths]
        + [jax.ShapeDtypeStruct((6, 1024), F32)],
        compiler_params=params(),
        cost_estimate=SMALL_COST,
        name="alone_out",
    )(bounds, own, other)


def piece_sum_body(bounds, *refs):
    total = lambda i: (
        refs[i][...].astype(F32) + refs[i + 1][...] + refs[i + 2][...]
    ).astype(BF)
    kept, out = refs[12:]
    for group, ref in ((0, kept), (6, out)):
        ref[:, :512] = total(group)
        ref[:, 512:] = total(group + 3)


def piece_sum(bounds, a, b):
    n = 256
    keep = pl.BlockSpec((n, 512), lambda i, s: (i + 2 - 2 * s[4], 0))
    send = pl.BlockSpec((n, 512), lambda i, s: (i + 2 * s[4], 0))
    row = pl.BlockSpec((n, 1024), lambda i, s: (i, 0))
    return pl.pallas_call(
        piece_sum_body,
        grid_spec=pltpu.PrefetchScalarGridSpec(
            num_scalar_prefetch=1,
            grid=(2,),
            in_specs=[keep] * 6 + [send] * 6,
            out_specs=[row, row],
        ),
        out_shape=[jax.ShapeDtypeStruct((512, 1024), BF)] * 2,
        compiler_params=params(),
        cost_estimate=SMALL_COST,
        name="piece_sum",
    )(bounds, *a, *b, *a, *b)


def relay_body(first, second, kept, got, left, right, total):
    left[...] = first[0]
    right[...] = second[0]
    total[...] = (kept[...].astype(F32) + got[...]).astype(BF)


def relay(first, second, kept, got):
    n = first.shape[1] // 2
    row = pl.BlockSpec((n, 512), lambda i: (i, 0))
    half = lambda k: pl.BlockSpec((1, n, 512), lambda i: (k, i, 0))
    return pl.pallas_call(
        relay_body,
        grid=(2,),
        in_specs=[half(0), half(1), row, row],
        out_specs=[row] * 3,
        out_shape=[jax.ShapeDtypeStruct((2 * n, 512), BF)] * 3,
        compiler_params=pltpu.CompilerParams(vmem_limit_bytes=FULL_VMEM),
        cost_estimate=SMALL_COST,
        name="relay",
    )(first, second, kept, got)


def halves_body(first, second, left, right):
    left[...] = first[...]
    right[...] = second[...]


def pack_halves(first, second):
    n = 256
    out = pl.BlockSpec((n, 512), lambda i: (i, 0))
    return pl.pallas_call(
        halves_body,
        grid=(4,),
        in_specs=[out, pl.BlockSpec((n, 512), lambda i: (i, 1))],
        out_specs=[out, out],
        out_shape=[jax.ShapeDtypeStruct((1024, 512), BF)] * 2,
        compiler_params=pltpu.CompilerParams(vmem_limit_bytes=FULL_VMEM),
        cost_estimate=SMALL_COST,
        name="pack_halves",
    )(first, second)


def pair_sum_body(a, b, c, d, first, second):
    first[...] = (a[...].astype(F32) + b[...]).astype(BF)
    second[...] = (c[...].astype(F32) + d[...]).astype(BF)


def pair_sum(a, b, c, d):
    n = a.shape[0] // 2
    row = pl.BlockSpec((n, a.shape[1]), lambda i: (i, 0))
    return pl.pallas_call(
        pair_sum_body,
        grid=(2,),
        in_specs=[row] * 4,
        out_specs=[row, row],
        out_shape=[jax.ShapeDtypeStruct(a.shape, BF)] * 2,
        compiler_params=pltpu.CompilerParams(vmem_limit_bytes=FULL_VMEM),
        cost_estimate=SMALL_COST,
        name="pair_sum",
    )(a, b, c, d)


def swap(value, step):
    return lax.ppermute(value, "tensor", [(i, i ^ step) for i in range(4)])


def twin(value):
    return lax.ppermute(value, "ctx", [(0, 1), (1, 0)])


def exchange(value):
    return lax.all_to_all(value, ("ctx", "tensor"), 0, 0, tiled=True)


def dp_swap(value, step):
    return lax.ppermute(value, "dp", [(i, i ^ step) for i in range(4)])


MIDDLE = [(1, 2), (2, 1), (0, 3), (3, 0)]
NEAR = [(0, 1), (1, 0), (2, 3), (3, 2)]


class DpSum:
    def __init__(self):
        self.four = lax.axis_size("dp") == 4
        place = lax.axis_index("dp")
        self.inner = (place == 1) | (place == 2)

    def first(self, kept, sent):
        if self.four:
            return lax.ppermute(sent, "dp", NEAR)
        self.rest = lax.psum(sent, "dp")
        return lax.psum(kept, "dp")

    def middle(self, value):
        return lax.ppermute(value, "dp", MIDDLE) if self.four else value

    def last(self, value):
        return lax.ppermute(value, "dp", NEAR) if self.four else value

    def add(self, kept, got):
        return plus(kept, got) if self.four else got

    def end(self, kept, got):
        if not self.four:
            return jnp.concatenate([kept, self.rest], axis=0)
        return jnp.concatenate(
            [jnp.where(self.inner, kept, got), jnp.where(self.inner, got, kept)], axis=0
        )


def together(*values):
    return lax.optimization_barrier(values)


def after(value, *before):
    return lax.optimization_barrier((value, before))[0]


def plus(a, b):
    return (a.astype(F32) + b.astype(F32)).astype(BF)


def block_at(value, index, count):
    return lax.dynamic_slice_in_dim(value, index * count, count, 0)


def merge_body(bounds, own, got, *outs):
    total = (own[...].astype(F32) + got[...].astype(F32)).astype(BF)
    for i in range(4):

        @pl.when(pl.program_id(0) == i)
        def _(i=i):
            outs[2 * i][...] = total[:, :512]
            outs[2 * i + 1][...] = total[:, 512:]


def merge(bounds, own, got):
    count = own.shape[0] // 4
    block = pl.BlockSpec((count, 1024), lambda i, b: (i ^ b[2], 0))
    once = pl.BlockSpec((count, 512), lambda i, b: (0, 0), pipeline_mode=pl.Buffered(1))
    return pl.pallas_call(
        merge_body,
        grid_spec=pltpu.PrefetchScalarGridSpec(
            num_scalar_prefetch=1,
            grid=(4,),
            in_specs=[block, block],
            out_specs=[once] * 8,
        ),
        out_shape=[jax.ShapeDtypeStruct((count, 512), BF)] * 8,
        compiler_params=params(),
        cost_estimate=SMALL_COST,
        name="merge",
    )(bounds, own, got)


def finish_body(bounds, l0, r0, l1, r1, l2, r2, tok, dhid, gain, out):
    three = lambda a, b, c: (a[...].astype(F32) + b[...]) + c[...]
    grad = jnp.concatenate([three(l0, l1, l2), three(r0, r1, r2)], axis=1)
    values = tok[...].astype(F32)
    scale = lax.rsqrt(jnp.mean(values * values, axis=-1, keepdims=True) + EPSILON)
    weighted = grad * gain[...]
    mean = jnp.mean(weighted * values, axis=-1, keepdims=True)
    total = dhid[...] + scale * weighted - values * (scale * scale * scale * mean)
    out[0] = total[:, :512].astype(BF)
    out[1] = total[:, 512:].astype(BF)


def finish(bounds, state, tokens, dhid, gain):
    count = dhid.shape[0]
    n = count // 2
    half = pl.BlockSpec((n, 512), lambda i, b: (i, 0))
    row = pl.BlockSpec((n, 1024), lambda i, b: (i, 0))
    return pl.pallas_call(
        finish_body,
        grid_spec=pltpu.PrefetchScalarGridSpec(
            num_scalar_prefetch=1,
            grid=(2,),
            in_specs=[half] * 6
            + [pl.BlockSpec((n, 1024), lambda i, b: (2 * b[2] + i, 0)), row, whole((1, 1024))],
            out_specs=pl.BlockSpec((2, n, 512), lambda i, b: (0, i, 0)),
        ),
        out_shape=jax.ShapeDtypeStruct((2, count, 512), BF),
        compiler_params=params(),
        cost_estimate=SMALL_COST,
        name="finish",
    )(bounds, *state, tokens, dhid, gain)


def rope_tables(count):
    exponent = np.arange(0, HEAD_SIZE, 2).astype(np.float32) / np.float32(HEAD_SIZE)
    frequency = (np.float32(ROPE_BASE) ** (-exponent)).astype(np.float32)
    angles = np.arange(count).astype(np.float32)[:, None] * frequency[None, :]
    angles = np.concatenate([angles] * 4, axis=1)
    return (np.cos(angles).astype(np.float32), np.sin(angles).astype(np.float32))


def local(
    tokens, doc_ids, norm_gain, q_proj, key_value_weight, o_proj, z_proj, x_proj, dt_proj,
    bc_proj, conv_x, xconv_bias, conv_bc, bcconv_bias, dt_bias, a_log, skip_gain, gated_gain,
    out_proj, mlp_gain, gate_proj, up_proj, down_proj, out_grad,
):
    t, c = lax.axis_index("tensor"), lax.axis_index("ctx")
    own_tokens, grad_out = tokens[0], out_grad[0]
    own = own_tokens.shape[0]
    full = 2 * own
    mine = own // 4
    other_tokens = twin(own_tokens)

    def cols(w):
        n = w.shape[-1] // 2
        return lax.dynamic_slice_in_dim(w, c * n, n, w.ndim - 1)

    def rows(w):
        return block_at(w, c, w.shape[0] // 2)

    here = jnp.stack([jnp.zeros((), jnp.int32), jnp.zeros((), jnp.int32), t, c]).astype(jnp.int32)
    weight, pack0 = prepare(
        here, gate_proj, up_proj, down_proj, out_proj, o_proj, key_value_weight, q_proj,
        x_proj, z_proj, dt_proj.T, bc_proj,
    )
    weight, pack0, doc_ids = together(weight, pack0, doc_ids)
    pack1, pack2 = swap(pack0, 1), swap(pack0, 2)
    docs = doc_ids[0]
    place_dp = lax.axis_index("dp")
    inner = (place_dp == 1) | (place_dp == 2) | (lax.axis_size("dp") != 4)
    bounds = jnp.stack([jnp.sum(docs < 1), jnp.sum(docs < 2), t, c, inner]).astype(jnp.int32)
    own_gain = rows(gated_gain)
    gain0 = jnp.concatenate([own_gain, jnp.ones((64,), F32)])
    gain0 = jnp.broadcast_to(gain0[None, None], (8, 1, 256))

    cos, sin = rope_tables(full)
    cos, sin = jnp.asarray(cos), jnp.asarray(sin)
    steps = own // PROJ_ROWS
    own_off = jnp.reshape(c * steps, (1,)).astype(jnp.int32)
    other_off = jnp.reshape((1 - c) * steps, (1,)).astype(jnp.int32)
    gain_row = norm_gain[None]
    first = project(own_off, own_tokens, gain_row, weight, cos, sin)
    normed, qp, kv, xbc, z, dt_raw = project(
        other_off, other_tokens, gain_row, weight, cos, sin, before=first
    )

    pad = lambda v: jnp.zeros(v.shape[:-1] + (64,), F32)
    cx, cb = cols(conv_x), cols(xconv_bias)
    taps = jnp.concatenate([cx, pad(cx), conv_bc], axis=1)
    taps = jnp.concatenate([taps, jnp.zeros_like(taps)], axis=0)
    bias = jnp.concatenate([cb, pad(cb), bcconv_bias])[None]
    head = jnp.stack([cols(dt_bias), -jnp.exp(cols(a_log))], axis=1)
    head = jnp.pad(head, ((0, 5), (0, 126)))
    skip = jnp.pad(jnp.repeat(cols(skip_gain), MP), (0, 64))[None]
    xbc, gain0 = together(xbc, gain0)
    gains = exchange(gain0)
    g01, g2, y, states, pre = scan_forward(bounds, xbc, z, dt_raw, taps, bias, head, skip)
    g2, g01, pack1, pack2, gains = together(g2, g01, pack1, pack2, gains)
    left3, right3 = pack_halves(pack1, pack2)
    qp, left3, right3, g01 = together(qp, left3, right3, g01)
    left3, right3 = swap(left3, 2), swap(right3, 1)
    near = [pack0, pack1, pack2]
    far = [twin(v) for v in near]
    g_rows = exchange(g01.reshape(8, mine, 128))
    tile, keep = attend(bounds, qp, kv, g2)
    tile, g_rows, far, left3, right3 = together(tile, g_rows, far, left3, right3)
    h_rows = exchange(tile.reshape(8, mine, 128))
    packs = near + [left3, right3] + far + [twin(left3), twin(right3)]

    res = row_stage(bounds, g_rows, h_rows, own_tokens, grad_out, mlp_gain[None], gains, packs)
    layer_rows, two, dmix, dhid = res[0:4]
    act, dgu, gn = list(res[4:6]), list(res[6:8]), list(res[8:10])
    mlp_part, gain_part = res[12:14]
    grad_rows = block_at(grad_out, t, mine)
    dn, late = exchange(res[10]), res[11]
    far_w = weight_stage(two, grad_rows, dmix, dgu[1], act[1], gn[1])
    far_w = [twin(v) for v in far_w]
    near_w = weight_stage(two, grad_rows, dmix, dgu[0], act[0], gn[0], *far_w)
    dn, near_w, late = together(dn, near_w, late)
    sum_a, sum_b = near_w[:4], near_w[4:]
    late = exchange(late)

    a3, b3 = swap(sum_a[3], 1), swap(sum_b[3], 2)
    a1, b2 = swap(sum_a[1], 1), swap(sum_b[2], 2)
    da = attend_back(bounds, qp, kv, keep, dn, cos, sin)
    da, a3, b3, late = together(da, a3, b3, late)
    a_next, b_next = pair_sum(sum_a[2], a3, sum_b[1], b3)
    xbc, a_next, b_next = together(xbc, a_next, b_next)
    a_next, b_next = swap(a_next, 2), swap(b_next, 1)
    own_gain_row = jnp.pad(own_gain, (0, 64))[None]
    zeros = [
        jnp.zeros((256, 128), F32),
        jnp.zeros((8, 512), F32),
        jnp.zeros((8, 512), F32),
        jnp.zeros((16, CHUNK), F32),
    ]
    back = lambda part, carry, made, data: scan_back(
        part, carry, made, bounds, data, pre, z, y, dt_raw, states, late, dn, taps, head, skip,
        own_gain_row,
    )
    ds, dt_grad, *carry = back(0, zeros, [], xbc)
    ds, a1, b2, a_next, b_next = together(ds, a1, b2, a_next, b_next)
    kept, out = piece_sum(bounds, (sum_a[0], a1, a_next), (sum_b[0], b2, b_next))
    sums, single = DpSum(), DpSum()
    xbc, out, kept, layer_rows = together(xbc, out, kept, layer_rows)
    got = sums.first(kept, out)
    layer1, layer2 = swap(layer_rows, 1), swap(layer_rows, 2)
    conv_carry = (carry[2], carry[3], carry[0], carry[1])
    ds, dt_grad, conv_acc, head_acc, _, _ = back(1, conv_carry, [ds, dt_grad], xbc)
    ds, got, layer1, layer2 = together(ds, got, layer1, layer2)

    kept = sums.add(kept, got)
    parts = [block_at(kept, i, kept.shape[0] // 4) for i in range(4)]
    layer3 = [layer1[0], layer2[1]]
    ds, layer3, parts, kept = together(ds, layer3, parts, kept)
    got0 = sums.middle(parts[0])
    layer3 = [swap(layer3[0], 2), swap(layer3[1], 1)]
    grad_other, gain_other = input_grad(other_off, da, ds, dt_grad, weight, normed)
    grad_other, ds, layer3, got0 = together(grad_other, ds, layer3, got0)
    four = lax.axis_size("dp") == 4
    sent = twin(grad_other)
    got1 = sums.middle(parts[1])
    grad_own, gain_own = input_grad(own_off, da, ds, dt_grad, weight, normed)
    grad_own, sent, got1 = together(grad_own, sent, got1)
    got2 = sums.middle(parts[2])
    pieces = merge(bounds, grad_own, sent)
    ds, pieces = together(ds, pieces)
    l0, r0, l1, r1, l2, r2, l3, r3 = pieces
    low_rows = sums.add(jnp.concatenate(parts[:2]), jnp.concatenate([got0, got1]))
    heads = jnp.concatenate(
        [
            jnp.sum(conv_acc[5, :192].reshape(3, 64), axis=1),
            jnp.sum(head_acc[0:3], axis=1),
            jnp.sum(head_acc[8:11], axis=1),
        ]
    )
    place = c * 4 + t
    own_small = jnp.pad(jnp.concatenate([conv_acc[:5, :192].reshape(-1), heads]), (0, 55))
    at_own = lax.dynamic_update_slice_in_dim(
        jnp.zeros((8, 1024), F32), own_small[None], place, 0
    )
    norm_part = (gain_other[0] + gain_own[0]) / norm_gain
    flat = jnp.concatenate(
        [at_own.reshape(-1), gain_part.reshape(-1), conv_acc[:5, 256:].reshape(-1), mlp_part[0]]
        + [norm_part]
    )
    flat = jnp.pad(flat, (0, (-flat.shape[0]) % 1024)).reshape(1, -1, 128)
    flat = jnp.broadcast_to(flat, (8,) + flat.shape[1:])
    ds, l0, r0, l1, r1, l2, r2, l3, r3, flat, low_rows, got2 = together(
        ds, l0, r0, l1, r1, l2, r2, l3, r3, flat, low_rows, got2
    )
    l3, r3 = swap(l3, 1), swap(r3, 2)
    got3 = sums.middle(parts[3])
    flat = exchange(flat)
    alone, out, turned = alone_grad(bounds, normed, da, ds, dt_grad)
    alone, out, turned, l3, r3, got3, flat = together(alone, out, turned, l3, r3, got3, flat)
    l2, r1 = pair_sum(l2, l3, r1, r3)
    flat = jnp.sum(flat, axis=0)
    high_rows = sums.add(jnp.concatenate(parts[2:]), jnp.concatenate([got2, got3]))
    count = alone.shape[0]
    if four:
        out = jnp.concatenate([out, low_rows[:, :512], low_rows[:, 512:]])
    l1, r2, l2, r1, flat, out, alone, high_rows, turned = together(
        l1, r2, l2, r1, flat, out, alone, high_rows, turned
    )
    l2, r1 = swap(l2, 2), swap(r1, 1)
    l1, r2 = swap(l1, 1), swap(r2, 2)
    got = single.first(alone, out)
    shared = shared_grad(bounds, normed, da, ds, turned)
    l1, r2, l2, r1, got, shared = together(l1, r2, l2, r1, got, shared)
    if four:
        half = count + low_rows.shape[0]
        got_low = jnp.concatenate([got[count:half], got[half:]], axis=1)
    else:
        got_low = low_rows
    got_alone = got[:count]
    token_rows = finish(bounds, [l0, r0, l1, r1, l2, r2], own_tokens, dhid, norm_gain[None])
    alone = single.add(alone, got_alone)
    shared = shared.reshape(8, 128, 512)
    token_rows, alone, high_rows, flat, shared, layer_rows, layer1, layer2, layer3 = together(
        token_rows, alone, high_rows, flat, shared, layer_rows, layer1, layer2, layer3
    )
    tok1, tok2 = swap(token_rows, 1), swap(token_rows, 2)
    got = single.middle(alone)
    got_high = sums.last(high_rows)
    flat_got = dp_swap(flat, 1) if four else lax.psum(flat, "dp")
    shared = exchange(shared)
    layer_out = assemble(bounds, [layer_rows, layer1, layer2, *layer3])
    tok1, tok2, got, flat_got, got_high, shared, layer_out = together(
        tok1, tok2, got, flat_got, got_high, shared, layer_out
    )
    both = sums.end(
        jnp.concatenate([low_rows, high_rows]), jnp.concatenate([got_low, got_high])
    )
    shared = jnp.sum(shared.astype(F32), axis=0).astype(BF)
    if four:
        shared = jnp.broadcast_to(shared[None], (4, 128, 512))
    flat = flat + flat_got if four else flat_got
    *tok3, total = relay(tok1, tok2, alone, got)
    alone = total if four else single.add(alone, got)
    tok3, alone, flat, both, shared = together(tok3, alone, flat, both, shared)
    twin_piece = twin(both)
    tok3 = [swap(tok3[0], 2), swap(tok3[1], 1)]
    got = single.last(alone)
    flat_got = dp_swap(flat, 2) if four else flat
    if four:
        shared = lax.all_to_all(shared, "dp", 0, 0, tiled=True)
    else:
        shared = lax.psum(shared.astype(F32), "dp")[None]
    outs = piece_out(bounds, both, twin_piece)
    tok3, got, flat_got, outs, shared = together(tok3, got, flat_got, outs, shared)
    alone = single.end(alone, got)
    shared = jnp.sum(shared.astype(F32), axis=0).astype(BF)
    shared = jnp.broadcast_to(shared[None], (8, 128, 512))
    alone, tok3, shared = together(alone, tok3, shared)
    alone_twin = twin(alone)
    shared = exchange(shared)
    tokens_grad = assemble(bounds, [token_rows, tok1, tok2, *tok3])
    alone, alone_twin, tokens_grad = together(alone, alone_twin, tokens_grad)
    shared = shared.reshape(1024, 512).astype(F32)
    kv_out, bc_out = shared[:, :256], shared[:, 256:]
    q_out, z_out, x_out, dt_out = alone_out(bounds, alone, alone_twin)
    flat = flat + flat_got if four else flat_got
    flat = flat.reshape(-1)
    norm_sum = flat[12544:13568]
    small = flat[:8192].reshape(8, 1024)
    gain_sum = flat[8192:10240].reshape(8, 256)
    bc_sum = flat[10240:11520].reshape(5, 256)
    mlp_sum = flat[11520:12544]
    both_cores = lambda v: jnp.stack([lax.dynamic_index_in_dim(v, k * 4 + t, 0, False) for k in range(2)])
    small = both_cores(small)
    gain_sum = both_cores(gain_sum)[:, :192].reshape(-1)
    conv_small = small[:, :960].reshape(2, 5, 192)
    conv_small = jnp.concatenate([conv_small[0], conv_small[1]], axis=1)
    head_small = small[:, 960:969].reshape(2, 3, 3)
    per_head_sum = lambda i: head_small[:, i].reshape(-1)

    gate_out, up_out, down_out, mix_out, att_out = outs
    return (
        layer_out[None],
        tokens_grad[None],
        norm_sum,
        q_out,
        kv_out,
        att_out,
        z_out,
        x_out,
        dt_out.T,
        bc_out,
        conv_small[:4],
        conv_small[4],
        bc_sum[:4],
        bc_sum[4],
        per_head_sum(2),
        per_head_sum(1),
        per_head_sum(0),
        gain_sum,
        mix_out,
        mlp_sum,
        gate_out,
        up_out,
        down_out,
    )


def solution(mesh):
    placed = (
        P("dp", "ctx", None),
        P("dp", None),
        P(),
        P(None, "tensor"),
        P(),
        P("tensor", None),
        P(None, "tensor"),
        P(None, "tensor"),
        P(None, "tensor"),
        P(),
        P(None, "tensor"),
        P("tensor"),
        P(),
        P(),
        P("tensor"),
        P("tensor"),
        P("tensor"),
        P("tensor"),
        P("tensor", None),
        P(),
        P(None, "tensor"),
        P(None, "tensor"),
        P("tensor", None),
        P("dp", "ctx", None),
    )
    return jax.shard_map(
        local,
        mesh=mesh,
        in_specs=placed,
        out_specs=(
            P("dp", "ctx", None),
            P("dp", "ctx", None),
            P(),
            P(None, "tensor"),
            P(),
            P("tensor", None),
            P(None, "tensor"),
            P(None, "tensor"),
            P(None, "tensor"),
            P(),
            P(None, "tensor"),
            P("tensor"),
            P(),
            P(),
            P("tensor"),
            P("tensor"),
            P("tensor"),
            P("tensor"),
            P("tensor", None),
            P(),
            P(None, "tensor"),
            P(None, "tensor"),
            P("tensor", None),
        ),
        check_vma=False,
    )
```

```python
import functools

import jax
import numpy as np
import jax.numpy as jnp
from jax import lax
from jax.experimental import pallas as pl
from jax.experimental.pallas import tpu as pltpu
from jax.sharding import PartitionSpec as P

BF, F32 = jnp.bfloat16, jnp.float32
EPSILON = 1e-05
ROPE_BASE = 100000000000.0
HEAD_SIZE = 64
MP = 64
PROJ_ROWS = 512
BQ = 512
CHUNK = 256
VMEM_LIMIT = 48 * 1024 * 1024
FULL_VMEM = 60 * 1024 * 1024
SMALL_COST = pl.CostEstimate(flops=1000000, bytes_accessed=100000, transcendentals=0)


def dot(left, right, dims=((1,), (0,)), precision=None):
    return lax.dot_general(
        left, right, (dims, ((), ())), precision=precision, preferred_element_type=F32
    )


def dot_bt(left, right):
    return dot(left, right, ((1,), (1,)))


def dot_at(left, right):
    return dot(left, right, ((0,), (0,)))


def lanes(shape):
    return lax.broadcasted_iota(jnp.int32, shape, len(shape) - 1)


def rows_of(shape):
    return lax.broadcasted_iota(jnp.int32, shape, 0)


def doc_start(pos, first, second):
    return jnp.where(pos >= second, second, jnp.where(pos >= first, first, 0))


def halves(low, high):
    return jnp.where(lanes((1, 128)) < 64, low, high)


def params(**kw):
    return pltpu.CompilerParams(vmem_limit_bytes=VMEM_LIMIT, **kw)


def whole(shape):
    return pl.BlockSpec(shape, lambda *_: (0,) * len(shape))


def proj_body(off, tok, gain, weight, cos, sin, *refs):
    normed_ref, qp_ref, kv_ref, xbc_ref, z_ref, dt_ref = refs[-6:]
    values = tok[...].astype(F32)
    scale = lax.rsqrt(jnp.mean(values * values, axis=-1, keepdims=True) + EPSILON)
    normed = (values * scale * gain[...]).astype(BF)
    normed_ref[...] = normed
    c, s = cos[...], sin[...]
    left = lanes((1, 128)) < 64
    att = dot(normed, weight[:, :384])
    kv, turned, qd = att[:, :128], att[:, 128:256], att[:, 256:]
    kv_ref[...] = jnp.where(left, kv * c + turned * s, kv).astype(BF)
    q_rot = qd * c + pltpu.roll(turned, 64, 1) * s
    qp_ref[...] = jnp.where(left, q_rot.astype(BF) * 0.125, 0.0).astype(BF)
    dt_ref[...] = qd.T[64:72, :]
    ssm = dot(normed, weight[:, 384:])
    x2z2 = ssm[:, 128:256]
    xbc_ref[:, :128] = ssm[:, :128].astype(BF)
    xbc_ref[:, 128:256] = jnp.where(left, x2z2, 0.0).astype(BF)
    xbc_ref[:, 256:] = ssm[:, 384:].astype(BF)
    z_ref[:, :128] = ssm[:, 256:384]
    z_ref[:, 128:] = jnp.where(left, pltpu.roll(x2z2, 64, 1), 0.0)


def project(off, tokens, gain, weight, cos, sin, before=None):
    own = tokens.shape[0]
    full = cos.shape[0]
    n = PROJ_ROWS
    outs = [
        jax.ShapeDtypeStruct((full, 1024), BF),
        jax.ShapeDtypeStruct((full, 128), BF),
        jax.ShapeDtypeStruct((full, 128), BF),
        jax.ShapeDtypeStruct((full, 512), BF),
        jax.ShapeDtypeStruct((full, 256), F32),
        jax.ShapeDtypeStruct((8, full), F32),
    ]
    at = lambda i, off: (off[0] + i, 0)
    out_specs = [pl.BlockSpec((n, o.shape[1]), at) for o in outs[:5]]
    out_specs.append(pl.BlockSpec((8, n), lambda i, off: (0, off[0] + i)))
    in_specs = [
        pl.BlockSpec((n, 1024), lambda i, off: (i, 0)),
        whole((1, 1024)),
        whole((1024, 1024)),
        pl.BlockSpec((n, 128), at),
        pl.BlockSpec((n, 128), at),
    ]
    args = [off, tokens, gain, weight, cos, sin]
    alias = {}
    if before is not None:
        in_specs += [pl.BlockSpec(memory_space=pl.ANY)] * 6
        args += list(before)
        alias = {6 + i: i for i in range(6)}
    return pl.pallas_call(
        proj_body,
        grid_spec=pltpu.PrefetchScalarGridSpec(
            num_scalar_prefetch=1, grid=(own // n,), in_specs=in_specs, out_specs=out_specs
        ),
        out_shape=outs,
        input_output_aliases=alias,
        compiler_params=params(),
        cost_estimate=SMALL_COST,
        name="norm_project",
    )(*args)


def turned_lanes(value):
    low = lanes((1, 128)) % 64 < 32
    return jnp.where(low, -pltpu.roll(value, 96, 1), pltpu.roll(value, 32, 1))


def prep_body(bounds, gate, up, down, mix, att, kv, q, x, z, dt, bc, weight, pack):
    n = gate.shape[0]
    pack[:, :256] = gate[...]
    pack[:, 256:512] = up[...]
    pack[:, 512:768] = down[...].T
    pack[:, 768:] = jnp.concatenate([mix[...], att[...]], axis=0).T
    first, low_kv = bounds[3] == 0, bounds[2] // 2 == 0
    lane = lanes((1, 128))
    left = lane < 64
    tile = lambda ref, i: ref[:, 128 * i : 128 * i + 128].astype(F32)
    swapped = lambda v: pltpu.roll(v, 64, 1)
    keys, values = tile(kv, 0), tile(kv, 1)
    keys = jnp.where(low_kv, keys, swapped(keys))
    values = jnp.where(low_kv, swapped(values), values)
    query = tile(q, 0)
    query = jnp.where(first, query, swapped(query))
    steps = jnp.concatenate([dt[...].astype(F32), jnp.zeros((122, n), F32)], axis=0).T
    steps = jnp.where(lane < 3, jnp.where(first, steps, pltpu.roll(steps, 125, 1)), 0.0)

    def heads(ref):
        a, b, d = tile(ref, 0), tile(ref, 1), swapped(tile(ref, 2))
        return jnp.where(first, a, jnp.where(left, swapped(b), d)), jnp.where(first, b, d)

    x01, x2 = heads(x)
    z01, z2 = heads(z)
    tiles = [
        jnp.where(left, keys, values),
        jnp.where(left, turned_lanes(keys), swapped(turned_lanes(query))),
        jnp.where(left, query, swapped(steps)),
        x01,
        jnp.where(left, x2, swapped(z2)),
        z01,
    ]
    for i, value in enumerate(tiles):
        weight[:, 128 * i : 128 * i + 128] = value.astype(BF)
    weight[:, 768:] = bc[...]


def prepare(bounds, gate, up, down, mix, att, kv, q, x, z, dt, bc):
    n = 256
    row = lambda w: pl.BlockSpec((n, w), lambda i, b: (i, 0))
    col = lambda h: pl.BlockSpec((h, n), lambda i, b: (b[3], i))
    mine = pl.BlockSpec((n, 256), lambda i, b: (i, b[3]))
    return pl.pallas_call(
        prep_body,
        grid_spec=pltpu.PrefetchScalarGridSpec(
            num_scalar_prefetch=1,
            grid=(4,),
            in_specs=[mine, mine, col(256), col(192), col(64)]
            + [row(256), row(128), row(384), row(384)]
            + [pl.BlockSpec((6, n), lambda i, b: (0, i)), row(256)],
            out_specs=[row(1024), row(1024)],
        ),
        out_shape=[jax.ShapeDtypeStruct((1024, 1024), BF)] * 2,
        compiler_params=pltpu.CompilerParams(vmem_limit_bytes=FULL_VMEM),
        cost_estimate=SMALL_COST,
        name="prepare",
    )(bounds, gate, up, down, mix, att, kv, q, x, z, dt, bc)


def block_range(qi, bounds):
    first, second = bounds[0], bounds[1]
    q0 = qi * BQ
    low = doc_start(q0, first, second) // BQ
    inner = (doc_start(q0 + BQ - 1, first, second) + BQ - 1) // BQ
    return low, jnp.minimum(jnp.maximum(inner, low), qi)


def allowed_rows(qi, kb, bounds):
    q = qi * BQ + lanes((1, BQ))
    k = kb * BQ + rows_of((BQ, 1))
    return (k <= q) & (k >= doc_start(q, bounds[0], bounds[1]))


def allowed_keys(qi, kb, bounds):
    q = qi * BQ + rows_of((BQ, 1))
    k = kb * BQ + lanes((1, BQ))
    start = doc_start(q, bounds[0], bounds[1])
    return (k <= q) & (k >= start)


def attend_body(bounds, qp, kv, g2, out_ref, keep_ref):
    qi = pl.program_id(0)
    low, inner = block_range(qi, bounds)
    q = qp[...]

    def step(kb, carry, masked):
        top, total, acc = carry
        k = kv[pl.ds(pl.multiple_of(kb * BQ, BQ), BQ), :]
        s = dot_bt(q, k)
        if masked:
            s = jnp.where(allowed_keys(qi, kb, bounds), s, -1e30)
        new_top = jnp.maximum(top, jnp.max(s, axis=1, keepdims=True))
        p = jnp.exp(s - new_top)
        fade = jnp.exp(top - new_top)
        total = total * fade + jnp.sum(p, axis=1, keepdims=True)
        acc = acc * fade + dot(p.astype(BF), k)
        return new_top, total, acc

    carry = (jnp.full((BQ, 1), -1e30, F32), jnp.zeros((BQ, 1), F32), jnp.zeros((BQ, 128), F32))
    carry = lax.fori_loop(low, inner, lambda kb, c: step(kb, c, True), carry)
    carry = lax.fori_loop(inner, qi, lambda kb, c: step(kb, c, False), carry)
    top, total, acc = step(qi, carry, True)
    out = acc / total
    left = lanes((1, 128)) < 64
    out_ref[...] = jnp.where(left, g2[...], out.astype(BF))
    keep_ref[...] = jnp.where(left, top + jnp.log(total), out)


def attend(bounds, qp, kv, g2):
    full = qp.shape[0]
    block = pl.BlockSpec((BQ, 128), lambda i, *_: (i, 0))
    return pl.pallas_call(
        attend_body,
        grid_spec=pltpu.PrefetchScalarGridSpec(
            num_scalar_prefetch=1,
            grid=(full // BQ,),
            in_specs=[block, whole((full, 128)), block],
            out_specs=[block, block],
        ),
        out_shape=[
            jax.ShapeDtypeStruct((full, 128), BF),
            jax.ShapeDtypeStruct((full, 128), F32),
        ],
        compiler_params=params(),
        cost_estimate=SMALL_COST,
        name="attend",
    )(bounds, qp, kv, g2)


def attend_back_body(bounds, qp, kv, keep, grad, cos, sin, out_ref, acc_ref):
    blocks = pl.num_programs(0)
    qi = blocks - 1 - pl.program_id(0)
    left = lanes((1, 128)) < 64

    @pl.when(pl.program_id(0) == 0)
    def _():
        acc_ref[...] = jnp.zeros_like(acc_ref)

    low, inner = block_range(qi, bounds)
    q = qp[...]
    do = jnp.where(left, 0.0, grad[0].astype(F32))
    delta = jnp.sum(do * keep[...], axis=1, keepdims=True)
    do = do.astype(BF)
    stats = jnp.where(lanes((1, 128)) == 0, keep[...], delta).T
    lse, delta = stats[0:1, :], stats[1:2, :]

    def step(kb, dq, masked):
        at = pl.ds(pl.multiple_of(kb * BQ, BQ), BQ)
        k = kv[at, :]
        p = jnp.exp(dot_bt(k, q) - lse)
        if masked:
            p = jnp.where(allowed_rows(qi, kb, bounds), p, 0.0)
        ds = (p * (dot_bt(k, do) - delta)).astype(BF)
        acc_ref[at, :] += dot(ds, q) + dot(p.astype(BF), do)
        return dq + dot_at(ds, k)

    dq = jnp.zeros((BQ, 128), F32)
    dq = lax.fori_loop(low, inner, lambda kb, c: step(kb, c, True), dq)
    dq = lax.fori_loop(inner, qi, lambda kb, c: step(kb, c, False), dq)
    dq = step(qi, dq, True) * 0.125
    dkv = acc_ref[pl.ds(pl.multiple_of(qi * BQ, BQ), BQ), :]
    c, s = cos[...], sin[...]
    out_ref[:, :128] = jnp.where(left, dkv * c, dkv).astype(BF)
    out_ref[:, 128:256] = (jnp.where(left, dkv, pltpu.roll(dq, 64, 1)) * s).astype(BF)
    out_ref[:, 256:] = jnp.where(left, dq * c, 0.0).astype(BF)


def attend_back(bounds, qp, kv, keep, grad, cos, sin):
    full = qp.shape[0]
    n = full // BQ
    block = pl.BlockSpec((BQ, 128), lambda i, *_: (n - 1 - i, 0))
    return pl.pallas_call(
        attend_back_body,
        grid_spec=pltpu.PrefetchScalarGridSpec(
            num_scalar_prefetch=1,
            grid=(n,),
            in_specs=[
                block,
                whole((full, 128)),
                block,
                pl.BlockSpec((1, BQ, 128), lambda i, *_: (n - 1 - i, 0, 0)),
                block,
                block,
            ],
            out_specs=pl.BlockSpec((BQ, 384), lambda i, *_: (n - 1 - i, 0)),
            scratch_shapes=[pltpu.VMEM((full, 128), F32)],
        ),
        out_shape=jax.ShapeDtypeStruct((full, 384), BF),
        compiler_params=params(),
        cost_estimate=SMALL_COST,
        name="attend_back",
    )(bounds, qp, kv, keep, grad, cos, sin)


def tap_mask(first_row, count, shift, bounds):
    pos = first_row + rows_of((count, 1))
    return (pos - doc_start(pos, bounds[0], bounds[1]) >= shift).astype(F32)


def conv_taps(ext_ref, r0, bounds, taps, bias):
    pre = bias + taps[3:4, :] * ext_ref[pl.ds(8, CHUNK), :]
    for shift in (1, 2, 3):
        mask = tap_mask(r0, CHUNK, shift, bounds)
        pre = pre + taps[3 - shift : 4 - shift, :] * (ext_ref[pl.ds(8 - shift, CHUNK), :] * mask)
    return pre


def chunk_decay(r0, bounds, dt_raw, head, extra=None):
    lane = lanes((1, CHUNK))
    dt = jax.nn.softplus(dt_raw + head[:, 0:1])
    la = dt * head[:, 1:2]
    upper = (rows_of((CHUNK, CHUNK)) <= lanes((CHUNK, CHUNK))).astype(F32)
    cum = dot(la, upper, precision=lax.Precision.HIGHEST)
    rows = [cum, dt] if extra is None else [cum, dt, extra]
    used = 8 * len(rows)
    stacked = jnp.concatenate(rows + [jnp.zeros((CHUNK - used, CHUNK), F32)], axis=0).T
    cum_col, dt_col = stacked[:, 0:8], stacked[:, 8:16]
    pos = r0 + rows_of((CHUNK, 1))
    start = doc_start(pos, bounds[0], bounds[1])
    start_last = doc_start(r0 + CHUNK - 1, bounds[0], bounds[1])
    key = r0 + lane
    mask = (key <= pos) & (key >= start)
    enter = jnp.where(start < r0, jnp.exp(cum_col), 0.0)
    fade = jnp.where(pos >= start_last, jnp.exp(cum_last_row(cum_col) - cum_col), 0.0)
    keep = jnp.where(start_last < r0, jnp.exp(cum_last_row(cum_col)), 0.0)
    return dt, la, cum, dt_col, cum_col, mask, enter, fade, keep, stacked[:, 16:24]


def two_terms(value):
    high = value.astype(BF)
    return high, (value - high.astype(F32)).astype(BF)


def cum_last_row(cum_col):
    return cum_col[CHUNK - 1 : CHUNK, :]


def per_head(col):
    return halves(col[:, 0:1], col[:, 1:2]), col[:, 2:3]


def state_rows(keep):
    row = rows_of((256, 1))
    return jnp.where(row < 64, keep[:, 0:1], jnp.where(row < 128, keep[:, 1:2], keep[:, 2:3]))


def scan_body(
    bounds, xbc, z, dt_raw, taps, bias, head, skip, g01, g2, y_ref, s_ref, pre_ref, ext, state
):
    i = pl.program_id(0)
    r0 = i * CHUNK

    @pl.when(i == 0)
    def _():
        ext[pl.ds(0, 8), :] = jnp.zeros((8, 512), F32)
        state[...] = jnp.zeros_like(state)

    @pl.when(i > 0)
    def _():
        ext[pl.ds(0, 8), :] = ext[pl.ds(CHUNK, 8), :]

    ext[pl.ds(8, CHUNK), :] = xbc[...].astype(F32)
    pre = conv_taps(ext, r0, bounds, taps[...], bias[...])
    pre_ref[...] = pre
    conv = pre * jax.nn.sigmoid(pre)
    x01, x2 = conv[:, :128], conv[:, 128:256]
    b, c = conv[:, 256:384].astype(BF), conv[:, 384:].astype(BF)
    dt, la, cum, dt_col, cum_col, mask, enter, fade, keep, _ = chunk_decay(
        r0, bounds, dt_raw[...], head[...]
    )
    inner = dot_bt(c, b)
    x01b, x2b = x01.astype(BF), x2.astype(BF)
    ys = []
    for h in range(3):
        gap = cum_col[:, h : h + 1] - cum[h : h + 1, :]
        decay = jnp.exp(jnp.where(mask, gap, -1e30))
        m = (inner * decay * dt[h : h + 1, :]).astype(BF)
        ys.append(dot(m, x01b if h < 2 else x2b))
    s0 = state[...]
    s_ref[0] = s0
    s0b, s0c = two_terms(s0)
    carried = dot_bt(c, s0b) + dot_bt(c, s0c)
    e01, e2 = per_head(enter)
    y01 = halves(ys[0], ys[1]) + e01 * carried[:, :128] + skip[:, :128] * x01
    y2 = ys[2] + e2 * carried[:, 128:] + skip[:, 128:] * x2
    w01, w2 = per_head(fade * dt_col)
    xw = jnp.concatenate([(x01 * w01).astype(BF), (x2 * w2).astype(BF)], axis=1)
    state[...] = s0 * state_rows(keep) + dot_at(xw, b)
    y_ref[:, :128] = y01
    y_ref[:, 128:] = y2
    z01, z2 = z[:, :128], z[:, 128:]
    g01[...] = (y01 * (z01 * jax.nn.sigmoid(z01))).astype(BF)
    g2[...] = (y2 * (z2 * jax.nn.sigmoid(z2))).astype(BF)


def scan_forward(bounds, xbc, z, dt_raw, taps, bias, head, skip):
    full = xbc.shape[0]
    n = full // CHUNK
    row = lambda width: pl.BlockSpec((CHUNK, width), lambda i, *_: (i, 0))
    return pl.pallas_call(
        scan_body,
        grid_spec=pltpu.PrefetchScalarGridSpec(
            num_scalar_prefetch=1,
            grid=(n,),
            in_specs=[
                row(512),
                row(256),
                pl.BlockSpec((8, CHUNK), lambda i, *_: (0, i)),
                whole((8, 512)),
                whole((1, 512)),
                whole((8, 128)),
                whole((1, 256)),
            ],
            out_specs=[
                row(128),
                row(128),
                row(256),
                pl.BlockSpec((1, 256, 128), lambda i, *_: (i, 0, 0)),
                row(512),
            ],
            scratch_shapes=[pltpu.VMEM((CHUNK + 8, 512), F32), pltpu.VMEM((256, 128), F32)],
        ),
        out_shape=[
            jax.ShapeDtypeStruct((full, 128), BF),
            jax.ShapeDtypeStruct((full, 128), BF),
            jax.ShapeDtypeStruct((full, 256), F32),
            jax.ShapeDtypeStruct((n, 256, 128), F32),
            jax.ShapeDtypeStruct((full, 512), F32),
        ],
        compiler_params=params(),
        cost_estimate=SMALL_COST,
        name="scan_forward",
    )(bounds, xbc, z, dt_raw, taps, bias, head, skip)


def scalar_rows(terms):
    low = terms[0:2, :] + terms[2:4, :] + terms[4:6, :]
    high = terms[6:8, :] + terms[8:10, :] + terms[10:12, :]
    total = jnp.concatenate([low, high], axis=1)
    return jnp.concatenate([total, jnp.zeros((6, CHUNK), F32)], axis=0)


def scan_back_body(
    last, bounds, xbc, before, pre_ref, z, y, dt_raw, s0_ref, dn01, dn2, scal, taps, head, skip,
    gain,
    dstate_in, dext_in, acc_in, head_in, *refs,
):
    out_ref, dt_grad, acc, head_acc, dstate_out, dext_out, ext, dext, dstate = refs[-9:]
    step = pl.program_id(0)
    i = last - step
    r0 = i * CHUNK
    left = lanes((1, 128)) < 64

    @pl.when(step == 0)
    def _():
        dext[pl.ds(CHUNK, 8), :] = dext_in[...]
        dstate[...] = dstate_in[...]
        acc[...] = acc_in[...]
        head_acc[...] = head_in[...]

    @pl.when(step > 0)
    def _():
        dext[pl.ds(CHUNK, 8), :] = dext[pl.ds(0, 8), :]

    ext[pl.ds(0, 8), :] = before[...].astype(F32)[8:, :]
    ext[pl.ds(8, CHUNK), :] = xbc[...].astype(F32)
    weights = taps[...]
    pre = pre_ref[...]
    sig = jax.nn.sigmoid(pre)
    conv = pre * sig
    x01, x2 = conv[:, :128], conv[:, 128:256]
    b, c = conv[:, 256:384].astype(BF), conv[:, 384:].astype(BF)
    dt, la, cum, dt_col, cum_col, mask, enter, fade, keep, scalars = chunk_decay(
        r0, bounds, dt_raw[...], head[...], scalar_rows(scal[0].astype(F32))
    )
    row_scale, row_cross = scalars[:, 0:1], scalars[:, 1:2]

    def gate_back(dn, gain, zz, yy):
        s = jax.nn.sigmoid(zz)
        act = zz * s
        g = yy * act
        sent = g.astype(BF).astype(F32)
        ratio = jnp.where(g == 0.0, 1.0, sent / g)
        dg = (dn * gain * row_scale - sent * row_cross) * ratio
        return dg * act, dg * yy * (s + act * (1.0 - s))

    dy01, dz01 = gate_back(dn01[0].astype(F32), gain[:, :128], z[:, :128], y[:, :128])
    dy2, dz2 = gate_back(dn2[0].astype(F32), gain[:, 128:], z[:, 128:], y[:, 128:])
    dy2, dz2 = jnp.where(left, dy2, 0.0), jnp.where(left, dz2, 0.0)
    inner = dot_bt(b, c)
    x01b, x2b = x01.astype(BF), x2.astype(BF)
    dy01b, dy2b = dy01.astype(BF), dy2.astype(BF)
    zero = jnp.zeros_like(dy01b)
    parts = [(jnp.where(left, dy01b, zero), x01b), (jnp.where(left, zero, dy01b), x01b), (dy2b, x2b)]
    query = r0 + lanes((1, CHUNK))
    key = r0 + rows_of((CHUNK, 1))
    mask = (key <= query) & (key >= doc_start(query, bounds[0], bounds[1]))
    d_inner = jnp.zeros((CHUNK, CHUNK), F32)
    dxs, direct, row_sums = [], [], []
    for h in range(3):
        gap = cum[h : h + 1, :] - cum_col[:, h : h + 1]
        decay = jnp.exp(jnp.where(mask, gap, -1e30))
        dt_h = dt_col[:, h : h + 1]
        dyh, xh = parts[h]
        dm = dot_bt(xh, dyh)
        kept = inner * decay
        dxs.append(dot((kept * dt_h).astype(BF), dyh if h == 2 else dy01b))
        pulled = dm * kept
        d_inner = d_inner + dm * (decay * dt_h)
        direct.append(jnp.sum(pulled, axis=1, keepdims=True))
        row_sums.append(jnp.sum(pulled * dt_h, axis=0, keepdims=True))
    s0 = s0_ref[0]
    s0b, s0c = two_terms(s0)
    ds1 = dstate[...]
    ds1b, ds1c = two_terms(ds1)
    e01, e2 = per_head(enter)
    ey01, ey2 = dy01 * e01, dy2 * e2
    ey, eyc = two_terms(jnp.concatenate([ey01, ey2], axis=1))
    carried = dot_bt(c, s0b) + dot_bt(c, s0c)
    f01, f2 = per_head(fade)
    d01, d2 = per_head(dt_col)
    back = dot_bt(b, ds1b)
    fb01, fb2 = f01 * back[:, :128], f2 * back[:, 128:]
    xw = jnp.concatenate([(x01 * (f01 * d01)).astype(BF), (x2 * (f2 * d2)).astype(BF)], axis=1)
    d_innerb = d_inner.astype(BF)
    dc = dot_at(d_innerb, b) + dot(ey, s0b) + dot(eyc, s0b) + dot(ey, s0c)
    db = dot(d_innerb, c) + dot(xw, ds1b) + dot(xw, ds1c)
    dx01 = halves(dxs[0], dxs[1]) + d01 * fb01 + skip[:, :128] * dy01
    dx2 = dxs[2] + d2 * fb2 + skip[:, 128:] * dy2
    kept_rows = state_rows(keep)
    crossing = jnp.sum(ds1 * s0 * kept_rows, axis=1, keepdims=True)
    dstate[...] = ds1 * kept_rows + dot_at(ey, c) + dot_at(eyc, c)
    inter01, inter2 = ey01 * carried[:, :128], ey2 * carried[:, 128:]
    u01, u2 = x01 * fb01, x2 * fb2
    pick = lambda v, h: jnp.where(left if h == 0 else ~left, v, 0.0)
    side = lambda v01, v2, h: jnp.sum(pick(v01, h) if h < 2 else v2, axis=1, keepdims=True)
    lane = lanes((1, CHUNK))
    tile = jnp.zeros((CHUNK, CHUNK), F32)
    crossed = jnp.zeros((8, 1), F32)
    head_row = rows_of((8, 1))
    for h in range(3):
        u = side(u01, u2, h)
        pulled = u + direct[h]
        moved = side(inter01, inter2, h) - pulled * dt_col[:, h : h + 1]
        tile = jnp.where(lane == h, moved, jnp.where(lane == 8 + h, pulled, tile))
        total = jnp.sum(crossing[64 * h : 64 * h + 64, :], axis=0, keepdims=True)
        total = total + jnp.sum(u * dt_col[:, h : h + 1], axis=0, keepdims=True)
        crossed = jnp.where(head_row == h, total, crossed)
    tile = tile.T
    stack = lambda items: jnp.concatenate(items + [jnp.zeros((5, CHUNK), F32)], axis=0)
    dcum = tile[0:8, :] + stack(row_sums) + jnp.where(lane == CHUNK - 1, crossed, 0.0)
    lower = (rows_of((CHUNK, CHUNK)) >= lanes((CHUNK, CHUNK))).astype(F32)
    dla = dot(dcum, lower, precision=lax.Precision.HIGHEST)
    ddt = tile[8:16, :] + dla * head[:, 1:2]
    graw = ddt * jax.nn.sigmoid(dt_raw[...] + head[:, 0:1])
    dt_grad[...] = graw
    head_acc[0:8, :] += dla * la
    head_acc[8:16, :] += graw
    dpre = jnp.concatenate([dx01, dx2, db, dc], axis=1) * (sig + conv * (1.0 - sig))
    dext[pl.ds(0, CHUNK), :] = dpre
    din = weights[3:4, :] * dpre
    acc[3:4, :] += jnp.sum(dpre * ext[pl.ds(8, CHUNK), :], axis=0, keepdims=True)
    acc[4:5, :] += jnp.sum(dpre, axis=0, keepdims=True)
    acc[5:6, :128] += jnp.sum(dy01 * x01, axis=0, keepdims=True)
    acc[5:6, 128:256] += jnp.sum(dy2 * x2, axis=0, keepdims=True)
    for shift in (1, 2, 3):
        tap = 3 - shift
        now = tap_mask(r0, CHUNK, shift, bounds)
        acc[tap : tap + 1, :] += jnp.sum(
            dpre * (ext[pl.ds(8 - shift, CHUNK), :] * now), axis=0, keepdims=True
        )
        later = tap_mask(r0 + shift, CHUNK, shift, bounds)
        din = din + weights[tap : tap + 1, :] * (dext[pl.ds(shift, CHUNK), :] * later)
    out_ref[:, :128] = din[:, :128].astype(BF)
    out_ref[:, 128:256] = jnp.where(left, din[:, 128:256], pltpu.roll(dz2, 64, 1)).astype(BF)
    out_ref[:, 256:384] = dz01.astype(BF)
    out_ref[:, 384:] = din[:, 256:].astype(BF)

    @pl.when(step == pl.num_programs(0) - 1)
    def _():
        dstate_out[...] = dstate[...]
        dext_out[...] = dext[pl.ds(0, 8), :]


def scan_back(
    part, carry, before, bounds, xbc, pre, z, y, dt_raw, states, late, dn, taps, head, skip, gain
):
    full = xbc.shape[0]
    n = full // CHUNK
    half = n // 2
    last = n - 1 if part == 0 else half - 1
    row = lambda width: pl.BlockSpec((CHUNK, width), lambda i, *_: (last - i, 0))
    tall = CHUNK // 16
    per = n // 8
    sent = pl.BlockSpec((1, CHUNK, 128), lambda i, b: ((last - i) // per, (last - i) % per, 0))

    def terms(i, b):
        piece, rest = (last - i) // per, (last - i) % per
        return piece, per * (CHUNK // 16) + rest, 0

    carried = [whole((256, 128)), whole((8, 512)), whole((8, 512)), whole((16, CHUNK))]
    sds = jax.ShapeDtypeStruct
    args = [bounds, xbc, xbc, pre, z, y, dt_raw, states, late, dn, late, taps, head, skip, gain]
    args += list(carry) + list(before)
    alias = {len(args) - 2: 0, len(args) - 1: 1} if before else {}
    return pl.pallas_call(
        functools.partial(scan_back_body, last),
        grid_spec=pltpu.PrefetchScalarGridSpec(
            num_scalar_prefetch=1,
            grid=(half,),
            in_specs=[
                row(512),
                pl.BlockSpec((16, 512), lambda i, *_: (jnp.maximum((last - i) * tall - 1, 0), 0)),
                row(512),
                row(256),
                row(256),
                pl.BlockSpec((8, CHUNK), lambda i, *_: (0, last - i)),
                pl.BlockSpec((1, 256, 128), lambda i, *_: (last - i, 0, 0)),
                sent,
                sent,
                pl.BlockSpec((1, 16, 128), terms),
                whole((8, 512)),
                whole((8, 128)),
                whole((1, 256)),
                whole((1, 256)),
            ]
            + carried
            + [pl.BlockSpec(memory_space=pl.ANY)] * len(before),
            out_specs=[
                row(640),
                pl.BlockSpec((8, CHUNK), lambda i, *_: (0, last - i)),
                whole((8, 512)),
                whole((16, CHUNK)),
                whole((256, 128)),
                whole((8, 512)),
            ],
            scratch_shapes=[
                pltpu.VMEM((CHUNK + 8, 512), F32),
                pltpu.VMEM((CHUNK + 8, 512), F32),
                pltpu.VMEM((256, 128), F32),
            ],
        ),
        out_shape=[
            sds((full, 640), BF),
            sds((8, full), F32),
            sds((8, 512), F32),
            sds((16, CHUNK), F32),
            sds((256, 128), F32),
            sds((8, 512), F32),
        ],
        input_output_aliases=alias,
        compiler_params=params(),
        cost_estimate=SMALL_COST,
        name="scan_back",
    )(*args)


ROW_BLOCK = 256


def row_body(bounds, g, h, tok, gout, mlp_gain, gains, *refs):
    packs, refs = refs[:10], refs[10:]
    pa, pb, slots = [], [], []
    for k, base in enumerate((0, 5)):
        for r in range(4):
            first = packs[base + r]
            second = first.at[:, 512:] if r < 3 else packs[base + 4]
            pa.append(first.at[:, 0:512])
            pb.append(second)
            slots.append((bounds[3] ^ k) * 4 + (bounds[2] ^ r))
    gain_rows = [gains[slot] for slot in slots]
    out_ref, two_ref, dmix_ref, dhid_ref = refs[0:4]
    act_refs, dgu_refs, gn_refs = refs[4:6], refs[6:8], refs[8:10]
    dn, dn_late, mlp_acc, gain_acc = refs[10:14]
    step = pl.program_id(0)
    left = lanes((1, 128)) < 64
    width = 1536.0

    @pl.when(pl.program_id(0) == 0)
    def _():
        mlp_acc[...] = jnp.zeros_like(mlp_acc)
        gain_acc[...] = jnp.zeros_like(gain_acc)

    pieces = [(r, k) for k in range(2) for r in range(4)]

    def part(ref, s):
        return ref[slots[s]].astype(F32)

    squares = 0.0
    for s in range(8):
        first, second = part(g, s), part(h, s)
        squares = squares + first * first + jnp.where(left, second * second, 0.0)
    rg = lax.rsqrt(jnp.sum(squares, axis=1, keepdims=True) / width + EPSILON)
    mixed = 0.0
    for s, (r, k) in enumerate(pieces):
        gain = gain_rows[s]
        first = part(g, s) * rg * gain[:, :128]
        second = part(h, s)
        second = jnp.where(left, second * rg * gain[:, 128:], second)
        gn = jnp.concatenate([first.astype(BF), second.astype(BF)], axis=1)
        gn_refs[k][:, r * 256 : r * 256 + 256] = gn
        mixed = mixed + dot_bt(gn, pb[s][:, 256:])
    hidden = tok[...].astype(F32) + mixed
    scale = lax.rsqrt(jnp.mean(hidden * hidden, axis=-1, keepdims=True) + EPSILON)
    two = (hidden * scale * mlp_gain[...]).astype(BF)
    two_ref[...] = two
    grad = gout[...]
    ffn = 0.0
    dtwo = 0.0
    for s, (r, k) in enumerate(pieces):
        weight, down = pa[s][...], pb[s][:, :256]
        gu = dot(two, weight)
        gate, up = gu[:, :256], gu[:, 256:]
        sig = jax.nn.sigmoid(gate)
        silu = gate * sig
        act = (silu * up).astype(BF)
        act_refs[k][:, r * 256 : r * 256 + 256] = act
        ffn = ffn + dot_bt(act, down)
        dact = dot(grad, down)
        dgate = (dact * up * (sig + silu * (1.0 - sig))).astype(BF)
        dgu = jnp.concatenate([dgate, (dact * silu).astype(BF)], axis=1)
        dgu_refs[k][:, r * 512 : r * 512 + 512] = dgu
        dtwo = dtwo + dot_bt(dgu, weight)
    whole_out = (hidden + ffn).astype(BF)
    out_ref[0] = whole_out[:, :512]
    out_ref[1] = whole_out[:, 512:]
    weighted = dtwo * mlp_gain[...]
    mlp_acc[...] += jnp.sum(dtwo * (hidden * scale), axis=0, keepdims=True)
    mean = jnp.mean(weighted * hidden, axis=-1, keepdims=True)
    dhid = grad.astype(F32) + scale * weighted - hidden * (scale * scale * scale * mean)
    dhid_ref[...] = dhid
    dmix = dhid.astype(BF)
    dmix_ref[...] = dmix
    cross = 0.0
    for s, (r, k) in enumerate(pieces):
        dgn = dot(dmix, pb[s][:, 256:]).astype(BF)
        at = pl.ds(pl.multiple_of(step * ROW_BLOCK, ROW_BLOCK), ROW_BLOCK)
        dn[slots[s], at, :] = dgn[:, 128:]
        dn_late[slots[s], at, :] = dgn[:, :128]
        first, second = dgn[:, :128].astype(F32), dgn[:, 128:].astype(F32)
        gain = gain_rows[s]
        own1, own2 = part(g, s), jnp.where(left, part(h, s), 0.0)
        t1, t2 = first * own1, second * own2
        gain_acc[slots[s], :, :128] += jnp.sum(t1 * rg, axis=0, keepdims=True)
        gain_acc[slots[s], :, 128:] += jnp.sum(t2 * rg, axis=0, keepdims=True)
        cross = cross + t1 * gain[:, :128] + t2 * gain[:, 128:]
    cross = jnp.sum(cross, axis=1, keepdims=True) * (rg * rg * rg / width)
    lane = lanes((1, 128))
    tile = jnp.where(lane == 0, rg, jnp.where(lane == 1, cross, 0.0))
    pair = tile.T[0:2, :]
    high = pair.astype(BF)
    rest = pair - high.astype(F32)
    middle = rest.astype(BF)
    low = (rest - middle.astype(F32)).astype(BF)
    terms = [v.astype(F32) for v in (high, middle, low)]
    block = jnp.concatenate(
        [v[:, :128] for v in terms] + [v[:, 128:] for v in terms] + [jnp.zeros((4, 128), F32)],
        axis=0,
    ).astype(BF)
    for s in range(8):
        dn_late[s, pl.ds(pl.multiple_of(2 * ROW_BLOCK + step * 16, 16), 16), :] = block


def row_stage(bounds, g, h, tokens, gout, mlp_gain, gains, packs):
    n = ROW_BLOCK
    count = 2 * n
    row = lambda w: pl.BlockSpec((n, w), lambda i, b: (i, 0))
    part = pl.BlockSpec((n, 1024), lambda i, b: (2 * b[2] + i, 0))
    piece = pl.BlockSpec((8, n, 128), lambda i, b: (0, i, 0))
    once = lambda shape: pl.BlockSpec(
        shape, lambda i, b: (0,) * len(shape), pipeline_mode=pl.Buffered(1)
    )
    sds = jax.ShapeDtypeStruct
    widths = [1024] * 4 + [1024] * 2 + [2048] * 2 + [1024] * 2
    dtypes = [BF] * 3 + [F32] + [BF] * 6
    return pl.pallas_call(
        row_body,
        grid_spec=pltpu.PrefetchScalarGridSpec(
            num_scalar_prefetch=1,
            grid=(2,),
            in_specs=[piece, piece, part, part, whole((1, 1024)), whole((8, 1, 256))]
            + [once(p.shape) for p in packs],
            out_specs=[pl.BlockSpec((2, n, 512), lambda i, b: (0, i, 0))]
            + [row(w) for w in widths[1:]]
            + [once((8, count, 128)), once((8, count + 32, 128))]
            + [whole((1, 1024)), whole((8, 1, 256))],
        ),
        out_shape=[sds((2, count, 512), BF)]
        + [sds((count, w), d) for w, d in zip(widths[1:], dtypes[1:])]
        + [sds((8, count, 128), BF), sds((8, count + 32, 128), BF)]
        + [sds((1, 1024), F32), sds((8, 1, 256), F32)],
        compiler_params=pltpu.CompilerParams(vmem_limit_bytes=58 * 1024 * 1024),
        cost_estimate=SMALL_COST,
        name="row_stage",
    )(bounds, g, h, tokens, gout, mlp_gain, gains, *packs)


def weight_body(two, gout, dmix, dgu, act, gn, *refs):
    a = dot_at(two[...], dgu[...])
    b = jnp.concatenate([dot_at(gout[...], act[...]), dot_at(dmix[...], gn[...])], axis=1)
    if len(refs) == 2:
        refs[0][0] = a.astype(BF)
        refs[1][0] = b.astype(BF)
    else:
        a = (a + refs[0][0].astype(F32)).astype(BF)
        b = (b + refs[1][0].astype(F32)).astype(BF)
        for i in range(4):

            @pl.when(pl.program_id(0) == i)
            def _(i=i):
                refs[2 + i][...] = a
                refs[6 + i][...] = b


def weight_stage(two, gout, dmix, dgu, act, gn, *others):
    count = two.shape[0]
    col = lambda w: pl.BlockSpec((count, w), lambda i: (0, i))
    piece = pl.BlockSpec((1, 1024, 512), lambda i: (i, 0, 0))
    once = pl.BlockSpec((1024, 512), lambda i: (0, 0), pipeline_mode=pl.Buffered(1))
    sds = jax.ShapeDtypeStruct
    return pl.pallas_call(
        weight_body,
        grid=(4,),
        in_specs=[whole((count, 1024))] * 3
        + [col(512), col(256), col(256)]
        + [piece] * len(others),
        out_specs=[once] * 8 if others else [piece] * 2,
        out_shape=[sds((1024, 512), BF)] * 8 if others else [sds((4, 1024, 512), BF)] * 2,
        compiler_params=pltpu.CompilerParams(vmem_limit_bytes=FULL_VMEM),
        cost_estimate=SMALL_COST,
        name="weight_stage",
    )(two, gout, dmix, dgu, act, gn, *others)


def with_steps(da, dt_grad):
    count = da.shape[0]
    cols = jnp.concatenate([dt_grad, jnp.zeros((120, count), F32)], axis=0).T
    last = jnp.where(lanes((1, 128)) < 64, da[:, 256:].astype(F32), pltpu.roll(cols, 64, 1))
    return jnp.concatenate([da[:, :256], last.astype(BF)], axis=1)


def input_grad_body(off, da, ds, dt_grad, weight, normed, out_ref, gain_ref):
    left = with_steps(da[...], dt_grad[...])
    grad = dot_bt(left, weight[:, :384]) + dot_bt(ds[...], weight[:, 384:])
    out_ref[...] = grad.astype(BF)

    @pl.when(pl.program_id(0) == 0)
    def _():
        gain_ref[...] = jnp.zeros_like(gain_ref)

    gain_ref[...] += jnp.sum(grad * normed[...].astype(F32), axis=0, keepdims=True)


def input_grad(off, da, ds, dt_grad, weight, normed):
    n = PROJ_ROWS
    own = ds.shape[0] // 2
    at = lambda i, off: (off[0] + i, 0)
    return pl.pallas_call(
        input_grad_body,
        grid_spec=pltpu.PrefetchScalarGridSpec(
            num_scalar_prefetch=1,
            grid=(own // n,),
            in_specs=[
                pl.BlockSpec((n, 384), at),
                pl.BlockSpec((n, 640), at),
                pl.BlockSpec((8, n), lambda i, off: (0, off[0] + i)),
                whole((1024, 1024)),
                pl.BlockSpec((n, 1024), at),
            ],
            out_specs=[pl.BlockSpec((n, 1024), lambda i, off: (i, 0)), whole((1, 1024))],
        ),
        out_shape=[
            jax.ShapeDtypeStruct((own, 1024), BF),
            jax.ShapeDtypeStruct((1, 1024), F32),
        ],
        compiler_params=params(),
        cost_estimate=SMALL_COST,
        name="input_grad",
    )(off, da, ds, dt_grad, weight, normed)


def turned_back(value):
    low = lanes((1, 128)) % 64 < 32
    return jnp.where(low, pltpu.roll(value, 96, 1), -pltpu.roll(value, 32, 1))


def shared_grad_body(bounds, normed, da, ds1, ds2, turned, shared, acc):
    @pl.when(pl.program_id(0) == 0)
    def _():
        acc[...] = jnp.zeros_like(acc)

    cols = jnp.concatenate([da[...], ds1[...], ds2[...]], axis=1)
    acc[...] += dot_at(normed[...], cols)

    @pl.when(pl.program_id(0) == pl.num_programs(0) - 1)
    def _():
        left = lanes((1, 128)) < 64
        kv = acc[:, :128] + jnp.where(left, turned_back(turned[...]), 0.0)
        low = bounds[2] // 2 == 0
        swapped = pltpu.roll(kv, 64, 1)
        keys = jnp.where(left == low, jnp.where(low, kv, swapped), 0.0)
        values = jnp.where(left == low, jnp.where(low, swapped, kv), 0.0)
        shared[:, :128] = keys.astype(BF)
        shared[:, 128:256] = values.astype(BF)
        shared[:, 256:] = acc[:, 128:].astype(BF)


def shared_grad(bounds, normed, da, ds, turned):
    full = normed.shape[0]
    n = 512
    part = lambda w, col: pl.BlockSpec((n, w), lambda i, *_: (i, col))
    return pl.pallas_call(
        shared_grad_body,
        grid_spec=pltpu.PrefetchScalarGridSpec(
            num_scalar_prefetch=1,
            grid=(full // n,),
            in_specs=[part(1024, 0), part(128, 0), part(128, 3), part(128, 4)]
            + [whole((1024, 128))],
            out_specs=whole((1024, 512)),
            scratch_shapes=[pltpu.VMEM((1024, 384), F32)],
        ),
        out_shape=jax.ShapeDtypeStruct((1024, 512), BF),
        compiler_params=params(),
        cost_estimate=SMALL_COST,
        name="shared_grad",
    )(bounds, normed, da, ds, ds, turned)


def alone_grad_body(bounds, normed, da1, da2, ds, dt_grad, kept, sent, turned, acc):
    @pl.when(pl.program_id(0) == 0)
    def _():
        acc[...] = jnp.zeros_like(acc)

    count = da1.shape[0]
    cols = jnp.concatenate([dt_grad[...], jnp.zeros((120, count), F32)], axis=0).T
    last = jnp.where(lanes((1, 128)) < 64, da2[...].astype(F32), pltpu.roll(cols, 64, 1))
    acc[...] += dot_at(
        normed[...], jnp.concatenate([last.astype(BF), ds[...], da1[...]], axis=1)
    )

    @pl.when(pl.program_id(0) == pl.num_programs(0) - 1)
    def _():
        left = lanes((1, 128)) < 64
        side = acc[:, 512:]
        turned[...] = side
        query = jnp.where(left, pltpu.roll(turned_back(side), 64, 1), 0.0)
        first = (acc[:, :128] + query).astype(BF)
        half = first.shape[0] // 2

        def write(ref, low):
            ref[:, :128] = first[low : low + half]
            ref[:, 128:] = acc[pl.ds(low, half), 128:512].astype(BF)

        @pl.when(bounds[4] == 1)
        def _():
            write(kept, 0)
            write(sent, half)

        @pl.when(bounds[4] == 0)
        def _():
            write(kept, half)
            write(sent, 0)


def alone_grad(bounds, normed, da, ds, dt_grad):
    full = normed.shape[0]
    n = 512
    part = lambda w, col: pl.BlockSpec((n, w), lambda i, *_: (i, col))
    return pl.pallas_call(
        alone_grad_body,
        grid_spec=pltpu.PrefetchScalarGridSpec(
            num_scalar_prefetch=1,
            grid=(full // n,),
            in_specs=[
                part(1024, 0),
                part(128, 1),
                part(128, 2),
                part(384, 0),
                pl.BlockSpec((8, n), lambda i, *_: (0, i)),
            ],
            out_specs=[whole((512, 512))] * 2 + [whole((1024, 128))],
            scratch_shapes=[pltpu.VMEM((1024, 640), F32)],
        ),
        out_shape=[
            jax.ShapeDtypeStruct((512, 512), BF),
            jax.ShapeDtypeStruct((512, 512), BF),
            jax.ShapeDtypeStruct((1024, 128), F32),
        ],
        compiler_params=params(),
        cost_estimate=SMALL_COST,
        name="alone_grad",
    )(bounds, normed, da, da, ds, dt_grad)


def assemble_body(bounds, p0, p1, p2, l3, r3, out):
    step = pl.program_id(0)
    for r, ref in enumerate((p0, p1, p2)):

        @pl.when(step == r)
        def _(ref=ref):
            out[:, :512] = ref[0]
            out[:, 512:] = ref[1]

    @pl.when(step == 3)
    def _():
        out[:, :512] = l3[...]
        out[:, 512:] = r3[...]


def assemble(bounds, parts):
    count = parts[0].shape[1]
    return pl.pallas_call(
        assemble_body,
        grid_spec=pltpu.PrefetchScalarGridSpec(
            num_scalar_prefetch=1,
            grid=(4,),
            in_specs=[whole(p.shape) for p in parts],
            out_specs=pl.BlockSpec((count, 1024), lambda i, b: (i ^ b[2], 0)),
        ),
        out_shape=jax.ShapeDtypeStruct((4 * count, 1024), parts[0].dtype),
        compiler_params=pltpu.CompilerParams(vmem_limit_bytes=FULL_VMEM),
        cost_estimate=SMALL_COST,
        name="assemble",
    )(bounds, *parts)


def piece_out_body(bounds, a, b, other_a, other_b, gate, up, down, mix, att):
    first = bounds[3] == 0

    def pair(own, other):
        own, other = own.astype(F32), other.astype(F32)
        return jnp.where(first, own, other), jnp.where(first, other, own)

    low, high = pair(a[...], other_a[...])
    gate[:, :256], gate[:, 256:] = low[:, :256], high[:, :256]
    up[:, :256], up[:, 256:] = low[:, 256:], high[:, 256:]
    low, high = pair(b[...], other_b[...])
    down[:256, :], down[256:, :] = low[:, :256].T, high[:, :256].T
    low, high = low[:, 256:].T, high[:, 256:].T
    mix[:192, :], mix[192:, :] = low[:192], high[:192]
    att[:64, :], att[64:, :] = low[192:], high[192:]


def piece_out(bounds, both, other):
    n = 256
    row = pl.BlockSpec((n, 512), lambda i, *_: (i, 0))
    second = pl.BlockSpec((n, 512), lambda i, *_: (i, 1))
    col = lambda h: pl.BlockSpec((h, n), lambda i, *_: (0, i))
    sds = jax.ShapeDtypeStruct
    return pl.pallas_call(
        piece_out_body,
        grid_spec=pltpu.PrefetchScalarGridSpec(
            num_scalar_prefetch=1,
            grid=(4,),
            in_specs=[row, second, row, second],
            out_specs=[row, row, col(512), col(384), col(128)],
        ),
        out_shape=[
            sds((1024, 512), F32),
            sds((1024, 512), F32),
            sds((512, 1024), F32),
            sds((384, 1024), F32),
            sds((128, 1024), F32),
        ],
        compiler_params=params(),
        cost_estimate=SMALL_COST,
        name="piece_out",
    )(bounds, both, both, other, other)


def alone_out_body(bounds, own, other, q, z, x, dt):
    first = bounds[3] == 0
    lane = lanes((1, 128))
    left = lane < 64
    tile = lambda ref, i: ref[:, 128 * i : 128 * i + 128].astype(F32)
    u = [jnp.where(first, tile(own, i), tile(other, i)) for i in range(4)]
    v = [jnp.where(first, tile(other, i), tile(own, i)) for i in range(4)]
    swapped = lambda value: pltpu.roll(value, 64, 1)
    q[...] = jnp.where(left, u[0], swapped(v[0]))
    x[:, :128] = u[1]
    x[:, 128:256] = jnp.where(left, u[2], swapped(v[1]))
    x[:, 256:] = jnp.where(left, swapped(v[1]), swapped(v[2]))
    z[:, :128] = u[3]
    z[:, 128:256] = jnp.where(left, swapped(u[2]), swapped(v[3]))
    z[:, 256:] = jnp.where(left, swapped(v[3]), v[2])
    dt[...] = jnp.where(lane < 3, swapped(u[0]), pltpu.roll(v[0], 67, 1)).T[:6, :]


def alone_out(bounds, own, other):
    n = 256
    row = lambda w: pl.BlockSpec((n, w), lambda i, *_: (i, 0))
    widths = [128, 384, 384]
    return pl.pallas_call(
        alone_out_body,
        grid_spec=pltpu.PrefetchScalarGridSpec(
            num_scalar_prefetch=1,
            grid=(4,),
            in_specs=[row(512), row(512)],
            out_specs=[row(w) for w in widths] + [pl.BlockSpec((6, n), lambda i, *_: (0, i))],
        ),
        out_shape=[jax.ShapeDtypeStruct((1024, w), F32) for w in widths]
        + [jax.ShapeDtypeStruct((6, 1024), F32)],
        compiler_params=params(),
        cost_estimate=SMALL_COST,
        name="alone_out",
    )(bounds, own, other)


def piece_sum_body(bounds, *refs):
    total = lambda i: (
        refs[i][...].astype(F32) + refs[i + 1][...] + refs[i + 2][...]
    ).astype(BF)
    kept, out = refs[12:]
    for group, ref in ((0, kept), (6, out)):
        ref[:, :512] = total(group)
        ref[:, 512:] = total(group + 3)


def piece_sum(bounds, a, b):
    n = 256
    keep = pl.BlockSpec((n, 512), lambda i, s: (i + 2 - 2 * s[4], 0))
    send = pl.BlockSpec((n, 512), lambda i, s: (i + 2 * s[4], 0))
    row = pl.BlockSpec((n, 1024), lambda i, s: (i, 0))
    return pl.pallas_call(
        piece_sum_body,
        grid_spec=pltpu.PrefetchScalarGridSpec(
            num_scalar_prefetch=1,
            grid=(2,),
            in_specs=[keep] * 6 + [send] * 6,
            out_specs=[row, row],
        ),
        out_shape=[jax.ShapeDtypeStruct((512, 1024), BF)] * 2,
        compiler_params=params(),
        cost_estimate=SMALL_COST,
        name="piece_sum",
    )(bounds, *a, *b, *a, *b)


def relay_body(first, second, kept, got, left, right, total):
    left[...] = first[0]
    right[...] = second[0]
    total[...] = (kept[...].astype(F32) + got[...]).astype(BF)


def relay(first, second, kept, got):
    n = first.shape[1] // 2
    row = pl.BlockSpec((n, 512), lambda i: (i, 0))
    half = lambda k: pl.BlockSpec((1, n, 512), lambda i: (k, i, 0))
    return pl.pallas_call(
        relay_body,
        grid=(2,),
        in_specs=[half(0), half(1), row, row],
        out_specs=[row] * 3,
        out_shape=[jax.ShapeDtypeStruct((2 * n, 512), BF)] * 3,
        compiler_params=pltpu.CompilerParams(vmem_limit_bytes=FULL_VMEM),
        cost_estimate=SMALL_COST,
        name="relay",
    )(first, second, kept, got)


def halves_body(first, second, left, right):
    left[...] = first[...]
    right[...] = second[...]


def pack_halves(first, second):
    n = 256
    out = pl.BlockSpec((n, 512), lambda i: (i, 0))
    return pl.pallas_call(
        halves_body,
        grid=(4,),
        in_specs=[out, pl.BlockSpec((n, 512), lambda i: (i, 1))],
        out_specs=[out, out],
        out_shape=[jax.ShapeDtypeStruct((1024, 512), BF)] * 2,
        compiler_params=pltpu.CompilerParams(vmem_limit_bytes=FULL_VMEM),
        cost_estimate=SMALL_COST,
        name="pack_halves",
    )(first, second)


def pair_sum_body(a, b, c, d, first, second):
    first[...] = (a[...].astype(F32) + b[...]).astype(BF)
    second[...] = (c[...].astype(F32) + d[...]).astype(BF)


def pair_sum(a, b, c, d):
    n = a.shape[0] // 2
    row = pl.BlockSpec((n, a.shape[1]), lambda i: (i, 0))
    return pl.pallas_call(
        pair_sum_body,
        grid=(2,),
        in_specs=[row] * 4,
        out_specs=[row, row],
        out_shape=[jax.ShapeDtypeStruct(a.shape, BF)] * 2,
        compiler_params=pltpu.CompilerParams(vmem_limit_bytes=FULL_VMEM),
        cost_estimate=SMALL_COST,
        name="pair_sum",
    )(a, b, c, d)


def swap(value, step):
    return lax.ppermute(value, "tensor", [(i, i ^ step) for i in range(4)])


def twin(value):
    return lax.ppermute(value, "ctx", [(0, 1), (1, 0)])


def exchange(value):
    return lax.all_to_all(value, ("ctx", "tensor"), 0, 0, tiled=True)


def dp_swap(value, step):
    return lax.ppermute(value, "dp", [(i, i ^ step) for i in range(4)])


MIDDLE = [(1, 2), (2, 1), (0, 3), (3, 0)]
NEAR = [(0, 1), (1, 0), (2, 3), (3, 2)]


class DpSum:
    def __init__(self):
        self.four = lax.axis_size("dp") == 4
        place = lax.axis_index("dp")
        self.inner = (place == 1) | (place == 2)

    def first(self, kept, sent):
        if self.four:
            return lax.ppermute(sent, "dp", NEAR)
        self.rest = lax.psum(sent, "dp")
        return lax.psum(kept, "dp")

    def middle(self, value):
        return lax.ppermute(value, "dp", MIDDLE) if self.four else value

    def last(self, value):
        return lax.ppermute(value, "dp", NEAR) if self.four else value

    def add(self, kept, got):
        return plus(kept, got) if self.four else got

    def end(self, kept, got):
        if not self.four:
            return jnp.concatenate([kept, self.rest], axis=0)
        return jnp.concatenate(
            [jnp.where(self.inner, kept, got), jnp.where(self.inner, got, kept)], axis=0
        )


def together(*values):
    return lax.optimization_barrier(values)


def after(value, *before):
    return lax.optimization_barrier((value, before))[0]


def plus(a, b):
    return (a.astype(F32) + b.astype(F32)).astype(BF)


def block_at(value, index, count):
    return lax.dynamic_slice_in_dim(value, index * count, count, 0)


def merge_body(bounds, own, got, *outs):
    total = (own[...].astype(F32) + got[...].astype(F32)).astype(BF)
    for i in range(4):

        @pl.when(pl.program_id(0) == i)
        def _(i=i):
            outs[2 * i][...] = total[:, :512]
            outs[2 * i + 1][...] = total[:, 512:]


def merge(bounds, own, got):
    count = own.shape[0] // 4
    block = pl.BlockSpec((count, 1024), lambda i, b: (i ^ b[2], 0))
    once = pl.BlockSpec((count, 512), lambda i, b: (0, 0), pipeline_mode=pl.Buffered(1))
    return pl.pallas_call(
        merge_body,
        grid_spec=pltpu.PrefetchScalarGridSpec(
            num_scalar_prefetch=1,
            grid=(4,),
            in_specs=[block, block],
            out_specs=[once] * 8,
        ),
        out_shape=[jax.ShapeDtypeStruct((count, 512), BF)] * 8,
        compiler_params=params(),
        cost_estimate=SMALL_COST,
        name="merge",
    )(bounds, own, got)


def finish_body(bounds, l0, r0, l1, r1, l2, r2, tok, dhid, gain, out):
    three = lambda a, b, c: (a[...].astype(F32) + b[...]) + c[...]
    grad = jnp.concatenate([three(l0, l1, l2), three(r0, r1, r2)], axis=1)
    values = tok[...].astype(F32)
    scale = lax.rsqrt(jnp.mean(values * values, axis=-1, keepdims=True) + EPSILON)
    weighted = grad * gain[...]
    mean = jnp.mean(weighted * values, axis=-1, keepdims=True)
    total = dhid[...] + scale * weighted - values * (scale * scale * scale * mean)
    out[0] = total[:, :512].astype(BF)
    out[1] = total[:, 512:].astype(BF)


def finish(bounds, state, tokens, dhid, gain):
    count = dhid.shape[0]
    n = count // 2
    half = pl.BlockSpec((n, 512), lambda i, b: (i, 0))
    row = pl.BlockSpec((n, 1024), lambda i, b: (i, 0))
    return pl.pallas_call(
        finish_body,
        grid_spec=pltpu.PrefetchScalarGridSpec(
            num_scalar_prefetch=1,
            grid=(2,),
            in_specs=[half] * 6
            + [pl.BlockSpec((n, 1024), lambda i, b: (2 * b[2] + i, 0)), row, whole((1, 1024))],
            out_specs=pl.BlockSpec((2, n, 512), lambda i, b: (0, i, 0)),
        ),
        out_shape=jax.ShapeDtypeStruct((2, count, 512), BF),
        compiler_params=params(),
        cost_estimate=SMALL_COST,
        name="finish",
    )(bounds, *state, tokens, dhid, gain)


def rope_tables(count):
    exponent = np.arange(0, HEAD_SIZE, 2).astype(np.float32) / np.float32(HEAD_SIZE)
    frequency = (np.float32(ROPE_BASE) ** (-exponent)).astype(np.float32)
    angles = np.arange(count).astype(np.float32)[:, None] * frequency[None, :]
    angles = np.concatenate([angles] * 4, axis=1)
    return (np.cos(angles).astype(np.float32), np.sin(angles).astype(np.float32))


def local(
    tokens, doc_ids, norm_gain, q_proj, key_value_weight, o_proj, z_proj, x_proj, dt_proj,
    bc_proj, conv_x, xconv_bias, conv_bc, bcconv_bias, dt_bias, a_log, skip_gain, gated_gain,
    out_proj, mlp_gain, gate_proj, up_proj, down_proj, out_grad,
):
    t, c = lax.axis_index("tensor"), lax.axis_index("ctx")
    own_tokens, grad_out = tokens[0], out_grad[0]
    own = own_tokens.shape[0]
    full = 2 * own
    mine = own // 4
    other_tokens = twin(own_tokens)

    def cols(w):
        n = w.shape[-1] // 2
        return lax.dynamic_slice_in_dim(w, c * n, n, w.ndim - 1)

    def rows(w):
        return block_at(w, c, w.shape[0] // 2)

    here = jnp.stack([jnp.zeros((), jnp.int32), jnp.zeros((), jnp.int32), t, c]).astype(jnp.int32)
    weight, pack0 = prepare(
        here, gate_proj, up_proj, down_proj, out_proj, o_proj, key_value_weight, q_proj,
        x_proj, z_proj, dt_proj.T, bc_proj,
    )
    weight, pack0, doc_ids = together(weight, pack0, doc_ids)
    pack1, pack2 = swap(pack0, 1), swap(pack0, 2)
    docs = doc_ids[0]
    place_dp = lax.axis_index("dp")
    inner = (place_dp == 1) | (place_dp == 2) | (lax.axis_size("dp") != 4)
    bounds = jnp.stack([jnp.sum(docs < 1), jnp.sum(docs < 2), t, c, inner]).astype(jnp.int32)
    own_gain = rows(gated_gain)
    gain0 = jnp.concatenate([own_gain, jnp.ones((64,), F32)])
    gain0 = jnp.broadcast_to(gain0[None, None], (8, 1, 256))

    cos, sin = rope_tables(full)
    cos, sin = jnp.asarray(cos), jnp.asarray(sin)
    steps = own // PROJ_ROWS
    own_off = jnp.reshape(c * steps, (1,)).astype(jnp.int32)
    other_off = jnp.reshape((1 - c) * steps, (1,)).astype(jnp.int32)
    gain_row = norm_gain[None]
    first = project(own_off, own_tokens, gain_row, weight, cos, sin)
    normed, qp, kv, xbc, z, dt_raw = project(
        other_off, other_tokens, gain_row, weight, cos, sin, before=first
    )

    pad = lambda v: jnp.zeros(v.shape[:-1] + (64,), F32)
    cx, cb = cols(conv_x), cols(xconv_bias)
    taps = jnp.concatenate([cx, pad(cx), conv_bc], axis=1)
    taps = jnp.concatenate([taps, jnp.zeros_like(taps)], axis=0)
    bias = jnp.concatenate([cb, pad(cb), bcconv_bias])[None]
    head = jnp.stack([cols(dt_bias), -jnp.exp(cols(a_log))], axis=1)
    head = jnp.pad(head, ((0, 5), (0, 126)))
    skip = jnp.pad(jnp.repeat(cols(skip_gain), MP), (0, 64))[None]
    xbc, gain0 = together(xbc, gain0)
    gains = exchange(gain0)
    g01, g2, y, states, pre = scan_forward(bounds, xbc, z, dt_raw, taps, bias, head, skip)
    g2, g01, pack1, pack2, gains = together(g2, g01, pack1, pack2, gains)
    left3, right3 = pack_halves(pack1, pack2)
    qp, left3, right3, g01 = together(qp, left3, right3, g01)
    left3, right3 = swap(left3, 2), swap(right3, 1)
    near = [pack0, pack1, pack2]
    far = [twin(v) for v in near]
    g_rows = exchange(g01.reshape(8, mine, 128))
    tile, keep = attend(bounds, qp, kv, g2)
    tile, g_rows, far, left3, right3 = together(tile, g_rows, far, left3, right3)
    h_rows = exchange(tile.reshape(8, mine, 128))
    packs = near + [left3, right3] + far + [twin(left3), twin(right3)]

    res = row_stage(bounds, g_rows, h_rows, own_tokens, grad_out, mlp_gain[None], gains, packs)
    layer_rows, two, dmix, dhid = res[0:4]
    act, dgu, gn = list(res[4:6]), list(res[6:8]), list(res[8:10])
    mlp_part, gain_part = res[12:14]
    grad_rows = block_at(grad_out, t, mine)
    dn, late = exchange(res[10]), res[11]
    far_w = weight_stage(two, grad_rows, dmix, dgu[1], act[1], gn[1])
    far_w = [twin(v) for v in far_w]
    near_w = weight_stage(two, grad_rows, dmix, dgu[0], act[0], gn[0], *far_w)
    dn, near_w, late = together(dn, near_w, late)
    sum_a, sum_b = near_w[:4], near_w[4:]
    late = exchange(late)

    a3, b3 = swap(sum_a[3], 1), swap(sum_b[3], 2)
    a1, b2 = swap(sum_a[1], 1), swap(sum_b[2], 2)
    da = attend_back(bounds, qp, kv, keep, dn, cos, sin)
    da, a3, b3, late = together(da, a3, b3, late)
    a_next, b_next = pair_sum(sum_a[2], a3, sum_b[1], b3)
    xbc, a_next, b_next = together(xbc, a_next, b_next)
    a_next, b_next = swap(a_next, 2), swap(b_next, 1)
    own_gain_row = jnp.pad(own_gain, (0, 64))[None]
    zeros = [
        jnp.zeros((256, 128), F32),
        jnp.zeros((8, 512), F32),
        jnp.zeros((8, 512), F32),
        jnp.zeros((16, CHUNK), F32),
    ]
    back = lambda part, carry, made, data: scan_back(
        part, carry, made, bounds, data, pre, z, y, dt_raw, states, late, dn, taps, head, skip,
        own_gain_row,
    )
    ds, dt_grad, *carry = back(0, zeros, [], xbc)
    ds, a1, b2, a_next, b_next = together(ds, a1, b2, a_next, b_next)
    kept, out = piece_sum(bounds, (sum_a[0], a1, a_next), (sum_b[0], b2, b_next))
    sums, single = DpSum(), DpSum()
    xbc, out, kept, layer_rows = together(xbc, out, kept, layer_rows)
    got = sums.first(kept, out)
    layer1, layer2 = swap(layer_rows, 1), swap(layer_rows, 2)
    conv_carry = (carry[2], carry[3], carry[0], carry[1])
    ds, dt_grad, conv_acc, head_acc, _, _ = back(1, conv_carry, [ds, dt_grad], xbc)
    ds, got, layer1, layer2 = together(ds, got, layer1, layer2)

    kept = sums.add(kept, got)
    parts = [block_at(kept, i, kept.shape[0] // 4) for i in range(4)]
    layer3 = [layer1[0], layer2[1]]
    ds, layer3, parts, kept = together(ds, layer3, parts, kept)
    got0 = sums.middle(parts[0])
    layer3 = [swap(layer3[0], 2), swap(layer3[1], 1)]
    grad_other, gain_other = input_grad(other_off, da, ds, dt_grad, weight, normed)
    grad_other, ds, layer3, got0 = together(grad_other, ds, layer3, got0)
    four = lax.axis_size("dp") == 4
    sent = twin(grad_other)
    got1 = sums.middle(parts[1])
    grad_own, gain_own = input_grad(own_off, da, ds, dt_grad, weight, normed)
    grad_own, sent, got1 = together(grad_own, sent, got1)
    got2 = sums.middle(parts[2])
    pieces = merge(bounds, grad_own, sent)
    ds, pieces = together(ds, pieces)
    l0, r0, l1, r1, l2, r2, l3, r3 = pieces
    low_rows = sums.add(jnp.concatenate(parts[:2]), jnp.concatenate([got0, got1]))
    heads = jnp.concatenate(
        [
            jnp.sum(conv_acc[5, :192].reshape(3, 64), axis=1),
            jnp.sum(head_acc[0:3], axis=1),
            jnp.sum(head_acc[8:11], axis=1),
        ]
    )
    place = c * 4 + t
    own_small = jnp.pad(jnp.concatenate([conv_acc[:5, :192].reshape(-1), heads]), (0, 55))
    at_own = lax.dynamic_update_slice_in_dim(
        jnp.zeros((8, 1024), F32), own_small[None], place, 0
    )
    norm_part = (gain_other[0] + gain_own[0]) / norm_gain
    flat = jnp.concatenate(
        [at_own.reshape(-1), gain_part.reshape(-1), conv_acc[:5, 256:].reshape(-1), mlp_part[0]]
        + [norm_part]
    )
    flat = jnp.pad(flat, (0, (-flat.shape[0]) % 1024)).reshape(1, -1, 128)
    flat = jnp.broadcast_to(flat, (8,) + flat.shape[1:])
    ds, l0, r0, l1, r1, l2, r2, l3, r3, flat, low_rows, got2 = together(
        ds, l0, r0, l1, r1, l2, r2, l3, r3, flat, low_rows, got2
    )
    l3, r3 = swap(l3, 1), swap(r3, 2)
    got3 = sums.middle(parts[3])
    flat = exchange(flat)
    alone, out, turned = alone_grad(bounds, normed, da, ds, dt_grad)
    alone, out, turned, l3, r3, got3, flat = together(alone, out, turned, l3, r3, got3, flat)
    l2, r1 = pair_sum(l2, l3, r1, r3)
    flat = jnp.sum(flat, axis=0)
    high_rows = sums.add(jnp.concatenate(parts[2:]), jnp.concatenate([got2, got3]))
    count = alone.shape[0]
    if four:
        out = jnp.concatenate([out, low_rows[:, :512], low_rows[:, 512:]])
    l1, r2, l2, r1, flat, out, alone, high_rows, turned = together(
        l1, r2, l2, r1, flat, out, alone, high_rows, turned
    )
    l2, r1 = swap(l2, 2), swap(r1, 1)
    l1, r2 = swap(l1, 1), swap(r2, 2)
    got = single.first(alone, out)
    shared = shared_grad(bounds, normed, da, ds, turned)
    l1, r2, l2, r1, got, shared = together(l1, r2, l2, r1, got, shared)
    if four:
        half = count + low_rows.shape[0]
        got_low = jnp.concatenate([got[count:half], got[half:]], axis=1)
    else:
        got_low = low_rows
    got_alone = got[:count]
    token_rows = finish(bounds, [l0, r0, l1, r1, l2, r2], own_tokens, dhid, norm_gain[None])
    alone = single.add(alone, got_alone)
    shared = shared.reshape(8, 128, 512)
    token_rows, alone, high_rows, flat, shared, layer_rows, layer1, layer2, layer3 = together(
        token_rows, alone, high_rows, flat, shared, layer_rows, layer1, layer2, layer3
    )
    tok1, tok2 = swap(token_rows, 1), swap(token_rows, 2)
    got = single.middle(alone)
    got_high = sums.last(high_rows)
    flat_got = dp_swap(flat, 1) if four else lax.psum(flat, "dp")
    shared = exchange(shared)
    layer_out = assemble(bounds, [layer_rows, layer1, layer2, *layer3])
    tok1, tok2, got, flat_got, got_high, shared, layer_out = together(
        tok1, tok2, got, flat_got, got_high, shared, layer_out
    )
    both = sums.end(
        jnp.concatenate([low_rows, high_rows]), jnp.concatenate([got_low, got_high])
    )
    shared = jnp.sum(shared.astype(F32), axis=0).astype(BF)
    if four:
        shared = jnp.broadcast_to(shared[None], (4, 128, 512))
    flat = flat + flat_got if four else flat_got
    *tok3, total = relay(tok1, tok2, alone, got)
    alone = total if four else single.add(alone, got)
    tok3, alone, flat, both, shared = together(tok3, alone, flat, both, shared)
    twin_piece = twin(both)
    tok3 = [swap(tok3[0], 2), swap(tok3[1], 1)]
    got = single.last(alone)
    flat_got = dp_swap(flat, 2) if four else flat
    if four:
        shared = lax.all_to_all(shared, "dp", 0, 0, tiled=True)
    else:
        shared = lax.psum(shared.astype(F32), "dp")[None]
    outs = piece_out(bounds, both, twin_piece)
    tok3, got, flat_got, outs, shared = together(tok3, got, flat_got, outs, shared)
    alone = single.end(alone, got)
    shared = jnp.sum(shared.astype(F32), axis=0).astype(BF)
    shared = jnp.broadcast_to(shared[None], (8, 128, 512))
    alone, tok3, shared = together(alone, tok3, shared)
    alone_twin = twin(alone)
    shared = exchange(shared)
    tokens_grad = assemble(bounds, [token_rows, tok1, tok2, *tok3])
    alone, alone_twin, tokens_grad = together(alone, alone_twin, tokens_grad)
    shared = shared.reshape(1024, 512).astype(F32)
    kv_out, bc_out = shared[:, :256], shared[:, 256:]
    q_out, z_out, x_out, dt_out = alone_out(bounds, alone, alone_twin)
    flat = flat + flat_got if four else flat_got
    flat = flat.reshape(-1)
    norm_sum = flat[12544:13568]
    small = flat[:8192].reshape(8, 1024)
    gain_sum = flat[8192:10240].reshape(8, 256)
    bc_sum = flat[10240:11520].reshape(5, 256)
    mlp_sum = flat[11520:12544]
    both_cores = lambda v: jnp.stack([lax.dynamic_index_in_dim(v, k * 4 + t, 0, False) for k in range(2)])
    small = both_cores(small)
    gain_sum = both_cores(gain_sum)[:, :192].reshape(-1)
    conv_small = small[:, :960].reshape(2, 5, 192)
    conv_small = jnp.concatenate([conv_small[0], conv_small[1]], axis=1)
    head_small = small[:, 960:969].reshape(2, 3, 3)
    per_head_sum = lambda i: head_small[:, i].reshape(-1)

    gate_out, up_out, down_out, mix_out, att_out = outs
    return (
        layer_out[None],
        tokens_grad[None],
        norm_sum,
        q_out,
        kv_out,
        att_out,
        z_out,
        x_out,
        dt_out.T,
        bc_out,
        conv_small[:4],
        conv_small[4],
        bc_sum[:4],
        bc_sum[4],
        per_head_sum(2),
        per_head_sum(1),
        per_head_sum(0),
        gain_sum,
        mix_out,
        mlp_sum,
        gate_out,
        up_out,
        down_out,
    )


def solution(mesh):
    placed = (
        P("dp", "ctx", None),
        P("dp", None),
        P(),
        P(None, "tensor"),
        P(),
        P("tensor", None),
        P(None, "tensor"),
        P(None, "tensor"),
        P(None, "tensor"),
        P(),
        P(None, "tensor"),
        P("tensor"),
        P(),
        P(),
        P("tensor"),
        P("tensor"),
        P("tensor"),
        P("tensor"),
        P("tensor", None),
        P(),
        P(None, "tensor"),
        P(None, "tensor"),
        P("tensor", None),
        P("dp", "ctx", None),
    )
    return jax.shard_map(
        local,
        mesh=mesh,
        in_specs=placed,
        out_specs=(
            P("dp", "ctx", None),
            P("dp", "ctx", None),
            P(),
            P(None, "tensor"),
            P(),
            P("tensor", None),
            P(None, "tensor"),
            P(None, "tensor"),
            P(None, "tensor"),
            P(),
            P(None, "tensor"),
            P("tensor"),
            P(),
            P(),
            P("tensor"),
            P("tensor"),
            P("tensor"),
            P("tensor"),
            P("tensor", None),
            P(),
            P(None, "tensor"),
            P(None, "tensor"),
            P("tensor", None),
        ),
        check_vma=False,
    )
```
